32 devices in a mesh: wide: 8 (over y, x, core), narrow: 4 (over z).
Axes of the slice: x: 2, y: 2, z: 4, core: 2. Of those that a mesh axis runs over, the one named last changes fastest.
Arguments:
- token_ids: int32 [32, 512], P('wide'), may hold values from 0 to 30521
- doc_ids: int32 [32, 512], P(('wide', 'narrow')), may hold values from 0 to 5, never falling along the last dimension, each value on 1 to 256 neighbouring positions
- mlm_pos: int32 [32, 80], P(('wide', 'narrow')), may hold values from 0 to 511
- mlm_labels: int32 [32, 80], P('wide'), may hold values from 0 to 30521
- mlm_valid: int32 [32, 80], P('wide'), may hold values from 0 to 1, as said below
- table: float32 [30528, 1024], P('narrow', 'wide')
- table_m: float32 [30528, 1024], P('narrow', 'wide'), may hold values from -0.0012207031 to 0.0012207031
- table_v: float32 [30528, 1024], P('narrow', 'wide'), may hold values from 3.90625e-08 to 1.5625e-07
- small: float32 [528, 1024], replicated
- small_m: float32 [528, 1024], replicated, may hold values from -0.0012207031 to 0.0012207031
- small_v: float32 [528, 1024], replicated, may hold values from 3.90625e-08 to 1.5625e-07
- layer: float32 [1024, 12288], P('narrow', 'wide'), may hold values from -0.1875 to 0.1875
- layer_m: float32 [1024, 12288], P('narrow'), may hold values from -0.0012207031 to 0.0012207031
- layer_v: float32 [1024, 12288], P('narrow', 'wide'), may hold values from 3.90625e-08 to 1.5625e-07
- worker_err: float32 [8, 1024, 12288], P('wide', 'narrow'), may hold values from -0.00036621094 to 0.00036621094
- server_err: float32 [1024, 12288], P('narrow', 'wide'), may hold values from -0.00036621094 to 0.00036621094
Outputs:
- loss: float32 [2], replicated
- new_table: float32 [30528, 1024], P('narrow', 'wide')
- new_table_m: float32 [30528, 1024], P('narrow', 'wide')
- new_small: float32 [528, 1024], replicated
- new_small_m: float32 [528, 1024], replicated
- new_layer: float32 [1024, 12288], P('narrow', 'wide')
- new_layer_m: float32 [1024, 12288], P('narrow')
- new_worker_err: float32 [8, 1024, 12288], P('wide', 'narrow')
- new_server_err: float32 [1024, 12288], P('narrow', 'wide')
- norms: float32 [2, 6], replicated
The draws below stay inside these ranges and needn't reach their ends.
Inputs may be any that keep to these rules, and one draw needn't show every extreme that they name: `doc_ids`: document numbers never fall along a packed row. `mlm_valid`: the first masked slot of every packed row is valid.
All inputs are finite; a program needn't handle non-finite values. Where the reference program divides by a largest or mean magnitude, that divisor is 1e-20 or more.
Results may differ from the reference program's by a relative error of at most 0.012.
Values may be sent and summed in bfloat16 or wider, within the bound.
No kernel may reach another device: no remote copies, remote signals or barrier semaphores. Data moves between devices by JAX's collectives and lax.ppermute only.
A program may use at most 384 MiB of HBM per device.

```python
import math
import jax
import jax.numpy as jnp
import numpy as np
from jax import lax

D = 1024
HEADS = 16
HEAD = 64
FF = 4096
VREAL = 30522
L = 512
MPS = 80
SEQ_DEV = 1
V = 30528
SEQS = 32
WCOLS = 12288
SROWS = 528
WORKERS = 8
N_WIDE = 8
N_NARROW = 4


def draw_mlm_valid(key, part):
    key = jax.random.fold_in(key, 5)
    rolls = jax.random.randint(key, (SEQS, MPS), 0, 120)
    device = jnp.arange(SEQS) // SEQ_DEV
    wide_pos = device // N_NARROW
    narrow_pos = device % N_NARROW
    limit = 20 + 40 * wide_pos // max(N_WIDE - 1, 1) + 40 * narrow_pos // max(N_NARROW - 1, 1)
    keep = rolls < limit[:, None]
    first = (jnp.arange(MPS) == 0)[None]
    return (keep | first).astype(jnp.int32)


def draw_table(key, part):
    key = jax.random.fold_in(key, 7)
    place = jnp.arange(V, dtype=jnp.float32)[:, None] / (V - 1)
    noise = jax.random.normal(key, (V, D), jnp.float32)
    rise = 1.0 + 2.0 * place
    return noise * rise * D ** (-0.5)


def draw_small(key, part):
    key = jax.random.fold_in(key, 9)
    noise = jax.random.normal(key, (SROWS, D), jnp.float32)
    row = jnp.arange(SROWS)[:, None]
    base = L + 2
    gain_row = (row == base) | (row == base + 2) | (row == base + 4)
    scale = jnp.where(row < base, 0.05, 0.1)
    shift = jnp.where(gain_row, 1.0, 0.0)
    return shift + scale * noise


def set_ends(result, own_key, low, high):
    spot = [jax.random.randint(jax.random.fold_in(own_key, axis), (), 0, length) for axis, length in enumerate(result.shape)]
    main_axis = result.shape.index(max(result.shape))
    beside = spot[:main_axis] + [(spot[main_axis] + 1) % result.shape[main_axis]] + spot[main_axis + 1:]
    return result.at[tuple(spot)].set(low).at[tuple(beside)].set(high)


def block_scale(stream_key, dims, cuts, least, largest):
    factor_of, own = 1.0, jax.random.fold_in(stream_key, 6)
    for position, blocks in cuts:
        draws = jnp.exp(jax.random.uniform(jax.random.fold_in(own, position), (blocks,), jnp.float32, least / len(cuts), largest / len(cuts)))
        factor_of = factor_of * jnp.repeat(draws, dims[position] // blocks).reshape([-1 if axis == position else 1 for axis in range(len(dims))])
    return factor_of


def rank_bounds(amount, skew):
    loads = [(1 << 20) // math.isqrt(standing ** skew) + 1 for standing in range(1, amount + 1)]
    width = 1 + sum(loads) // (1 << 30)
    return np.cumsum(np.array([max(1, weight // width) for weight in loads]))


def skewed_ids(key, dims, number_of, lean):
    grid = rank_bounds(number_of, lean)
    lot = jax.random.randint(jax.random.fold_in(key, 1), dims, 0, int(grid[number_of - 1]))
    grade = jnp.searchsorted(jnp.asarray(grid, jnp.int32), lot, side="right")
    return jax.random.permutation(jax.random.fold_in(key, 2), number_of)[grade].astype(jnp.int32)


def length_profile(amount, total, bound, skew):
    weights = [(1 << 20) // math.isqrt(standing ** skew) + 1 for standing in range(2, amount + 1)]
    spare, given = total - bound - (amount - 1), [1] * (amount - 1)
    while spare > 0:
        candidates = [i for i in range(amount - 1) if given[i] < bound]
        whole, left = sum([weights[i] for i in candidates]), spare
        for i in candidates:
            addition = min(bound - given[i], max(1, left * weights[i] // whole), spare)
            given[i] = given[i] + addition
            spare = spare - addition
    return np.array([bound] + given)


def uneven_parts(stream_key, count, total, reach, slope):
    if count == 2:
        one = jax.random.randint(stream_key, (), max(1, total - reach), min(reach, total - 1) + 1)
        return jnp.stack([one, total - one])
    tallies = jnp.asarray(length_profile(count, total, reach, slope), jnp.int32)
    twos = (count - 1) // 2
    giver, taker = tallies[1:1 + 2 * twos:2], tallies[2:2 + 2 * twos:2]
    room = jnp.minimum(giver - 1, reach - taker)
    shifted = jax.random.randint(jax.random.fold_in(stream_key, 1), (twos,), 0, 1 << 20) % (room + 1)
    tallies = tallies.at[1:1 + 2 * twos:2].set(giver - shifted).at[2:2 + 2 * twos:2].set(taker + shifted)
    return tallies[jax.random.permutation(jax.random.fold_in(stream_key, 2), count)]


def gaussian(stream_key, dims, scale, most, pieces=(), kind=jnp.bfloat16):
    level = block_scale(stream_key, dims, pieces, -0.22, 0.18) if pieces else 1.0
    result = jax.random.normal(stream_key, dims, jnp.float32) * scale * level
    return jnp.minimum(jnp.maximum(result, -most), most).astype(kind)


def setup_inputs(seed: int = 0) -> dict:
    key_list = jax.random.split(jax.random.key(seed), 17)
    token_ids = set_ends(skewed_ids(key_list[0], (SEQS, L), VREAL, 2), jax.random.fold_in(key_list[0], 3), 0, VREAL - 1).astype(jnp.int32)
    doc_ids = jax.vmap(lambda own: jnp.searchsorted(jnp.cumsum(uneven_parts(own, 6, L, L // 2, 1)), jnp.arange(L), side="right"))(jax.random.split(key_list[1], SEQS)).reshape((SEQS, L)).astype(jnp.int32)
    mlm_pos = set_ends(jax.random.randint(key_list[2], (SEQS, MPS), 0, L), jax.random.fold_in(key_list[2], 1), 0, L - 1).astype(jnp.int32)
    mlm_labels = set_ends(skewed_ids(key_list[3], (SEQS, MPS), VREAL, 2), jax.random.fold_in(key_list[3], 3), 0, VREAL - 1).astype(jnp.int32)
    mlm_valid = draw_mlm_valid(jax.random.fold_in(key_list[16], 71), 0)
    table = draw_table(jax.random.fold_in(key_list[16], 71), 0)
    table_m = gaussian(key_list[6], (V, D), (0.01 / (SEQS * MPS) ** 0.5), 0.0012207031, ((0, 4), (1, 8)), jnp.float32)
    table_v = jnp.clip(jnp.exp(math.log(1.56249996052793e-07) - 1.3862944 * jax.random.uniform(key_list[7], (V, D), jnp.float32) ** block_scale(key_list[7], (V, D), ((0, 4), (1, 8)), -0.2, 0.2)), 3.906249901319825e-08, 1.56249996052793e-07)
    small = draw_small(jax.random.fold_in(key_list[16], 71), 0)
    small_m = gaussian(key_list[9], (SROWS, D), (0.01 / (SEQS * MPS) ** 0.5), 0.0012207031, (), jnp.float32)
    small_v = jnp.clip(jnp.exp(jax.random.uniform(key_list[10], (SROWS, D), jnp.float32, math.log(3.906249901319825e-08), math.log(1.56249996052793e-07))), 3.906249901319825e-08, 1.56249996052793e-07)
    layer = gaussian(key_list[11], (D, WCOLS), D ** -0.5, 0.1875, ((0, 4), (1, 8)), jnp.float32)
    layer_m = gaussian(key_list[12], (D, WCOLS), (0.01 / (SEQS * MPS) ** 0.5), 0.0012207031, ((0, 4),), jnp.float32)
    layer_v = jnp.clip(jnp.exp(math.log(1.56249996052793e-07) - 1.3862944 * jax.random.uniform(key_list[13], (D, WCOLS), jnp.float32) ** block_scale(key_list[13], (D, WCOLS), ((0, 4), (1, 8)), -0.2, 0.2)), 3.906249901319825e-08, 1.56249996052793e-07)
    worker_err = gaussian(key_list[14], (WORKERS, D, WCOLS), (0.003 / (SEQS * MPS) ** 0.5), 0.00036621094, ((0, 8), (1, 4)), jnp.float32)
    server_err = gaussian(key_list[15], (D, WCOLS), (0.003 / (SEQS * MPS) ** 0.5), 0.00036621094, ((0, 4), (1, 8)), jnp.float32)
    return dict(token_ids=token_ids, doc_ids=doc_ids, mlm_pos=mlm_pos, mlm_labels=mlm_labels, mlm_valid=mlm_valid, table=table, table_m=table_m, table_v=table_v, small=small, small_m=small_m, small_v=small_v, layer=layer, layer_m=layer_m, layer_v=layer_v, worker_err=worker_err, server_err=server_err)


@jax.custom_vjp
def low(v):
    return lax.optimization_barrier(v.astype(jnp.bfloat16)).astype(jnp.float32)

@jax.custom_vjp
def low_back(v):
    return v

def low_keep(v):
    return (low(v), None)

def low_pass(kept, grad):
    return (grad,)

def back_keep(v):
    return (v, None)

def back_low(kept, grad):
    return (low(grad),)
low.defvjp(low_keep, low_pass)
low_back.defvjp(back_keep, back_low)
HIGH = lax.Precision.HIGHEST
LN_EPS = 1e-12
BETA = 0.9
DECAY = 0.01
RATE = 0.25
OPT_EPS = 1e-06
MAG_EPS = 1e-08

def norm_rows(x, gain, shift):
    mean = lax.optimization_barrier(jnp.mean(x, axis=-1, keepdims=True))
    cent = x - mean
    var = lax.optimization_barrier(jnp.mean(cent * cent, axis=-1, keepdims=True))
    return cent * lax.rsqrt(var + LN_EPS) * gain + shift

def sequence_loss(params, ids, docs, mpos, labels, valid, count):
    table, small, layer = params
    tlow = low(table)
    wlow = low(layer)
    base = L + 2
    rows = low_back(tlow[ids])
    seg = jnp.where((docs % 2 == 0)[:, None], small[L][None], small[L + 1][None])
    x0 = norm_rows(rows + small[0:L] + seg, small[base], small[base + 1])
    act = low(x0)
    bias = jnp.concatenate([small[base + 6], jnp.zeros((D,), small.dtype), small[base + 7]])
    qkv = low(low_back(jnp.dot(act, wlow[:, 0:3 * D], precision=HIGH) + bias))
    heads = qkv.reshape(L, 3, HEADS, HEAD)
    raw = low_back(jnp.einsum('qhd,khd->hqk', heads[:, 0], heads[:, 1], precision=HIGH) * 0.125)
    same = (docs[:, None] == docs[None, :])[None]
    scores = jnp.where(same, raw, -1000000000.0)
    top = lax.optimization_barrier(jnp.max(scores, axis=-1, keepdims=True))
    lse = top + jnp.log(lax.optimization_barrier(jnp.sum(jnp.exp(scores - top), axis=-1, keepdims=True)))
    prob = low(jnp.exp(scores - lse))
    out = jnp.einsum('hqk,khd->qhd', prob, heads[:, 2], precision=HIGH).reshape(L, D)
    out = low(low_back(out))
    attn = low_back(jnp.dot(out, wlow[:, 3 * D:4 * D], precision=HIGH) + small[base + 8])
    hone = norm_rows(x0 + attn, small[base + 2], small[base + 3])
    fin = low(hone)
    upper = low_back(jnp.dot(fin, wlow[:, 4 * D:4 * D + FF], precision=HIGH) + small[base + 10:].reshape(FF))
    gated = low(jax.nn.gelu(upper, approximate=False))
    ffn = low_back(jnp.dot(gated, wlow[:, 4 * D + FF:].T, precision=HIGH) + small[base + 9])
    htwo = norm_rows(hone + ffn, small[base + 4], small[base + 5])
    hmask = low(htwo[mpos])
    logits = low_back(jnp.dot(hmask, tlow.T, precision=HIGH))
    logits = jnp.where((jnp.arange(V) < VREAL)[None], logits, -1000000000.0)
    ztop = lax.optimization_barrier(jnp.max(logits, axis=-1, keepdims=True))
    zlse = ztop[:, 0] + jnp.log(lax.optimization_barrier(jnp.sum(jnp.exp(logits - ztop), axis=-1)))
    pick = jnp.take_along_axis(logits, labels[:, None], axis=1)[:, 0]
    raw_sum = jnp.sum(valid * (zlse - pick))
    return (raw_sum / count, raw_sum)

def worker_sums(params, ids, docs, mpos, labels, valid, count):

    def step(total, item):
        scaled, pull, raw_sum = jax.vjp(lambda p: sequence_loss(p, *item, count), params, has_aux=True)
        grads = pull(jnp.ones((), scaled.dtype))[0]
        return ((jax.tree.map(jnp.add, total[0], grads), total[1] + raw_sum), None)
    zero = jax.tree.map(jnp.zeros_like, params)
    (grads, raw), _ = lax.scan(step, (zero, jnp.zeros((), count.dtype)), (ids, docs, mpos, labels, valid))
    return (grads, raw)

def reference(token_ids, doc_ids, mlm_pos, mlm_labels, mlm_valid, table, table_m, table_v, small, small_m, small_v, layer, layer_m, layer_v, worker_err, server_err):
    count = jnp.sum(mlm_valid).astype(jnp.float32)
    valid = mlm_valid.astype(jnp.float32)
    per = SEQ_DEV * N_NARROW

    def split(x):
        return x.reshape((N_WIDE, per) + x.shape[1:])
    params = (table, small, layer)

    def worker(carry, item):
        ids, docs, mpos, labels, flags, err = item
        grads, raw = worker_sums(params, ids, docs, mpos, labels, flags, count)
        span = (BETA * layer_m + (1.0 - BETA) * grads[2] + err).reshape(N_NARROW, D // N_NARROW, WCOLS)
        scale = lax.optimization_barrier(jnp.mean(jnp.abs(span), axis=(1, 2), keepdims=True)) + MAG_EPS
        sent = scale * jnp.tanh(span / scale)
        carry = (carry[0] + grads[0], carry[1] + grads[1], carry[2] + raw)
        return (carry, (sent.reshape(D, WCOLS), (span - sent).reshape(D, WCOLS)))
    init = (jnp.zeros_like(table), jnp.zeros_like(small), jnp.zeros((), table.dtype))
    items = (split(token_ids), split(doc_ids), split(mlm_pos), split(mlm_labels), split(valid), worker_err)
    (table_grad, small_grad, loss_sum), (sent, new_worker) = lax.scan(worker, init, items)

    def blocks(x):
        return x.reshape(N_NARROW, D // N_NARROW, N_WIDE, WCOLS // N_WIDE)
    server_in = blocks(lax.optimization_barrier(jnp.mean(sent, axis=0))) + blocks(server_err)
    sscale = lax.optimization_barrier(jnp.mean(jnp.abs(server_in), axis=(1, 3), keepdims=True)) + MAG_EPS
    server_out = sscale * jnp.tanh(server_in / sscale)
    new_server = (server_in - server_out).reshape(D, WCOLS)
    new_m = server_out.reshape(D, WCOLS)
    layer_upd = new_m / (jnp.sqrt(layer_v) + OPT_EPS) + DECAY * layer
    col = jnp.arange(WCOLS)
    which = (col >= 3 * D).astype(jnp.int32) + (col >= 4 * D).astype(jnp.int32) + (col >= 4 * D + FF).astype(jnp.int32)
    onehot = (which[:, None] == jnp.arange(4)[None]).astype(layer.dtype)
    wsq = lax.optimization_barrier(jnp.sum(lax.optimization_barrier(jnp.sum(layer * layer, axis=0))[:, None] * onehot, axis=0))
    usq = lax.optimization_barrier(jnp.sum(lax.optimization_barrier(jnp.sum(layer_upd * layer_upd, axis=0))[:, None] * onehot, axis=0))
    table_mom = BETA * table_m + (1.0 - BETA) * table_grad
    table_upd = table_mom / (jnp.sqrt(table_v) + OPT_EPS) + DECAY * table
    small_mom = BETA * small_m + (1.0 - BETA) * small_grad
    small_upd = small_mom / (jnp.sqrt(small_v) + OPT_EPS) + DECAY * small
    wnorm = jnp.sqrt(jnp.concatenate([wsq, jnp.sum(table * table)[None], jnp.sum(small * small)[None]]))
    unorm = jnp.sqrt(jnp.concatenate([usq, jnp.sum(table_upd * table_upd)[None], jnp.sum(small_upd * small_upd)[None]]))
    ratio = wnorm / unorm
    new_layer = layer - RATE * lax.optimization_barrier(jnp.sum(onehot * ratio[None, 0:4], axis=1))[None] * layer_upd
    new_table = table - RATE * ratio[4] * table_upd
    new_small = small - RATE * ratio[5] * small_upd
    return (jnp.stack([loss_sum, count]), new_table, table_mom, new_small, small_mom, new_layer, new_m, new_worker, new_server, jnp.stack([wnorm, unorm]))
```

```python
import jax
import jax.numpy as jnp
from jax import lax
from jax.sharding import PartitionSpec as P

D = 1024
HEADS = 16
HEAD = 64
FF = 4096
VREAL = 30522
L = 512
MPS = 80


LN_EPS = 1e-12
BETA = 0.9
DECAY = 0.01
RATE = 0.25
OPT_EPS = 1e-06
MAG_EPS = 1e-08


def joined(value, axis, join):
    pieces = jax.tree.map(lambda part: lax.all_gather(part, axis), value)
    head = jax.tree.map(lambda part: part[0], pieces)
    tail = jax.tree.map(lambda part: part[1:], pieces)
    subtotal, _ = lax.scan(lambda subtotal, slab: (join(subtotal, slab), None), head, tail)
    return subtotal


def norm_rows(x, gain, shift):
    mean = jnp.mean(x, axis=-1, keepdims=True)
    cent = x - mean
    var = jnp.mean(cent * cent, axis=-1, keepdims=True)
    return cent * lax.rsqrt(var + LN_EPS) * gain + shift


def gelu_exact(upper):
    return jax.nn.gelu(upper, approximate=False)


def matmul(left, right):
    return jnp.dot(left, right, preferred_element_type=jnp.float32)


def matmul_tn(left, right):
    return lax.dot_general(
        left, right, (((0,), (0,)), ((), ())), preferred_element_type=jnp.float32
    )


def matmul_nt(left, right):
    return lax.dot_general(
        left, right, (((1,), (1,)), ((), ())), preferred_element_type=jnp.float32
    )


def score_block(heads, docs):
    raw = (
        jnp.einsum(
            "sqhd,skhd->shqk", heads[:, :, 0], heads[:, :, 1], preferred_element_type=jnp.float32
        )
        * 0.125
    )
    same = (docs[:, :, None] == docs[:, None, :])[:, None]
    return jnp.where(same, raw, -1000000000.0)


def merge_rows(first, second):
    peak = jnp.maximum(first[0], second[0])
    total = first[1] * jnp.exp(first[0] - peak) + second[1] * jnp.exp(second[0] - peak)
    return (peak, total, first[2] + second[2])


def layer_forward(embedded, docs, small, weights):
    seqs = docs.shape[0]
    base = L + 2
    x0 = norm_rows(embedded, small[base], small[base + 1])
    act = x0.astype(jnp.bfloat16)
    bias = jnp.concatenate([small[base + 6], jnp.zeros((D,), jnp.float32), small[base + 7]])
    qkv = (matmul(act, weights[:, 0 : 3 * D]) + bias).astype(jnp.bfloat16)
    heads = qkv.reshape(seqs, L, 3, HEADS, HEAD)
    scores = score_block(heads, docs)
    top = jnp.max(scores, axis=-1, keepdims=True)
    lse = top + jnp.log(jnp.sum(jnp.exp(scores - top), axis=-1, keepdims=True))
    prob = jnp.exp(scores - lse).astype(jnp.bfloat16)
    out = jnp.einsum("shqk,skhd->sqhd", prob, heads[:, :, 2], preferred_element_type=jnp.float32)
    out = out.reshape(seqs * L, D).astype(jnp.bfloat16)
    rone = x0 + (matmul(out, weights[:, 3 * D : 4 * D]) + small[base + 8])
    hone = norm_rows(rone, small[base + 2], small[base + 3])
    fin = hone.astype(jnp.bfloat16)
    upper = matmul(fin, weights[:, 4 * D : 4 * D + FF]) + small[base + 10 :].reshape(FF)
    gated = gelu_exact(upper).astype(jnp.bfloat16)
    rtwo = hone + (matmul_nt(gated, weights[:, 4 * D + FF :]) + small[base + 9])
    htwo = norm_rows(rtwo, small[base + 4], small[base + 5])
    return (htwo, (embedded, act, qkv, lse, out, rone, fin, upper, gated, rtwo))


def layer_backward(dhtwo, kept, docs, small, weights):
    embedded, act, qkv, lse, out, rone, fin, upper, gated, rtwo = kept
    seqs = docs.shape[0]
    base = L + 2
    _, pull = jax.vjp(norm_rows, rtwo, small[base + 4], small[base + 5])
    drtwo, dgain_two, dshift_two = pull(dhtwo)
    dffn = drtwo.astype(jnp.bfloat16)
    dgated = matmul(dffn, weights[:, 4 * D + FF :])
    _, pull = jax.vjp(gelu_exact, upper)
    dupper = pull(dgated)[0].astype(jnp.bfloat16)
    dhone = drtwo + matmul_nt(dupper, weights[:, 4 * D : 4 * D + FF])
    _, pull = jax.vjp(norm_rows, rone, small[base + 2], small[base + 3])
    drone, dgain_one, dshift_one = pull(dhone)
    dattn = drone.astype(jnp.bfloat16)
    dout = (
        matmul_nt(dattn, weights[:, 3 * D : 4 * D])
        .astype(jnp.bfloat16)
        .reshape(seqs, L, HEADS, HEAD)
    )
    heads = qkv.reshape(seqs, L, 3, HEADS, HEAD)
    prob = jnp.exp(score_block(heads, docs) - lse)
    dvalue = jnp.einsum(
        "shqk,sqhd->skhd", prob.astype(jnp.bfloat16), dout, preferred_element_type=jnp.float32
    )
    dprob = jnp.einsum("sqhd,skhd->shqk", dout, heads[:, :, 2], preferred_element_type=jnp.float32)
    dscore = (prob * (dprob - jnp.sum(prob * dprob, axis=-1, keepdims=True))).astype(jnp.bfloat16)
    dquery = (
        jnp.einsum("shqk,skhd->sqhd", dscore, heads[:, :, 1], preferred_element_type=jnp.float32)
        * 0.125
    )
    dkey = (
        jnp.einsum("shqk,sqhd->skhd", dscore, heads[:, :, 0], preferred_element_type=jnp.float32)
        * 0.125
    )
    dqkv = jnp.stack([dquery, dkey, dvalue], axis=2).reshape(seqs * L, 3 * D).astype(jnp.bfloat16)
    dxzero = drone + matmul_nt(dqkv, weights[:, 0 : 3 * D])
    _, pull = jax.vjp(norm_rows, embedded, small[base], small[base + 1])
    dembed, dgain_emb, dshift_emb = pull(dxzero)
    bias_qkv = jnp.sum(dqkv, axis=0, dtype=jnp.float32)
    vectors = jnp.stack(
        [
            dgain_emb,
            dshift_emb,
            dgain_one,
            dshift_one,
            dgain_two,
            dshift_two,
            bias_qkv[0:D],
            bias_qkv[2 * D : 3 * D],
            jnp.sum(dattn, axis=0, dtype=jnp.float32),
            jnp.sum(dffn, axis=0, dtype=jnp.float32),
        ]
    )
    bias_up = jnp.sum(dupper, axis=0, dtype=jnp.float32).reshape(FF // D, D)
    return (
        dembed,
        jnp.concatenate([vectors, bias_up], axis=0),
        (act, dqkv, out, dattn, fin, dupper, dffn, gated),
    )


def swap_pairs(size, bit):
    return [(place, place ^ bit) for place in range(size)]


def summed_over(value, axis):
    size = lax.axis_size(axis)
    if size & (size - 1):
        return lax.psum(value, axis)
    bit = 1
    while bit < size:
        value = value + lax.ppermute(value, axis, swap_pairs(size, bit))
        bit *= 2
    return value


def worker_piece(left, right):
    grad = matmul_tn(left, right).astype(jnp.bfloat16)
    return lax.psum_scatter(grad, "narrow", scatter_dimension=0, tiled=True).astype(jnp.float32)


def paired_piece(left, right):
    n_wide, n_narrow = lax.axis_size("wide"), lax.axis_size("narrow")
    core = lax.axis_index("wide") % 2
    narrow_me = lax.axis_index("narrow")
    pair, side = narrow_me // 2, narrow_me % 2
    rows = D // n_narrow

    def block(core_of, side_of):
        part = lax.dynamic_slice_in_dim(left, (2 * core_of + side_of) * rows, rows, 1)
        return matmul_tn(part, right)

    cores = swap_pairs(n_wide, 1)
    sides = swap_pairs(n_narrow, 1)
    moves = []
    for wide in range(n_wide):
        for narrow in range(n_narrow):
            if narrow // 2 != wide % 2:
                target_wide = wide - wide % 2 + narrow // 2
                target_narrow = 2 * (wide % 2) + narrow % 2
                moves.append((wide * n_narrow + narrow, target_wide * n_narrow + target_narrow))
    away = lax.ppermute(block(1 - core, 1 - side).astype(jnp.bfloat16), "wide", cores)
    near = lax.ppermute(block(1 - core, side).astype(jnp.bfloat16), "wide", cores)
    away = (block(core, 1 - side) + away.astype(jnp.float32)).astype(jnp.bfloat16)
    away = lax.ppermute(away, "narrow", sides)
    total = block(core, side) + near.astype(jnp.float32) + away.astype(jnp.float32)
    total = total.astype(jnp.bfloat16)
    moved = lax.ppermute(total, ("wide", "narrow"), moves)
    return jnp.where(pair == core, total, moved).astype(jnp.float32)


def hosted_rows(token_ids, mlm_labels, mlm_valid, doc_ids, mlm_pos):
    n_wide, n_narrow = lax.axis_size("wide"), lax.axis_size("narrow")
    core = lax.axis_index("wide") % 2
    packed = jnp.concatenate([token_ids, mlm_labels, mlm_valid], axis=1)
    other = lax.ppermute(packed, "wide", swap_pairs(n_wide, 1))
    both = jnp.where(core == 0, jnp.stack([packed, other]), jnp.stack([other, packed]))
    both = both.reshape(2, 2, 2, packed.shape[1])
    column = lax.dynamic_index_in_dim(both, core, 2, keepdims=False).reshape(4, packed.shape[1])
    moves = []
    for wide in range(n_wide):
        for row in range(n_narrow):
            target_wide = wide - wide % 2 + row % 2
            target_narrow = 2 * (wide % 2) + row // 2
            moves.append((wide * n_narrow + row, target_wide * n_narrow + target_narrow))
    own = lax.ppermute(jnp.concatenate([doc_ids, mlm_pos], axis=1), ("wide", "narrow"), moves)
    return (
        column[:, 0:L],
        column[:, L : L + MPS],
        column[:, L + MPS :],
        own[:, 0:L],
        own[:, L:],
    )


def scattered_sum(sent):
    n_wide = lax.axis_size("wide")
    wide_me = lax.axis_index("wide")
    rows, cols = sent.shape
    part = cols // n_wide
    if n_wide != 8:
        whole = lax.psum(sent.astype(jnp.bfloat16), "wide").astype(jnp.float32)
        return lax.dynamic_slice_in_dim(whole, wide_me * part, part, 1)
    core, x, y = wide_me % 2, wide_me // 2 % 2, wide_me // 4
    blocks = sent.reshape(rows, 2, 2, 2, part)

    def step(value, dim, place, bit):
        give = lax.dynamic_index_in_dim(value, 1 - place, dim, keepdims=False).astype(jnp.bfloat16)
        keep = lax.dynamic_index_in_dim(value, place, dim, keepdims=False)
        take = lax.ppermute(give, "wide", swap_pairs(n_wide, bit))
        return keep.astype(jnp.float32) + take.astype(jnp.float32)

    blocks = step(blocks, 3, core, 1)
    upper, lower = blocks[0 : rows // 2], blocks[rows // 2 :]
    upper, lower = step(upper, 2, x, 2), step(lower, 1, y, 4)
    upper, lower = step(upper, 1, y, 4), step(lower, 1, x, 2)
    return jnp.concatenate([upper, lower], axis=0)


def shards(
    token_ids,
    doc_ids,
    mlm_pos,
    mlm_labels,
    mlm_valid,
    table,
    table_m,
    table_v,
    small,
    small_m,
    small_v,
    layer,
    layer_m,
    layer_v,
    worker_err,
    server_err,
):
    n_wide = lax.axis_size("wide")
    narrow_me = lax.axis_index("narrow")
    wide_me = lax.axis_index("wide")
    n_narrow = lax.axis_size("narrow")
    seqs = doc_ids.shape[0]
    paired = n_wide % 2 == 0 and n_narrow == 4 and seqs == 1
    count = summed_over(jnp.sum(mlm_valid.astype(jnp.float32)), "wide")
    if paired:
        token_ids, mlm_labels, mlm_valid, doc_ids, mlm_pos = hosted_rows(
            token_ids, mlm_labels, mlm_valid, doc_ids, mlm_pos
        )
    table_cols = lax.all_gather(table.astype(jnp.bfloat16), "wide", axis=1, tiled=True)
    layer_rows = lax.all_gather(layer.astype(jnp.bfloat16), "narrow", axis=0, tiled=True)
    weights = lax.all_gather(layer_rows, "wide", axis=1, tiled=True)
    vshard = table_cols.shape[0]
    local_ids = token_ids - narrow_me * vshard
    inside = (local_ids >= 0) & (local_ids < vshard)
    picked = jnp.take(table_cols, jnp.clip(local_ids, 0, vshard - 1), axis=0)
    picked = jnp.where(inside[..., None], picked.astype(jnp.float32), 0.0)
    looked = lax.psum_scatter(
        picked.astype(jnp.bfloat16), "narrow", scatter_dimension=0, tiled=True
    ).astype(jnp.float32)
    even_doc = (doc_ids % 2 == 0)[..., None]
    embedded = looked + small[0:L][None] + jnp.where(even_doc, small[L], small[L + 1])
    htwo, kept = layer_forward(embedded.reshape(seqs * L, D), doc_ids, small, weights)
    hmask = jnp.take_along_axis(htwo.reshape(seqs, L, D), mlm_pos[..., None], axis=1)
    hmask = hmask.reshape(seqs * MPS, D).astype(jnp.bfloat16)
    group_h = lax.all_gather(hmask, "narrow", axis=0, tiled=True)
    vocab = narrow_me * vshard + jnp.arange(vshard)
    logits = jnp.where((vocab < VREAL)[None], matmul_nt(group_h, table_cols), -1000000000.0)
    labels = mlm_labels.reshape(-1)
    hit = vocab[None] == labels[:, None]
    top = jnp.max(logits, axis=1)
    total = jnp.sum(jnp.exp(logits - top[:, None]), axis=1)
    target = jnp.sum(jnp.where(hit, logits, 0.0), axis=1)
    top, total, target = joined((top, total, target), "narrow", merge_rows)
    lse = top + jnp.log(total)
    flags = mlm_valid.reshape(-1).astype(jnp.float32)
    own = seqs * MPS
    own_loss = lax.dynamic_slice_in_dim(flags * (lse - target), narrow_me * own, own)
    dlogit = (
        (jnp.exp(logits - lse[:, None]) - hit.astype(jnp.float32)) * (flags / count)[:, None]
    ).astype(jnp.bfloat16)
    dhmask = lax.psum_scatter(matmul(dlogit, table_cols), "narrow", scatter_dimension=0, tiled=True)
    table_head = matmul_tn(dlogit, group_h)
    dhtwo = (
        jnp.zeros((seqs, L, D), jnp.float32)
        .at[jnp.arange(seqs)[:, None], mlm_pos]
        .add(dhmask.reshape(seqs, MPS, D))
    )
    dembed, vectors, saved = layer_backward(
        dhtwo.reshape(seqs * L, D), kept, doc_ids, small, weights
    )
    act, dqkv, out, dattn, fin, dupper, dffn, gated = saved
    piece = paired_piece if paired else worker_piece
    worker_grad = jnp.concatenate(
        [piece(act, dqkv), piece(out, dattn), piece(fin, dupper), piece(dffn, gated)], axis=1
    )
    dembed_rows = dembed.reshape(seqs, L, D)
    seg_even = jnp.sum(jnp.where(even_doc, dembed_rows, 0.0), axis=(0, 1))
    seg_odd = jnp.sum(jnp.where(even_doc, 0.0, dembed_rows), axis=(0, 1))
    small_grad = jnp.concatenate(
        [jnp.sum(dembed_rows, axis=0), seg_even[None], seg_odd[None], vectors], axis=0
    )
    group_rows = lax.all_gather(dembed_rows.astype(jnp.bfloat16), "narrow", axis=0, tiled=True)
    slots = jnp.where(inside, local_ids, vshard).reshape(-1)
    table_grad = table_head.at[slots].add(
        group_rows.reshape(-1, D).astype(jnp.float32), mode="drop"
    )
    table_grad = lax.psum_scatter(
        table_grad.astype(jnp.bfloat16), "wide", scatter_dimension=1, tiled=True
    ).astype(jnp.float32)
    span = BETA * layer_m + (1.0 - BETA) * worker_grad + worker_err[0]
    scale = jnp.mean(jnp.abs(span)) + MAG_EPS
    sent = scale * jnp.tanh(span / scale)
    new_worker = (span - sent)[None]
    part_cols = layer.shape[1]
    mixed = scattered_sum(sent) / n_wide
    server_in = mixed + server_err
    sscale = jnp.mean(jnp.abs(server_in)) + MAG_EPS
    server_out = sscale * jnp.tanh(server_in / sscale)
    new_server = server_in - server_out
    new_m = lax.all_gather(server_out.astype(jnp.bfloat16), "wide", axis=1, tiled=True).astype(
        server_out.dtype
    )
    layer_upd = server_out / (jnp.sqrt(layer_v) + OPT_EPS) + DECAY * layer
    column = wide_me * part_cols + jnp.arange(part_cols)
    which = (
        (column >= 3 * D).astype(jnp.int32)
        + (column >= 4 * D).astype(jnp.int32)
        + (column >= 4 * D + FF).astype(jnp.int32)
    )
    onehot = (which[:, None] == jnp.arange(4)[None]).astype(jnp.float32)
    wsq = jnp.sum(jnp.sum(layer * layer, axis=0)[:, None] * onehot, axis=0)
    usq = jnp.sum(jnp.sum(layer_upd * layer_upd, axis=0)[:, None] * onehot, axis=0)
    table_mom = BETA * table_m + (1.0 - BETA) * table_grad
    table_upd = table_mom / (jnp.sqrt(table_v) + OPT_EPS) + DECAY * table
    parts = jnp.concatenate(
        [
            wsq,
            usq,
            jnp.sum(table * table)[None],
            jnp.sum(table_upd * table_upd)[None],
            jnp.sum(own_loss)[None],
        ]
    )
    small_grad = lax.psum(small_grad, ("wide", "narrow"))
    sums = summed_over(summed_over(parts, "wide"), "narrow")
    loss_sum = sums[10]
    small_mom = BETA * small_m + (1.0 - BETA) * small_grad
    small_upd = small_mom / (jnp.sqrt(small_v) + OPT_EPS) + DECAY * small
    wnorm = jnp.sqrt(jnp.concatenate([sums[0:4], sums[8:9], jnp.sum(small * small)[None]]))
    unorm = jnp.sqrt(jnp.concatenate([sums[4:8], sums[9:10], jnp.sum(small_upd * small_upd)[None]]))
    ratio = wnorm / unorm
    new_layer = layer - RATE * jnp.sum(onehot * ratio[None, 0:4], axis=1)[None] * layer_upd
    new_table = table - RATE * ratio[4] * table_upd
    new_small = small - RATE * ratio[5] * small_upd
    return (
        jnp.stack([loss_sum, count]),
        new_table,
        table_mom,
        new_small,
        small_mom,
        new_layer,
        new_m,
        new_worker,
        new_server,
        jnp.stack([wnorm, unorm]),
    )


def solution(mesh):
    placed = (
        P("wide", None),
        P(("wide", "narrow"), None),
        P(("wide", "narrow"), None),
        P("wide", None),
        P("wide", None),
        P("narrow", "wide"),
        P("narrow", "wide"),
        P("narrow", "wide"),
        P(),
        P(),
        P(),
        P("narrow", "wide"),
        P("narrow", None),
        P("narrow", "wide"),
        P("wide", "narrow", None),
        P("narrow", "wide"),
    )
    return jax.shard_map(
        shards,
        mesh=mesh,
        in_specs=placed,
        out_specs=(
            P(),
            P("narrow", "wide"),
            P("narrow", "wide"),
            P(),
            P(),
            P("narrow", "wide"),
            P("narrow", None),
            P("wide", "narrow", None),
            P("narrow", "wide"),
            P(),
        ),
        check_vma=False,
    )
```

```python
import jax
import jax.numpy as jnp
from jax import lax
from jax.sharding import PartitionSpec as P

D = 1024
HEADS = 16
HEAD = 64
FF = 4096
VREAL = 30522
L = 512
MPS = 80


LN_EPS = 1e-12
BETA = 0.9
DECAY = 0.01
RATE = 0.25
OPT_EPS = 1e-06
MAG_EPS = 1e-08


def joined(value, axis, join):
    pieces = jax.tree.map(lambda part: lax.all_gather(part, axis), value)
    head = jax.tree.map(lambda part: part[0], pieces)
    tail = jax.tree.map(lambda part: part[1:], pieces)
    subtotal, _ = lax.scan(lambda subtotal, slab: (join(subtotal, slab), None), head, tail)
    return subtotal


def norm_rows(x, gain, shift):
    mean = jnp.mean(x, axis=-1, keepdims=True)
    cent = x - mean
    var = jnp.mean(cent * cent, axis=-1, keepdims=True)
    return cent * lax.rsqrt(var + LN_EPS) * gain + shift


def gelu_exact(upper):
    return jax.nn.gelu(upper, approximate=False)


def matmul(left, right):
    return jnp.dot(left, right, preferred_element_type=jnp.float32)


def matmul_tn(left, right):
    return lax.dot_general(
        left, right, (((0,), (0,)), ((), ())), preferred_element_type=jnp.float32
    )


def matmul_nt(left, right):
    return lax.dot_general(
        left, right, (((1,), (1,)), ((), ())), preferred_element_type=jnp.float32
    )


def score_block(heads, docs):
    raw = (
        jnp.einsum(
            "sqhd,skhd->shqk", heads[:, :, 0], heads[:, :, 1], preferred_element_type=jnp.float32
        )
        * 0.125
    )
    same = (docs[:, :, None] == docs[:, None, :])[:, None]
    return jnp.where(same, raw, -1000000000.0)


def merge_rows(first, second):
    peak = jnp.maximum(first[0], second[0])
    total = first[1] * jnp.exp(first[0] - peak) + second[1] * jnp.exp(second[0] - peak)
    return (peak, total, first[2] + second[2])


def layer_forward(embedded, docs, small, weights):
    seqs = docs.shape[0]
    base = L + 2
    x0 = norm_rows(embedded, small[base], small[base + 1])
    act = x0.astype(jnp.bfloat16)
    bias = jnp.concatenate([small[base + 6], jnp.zeros((D,), jnp.float32), small[base + 7]])
    qkv = (matmul(act, weights[:, 0 : 3 * D]) + bias).astype(jnp.bfloat16)
    heads = qkv.reshape(seqs, L, 3, HEADS, HEAD)
    scores = score_block(heads, docs)
    top = jnp.max(scores, axis=-1, keepdims=True)
    lse = top + jnp.log(jnp.sum(jnp.exp(scores - top), axis=-1, keepdims=True))
    prob = jnp.exp(scores - lse).astype(jnp.bfloat16)
    out = jnp.einsum("shqk,skhd->sqhd", prob, heads[:, :, 2], preferred_element_type=jnp.float32)
    out = out.reshape(seqs * L, D).astype(jnp.bfloat16)
    rone = x0 + (matmul(out, weights[:, 3 * D : 4 * D]) + small[base + 8])
    hone = norm_rows(rone, small[base + 2], small[base + 3])
    fin = hone.astype(jnp.bfloat16)
    upper = matmul(fin, weights[:, 4 * D : 4 * D + FF]) + small[base + 10 :].reshape(FF)
    gated = gelu_exact(upper).astype(jnp.bfloat16)
    rtwo = hone + (matmul_nt(gated, weights[:, 4 * D + FF :]) + small[base + 9])
    htwo = norm_rows(rtwo, small[base + 4], small[base + 5])
    return (htwo, (embedded, act, qkv, lse, out, rone, fin, upper, gated, rtwo))


def layer_backward(dhtwo, kept, docs, small, weights):
    embedded, act, qkv, lse, out, rone, fin, upper, gated, rtwo = kept
    seqs = docs.shape[0]
    base = L + 2
    _, pull = jax.vjp(norm_rows, rtwo, small[base + 4], small[base + 5])
    drtwo, dgain_two, dshift_two = pull(dhtwo)
    dffn = drtwo.astype(jnp.bfloat16)
    down = WorkerPiece(dffn, gated)
    dgated = matmul(dffn, weights[:, 4 * D + FF :])
    _, pull = jax.vjp(gelu_exact, upper)
    dupper = pull(dgated)[0].astype(jnp.bfloat16)
    dupper, _ = after(dupper, *down.waits())
    down.across()
    up = WorkerPiece(fin, dupper)
    dhone = drtwo + matmul_nt(dupper, weights[:, 4 * D : 4 * D + FF])
    _, pull = jax.vjp(norm_rows, rone, small[base + 2], small[base + 3])
    drone, dgain_one, dshift_one = pull(dhone)
    dattn = drone.astype(jnp.bfloat16)
    attn = WorkerPiece(out, dattn)
    dout = matmul_nt(dattn, weights[:, 3 * D : 4 * D]).astype(jnp.bfloat16)
    dout, _ = after(dout, *up.waits(), *attn.waits())
    up.across()
    attn.across()
    dout = dout.reshape(seqs, L, HEADS, HEAD)
    heads = qkv.reshape(seqs, L, 3, HEADS, HEAD)
    prob = jnp.exp(score_block(heads, docs) - lse)
    dvalue = jnp.einsum(
        "shqk,sqhd->skhd", prob.astype(jnp.bfloat16), dout, preferred_element_type=jnp.float32
    )
    dprob = jnp.einsum("sqhd,skhd->shqk", dout, heads[:, :, 2], preferred_element_type=jnp.float32)
    dscore = (prob * (dprob - jnp.sum(prob * dprob, axis=-1, keepdims=True))).astype(jnp.bfloat16)
    dscore, _ = after(dscore, *down.waits_across())
    grad_down = down.finish()
    dquery = (
        jnp.einsum("shqk,skhd->sqhd", dscore, heads[:, :, 1], preferred_element_type=jnp.float32)
        * 0.125
    )
    dkey = (
        jnp.einsum("shqk,sqhd->skhd", dscore, heads[:, :, 0], preferred_element_type=jnp.float32)
        * 0.125
    )
    dqkv = jnp.stack([dquery, dkey, dvalue], axis=2).reshape(seqs * L, 3 * D).astype(jnp.bfloat16)
    qkv_piece = WorkerPiece(act, dqkv)
    dxzero = drone + matmul_nt(dqkv, weights[:, 0 : 3 * D])
    _, pull = jax.vjp(norm_rows, embedded, small[base], small[base + 1])
    dembed, dgain_emb, dshift_emb = pull(dxzero)
    dembed, _ = after(dembed, *qkv_piece.waits(), *attn.waits_across())
    qkv_piece.across()
    grads = jnp.concatenate(
        [qkv_piece.finish(), attn.finish(), up.finish(), grad_down], axis=1
    )
    bias_qkv = jnp.sum(dqkv, axis=0, dtype=jnp.float32)
    vectors = jnp.stack(
        [
            dgain_emb,
            dshift_emb,
            dgain_one,
            dshift_one,
            dgain_two,
            dshift_two,
            bias_qkv[0:D],
            bias_qkv[2 * D : 3 * D],
            jnp.sum(dattn, axis=0, dtype=jnp.float32),
            jnp.sum(dffn, axis=0, dtype=jnp.float32),
        ]
    )
    bias_up = jnp.sum(dupper, axis=0, dtype=jnp.float32).reshape(FF // D, D)
    return (dembed, jnp.concatenate([vectors, bias_up], axis=0), grads)


def paired_mesh():
    return lax.axis_size("wide") == 8 and lax.axis_size("narrow") == 4


def after(values, *awaited):
    return lax.optimization_barrier((values, awaited))


def swap_pairs(size, bit):
    return [(place, place ^ bit) for place in range(size)]


def cycle(size, by):
    return [(place, (place + by) % size) for place in range(size)]


def summed_over(value, axis):
    size = lax.axis_size(axis)
    if size & (size - 1):
        return lax.psum(value, axis)
    bit = 1
    while bit < size:
        value = value + lax.ppermute(value, axis, swap_pairs(size, bit))
        bit *= 2
    return value


def gathered_near(value):
    size = lax.axis_size("narrow")
    rows = value.shape[0]
    around = [value]
    for by in range(1, size):
        around.append(lax.ppermute(value, "narrow", cycle(size, size - by)))
    twice = jnp.concatenate(around + around[:-1], axis=0)
    start = lax.rem(size - lax.axis_index("narrow"), size) * rows
    return lax.dynamic_slice_in_dim(twice, start, size * rows, 0)


def scattered_near(value):
    size = lax.axis_size("narrow")
    rows = value.shape[0] // size
    place = lax.axis_index("narrow")
    total = lax.dynamic_slice_in_dim(value, place * rows, rows, 0)
    for by in range(1, size):
        target = lax.rem(place + by, size)
        give = lax.dynamic_slice_in_dim(value, target * rows, rows, 0).astype(jnp.bfloat16)
        take = lax.ppermute(give, "narrow", cycle(size, by))
        total = total + take.astype(jnp.float32)
    return total


def chain_gather(value):
    size = lax.axis_size("narrow")
    rows = value.shape[0]
    rising, falling = value, value
    low, high = [], []
    for step in range(1, size):
        rising = lax.ppermute(rising, "narrow", [(i, i + 1) for i in range(step - 1, size - 1)])
        falling = lax.ppermute(falling, "narrow", [(i, i - 1) for i in range(1, size - step + 1)])
        low.append(rising)
        high.append(falling)
    line = jnp.concatenate(low[::-1] + [value] + high, axis=0)
    start = (size - 1 - lax.axis_index("narrow")) * rows
    return lax.dynamic_slice_in_dim(line, start, size * rows, 0)


def chain_scatter(value):
    size = lax.axis_size("narrow")
    place = lax.axis_index("narrow")

    def block(index):
        return lax.dynamic_index_in_dim(value, jnp.clip(index, 0, size - 1), 0, keepdims=False)

    rising, falling = None, None
    for step in range(1, size):
        up, down = block(size - step + place), block(step + place - size)
        if rising is not None:
            up, down = up + rising, down + falling
        rising = lax.ppermute(up, "narrow", [(i, i + 1) for i in range(step)])
        falling = lax.ppermute(down, "narrow", [(size - 1 - i, size - 2 - i) for i in range(step)])
    return block(place) + rising + falling


class WorkerPiece:
    def __init__(self, left, right):
        self.left, self.right = left, right
        self.paired = paired_mesh()
        if not self.paired:
            return
        self.core = lax.axis_index("wide") % 2
        self.pair, self.side = lax.axis_index("narrow") // 2, lax.axis_index("narrow") % 2
        cores = swap_pairs(lax.axis_size("wide"), 1)
        self.far = lax.ppermute(self.low(1 - self.core, 1 - self.side), "wide", cores)
        self.near = lax.ppermute(self.low(1 - self.core, self.side), "wide", cores)

    def block(self, core, side):
        rows = D // lax.axis_size("narrow")
        part = lax.dynamic_slice_in_dim(self.left, (2 * core + side) * rows, rows, 1)
        return matmul_tn(part, self.right)

    def low(self, core, side):
        return self.block(core, side).astype(jnp.bfloat16)

    def waits(self):
        return (self.far, self.near) if self.paired else ()

    def across(self):
        if self.paired:
            away = self.block(self.core, 1 - self.side) + self.far.astype(jnp.float32)
            sides = swap_pairs(lax.axis_size("narrow"), 1)
            self.away = lax.ppermute(away.astype(jnp.bfloat16), "narrow", sides)

    def waits_across(self):
        return (self.away,) if self.paired else ()

    def finish(self):
        if not self.paired:
            grad = matmul_tn(self.left, self.right).astype(jnp.bfloat16)
            return lax.psum_scatter(grad, "narrow", scatter_dimension=0, tiled=True)
        n_wide, n_narrow = lax.axis_size("wide"), lax.axis_size("narrow")
        total = self.block(self.core, self.side)
        total = total + self.near.astype(jnp.float32) + self.away.astype(jnp.float32)
        total = total.astype(jnp.bfloat16)
        moves = []
        for wide in range(n_wide):
            for narrow in range(n_narrow):
                if narrow // 2 != wide % 2:
                    target_wide = wide - wide % 2 + narrow // 2
                    target = target_wide * n_narrow + 2 * (wide % 2) + narrow % 2
                    moves.append((wide * n_narrow + narrow, target))
        moved = lax.ppermute(total, ("wide", "narrow"), moves)
        return jnp.where(self.pair == self.core, total, moved)


def hosted_rows(token_ids, mlm_labels, mlm_valid, doc_ids, mlm_pos):
    n_wide, n_narrow = lax.axis_size("wide"), lax.axis_size("narrow")
    core = lax.axis_index("wide") % 2
    packed = jnp.concatenate([token_ids, mlm_labels, mlm_valid], axis=1)
    other = lax.ppermute(packed, "wide", swap_pairs(n_wide, 1))
    both = jnp.where(core == 0, jnp.stack([packed, other]), jnp.stack([other, packed]))
    both = both.reshape(2, 2, 2, packed.shape[1])
    column = lax.dynamic_index_in_dim(both, core, 2, keepdims=False).reshape(4, packed.shape[1])
    moves = []
    for wide in range(n_wide):
        for row in range(n_narrow):
            target_wide = wide - wide % 2 + row % 2
            target_narrow = 2 * (wide % 2) + row // 2
            moves.append((wide * n_narrow + row, target_wide * n_narrow + target_narrow))
    own = lax.ppermute(jnp.concatenate([doc_ids, mlm_pos], axis=1), ("wide", "narrow"), moves)
    return (
        column[:, 0:L],
        column[:, L : L + MPS],
        column[:, L + MPS :],
        own[:, 0:L],
        own[:, L:],
    )


def wide_places():
    wide_me = lax.axis_index("wide")
    return wide_me % 2, wide_me // 2 % 2, wide_me // 4


def scattered_sum(sent):
    n_wide = lax.axis_size("wide")
    rows, cols = sent.shape
    part = cols // n_wide
    if not paired_mesh():
        whole = lax.psum(sent.astype(jnp.bfloat16), "wide").astype(jnp.float32)
        return lax.dynamic_slice_in_dim(whole, lax.axis_index("wide") * part, part, 1)
    core, x, y = wide_places()

    def block(value, place):
        return lax.dynamic_slice_in_dim(value, place * part, part, 1)

    give = [block(sent, 2 * chip + 1 - core).astype(jnp.bfloat16) for chip in range(4)]
    take = [lax.ppermute(part_of, "wide", swap_pairs(n_wide, 1)) for part_of in give]
    chips = jnp.stack([block(sent, 2 * chip + core) + take[chip] for chip in range(4)])
    half = rows // 2

    def send(value, bit):
        return lax.ppermute(value.astype(jnp.bfloat16), "wide", swap_pairs(n_wide, bit))

    def pick(value, index):
        return lax.dynamic_index_in_dim(value, index, 0, keepdims=False)

    upper, lower = chips[:, 0:half], chips[:, half:]
    upper_far = send(pick(upper, 2 * (1 - y) + 1 - x), 2)
    upper_near = send(pick(upper, 2 * y + 1 - x), 2)
    lower_far = send(pick(lower, 2 * (1 - y) + 1 - x), 4)
    lower_near = send(pick(lower, 2 * (1 - y) + x), 4)
    upper_far = send(pick(upper, 2 * (1 - y) + x) + upper_far, 4)
    lower_far = send(pick(lower, 2 * y + 1 - x) + lower_far, 2)
    own_upper = pick(upper, 2 * y + x) + upper_near + upper_far
    own_lower = pick(lower, 2 * y + x) + lower_near + lower_far
    return jnp.concatenate([own_upper, own_lower], axis=0)


def small_total(value):
    if not paired_mesh():
        return lax.psum(value, ("wide", "narrow"))
    n_wide, n_narrow = lax.axis_size("wide"), lax.axis_size("narrow")
    places = list(zip((1, 2, 4), wide_places()))
    for bit, place in places:
        half = value.shape[1] // 2
        give = lax.dynamic_slice_in_dim(value, (1 - place) * half, half, 1).astype(jnp.bfloat16)
        keep = lax.dynamic_slice_in_dim(value, place * half, half, 1)
        value = keep + lax.ppermute(give, "wide", swap_pairs(n_wide, bit)).astype(jnp.float32)
    bit = 1
    while bit < n_narrow:
        low = value.astype(jnp.bfloat16)
        other = lax.ppermute(low, "narrow", swap_pairs(n_narrow, bit))
        value = low.astype(jnp.float32) + other.astype(jnp.float32)
        bit *= 2
    value = value.astype(jnp.bfloat16)
    for bit, place in reversed(places):
        other = lax.ppermute(value, "wide", swap_pairs(n_wide, bit))
        first, second = jnp.where(place == 0, value, other), jnp.where(place == 0, other, value)
        value = jnp.concatenate([first, second], axis=1)
    return value.astype(jnp.float32)


def shards(
    token_ids,
    doc_ids,
    mlm_pos,
    mlm_labels,
    mlm_valid,
    table,
    table_m,
    table_v,
    small,
    small_m,
    small_v,
    layer,
    layer_m,
    layer_v,
    worker_err,
    server_err,
):
    n_wide = lax.axis_size("wide")
    narrow_me = lax.axis_index("narrow")
    wide_me = lax.axis_index("wide")
    seqs = doc_ids.shape[0]
    paired = paired_mesh()
    count = summed_over(jnp.sum(mlm_valid.astype(jnp.float32)), "wide")
    if paired:
        token_ids, mlm_labels, mlm_valid, doc_ids, mlm_pos = hosted_rows(
            token_ids, mlm_labels, mlm_valid, doc_ids, mlm_pos
        )
    table_cols = lax.all_gather(table.astype(jnp.bfloat16), "wide", axis=1, tiled=True)
    if paired:
        layer_rows = chain_gather(layer.astype(jnp.bfloat16))
    else:
        layer_rows = lax.all_gather(layer.astype(jnp.bfloat16), "narrow", axis=0, tiled=True)
    layer_rows, (table_cols,) = after(layer_rows, table_cols)
    weights = lax.all_gather(layer_rows, "wide", axis=1, tiled=True)
    vshard = table_cols.shape[0]
    local_ids = token_ids - narrow_me * vshard
    inside = (local_ids >= 0) & (local_ids < vshard)
    picked = jnp.take(table_cols, jnp.clip(local_ids, 0, vshard - 1), axis=0)
    picked = jnp.where(inside[..., None], picked.astype(jnp.float32), 0.0)
    picked = picked.astype(jnp.bfloat16)
    if paired:
        looked = chain_scatter(picked)[None]
    else:
        looked = lax.psum_scatter(picked, "narrow", scatter_dimension=0, tiled=True)
    looked = looked.astype(jnp.float32)
    even_doc = (doc_ids % 2 == 0)[..., None]
    embedded = looked + small[0:L][None] + jnp.where(even_doc, small[L], small[L + 1])
    htwo, kept = layer_forward(embedded.reshape(seqs * L, D), doc_ids, small, weights)
    hmask = jnp.take_along_axis(htwo.reshape(seqs, L, D), mlm_pos[..., None], axis=1)
    hmask = hmask.reshape(seqs * MPS, D).astype(jnp.bfloat16)
    if paired:
        group_h = gathered_near(hmask)
    else:
        group_h = lax.all_gather(hmask, "narrow", axis=0, tiled=True)
    vocab = narrow_me * vshard + jnp.arange(vshard)
    logits = jnp.where((vocab < VREAL)[None], matmul_nt(group_h, table_cols), -1000000000.0)
    labels = mlm_labels.reshape(-1)
    hit = vocab[None] == labels[:, None]
    top = jnp.max(logits, axis=1)
    total = jnp.sum(jnp.exp(logits - top[:, None]), axis=1)
    target = jnp.sum(jnp.where(hit, logits, 0.0), axis=1)
    if paired:
        stats = gathered_near(jnp.stack([top, total, target])[None])
        top, total, target = stats[0]
        for place in range(1, stats.shape[0]):
            top, total, target = merge_rows((top, total, target), tuple(stats[place]))
    else:
        top, total, target = joined((top, total, target), "narrow", merge_rows)
    lse = top + jnp.log(total)
    flags = mlm_valid.reshape(-1).astype(jnp.float32)
    own = seqs * MPS
    own_loss = lax.dynamic_slice_in_dim(flags * (lse - target), narrow_me * own, own)
    dlogit = (
        (jnp.exp(logits - lse[:, None]) - hit.astype(jnp.float32)) * (flags / count)[:, None]
    ).astype(jnp.bfloat16)
    dhmask = matmul(dlogit, table_cols)
    if paired:
        dhmask = scattered_near(dhmask)
    else:
        dhmask = lax.psum_scatter(dhmask, "narrow", scatter_dimension=0, tiled=True)
    table_head = matmul_tn(dlogit, group_h)
    dhtwo = (
        jnp.zeros((seqs, L, D), jnp.float32)
        .at[jnp.arange(seqs)[:, None], mlm_pos]
        .add(dhmask.reshape(seqs, MPS, D))
    )
    dembed, vectors, worker_grad = layer_backward(
        dhtwo.reshape(seqs * L, D), kept, doc_ids, small, weights
    )
    dembed_rows = dembed.reshape(seqs, L, D)
    seg_even = jnp.sum(jnp.where(even_doc, dembed_rows, 0.0), axis=(0, 1))
    seg_odd = jnp.sum(jnp.where(even_doc, 0.0, dembed_rows), axis=(0, 1))
    small_grad = jnp.concatenate(
        [jnp.sum(dembed_rows, axis=0), seg_even[None], seg_odd[None], vectors], axis=0
    )
    group_rows = lax.all_gather(dembed_rows.astype(jnp.bfloat16), "narrow", axis=0, tiled=True)
    slots = jnp.where(inside, local_ids, vshard).reshape(-1)
    table_grad = table_head.at[slots].add(
        group_rows.reshape(-1, D).astype(jnp.float32), mode="drop"
    )
    cut = table_grad.astype(jnp.bfloat16).reshape(vshard, n_wide, D // n_wide).transpose(1, 0, 2)
    table_grad = lax.psum_scatter(cut, "wide", scatter_dimension=0).astype(jnp.float32)
    span = BETA * layer_m + (1.0 - BETA) * worker_grad.astype(jnp.float32) + worker_err[0]
    scale = jnp.mean(jnp.abs(span)) + MAG_EPS
    sent = scale * jnp.tanh(span / scale)
    new_worker = (span - sent)[None]
    part_cols = layer.shape[1]
    mixed = scattered_sum(sent) / n_wide
    server_in = mixed + server_err
    sscale = jnp.mean(jnp.abs(server_in)) + MAG_EPS
    server_out = sscale * jnp.tanh(server_in / sscale)
    new_server = server_in - server_out
    new_m = lax.all_gather(server_out.astype(jnp.bfloat16), "wide", axis=1, tiled=True).astype(
        server_out.dtype
    )
    layer_upd = server_out / (jnp.sqrt(layer_v) + OPT_EPS) + DECAY * layer
    column = wide_me * part_cols + jnp.arange(part_cols)
    which = (
        (column >= 3 * D).astype(jnp.int32)
        + (column >= 4 * D).astype(jnp.int32)
        + (column >= 4 * D + FF).astype(jnp.int32)
    )
    onehot = (which[:, None] == jnp.arange(4)[None]).astype(jnp.float32)
    wsq = jnp.sum(jnp.sum(layer * layer, axis=0)[:, None] * onehot, axis=0)
    usq = jnp.sum(jnp.sum(layer_upd * layer_upd, axis=0)[:, None] * onehot, axis=0)
    table_mom = BETA * table_m + (1.0 - BETA) * table_grad
    table_upd = table_mom / (jnp.sqrt(table_v) + OPT_EPS) + DECAY * table
    parts = jnp.concatenate(
        [
            wsq,
            usq,
            jnp.sum(table * table)[None],
            jnp.sum(table_upd * table_upd)[None],
            jnp.sum(own_loss)[None],
        ]
    )
    small_grad = small_total(small_grad)
    sums = summed_over(summed_over(parts, "wide"), "narrow")
    loss_sum = sums[10]
    small_mom = BETA * small_m + (1.0 - BETA) * small_grad
    small_upd = small_mom / (jnp.sqrt(small_v) + OPT_EPS) + DECAY * small
    wnorm = jnp.sqrt(jnp.concatenate([sums[0:4], sums[8:9], jnp.sum(small * small)[None]]))
    unorm = jnp.sqrt(jnp.concatenate([sums[4:8], sums[9:10], jnp.sum(small_upd * small_upd)[None]]))
    ratio = wnorm / unorm
    new_layer = layer - RATE * jnp.sum(onehot * ratio[None, 0:4], axis=1)[None] * layer_upd
    new_table = table - RATE * ratio[4] * table_upd
    new_small = small - RATE * ratio[5] * small_upd
    return (
        jnp.stack([loss_sum, count]),
        new_table,
        table_mom,
        new_small,
        small_mom,
        new_layer,
        new_m,
        new_worker,
        new_server,
        jnp.stack([wnorm, unorm]),
    )


def solution(mesh):
    placed = (
        P("wide", None),
        P(("wide", "narrow"), None),
        P(("wide", "narrow"), None),
        P("wide", None),
        P("wide", None),
        P("narrow", "wide"),
        P("narrow", "wide"),
        P("narrow", "wide"),
        P(),
        P(),
        P(),
        P("narrow", "wide"),
        P("narrow", None),
        P("narrow", "wide"),
        P("wide", "narrow", None),
        P("narrow", "wide"),
    )
    return jax.shard_map(
        shards,
        mesh=mesh,
        in_specs=placed,
        out_specs=(
            P(),
            P("narrow", "wide"),
            P("narrow", "wide"),
            P(),
            P(),
            P("narrow", "wide"),
            P("narrow", None),
            P("wide", "narrow", None),
            P("narrow", "wide"),
            P(),
        ),
        check_vma=False,
    )
```

```python
import jax
import jax.numpy as jnp
from jax import lax
from jax.experimental import pallas as pl
from jax.experimental.pallas import tpu as pltpu
from jax.sharding import PartitionSpec as P

D = 1024
HEADS = 16
HEAD = 64
FF = 4096
VREAL = 30522
L = 512
MPS = 80


LN_EPS = 1e-12
BETA = 0.9
DECAY = 0.01
RATE = 0.25
OPT_EPS = 1e-06
MAG_EPS = 1e-08


def joined(value, axis, join):
    pieces = jax.tree.map(lambda part: lax.all_gather(part, axis), value)
    head = jax.tree.map(lambda part: part[0], pieces)
    tail = jax.tree.map(lambda part: part[1:], pieces)
    subtotal, _ = lax.scan(lambda subtotal, slab: (join(subtotal, slab), None), head, tail)
    return subtotal


def norm_rows(x, gain, shift):
    mean = jnp.mean(x, axis=-1, keepdims=True)
    cent = x - mean
    var = jnp.mean(cent * cent, axis=-1, keepdims=True)
    return cent * lax.rsqrt(var + LN_EPS) * gain + shift


def gelu_exact(upper):
    return jax.nn.gelu(upper, approximate=False)


def matmul(left, right):
    return jnp.dot(left, right, preferred_element_type=jnp.float32)


def matmul_tn(left, right):
    return lax.dot_general(
        left, right, (((0,), (0,)), ((), ())), preferred_element_type=jnp.float32
    )


def matmul_nt(left, right):
    return lax.dot_general(
        left, right, (((1,), (1,)), ((), ())), preferred_element_type=jnp.float32
    )


def score_block(heads, docs):
    raw = (
        jnp.einsum(
            "sqhd,skhd->shqk", heads[:, :, 0], heads[:, :, 1], preferred_element_type=jnp.float32
        )
        * 0.125
    )
    same = (docs[:, :, None] == docs[:, None, :])[:, None]
    return jnp.where(same, raw, -1000000000.0)


def merge_rows(first, second):
    peak = jnp.maximum(first[0], second[0])
    total = first[1] * jnp.exp(first[0] - peak) + second[1] * jnp.exp(second[0] - peak)
    return (peak, total, first[2] + second[2])


def layer_forward(embedded, docs, small, weights):
    seqs = docs.shape[0]
    base = L + 2
    x0 = norm_rows(embedded, small[base], small[base + 1])
    act = x0.astype(jnp.bfloat16)
    bias = jnp.concatenate([small[base + 6], jnp.zeros((D,), jnp.float32), small[base + 7]])
    qkv = (matmul(act, weights[:, 0 : 3 * D]) + bias).astype(jnp.bfloat16)
    heads = qkv.reshape(seqs, L, 3, HEADS, HEAD)
    scores = score_block(heads, docs)
    top = jnp.max(scores, axis=-1, keepdims=True)
    lse = top + jnp.log(jnp.sum(jnp.exp(scores - top), axis=-1, keepdims=True))
    prob = jnp.exp(scores - lse).astype(jnp.bfloat16)
    out = jnp.einsum("shqk,skhd->sqhd", prob, heads[:, :, 2], preferred_element_type=jnp.float32)
    out = out.reshape(seqs * L, D).astype(jnp.bfloat16)
    rone = x0 + (matmul(out, weights[:, 3 * D : 4 * D]) + small[base + 8])
    hone = norm_rows(rone, small[base + 2], small[base + 3])
    fin = hone.astype(jnp.bfloat16)
    upper = matmul(fin, weights[:, 4 * D : 4 * D + FF]) + small[base + 10 :].reshape(FF)
    gated = gelu_exact(upper).astype(jnp.bfloat16)
    rtwo = hone + (matmul_nt(gated, weights[:, 4 * D + FF :]) + small[base + 9])
    htwo = norm_rows(rtwo, small[base + 4], small[base + 5])
    return (htwo, (embedded, act, qkv, lse, out, rone, fin, upper, gated, rtwo))


def layer_backward(dhtwo, kept, docs, small, weights):
    embedded, act, qkv, lse, out, rone, fin, upper, gated, rtwo = kept
    seqs = docs.shape[0]
    base = L + 2
    _, pull = jax.vjp(norm_rows, rtwo, small[base + 4], small[base + 5])
    drtwo, dgain_two, dshift_two = pull(dhtwo)
    dffn = drtwo.astype(jnp.bfloat16)
    down = WorkerPiece((dffn, gated))
    dgated = matmul(dffn, weights[:, 4 * D + FF :])
    _, pull = jax.vjp(gelu_exact, upper)
    dupper = pull(dgated)[0].astype(jnp.bfloat16)
    dupper = down.received(dupper)
    down.across()
    up = WorkerPiece((fin, dupper))
    dhone = drtwo + matmul_nt(dupper, weights[:, 4 * D : 4 * D + FF])
    _, pull = jax.vjp(norm_rows, rone, small[base + 2], small[base + 3])
    drone, dgain_one, dshift_one = pull(dhone)
    dattn = drone.astype(jnp.bfloat16)
    dout = matmul_nt(dattn, weights[:, 3 * D : 4 * D]).astype(jnp.bfloat16)
    dout = up.received(dout)
    up.across()
    dout = dout.reshape(seqs, L, HEADS, HEAD)
    heads = qkv.reshape(seqs, L, 3, HEADS, HEAD)
    prob = jnp.exp(score_block(heads, docs) - lse)
    dvalue = jnp.einsum(
        "shqk,sqhd->skhd", prob.astype(jnp.bfloat16), dout, preferred_element_type=jnp.float32
    )
    dout, dvalue = down.crossed(dout, dvalue)
    if down.paired:
        down.finish()
    dprob = jnp.einsum("sqhd,skhd->shqk", dout, heads[:, :, 2], preferred_element_type=jnp.float32)
    dscore = (prob * (dprob - jnp.sum(prob * dprob, axis=-1, keepdims=True))).astype(jnp.bfloat16)
    dquery = (
        jnp.einsum("shqk,skhd->sqhd", dscore, heads[:, :, 1], preferred_element_type=jnp.float32)
        * 0.125
    )
    dkey = (
        jnp.einsum("shqk,sqhd->skhd", dscore, heads[:, :, 0], preferred_element_type=jnp.float32)
        * 0.125
    )
    dqkv = jnp.stack([dquery, dkey, dvalue], axis=2).reshape(seqs * L, 3 * D).astype(jnp.bfloat16)
    (dqkv,) = up.crossed(dqkv)
    if up.paired:
        up.finish()
    mixed = WorkerPiece((act, dqkv), (out, dattn))
    dxzero = drone + matmul_nt(dqkv, weights[:, 0 : 3 * D])
    _, pull = jax.vjp(norm_rows, embedded, small[base], small[base + 1])
    dembed, dgain_emb, dshift_emb = pull(dxzero)
    dembed = mixed.received(dembed)
    if down.paired:
        dembed, down.result = together(dembed, down.result)
    bias_qkv = jnp.sum(dqkv, axis=0, dtype=jnp.float32)
    vectors = jnp.stack(
        [
            dgain_emb,
            dshift_emb,
            dgain_one,
            dshift_one,
            dgain_two,
            dshift_two,
            bias_qkv[0:D],
            bias_qkv[2 * D : 3 * D],
            jnp.sum(dattn, axis=0, dtype=jnp.float32),
            jnp.sum(dffn, axis=0, dtype=jnp.float32),
        ]
    )
    bias_up = jnp.sum(dupper, axis=0, dtype=jnp.float32).reshape(FF // D, D)
    return (dembed, jnp.concatenate([vectors, bias_up], axis=0), (mixed, up, down))


def paired_mesh():
    return lax.axis_size("wide") == 8 and lax.axis_size("narrow") == 4


def together(*values):
    return lax.optimization_barrier(values)


def swap_pairs(size, bit):
    return [(place, place ^ bit) for place in range(size)]


def cycle(size, by):
    return [(place, (place + by) % size) for place in range(size)]


def summed_over(value, axis):
    size = lax.axis_size(axis)
    if size & (size - 1):
        return lax.psum(value, axis)
    bit = 1
    while bit < size:
        value = value + lax.ppermute(value, axis, swap_pairs(size, bit))
        bit *= 2
    return value


def gathered_near(value):
    size = lax.axis_size("narrow")
    rows = value.shape[0]
    around = [value]
    for by in range(1, size):
        around.append(lax.ppermute(value, "narrow", cycle(size, size - by)))
    twice = jnp.concatenate(around + around[:-1], axis=0)
    start = lax.rem(size - lax.axis_index("narrow"), size) * rows
    return lax.dynamic_slice_in_dim(twice, start, size * rows, 0)


def scattered_near(value):
    size = lax.axis_size("narrow")
    rows = value.shape[0] // size
    place = lax.axis_index("narrow")
    total = lax.dynamic_slice_in_dim(value, place * rows, rows, 0)
    for by in range(1, size):
        target = lax.rem(place + by, size)
        give = lax.dynamic_slice_in_dim(value, target * rows, rows, 0).astype(jnp.bfloat16)
        take = lax.ppermute(give, "narrow", cycle(size, by))
        total = total + take.astype(jnp.float32)
    return total


def chain_gather(value):
    size = lax.axis_size("narrow")
    rows = value.shape[0]
    rising, falling = value, value
    low, high = [], []
    for step in range(1, size):
        rising = lax.ppermute(rising, "narrow", [(i, i + 1) for i in range(step - 1, size - 1)])
        falling = lax.ppermute(falling, "narrow", [(i, i - 1) for i in range(1, size - step + 1)])
        low.append(rising)
        high.append(falling)
    line = jnp.concatenate(low[::-1] + [value] + high, axis=0)
    start = (size - 1 - lax.axis_index("narrow")) * rows
    return lax.dynamic_slice_in_dim(line, start, size * rows, 0)


def chain_scatter(value):
    size = lax.axis_size("narrow")
    place = lax.axis_index("narrow")

    def block(index):
        return lax.dynamic_index_in_dim(value, jnp.clip(index, 0, size - 1), 0, keepdims=False)

    rising, falling = None, None
    for step in range(1, size):
        up, down = block(size - step + place), block(step + place - size)
        if rising is not None:
            up, down = up + rising, down + falling
        rising = lax.ppermute(up, "narrow", [(i, i + 1) for i in range(step)])
        falling = lax.ppermute(down, "narrow", [(size - 1 - i, size - 2 - i) for i in range(step)])
    return block(place) + rising + falling


class WorkerPiece:
    def __init__(self, *pairs):
        self.pairs = pairs
        self.paired = paired_mesh()
        if not self.paired:
            return
        self.core = lax.axis_index("wide") % 2
        self.pair, self.side = lax.axis_index("narrow") // 2, lax.axis_index("narrow") % 2
        cores = swap_pairs(lax.axis_size("wide"), 1)
        self.far = lax.ppermute(self.block(1 - self.core, 1 - self.side), "wide", cores)
        self.near = lax.ppermute(self.block(1 - self.core, self.side), "wide", cores)

    def block(self, core, side, *terms):
        rows = D // lax.axis_size("narrow")
        blocks, start = [], 0
        for left, right in self.pairs:
            part = lax.dynamic_slice_in_dim(left, (2 * core + side) * rows, rows, 1)
            total = matmul_tn(part, right)
            for term in terms:
                total = total + term[:, start : start + right.shape[1]].astype(jnp.float32)
            blocks.append(total.astype(jnp.bfloat16))
            start += right.shape[1]
        return blocks[0] if len(blocks) == 1 else jnp.concatenate(blocks, axis=1)

    def received(self, value):
        if self.paired:
            value, self.far, self.near = together(value, self.far, self.near)
        return value

    def across(self):
        if self.paired:
            sides = swap_pairs(lax.axis_size("narrow"), 1)
            away = self.block(self.core, 1 - self.side, self.far)
            self.away = lax.ppermute(away, "narrow", sides)

    def crossed(self, *values):
        if self.paired:
            *values, self.away = together(*values, self.away)
        return values

    def finish(self):
        if not self.paired:
            blocks = [matmul_tn(left, right).astype(jnp.bfloat16) for left, right in self.pairs]
            grad = jnp.concatenate(blocks, axis=1)
            self.result = lax.psum_scatter(grad, "narrow", scatter_dimension=0, tiled=True)
            return
        n_wide, n_narrow = lax.axis_size("wide"), lax.axis_size("narrow")
        total = self.block(self.core, self.side, self.near, self.away)
        moves = []
        for wide in range(n_wide):
            for narrow in range(n_narrow):
                if narrow // 2 != wide % 2:
                    target_wide = wide - wide % 2 + narrow // 2
                    target = target_wide * n_narrow + 2 * (wide % 2) + narrow % 2
                    moves.append((wide * n_narrow + narrow, target))
        moved = lax.ppermute(total, ("wide", "narrow"), moves)
        self.result = jnp.where(self.pair == self.core, total, moved)


def hosted_rows(token_ids, mlm_labels, mlm_valid, doc_ids, mlm_pos):
    n_wide, n_narrow = lax.axis_size("wide"), lax.axis_size("narrow")
    packed = jnp.concatenate([token_ids, mlm_labels, mlm_valid], axis=1)[None]
    for bit, place in zip((1, 2, 4), wide_places()):
        other = lax.ppermute(packed, "wide", swap_pairs(n_wide, bit))
        first, second = jnp.where(place == 0, packed, other), jnp.where(place == 0, other, packed)
        packed = jnp.concatenate([first, second], axis=0)
    width = packed.shape[2]
    hosted = packed.reshape(n_wide // 2, 2, 2, 2, width).transpose(1, 2, 0, 3, 4)
    hosted = hosted.reshape(n_narrow, n_wide, width)
    column = lax.dynamic_index_in_dim(hosted, lax.axis_index("wide"), 1, keepdims=False)
    moves = []
    for wide in range(n_wide):
        for row in range(n_narrow):
            target_wide = wide - wide % 2 + row % 2
            target_narrow = 2 * (wide % 2) + row // 2
            moves.append((wide * n_narrow + row, target_wide * n_narrow + target_narrow))
    own = lax.ppermute(jnp.concatenate([doc_ids, mlm_pos], axis=1), ("wide", "narrow"), moves)
    return (
        hosted[:, :, 0:L],
        column[:, L : L + MPS],
        column[:, L + MPS :],
        own[:, 0:L],
        own[:, L:],
    )


FREE = pl.CostEstimate(flops=0, bytes_accessed=0, transcendentals=0)
STREAMS = 4


def take_kernel(ids_ref, table_ref, out_ref, held, rows):
    step, count, size = pl.program_id(0), out_ref.shape[0], table_ref.shape[0]

    @pl.when(step == 0)
    def _():
        held[0:size, :] = table_ref[...]
        held[size:, :] = jnp.zeros((8, table_ref.shape[1]), jnp.float32)

    @pl.loop(0, count, step=16)
    def _(first):
        for by in range(16):
            place = ids_ref[step * count + first + by]
            rows[pl.ds(first + by, 1), :] = held[pl.ds(place, 1), :]

    out_ref[...] = rows[...].astype(out_ref.dtype)


def taken_rows(ids, table):
    size, cols = table.shape
    chunk = 2048
    return pl.pallas_call(
        take_kernel,
        grid_spec=pltpu.PrefetchScalarGridSpec(
            num_scalar_prefetch=1,
            grid=(ids.shape[0] // chunk,),
            in_specs=[pl.BlockSpec((size, cols), lambda step, ids: (0, 0))],
            out_specs=pl.BlockSpec((chunk, cols), lambda step, ids: (step, 0)),
            scratch_shapes=[
                pltpu.VMEM((size + 8, cols), jnp.float32),
                pltpu.VMEM((chunk, cols), jnp.float32),
            ],
        ),
        out_shape=jax.ShapeDtypeStruct((ids.shape[0], cols), jnp.bfloat16),
        compiler_params=pltpu.CompilerParams(vmem_limit_bytes=32 * 2**20),
        cost_estimate=FREE,
        name="take_rows",
    )(ids, table)


def add_kernel(ids_ref, rows_ref, out_ref, rows, *sums):
    step, count, size = pl.program_id(0), rows_ref.shape[1], out_ref.shape[0]
    stream = pl.num_programs(0) * count

    @pl.when(step == 0)
    def _():
        for part in sums:
            part[...] = jnp.zeros_like(part)

    rows[...] = rows_ref[...].astype(jnp.float32)

    @pl.loop(0, count, step=8)
    def _(first):
        for by in range(8):
            for index, part in enumerate(sums):
                place = ids_ref[index * stream + step * count + first + by]
                part[pl.ds(place, 1), :] += rows[index, pl.ds(first + by, 1), :]

    @pl.when(step == pl.num_programs(0) - 1)
    def _():
        total = sums[0][0:size, :]
        for part in sums[1:]:
            total = total + part[0:size, :]
        out_ref[...] = total


def added_rows(ids, values, size):
    count, cols = values.shape
    chunk = 512
    return pl.pallas_call(
        add_kernel,
        grid_spec=pltpu.PrefetchScalarGridSpec(
            num_scalar_prefetch=1,
            grid=(count // STREAMS // chunk,),
            in_specs=[pl.BlockSpec((STREAMS, chunk, cols), lambda step, ids: (0, step, 0))],
            out_specs=pl.BlockSpec((size, cols), lambda step, ids: (0, 0)),
            scratch_shapes=[pltpu.VMEM((STREAMS, chunk, cols), jnp.float32)]
            + [pltpu.VMEM((size + 8, cols), jnp.float32)] * STREAMS,
        ),
        out_shape=jax.ShapeDtypeStruct((size, cols), jnp.float32),
        compiler_params=pltpu.CompilerParams(vmem_limit_bytes=40 * 2**20),
        cost_estimate=FREE,
        name="add_rows",
    )(ids, values.reshape(STREAMS, count // STREAMS, cols))


def wide_places():
    wide_me = lax.axis_index("wide")
    return wide_me % 2, wide_me // 2 % 2, wide_me // 4


def scattered_sum(sent):
    n_wide = lax.axis_size("wide")
    rows, cols = sent.shape
    part = cols // n_wide
    if not paired_mesh():
        whole = lax.psum(sent.astype(jnp.bfloat16), "wide").astype(jnp.float32)
        return lax.dynamic_slice_in_dim(whole, lax.axis_index("wide") * part, part, 1)
    core, x, y = wide_places()

    def block(value, place):
        return lax.dynamic_slice_in_dim(value, place * part, part, 1)

    give = [block(sent, 2 * chip + 1 - core).astype(jnp.bfloat16) for chip in range(4)]
    take = [lax.ppermute(part_of, "wide", swap_pairs(n_wide, 1)) for part_of in give]
    chips = jnp.stack([block(sent, 2 * chip + core) + take[chip] for chip in range(4)])
    half = rows // 2

    def send(value, bit):
        return lax.ppermute(value.astype(jnp.bfloat16), "wide", swap_pairs(n_wide, bit))

    def pick(value, index):
        return lax.dynamic_index_in_dim(value, index, 0, keepdims=False)

    upper, lower = chips[:, 0:half], chips[:, half:]
    upper_far = send(pick(upper, 2 * (1 - y) + 1 - x), 2)
    upper_near = send(pick(upper, 2 * y + 1 - x), 2)
    lower_far = send(pick(lower, 2 * (1 - y) + 1 - x), 4)
    lower_near = send(pick(lower, 2 * (1 - y) + x), 4)
    upper_far = send(pick(upper, 2 * (1 - y) + x) + upper_far, 4)
    lower_far = send(pick(lower, 2 * y + 1 - x) + lower_far, 2)
    own_upper = pick(upper, 2 * y + x) + upper_near + upper_far
    own_lower = pick(lower, 2 * y + x) + lower_near + lower_far
    return jnp.concatenate([own_upper, own_lower], axis=0)


def small_total(value):
    if not paired_mesh():
        return lax.psum(value, ("wide", "narrow"))
    n_wide, n_narrow = lax.axis_size("wide"), lax.axis_size("narrow")
    places = list(zip((1, 2, 4), wide_places()))
    for bit, place in places:
        half = value.shape[1] // 2
        give = lax.dynamic_slice_in_dim(value, (1 - place) * half, half, 1).astype(jnp.bfloat16)
        keep = lax.dynamic_slice_in_dim(value, place * half, half, 1)
        value = keep + lax.ppermute(give, "wide", swap_pairs(n_wide, bit)).astype(jnp.float32)
    bit = 1
    while bit < n_narrow:
        low = value.astype(jnp.bfloat16)
        other = lax.ppermute(low, "narrow", swap_pairs(n_narrow, bit))
        value = low.astype(jnp.float32) + other.astype(jnp.float32)
        bit *= 2
    value = value.astype(jnp.bfloat16)
    for bit, place in reversed(places):
        other = lax.ppermute(value, "wide", swap_pairs(n_wide, bit))
        first, second = jnp.where(place == 0, value, other), jnp.where(place == 0, other, value)
        value = jnp.concatenate([first, second], axis=1)
    return value.astype(jnp.float32)


def shards(
    token_ids,
    doc_ids,
    mlm_pos,
    mlm_labels,
    mlm_valid,
    table,
    table_m,
    table_v,
    small,
    small_m,
    small_v,
    layer,
    layer_m,
    layer_v,
    worker_err,
    server_err,
):
    n_wide, n_narrow = lax.axis_size("wide"), lax.axis_size("narrow")
    narrow_me = lax.axis_index("narrow")
    wide_me = lax.axis_index("wide")
    seqs = doc_ids.shape[0]
    paired = paired_mesh()
    vshard = table.shape[0]
    count = summed_over(jnp.sum(mlm_valid.astype(jnp.float32)), "wide")
    table_low, layer_low = table.astype(jnp.bfloat16), layer.astype(jnp.bfloat16)
    if paired:
        token_ids, mlm_labels, mlm_valid, doc_ids, mlm_pos = hosted_rows(
            token_ids, mlm_labels, mlm_valid, doc_ids, mlm_pos
        )
        layer_rows = chain_gather(layer_low)
    else:
        layer_rows = lax.all_gather(layer_low, "narrow", axis=0, tiled=True)
    weights = lax.all_gather(layer_rows, "wide", axis=1, tiled=True)
    local_ids = token_ids - narrow_me * vshard
    inside = (local_ids >= 0) & (local_ids < vshard)
    if paired:
        slots = jnp.where(inside, local_ids, vshard).reshape(-1)
        picked = taken_rows(slots, table).reshape(n_narrow, n_wide * L, -1)
        looked = chain_scatter(picked).reshape(n_wide, L, -1)
        looked = lax.all_to_all(looked, "wide", 0, 0)
        looked = looked.transpose(1, 0, 2).reshape(1, L, D)
        table_low, weights = together(table_low, weights)
        table_cols = lax.all_gather(table_low, "wide", axis=1, tiled=True)
    else:
        slots = jnp.where(inside, local_ids, vshard).reshape(-1)
        table_cols = lax.all_gather(table_low, "wide", axis=1, tiled=True)
        picked = jnp.take(table_cols, jnp.clip(local_ids, 0, vshard - 1), axis=0)
        picked = jnp.where(inside[..., None], picked, 0.0)
        looked = lax.psum_scatter(picked, "narrow", scatter_dimension=0, tiled=True)
    looked = looked.astype(jnp.float32)
    even_doc = (doc_ids % 2 == 0)[..., None]
    embedded = looked + small[0:L][None] + jnp.where(even_doc, small[L], small[L + 1])
    htwo, kept = layer_forward(embedded.reshape(seqs * L, D), doc_ids, small, weights)
    hmask = jnp.take_along_axis(htwo.reshape(seqs, L, D), mlm_pos[..., None], axis=1)
    hmask = hmask.reshape(seqs * MPS, D).astype(jnp.bfloat16)
    if paired:
        group_h = gathered_near(hmask)
    else:
        group_h = lax.all_gather(hmask, "narrow", axis=0, tiled=True)
    vocab = narrow_me * vshard + jnp.arange(vshard)
    logits = jnp.where((vocab < VREAL)[None], matmul_nt(group_h, table_cols), -1000000000.0)
    labels = mlm_labels.reshape(-1)
    hit = vocab[None] == labels[:, None]
    top = jnp.max(logits, axis=1)
    total = jnp.sum(jnp.exp(logits - top[:, None]), axis=1)
    target = jnp.sum(jnp.where(hit, logits, 0.0), axis=1)
    if paired:
        stats = gathered_near(jnp.stack([top, total, target])[None])
        top, total, target = stats[0]
        for place in range(1, stats.shape[0]):
            top, total, target = merge_rows((top, total, target), tuple(stats[place]))
    else:
        top, total, target = joined((top, total, target), "narrow", merge_rows)
    lse = top + jnp.log(total)
    flags = mlm_valid.reshape(-1).astype(jnp.float32)
    own = seqs * MPS
    own_loss = lax.dynamic_slice_in_dim(flags * (lse - target), narrow_me * own, own)
    dlogit = (
        (jnp.exp(logits - lse[:, None]) - hit.astype(jnp.float32)) * (flags / count)[:, None]
    ).astype(jnp.bfloat16)
    dhmask = matmul(dlogit, table_cols)
    if paired:
        dhmask = scattered_near(dhmask)
    else:
        dhmask = lax.psum_scatter(dhmask, "narrow", scatter_dimension=0, tiled=True)
    dhtwo = (
        jnp.zeros((seqs, L, D), jnp.float32)
        .at[jnp.arange(seqs)[:, None], mlm_pos]
        .add(dhmask.reshape(seqs, MPS, D))
    )
    dembed, vectors, pieces = layer_backward(
        dhtwo.reshape(seqs * L, D), kept, doc_ids, small, weights
    )
    dembed_rows = dembed.reshape(seqs, L, D)
    seg_even = jnp.sum(jnp.where(even_doc, dembed_rows, 0.0), axis=(0, 1))
    seg_odd = jnp.sum(jnp.where(even_doc, 0.0, dembed_rows), axis=(0, 1))
    small_grad = jnp.concatenate(
        [jnp.sum(dembed_rows, axis=0), seg_even[None], seg_odd[None], vectors], axis=0
    )
    mixed = pieces[0]
    if paired:
        cut = dembed.astype(jnp.bfloat16).reshape(L, n_wide, D // n_wide).transpose(1, 0, 2)
        cut = lax.all_to_all(cut, "wide", 0, 0).reshape(n_wide * L, D // n_wide)
        cut, small_grad, dlogit = together(mixed.received(cut), small_grad, dlogit)
        mixed.across()
        group_rows = lax.all_gather(cut, "narrow", axis=0, tiled=True)
        (group_rows,) = mixed.crossed(group_rows)
        mixed.finish()
        blocks = group_h.reshape(-1, n_wide, D // n_wide)
        table_head = jnp.einsum("sv,swc->wvc", dlogit, blocks, preferred_element_type=jnp.float32)
        table_head = table_head.astype(jnp.bfloat16)
        table_head = lax.psum_scatter(table_head, "wide", scatter_dimension=0)
        table_grad = added_rows(slots, group_rows, vshard)
        table_grad = table_grad + table_head.astype(jnp.float32)
    else:
        mixed.finish()
        pieces[1].finish()
        pieces[2].finish()
        group_rows = lax.all_gather(dembed_rows.astype(jnp.bfloat16), "narrow", axis=0, tiled=True)
        table_grad = matmul_tn(dlogit, group_h).at[slots].add(
            group_rows.reshape(-1, D).astype(jnp.float32), mode="drop"
        )
        cut = table_grad.astype(jnp.bfloat16).reshape(vshard, n_wide, D // n_wide)
        table_grad = lax.psum_scatter(cut.transpose(1, 0, 2), "wide", scatter_dimension=0)
        table_grad = table_grad.astype(jnp.float32)
    small_grad = small_total(small_grad)
    small_mom = BETA * small_m + (1.0 - BETA) * small_grad
    small_upd = small_mom / (jnp.sqrt(small_v) + OPT_EPS) + DECAY * small
    small_norms = (jnp.sum(small * small)[None], jnp.sum(small_upd * small_upd)[None])
    table_mom = BETA * table_m + (1.0 - BETA) * table_grad
    table_upd = table_mom / (jnp.sqrt(table_v) + OPT_EPS) + DECAY * table
    table_norms = (jnp.sum(table * table)[None], jnp.sum(table_upd * table_upd)[None])
    worker_grad = jnp.concatenate([piece.result for piece in pieces], axis=1)
    if paired:
        worker_grad, table_norms, small_norms = together(worker_grad, table_norms, small_norms)
    span = BETA * layer_m + (1.0 - BETA) * worker_grad.astype(jnp.float32) + worker_err[0]
    scale = jnp.mean(jnp.abs(span)) + MAG_EPS
    sent = scale * jnp.tanh(span / scale)
    new_worker = (span - sent)[None]
    part_cols = layer.shape[1]
    mixed = scattered_sum(sent) / n_wide
    server_in = mixed + server_err
    sscale = jnp.mean(jnp.abs(server_in)) + MAG_EPS
    server_out = sscale * jnp.tanh(server_in / sscale)
    new_server = server_in - server_out
    new_m = lax.all_gather(server_out.astype(jnp.bfloat16), "wide", axis=1, tiled=True).astype(
        server_out.dtype
    )
    layer_upd = server_out / (jnp.sqrt(layer_v) + OPT_EPS) + DECAY * layer
    column = wide_me * part_cols + jnp.arange(part_cols)
    which = (
        (column >= 3 * D).astype(jnp.int32)
        + (column >= 4 * D).astype(jnp.int32)
        + (column >= 4 * D + FF).astype(jnp.int32)
    )
    onehot = (which[:, None] == jnp.arange(4)[None]).astype(jnp.float32)
    wsq = jnp.sum(jnp.sum(layer * layer, axis=0)[:, None] * onehot, axis=0)
    usq = jnp.sum(jnp.sum(layer_upd * layer_upd, axis=0)[:, None] * onehot, axis=0)
    parts = jnp.concatenate([wsq, usq, *table_norms, jnp.sum(own_loss)[None]])
    sums = summed_over(summed_over(parts, "wide"), "narrow")
    loss_sum = sums[10]
    wnorm = jnp.sqrt(jnp.concatenate([sums[0:4], sums[8:9], small_norms[0]]))
    unorm = jnp.sqrt(jnp.concatenate([sums[4:8], sums[9:10], small_norms[1]]))
    ratio = wnorm / unorm
    new_layer = layer - RATE * jnp.sum(onehot * ratio[None, 0:4], axis=1)[None] * layer_upd
    new_table = table - RATE * ratio[4] * table_upd
    new_small = small - RATE * ratio[5] * small_upd
    return (
        jnp.stack([loss_sum, count]),
        new_table,
        table_mom,
        new_small,
        small_mom,
        new_layer,
        new_m,
        new_worker,
        new_server,
        jnp.stack([wnorm, unorm]),
    )


def solution(mesh):
    placed = (
        P("wide", None),
        P(("wide", "narrow"), None),
        P(("wide", "narrow"), None),
        P("wide", None),
        P("wide", None),
        P("narrow", "wide"),
        P("narrow", "wide"),
        P("narrow", "wide"),
        P(),
        P(),
        P(),
        P("narrow", "wide"),
        P("narrow", None),
        P("narrow", "wide"),
        P("wide", "narrow", None),
        P("narrow", "wide"),
    )
    return jax.shard_map(
        shards,
        mesh=mesh,
        in_specs=placed,
        out_specs=(
            P(),
            P("narrow", "wide"),
            P("narrow", "wide"),
            P(),
            P(),
            P("narrow", "wide"),
            P("narrow", None),
            P("wide", "narrow", None),
            P("narrow", "wide"),
            P(),
        ),
        check_vma=False,
    )
```

```python
import jax
import jax.numpy as jnp
from jax import lax
from jax.experimental import pallas as pl
from jax.experimental.pallas import tpu as pltpu
from jax.sharding import PartitionSpec as P

D = 1024
HEADS = 16
HEAD = 64
FF = 4096
VREAL = 30522
L = 512
MPS = 80


LN_EPS = 1e-12
BETA = 0.9
DECAY = 0.01
RATE = 0.25
OPT_EPS = 1e-06
MAG_EPS = 1e-08

FREE = pl.CostEstimate(flops=0, bytes_accessed=0, transcendentals=0)


def joined(value, axis, join):
    pieces = jax.tree.map(lambda part: lax.all_gather(part, axis), value)
    head = jax.tree.map(lambda part: part[0], pieces)
    tail = jax.tree.map(lambda part: part[1:], pieces)
    subtotal, _ = lax.scan(lambda subtotal, slab: (join(subtotal, slab), None), head, tail)
    return subtotal


def norm_rows(x, gain, shift):
    mean = jnp.mean(x, axis=-1, keepdims=True)
    cent = x - mean
    var = jnp.mean(cent * cent, axis=-1, keepdims=True)
    return cent * lax.rsqrt(var + LN_EPS) * gain + shift


def gelu_exact(upper):
    return jax.nn.gelu(upper, approximate=False)


def matmul(left, right):
    return jnp.dot(left, right, preferred_element_type=jnp.float32)


def matmul_tn(left, right):
    return lax.dot_general(
        left, right, (((0,), (0,)), ((), ())), preferred_element_type=jnp.float32
    )


def matmul_nt(left, right):
    return lax.dot_general(
        left, right, (((1,), (1,)), ((), ())), preferred_element_type=jnp.float32
    )


def attend_kernel(q_ref, k_ref, v_ref, key_doc_ref, query_doc_ref, out_ref, lse_ref):
    same = key_doc_ref[...] == query_doc_ref[...]
    lane = lax.broadcasted_iota(jnp.int32, (1, 2 * HEAD), 1)
    outs = []
    for head in range(2):
        mine = lane // HEAD == head
        query = jnp.where(mine, q_ref[...] * 0.125, 0).astype(jnp.bfloat16)
        scores = jnp.where(same, matmul_nt(k_ref[...], query), -1000000000.0)
        top = jnp.max(scores, axis=0, keepdims=True)
        power = jnp.exp(scores - top)
        total = jnp.sum(power, axis=0, keepdims=True)
        lse_ref[0, head : head + 1, :] = top + jnp.log(total)
        prob = (power * (1.0 / total)).astype(jnp.bfloat16)
        outs.append(matmul_tn(prob, v_ref[...]))
    out_ref[...] = jnp.where(lane < HEAD, outs[0], outs[1]).astype(jnp.bfloat16)


def head_pairs(offset):
    return pl.BlockSpec((L, 2 * HEAD), lambda pair: (0, offset * HEADS // 2 + pair))


def attend(qkv, docs):
    return pl.pallas_call(
        attend_kernel,
        grid=(HEADS // 2,),
        in_specs=[
            head_pairs(0),
            head_pairs(1),
            head_pairs(2),
            pl.BlockSpec((L, 1), lambda pair: (0, 0)),
            pl.BlockSpec((1, L), lambda pair: (0, 0)),
        ],
        out_specs=[head_pairs(0), pl.BlockSpec((1, 2, L), lambda pair: (pair, 0, 0))],
        out_shape=[
            jax.ShapeDtypeStruct((L, D), jnp.bfloat16),
            jax.ShapeDtypeStruct((HEADS // 2, 2, L), jnp.float32),
        ],
        compiler_params=pltpu.CompilerParams(vmem_limit_bytes=40 * 2**20),
        cost_estimate=FREE,
        name="attend",
    )(qkv, qkv, qkv, docs.reshape(L, 1), docs.reshape(1, L))


def attend_back_kernel(q_ref, k_ref, v_ref, do_ref, lse_ref, key_doc_ref, query_doc_ref, out_ref):
    pair = pl.program_id(0)
    same = key_doc_ref[...] == query_doc_ref[...]
    lane = lax.broadcasted_iota(jnp.int32, (1, 2 * HEAD), 1)
    both = []
    for head in range(2):
        mine = lane // HEAD == head
        query = jnp.where(mine, q_ref[...] * 0.125, 0).astype(jnp.bfloat16)
        dout = jnp.where(mine, do_ref[...], 0).astype(jnp.bfloat16)
        scores = jnp.where(same, matmul_nt(k_ref[...], query), -1000000000.0)
        prob = jnp.exp(scores - lse_ref[0, head : head + 1, :])
        dvalue = matmul(prob.astype(jnp.bfloat16), dout)
        dprob = matmul_nt(v_ref[...], dout)
        delta = jnp.sum(prob * dprob, axis=0, keepdims=True)
        dscore = (prob * (dprob - delta)).astype(jnp.bfloat16)
        both.append((matmul_tn(dscore, k_ref[...]) * 0.125, matmul(dscore, query), dvalue))
    for part in range(3):
        value = jnp.where(lane < HEAD, both[0][part], both[1][part]).astype(jnp.bfloat16)
        start = pl.multiple_of(part * D + pair * 2 * HEAD, 2 * HEAD)
        out_ref[:, pl.ds(start, 2 * HEAD)] = value


def attend_back(qkv, dout, lse, docs):
    return pl.pallas_call(
        attend_back_kernel,
        grid=(HEADS // 2,),
        in_specs=[
            head_pairs(0),
            head_pairs(1),
            head_pairs(2),
            head_pairs(0),
            pl.BlockSpec((1, 2, L), lambda pair: (pair, 0, 0)),
            pl.BlockSpec((L, 1), lambda pair: (0, 0)),
            pl.BlockSpec((1, L), lambda pair: (0, 0)),
        ],
        out_specs=pl.BlockSpec((L, 3 * D), lambda pair: (0, 0)),
        out_shape=jax.ShapeDtypeStruct((L, 3 * D), jnp.bfloat16),
        compiler_params=pltpu.CompilerParams(vmem_limit_bytes=40 * 2**20),
        cost_estimate=FREE,
        name="attend_back",
    )(qkv, qkv, qkv, dout, lse, docs.reshape(L, 1), docs.reshape(1, L))


def merge_rows(first, second):
    peak = jnp.maximum(first[0], second[0])
    total = first[1] * jnp.exp(first[0] - peak) + second[1] * jnp.exp(second[0] - peak)
    return (peak, total, first[2] + second[2])


def layer_forward(embedded, docs, small, weights):
    base = L + 2
    x0 = norm_rows(embedded, small[base], small[base + 1])
    act = x0.astype(jnp.bfloat16)
    bias = jnp.concatenate([small[base + 6], jnp.zeros((D,), jnp.float32), small[base + 7]])
    qkv = (matmul(act, weights[:, 0 : 3 * D]) + bias).astype(jnp.bfloat16)
    out, lse = attend(qkv, docs)
    rone = x0 + (matmul(out, weights[:, 3 * D : 4 * D]) + small[base + 8])
    hone = norm_rows(rone, small[base + 2], small[base + 3])
    fin = hone.astype(jnp.bfloat16)
    upper = matmul(fin, weights[:, 4 * D : 4 * D + FF]) + small[base + 10 :].reshape(FF)
    gated = gelu_exact(upper).astype(jnp.bfloat16)
    rtwo = hone + (matmul_nt(gated, weights[:, 4 * D + FF :]) + small[base + 9])
    htwo = norm_rows(rtwo, small[base + 4], small[base + 5])
    return (htwo, (embedded, act, qkv, lse, out, rone, fin, upper, gated, rtwo))


def layer_backward(dhtwo, kept, docs, small, weights):
    embedded, act, qkv, lse, out, rone, fin, upper, gated, rtwo = kept
    base = L + 2
    _, pull = jax.vjp(norm_rows, rtwo, small[base + 4], small[base + 5])
    drtwo, dgain_two, dshift_two = pull(dhtwo)
    dffn = drtwo.astype(jnp.bfloat16)
    down = WorkerPiece((dffn, gated))
    dgated = matmul(dffn, weights[:, 4 * D + FF :])
    _, pull = jax.vjp(gelu_exact, upper)
    dupper = pull(dgated)[0].astype(jnp.bfloat16)
    dupper = down.received(dupper)
    down.across()
    up = WorkerPiece((fin, dupper))
    dhone = drtwo + matmul_nt(dupper, weights[:, 4 * D : 4 * D + FF])
    _, pull = jax.vjp(norm_rows, rone, small[base + 2], small[base + 3])
    drone, dgain_one, dshift_one = pull(dhone)
    dattn = drone.astype(jnp.bfloat16)
    dout = matmul_nt(dattn, weights[:, 3 * D : 4 * D]).astype(jnp.bfloat16)
    dout = up.received(dout)
    up.across()
    dqkv = attend_back(qkv, dout, lse, docs)
    (dqkv,) = down.crossed(dqkv)
    down.finish()
    mixed = WorkerPiece((act, dqkv), (out, dattn))
    dxzero = drone + matmul_nt(dqkv, weights[:, 0 : 3 * D])
    _, pull = jax.vjp(norm_rows, embedded, small[base], small[base + 1])
    dembed, dgain_emb, dshift_emb = pull(dxzero)
    dembed = mixed.received(dembed)
    dembed, mixed.far = up.crossed(dembed, mixed.far) if up.paired else (dembed, None)
    up.finish()
    mixed.across()
    bias_qkv = jnp.sum(dqkv, axis=0, dtype=jnp.float32)
    vectors = jnp.stack(
        [
            dgain_emb,
            dshift_emb,
            dgain_one,
            dshift_one,
            dgain_two,
            dshift_two,
            bias_qkv[0:D],
            bias_qkv[2 * D : 3 * D],
            jnp.sum(dattn, axis=0, dtype=jnp.float32),
            jnp.sum(dffn, axis=0, dtype=jnp.float32),
        ]
    )
    bias_up = jnp.sum(dupper, axis=0, dtype=jnp.float32).reshape(FF // D, D)
    return (dembed, jnp.concatenate([vectors, bias_up], axis=0), (mixed, up, down))


def paired_mesh():
    return lax.axis_size("wide") == 8 and lax.axis_size("narrow") == 4


def together(*values):
    return lax.optimization_barrier(values)


def swap_pairs(size, bit):
    return [(place, place ^ bit) for place in range(size)]


def cycle(size, by):
    return [(place, (place + by) % size) for place in range(size)]


def summed_over(value, axis):
    size = lax.axis_size(axis)
    if size & (size - 1):
        return lax.psum(value, axis)
    bit = 1
    while bit < size:
        value = value + lax.ppermute(value, axis, swap_pairs(size, bit))
        bit *= 2
    return value


def gathered_near(value):
    size = lax.axis_size("narrow")
    rows = value.shape[0]
    around = [value]
    for by in range(1, size):
        around.append(lax.ppermute(value, "narrow", cycle(size, size - by)))
    twice = jnp.concatenate(around + around[:-1], axis=0)
    start = lax.rem(size - lax.axis_index("narrow"), size) * rows
    return lax.dynamic_slice_in_dim(twice, start, size * rows, 0)


def scattered_near(value):
    size = lax.axis_size("narrow")
    rows = value.shape[0] // size
    place = lax.axis_index("narrow")
    total = lax.dynamic_slice_in_dim(value, place * rows, rows, 0)
    for by in range(1, size):
        target = lax.rem(place + by, size)
        give = lax.dynamic_slice_in_dim(value, target * rows, rows, 0).astype(jnp.bfloat16)
        take = lax.ppermute(give, "narrow", cycle(size, by))
        total = total + take.astype(jnp.float32)
    return total


def chain_gather(value):
    size = lax.axis_size("narrow")
    rows = value.shape[0]
    rising, falling = value, value
    low, high = [], []
    for step in range(1, size):
        rising = lax.ppermute(rising, "narrow", [(i, i + 1) for i in range(step - 1, size - 1)])
        falling = lax.ppermute(falling, "narrow", [(i, i - 1) for i in range(1, size - step + 1)])
        low.append(rising)
        high.append(falling)
    line = jnp.concatenate(low[::-1] + [value] + high, axis=0)
    start = (size - 1 - lax.axis_index("narrow")) * rows
    return lax.dynamic_slice_in_dim(line, start, size * rows, 0)


def chain_scatter(value):
    size = lax.axis_size("narrow")
    place = lax.axis_index("narrow")

    def block(index):
        return lax.dynamic_index_in_dim(value, jnp.clip(index, 0, size - 1), 0, keepdims=False)

    rising, falling = None, None
    for step in range(1, size):
        up, down = block(size - step + place), block(step + place - size)
        if rising is not None:
            up, down = up + rising, down + falling
        rising = lax.ppermute(up, "narrow", [(i, i + 1) for i in range(step)])
        falling = lax.ppermute(down, "narrow", [(size - 1 - i, size - 2 - i) for i in range(step)])
    return block(place) + rising + falling


class WorkerPiece:
    def __init__(self, *pairs):
        self.pairs = pairs
        self.paired = paired_mesh()
        if not self.paired:
            return
        self.core = lax.axis_index("wide") % 2
        self.pair, self.side = lax.axis_index("narrow") // 2, lax.axis_index("narrow") % 2
        cores = swap_pairs(lax.axis_size("wide"), 1)
        self.far = lax.ppermute(self.block(1 - self.core, 1 - self.side), "wide", cores)
        self.near = lax.ppermute(self.block(1 - self.core, self.side), "wide", cores)

    def block(self, core, side, *terms):
        rows = D // lax.axis_size("narrow")
        blocks, start = [], 0
        for left, right in self.pairs:
            part = lax.dynamic_slice_in_dim(left, (2 * core + side) * rows, rows, 1)
            total = matmul_tn(part, right)
            for term in terms:
                total = total + term[:, start : start + right.shape[1]].astype(jnp.float32)
            blocks.append(total.astype(jnp.bfloat16))
            start += right.shape[1]
        return blocks[0] if len(blocks) == 1 else jnp.concatenate(blocks, axis=1)

    def received(self, value):
        if self.paired:
            value, self.far, self.near = together(value, self.far, self.near)
        return value

    def across(self):
        if self.paired:
            sides = swap_pairs(lax.axis_size("narrow"), 1)
            away = self.block(self.core, 1 - self.side, self.far)
            self.away = lax.ppermute(away, "narrow", sides)

    def crossed(self, *values):
        if self.paired:
            *values, self.away = together(*values, self.away)
        return values

    def finish(self):
        if not self.paired:
            blocks = [matmul_tn(left, right).astype(jnp.bfloat16) for left, right in self.pairs]
            grad = jnp.concatenate(blocks, axis=1)
            self.result = lax.psum_scatter(grad, "narrow", scatter_dimension=0, tiled=True)
            return
        n_wide, n_narrow = lax.axis_size("wide"), lax.axis_size("narrow")
        total = self.block(self.core, self.side, self.near, self.away)
        moves = []
        for wide in range(n_wide):
            for narrow in range(n_narrow):
                if narrow // 2 != wide % 2:
                    target_wide = wide - wide % 2 + narrow // 2
                    target = target_wide * n_narrow + 2 * (wide % 2) + narrow % 2
                    moves.append((wide * n_narrow + narrow, target))
        moved = lax.ppermute(total, ("wide", "narrow"), moves)
        self.result = jnp.where(self.pair == self.core, total, moved)


def hosted_rows(token_ids, mlm_labels, mlm_valid, doc_ids, mlm_pos):
    n_wide, n_narrow = lax.axis_size("wide"), lax.axis_size("narrow")
    packed = jnp.concatenate([token_ids, mlm_labels, mlm_valid], axis=1)[None]
    for bit, place in zip((1, 2, 4), wide_places()):
        other = lax.ppermute(packed, "wide", swap_pairs(n_wide, bit))
        first, second = jnp.where(place == 0, packed, other), jnp.where(place == 0, other, packed)
        packed = jnp.concatenate([first, second], axis=0)
    width = packed.shape[2]
    hosted = packed.reshape(n_wide // 2, 2, 2, 2, width).transpose(1, 2, 0, 3, 4)
    hosted = hosted.reshape(n_narrow, n_wide, width)
    column = lax.dynamic_index_in_dim(hosted, lax.axis_index("wide"), 1, keepdims=False)
    moves = []
    for wide in range(n_wide):
        for row in range(n_narrow):
            target_wide = wide - wide % 2 + row % 2
            target_narrow = 2 * (wide % 2) + row // 2
            moves.append((wide * n_narrow + row, target_wide * n_narrow + target_narrow))
    own = lax.ppermute(jnp.concatenate([doc_ids, mlm_pos], axis=1), ("wide", "narrow"), moves)
    return (
        hosted[:, :, 0:L],
        column[:, L : L + MPS],
        column[:, L + MPS :],
        own[:, 0:L],
        own[:, L:],
    )


STREAMS = 4


def take_kernel(ids_ref, table_ref, out_ref, held, rows):
    step, count, size = pl.program_id(0), out_ref.shape[0], table_ref.shape[0]

    @pl.when(step == 0)
    def _():
        held[0:size, :] = table_ref[...]
        held[size:, :] = jnp.zeros((8, table_ref.shape[1]), jnp.float32)

    @pl.loop(0, count, step=16)
    def _(first):
        for by in range(16):
            place = ids_ref[step * count + first + by]
            rows[pl.ds(first + by, 1), :] = held[pl.ds(place, 1), :]

    out_ref[...] = rows[...].astype(out_ref.dtype)


def taken_rows(ids, table):
    size, cols = table.shape
    chunk = 2048
    return pl.pallas_call(
        take_kernel,
        grid_spec=pltpu.PrefetchScalarGridSpec(
            num_scalar_prefetch=1,
            grid=(ids.shape[0] // chunk,),
            in_specs=[pl.BlockSpec((size, cols), lambda step, ids: (0, 0))],
            out_specs=pl.BlockSpec((chunk, cols), lambda step, ids: (step, 0)),
            scratch_shapes=[
                pltpu.VMEM((size + 8, cols), jnp.float32),
                pltpu.VMEM((chunk, cols), jnp.float32),
            ],
        ),
        out_shape=jax.ShapeDtypeStruct((ids.shape[0], cols), jnp.bfloat16),
        compiler_params=pltpu.CompilerParams(vmem_limit_bytes=32 * 2**20),
        cost_estimate=FREE,
        name="take_rows",
    )(ids, table)


def add_kernel(ids_ref, rows_ref, out_ref, rows, *sums):
    step, count, size = pl.program_id(0), rows_ref.shape[1], out_ref.shape[0]
    stream = pl.num_programs(0) * count

    @pl.when(step == 0)
    def _():
        for part in sums:
            part[...] = jnp.zeros_like(part)

    rows[...] = rows_ref[...].astype(jnp.float32)

    @pl.loop(0, count, step=8)
    def _(first):
        for by in range(8):
            for index, part in enumerate(sums):
                place = ids_ref[index * stream + step * count + first + by]
                part[pl.ds(place, 1), :] += rows[index, pl.ds(first + by, 1), :]

    @pl.when(step == pl.num_programs(0) - 1)
    def _():
        total = sums[0][0:size, :]
        for part in sums[1:]:
            total = total + part[0:size, :]
        out_ref[...] = total


def added_rows(ids, values, size):
    count, cols = values.shape
    chunk = 512
    return pl.pallas_call(
        add_kernel,
        grid_spec=pltpu.PrefetchScalarGridSpec(
            num_scalar_prefetch=1,
            grid=(count // STREAMS // chunk,),
            in_specs=[pl.BlockSpec((STREAMS, chunk, cols), lambda step, ids: (0, step, 0))],
            out_specs=pl.BlockSpec((size, cols), lambda step, ids: (0, 0)),
            scratch_shapes=[pltpu.VMEM((STREAMS, chunk, cols), jnp.float32)]
            + [pltpu.VMEM((size + 8, cols), jnp.float32)] * STREAMS,
        ),
        out_shape=jax.ShapeDtypeStruct((size, cols), jnp.float32),
        compiler_params=pltpu.CompilerParams(vmem_limit_bytes=40 * 2**20),
        cost_estimate=pl.CostEstimate(flops=0, bytes_accessed=10**8, transcendentals=0),
        name="add_rows",
    )(ids, values.reshape(STREAMS, count // STREAMS, cols))


def wide_places():
    wide_me = lax.axis_index("wide")
    return wide_me % 2, wide_me // 2 % 2, wide_me // 4


def scattered_sum(sent):
    n_wide = lax.axis_size("wide")
    rows, cols = sent.shape
    part = cols // n_wide
    if not paired_mesh():
        whole = lax.psum(sent.astype(jnp.bfloat16), "wide").astype(jnp.float32)
        return lax.dynamic_slice_in_dim(whole, lax.axis_index("wide") * part, part, 1)
    core, x, y = wide_places()

    def block(value, place):
        return lax.dynamic_slice_in_dim(value, place * part, part, 1)

    give = [block(sent, 2 * chip + 1 - core).astype(jnp.bfloat16) for chip in range(4)]
    take = [lax.ppermute(part_of, "wide", swap_pairs(n_wide, 1)) for part_of in give]
    chips = jnp.stack([block(sent, 2 * chip + core) + take[chip] for chip in range(4)])
    half = rows // 2

    def send(value, bit):
        return lax.ppermute(value.astype(jnp.bfloat16), "wide", swap_pairs(n_wide, bit))

    def pick(value, index):
        return lax.dynamic_index_in_dim(value, index, 0, keepdims=False)

    upper, lower = chips[:, 0:half], chips[:, half:]
    upper_far = send(pick(upper, 2 * (1 - y) + 1 - x), 2)
    upper_near = send(pick(upper, 2 * y + 1 - x), 2)
    lower_far = send(pick(lower, 2 * (1 - y) + 1 - x), 4)
    lower_near = send(pick(lower, 2 * (1 - y) + x), 4)
    upper_far = send(pick(upper, 2 * (1 - y) + x) + upper_far, 4)
    lower_far = send(pick(lower, 2 * y + 1 - x) + lower_far, 2)
    own_upper = pick(upper, 2 * y + x) + upper_near + upper_far
    own_lower = pick(lower, 2 * y + x) + lower_near + lower_far
    return jnp.concatenate([own_upper, own_lower], axis=0)


def small_halved(value):
    n_wide = lax.axis_size("wide")
    for bit, place in zip((1, 2, 4), wide_places()):
        half = value.shape[1] // 2
        give = lax.dynamic_slice_in_dim(value, (1 - place) * half, half, 1).astype(jnp.bfloat16)
        keep = lax.dynamic_slice_in_dim(value, place * half, half, 1)
        value = keep + lax.ppermute(give, "wide", swap_pairs(n_wide, bit)).astype(jnp.float32)
    return value


def small_total(value):
    if not paired_mesh():
        return lax.psum(value, ("wide", "narrow"))
    n_wide, n_narrow = lax.axis_size("wide"), lax.axis_size("narrow")
    bit = 1
    while bit < n_narrow:
        low = value.astype(jnp.bfloat16)
        other = lax.ppermute(low, "narrow", swap_pairs(n_narrow, bit))
        value = low.astype(jnp.float32) + other.astype(jnp.float32)
        bit *= 2
    value = value.astype(jnp.bfloat16)
    for bit, place in reversed(list(zip((1, 2, 4), wide_places()))):
        other = lax.ppermute(value, "wide", swap_pairs(n_wide, bit))
        first, second = jnp.where(place == 0, value, other), jnp.where(place == 0, other, value)
        value = jnp.concatenate([first, second], axis=1)
    return value.astype(jnp.float32)


def shards(
    token_ids,
    doc_ids,
    mlm_pos,
    mlm_labels,
    mlm_valid,
    table,
    table_m,
    table_v,
    small,
    small_m,
    small_v,
    layer,
    layer_m,
    layer_v,
    worker_err,
    server_err,
):
    n_wide, n_narrow = lax.axis_size("wide"), lax.axis_size("narrow")
    narrow_me = lax.axis_index("narrow")
    wide_me = lax.axis_index("wide")
    seqs = doc_ids.shape[0]
    paired = paired_mesh()
    vshard = table.shape[0]
    count = summed_over(jnp.sum(mlm_valid.astype(jnp.float32)), "wide")
    table_low, layer_low = table.astype(jnp.bfloat16), layer.astype(jnp.bfloat16)
    if paired:
        token_ids, mlm_labels, mlm_valid, doc_ids, mlm_pos = hosted_rows(
            token_ids, mlm_labels, mlm_valid, doc_ids, mlm_pos
        )
        layer_rows = chain_gather(layer_low)
    else:
        layer_rows = lax.all_gather(layer_low, "narrow", axis=0, tiled=True)
    weights = lax.all_gather(layer_rows, "wide", axis=1, tiled=True)
    local_ids = token_ids - narrow_me * vshard
    inside = (local_ids >= 0) & (local_ids < vshard)
    if paired:
        slots = jnp.where(inside, local_ids, vshard).reshape(-1)
        picked = taken_rows(slots, table).reshape(n_narrow, n_wide * L, -1)
        looked = chain_scatter(picked).reshape(n_wide, L, -1)
        looked = lax.all_to_all(looked, "wide", 0, 0)
        looked = looked.transpose(1, 0, 2).reshape(1, L, D)
        table_low, weights, looked = together(table_low, weights, looked)
        table_cols = lax.all_gather(table_low, "wide", axis=1, tiled=True)
    else:
        slots = jnp.where(inside, local_ids, vshard).reshape(-1)
        table_cols = lax.all_gather(table_low, "wide", axis=1, tiled=True)
        picked = jnp.take(table_cols, jnp.clip(local_ids, 0, vshard - 1), axis=0)
        picked = jnp.where(inside[..., None], picked, 0.0)
        looked = lax.psum_scatter(picked, "narrow", scatter_dimension=0, tiled=True)
    looked = looked.astype(jnp.float32)
    even_doc = (doc_ids % 2 == 0)[..., None]
    embedded = looked + small[0:L][None] + jnp.where(even_doc, small[L], small[L + 1])
    htwo, kept = layer_forward(embedded.reshape(seqs * L, D), doc_ids, small, weights)
    hmask = jnp.take_along_axis(htwo.reshape(seqs, L, D), mlm_pos[..., None], axis=1)
    hmask = hmask.reshape(seqs * MPS, D).astype(jnp.bfloat16)
    if paired:
        group_h = gathered_near(hmask)
    else:
        group_h = lax.all_gather(hmask, "narrow", axis=0, tiled=True)
    vocab = narrow_me * vshard + jnp.arange(vshard)
    logits = jnp.where((vocab < VREAL)[None], matmul_nt(group_h, table_cols), -1000000000.0)
    labels = mlm_labels.reshape(-1)
    hit = vocab[None] == labels[:, None]
    top = jnp.max(logits, axis=1)
    total = jnp.sum(jnp.exp(logits - top[:, None]), axis=1)
    target = jnp.sum(jnp.where(hit, logits, 0.0), axis=1)
    if paired:
        stats = gathered_near(jnp.stack([top, total, target])[None])
        top, total, target = stats[0]
        for place in range(1, stats.shape[0]):
            top, total, target = merge_rows((top, total, target), tuple(stats[place]))
    else:
        top, total, target = joined((top, total, target), "narrow", merge_rows)
    lse = top + jnp.log(total)
    flags = mlm_valid.reshape(-1).astype(jnp.float32)
    own = seqs * MPS
    own_loss = lax.dynamic_slice_in_dim(flags * (lse - target), narrow_me * own, own)
    dlogit = (
        (jnp.exp(logits - lse[:, None]) - hit.astype(jnp.float32)) * (flags / count)[:, None]
    ).astype(jnp.bfloat16)
    dhmask = matmul(dlogit, table_cols)
    if paired:
        dhmask = scattered_near(dhmask)
        blocks = group_h.reshape(-1, n_wide, D // n_wide)
        table_head = jnp.einsum("sv,swc->wvc", dlogit, blocks, preferred_element_type=jnp.float32)
        table_head, dhmask = together(table_head.astype(jnp.bfloat16), dhmask)
        table_head = lax.psum_scatter(table_head, "wide", scatter_dimension=0)
    else:
        dhmask = lax.psum_scatter(dhmask, "narrow", scatter_dimension=0, tiled=True)
    dhtwo = (
        jnp.zeros((seqs, L, D), jnp.float32)
        .at[jnp.arange(seqs)[:, None], mlm_pos]
        .add(dhmask.reshape(seqs, MPS, D))
    )
    dembed, vectors, pieces = layer_backward(
        dhtwo.reshape(seqs * L, D), kept, doc_ids, small, weights
    )
    dembed_rows = dembed.reshape(seqs, L, D)
    seg_even = jnp.sum(jnp.where(even_doc, dembed_rows, 0.0), axis=(0, 1))
    seg_odd = jnp.sum(jnp.where(even_doc, 0.0, dembed_rows), axis=(0, 1))
    small_grad = jnp.concatenate(
        [jnp.sum(dembed_rows, axis=0), seg_even[None], seg_odd[None], vectors], axis=0
    )
    mixed = pieces[0]
    if paired:
        cut = dembed.astype(jnp.bfloat16).reshape(L, n_wide, D // n_wide).transpose(1, 0, 2)
        cut = lax.all_to_all(cut, "wide", 0, 0).reshape(n_wide * L, D // n_wide)
        small_grad = small_halved(small_grad)
        down, up = pieces[2], pieces[1]
        cut, mixed.away, small_grad, down.result, up.result, table_head = together(
            cut, mixed.away, small_grad, down.result, up.result, table_head
        )
        mixed.finish()
        cut, mixed.result = together(cut, mixed.result)
        group_rows = lax.all_gather(cut, "narrow", axis=0, tiled=True)
    else:
        mixed.finish()
        group_rows = lax.all_gather(dembed_rows.astype(jnp.bfloat16), "narrow", axis=0, tiled=True)
        table_grad = matmul_tn(dlogit, group_h).at[slots].add(
            group_rows.reshape(-1, D).astype(jnp.float32), mode="drop"
        )
        cut = table_grad.astype(jnp.bfloat16).reshape(vshard, n_wide, D // n_wide)
        table_grad = lax.psum_scatter(cut.transpose(1, 0, 2), "wide", scatter_dimension=0)
        table_grad = table_grad.astype(jnp.float32)
    worker_grad = jnp.concatenate([piece.result for piece in pieces], axis=1)
    span = BETA * layer_m + (1.0 - BETA) * worker_grad.astype(jnp.float32) + worker_err[0]
    scale = jnp.mean(jnp.abs(span)) + MAG_EPS
    sent = scale * jnp.tanh(span / scale)
    new_worker = (span - sent)[None]
    part_cols = layer.shape[1]
    server_in = scattered_sum(sent) / n_wide + server_err
    if paired:
        server_in, group_rows, small_grad = together(server_in, group_rows, small_grad)
        table_grad = added_rows(slots, group_rows, vshard)
        table_grad = table_grad + table_head.astype(jnp.float32)
    small_grad = small_total(small_grad)
    small_mom = BETA * small_m + (1.0 - BETA) * small_grad
    small_upd = small_mom / (jnp.sqrt(small_v) + OPT_EPS) + DECAY * small
    small_norms = (jnp.sum(small * small)[None], jnp.sum(small_upd * small_upd)[None])
    table_mom = BETA * table_m + (1.0 - BETA) * table_grad
    table_upd = table_mom / (jnp.sqrt(table_v) + OPT_EPS) + DECAY * table
    table_norms = (jnp.sum(table * table)[None], jnp.sum(table_upd * table_upd)[None])
    sscale = jnp.mean(jnp.abs(server_in)) + MAG_EPS
    server_out = sscale * jnp.tanh(server_in / sscale)
    new_server = server_in - server_out
    new_m = lax.all_gather(server_out.astype(jnp.bfloat16), "wide", axis=1, tiled=True).astype(
        server_out.dtype
    )
    layer_upd = server_out / (jnp.sqrt(layer_v) + OPT_EPS) + DECAY * layer
    column = wide_me * part_cols + jnp.arange(part_cols)
    which = (
        (column >= 3 * D).astype(jnp.int32)
        + (column >= 4 * D).astype(jnp.int32)
        + (column >= 4 * D + FF).astype(jnp.int32)
    )
    onehot = (which[:, None] == jnp.arange(4)[None]).astype(jnp.float32)
    wsq = jnp.sum(jnp.sum(layer * layer, axis=0)[:, None] * onehot, axis=0)
    usq = jnp.sum(jnp.sum(layer_upd * layer_upd, axis=0)[:, None] * onehot, axis=0)
    parts = jnp.concatenate([wsq, usq, *table_norms, jnp.sum(own_loss)[None]])
    sums = summed_over(summed_over(parts, "wide"), "narrow")
    loss_sum = sums[10]
    wnorm = jnp.sqrt(jnp.concatenate([sums[0:4], sums[8:9], small_norms[0]]))
    unorm = jnp.sqrt(jnp.concatenate([sums[4:8], sums[9:10], small_norms[1]]))
    ratio = wnorm / unorm
    new_layer = layer - RATE * jnp.sum(onehot * ratio[None, 0:4], axis=1)[None] * layer_upd
    new_table = table - RATE * ratio[4] * table_upd
    new_small = small - RATE * ratio[5] * small_upd
    return (
        jnp.stack([loss_sum, count]),
        new_table,
        table_mom,
        new_small,
        small_mom,
        new_layer,
        new_m,
        new_worker,
        new_server,
        jnp.stack([wnorm, unorm]),
    )


def solution(mesh):
    placed = (
        P("wide", None),
        P(("wide", "narrow"), None),
        P(("wide", "narrow"), None),
        P("wide", None),
        P("wide", None),
        P("narrow", "wide"),
        P("narrow", "wide"),
        P("narrow", "wide"),
        P(),
        P(),
        P(),
        P("narrow", "wide"),
        P("narrow", None),
        P("narrow", "wide"),
        P("wide", "narrow", None),
        P("narrow", "wide"),
    )
    return jax.shard_map(
        shards,
        mesh=mesh,
        in_specs=placed,
        out_specs=(
            P(),
            P("narrow", "wide"),
            P("narrow", "wide"),
            P(),
            P(),
            P("narrow", "wide"),
            P("narrow", None),
            P("wide", "narrow", None),
            P("narrow", "wide"),
            P(),
        ),
        check_vma=False,
    )
```

```python
import functools

import jax
import jax.numpy as jnp
from jax import lax
from jax.experimental import pallas as pl
from jax.experimental.pallas import tpu as pltpu
from jax.sharding import PartitionSpec as P

D = 1024
HEADS = 16
HEAD = 64
FF = 4096
VREAL = 30522
L = 512
MPS = 80


LN_EPS = 1e-12
BETA = 0.9
DECAY = 0.01
RATE = 0.25
OPT_EPS = 1e-06
MAG_EPS = 1e-08

FREE = pl.CostEstimate(flops=0, bytes_accessed=0, transcendentals=0)


def joined(value, axis, join):
    pieces = jax.tree.map(lambda part: lax.all_gather(part, axis), value)
    head = jax.tree.map(lambda part: part[0], pieces)
    tail = jax.tree.map(lambda part: part[1:], pieces)
    subtotal, _ = lax.scan(lambda subtotal, slab: (join(subtotal, slab), None), head, tail)
    return subtotal


def norm_rows(x, gain, shift):
    mean = jnp.mean(x, axis=-1, keepdims=True)
    cent = x - mean
    var = jnp.mean(cent * cent, axis=-1, keepdims=True)
    return cent * lax.rsqrt(var + LN_EPS) * gain + shift


def gelu_exact(upper):
    return jax.nn.gelu(upper, approximate=False)


def matmul(left, right):
    return jnp.dot(left, right, preferred_element_type=jnp.float32)


def matmul_tn(left, right):
    return lax.dot_general(
        left, right, (((0,), (0,)), ((), ())), preferred_element_type=jnp.float32
    )


def matmul_nt(left, right):
    return lax.dot_general(
        left, right, (((1,), (1,)), ((), ())), preferred_element_type=jnp.float32
    )


def attend_kernel(q_ref, k_ref, v_ref, key_doc_ref, query_doc_ref, out_ref, lse_ref):
    same = key_doc_ref[...] == query_doc_ref[...]
    lane = lax.broadcasted_iota(jnp.int32, (1, 2 * HEAD), 1)
    outs = []
    for head in range(2):
        mine = lane // HEAD == head
        query = jnp.where(mine, q_ref[...] * 0.125, 0).astype(jnp.bfloat16)
        scores = jnp.where(same, matmul_nt(k_ref[...], query), -1000000000.0)
        top = jnp.max(scores, axis=0, keepdims=True)
        power = jnp.exp(scores - top)
        total = jnp.sum(power, axis=0, keepdims=True)
        lse_ref[0, head : head + 1, :] = top + jnp.log(total)
        prob = (power * (1.0 / total)).astype(jnp.bfloat16)
        outs.append(matmul_tn(prob, v_ref[...]))
    out_ref[...] = jnp.where(lane < HEAD, outs[0], outs[1]).astype(jnp.bfloat16)


def head_pairs(offset):
    return pl.BlockSpec((L, 2 * HEAD), lambda pair: (0, offset * HEADS // 2 + pair))


def attend(qkv, docs):
    return pl.pallas_call(
        attend_kernel,
        grid=(HEADS // 2,),
        in_specs=[
            head_pairs(0),
            head_pairs(1),
            head_pairs(2),
            pl.BlockSpec((L, 1), lambda pair: (0, 0)),
            pl.BlockSpec((1, L), lambda pair: (0, 0)),
        ],
        out_specs=[head_pairs(0), pl.BlockSpec((1, 2, L), lambda pair: (pair, 0, 0))],
        out_shape=[
            jax.ShapeDtypeStruct((L, D), jnp.bfloat16),
            jax.ShapeDtypeStruct((HEADS // 2, 2, L), jnp.float32),
        ],
        compiler_params=pltpu.CompilerParams(vmem_limit_bytes=40 * 2**20),
        cost_estimate=FREE,
        name="attend",
    )(qkv, qkv, qkv, docs.reshape(L, 1), docs.reshape(1, L))


def attend_back_kernel(q_ref, k_ref, v_ref, do_ref, lse_ref, key_doc_ref, query_doc_ref, out_ref):
    pair = pl.program_id(0)
    same = key_doc_ref[...] == query_doc_ref[...]
    lane = lax.broadcasted_iota(jnp.int32, (1, 2 * HEAD), 1)
    both = []
    for head in range(2):
        mine = lane // HEAD == head
        query = jnp.where(mine, q_ref[...] * 0.125, 0).astype(jnp.bfloat16)
        dout = jnp.where(mine, do_ref[...], 0).astype(jnp.bfloat16)
        scores = jnp.where(same, matmul_nt(k_ref[...], query), -1000000000.0)
        prob = jnp.exp(scores - lse_ref[0, head : head + 1, :])
        dvalue = matmul(prob.astype(jnp.bfloat16), dout)
        dprob = matmul_nt(v_ref[...], dout)
        delta = jnp.sum(prob * dprob, axis=0, keepdims=True)
        dscore = (prob * (dprob - delta)).astype(jnp.bfloat16)
        both.append((matmul_tn(dscore, k_ref[...]) * 0.125, matmul(dscore, query), dvalue))
    for part in range(3):
        value = jnp.where(lane < HEAD, both[0][part], both[1][part]).astype(jnp.bfloat16)
        start = pl.multiple_of(part * D + pair * 2 * HEAD, 2 * HEAD)
        out_ref[:, pl.ds(start, 2 * HEAD)] = value


def attend_back(qkv, dout, lse, docs):
    return pl.pallas_call(
        attend_back_kernel,
        grid=(HEADS // 2,),
        in_specs=[
            head_pairs(0),
            head_pairs(1),
            head_pairs(2),
            head_pairs(0),
            pl.BlockSpec((1, 2, L), lambda pair: (pair, 0, 0)),
            pl.BlockSpec((L, 1), lambda pair: (0, 0)),
            pl.BlockSpec((1, L), lambda pair: (0, 0)),
        ],
        out_specs=pl.BlockSpec((L, 3 * D), lambda pair: (0, 0)),
        out_shape=jax.ShapeDtypeStruct((L, 3 * D), jnp.bfloat16),
        compiler_params=pltpu.CompilerParams(vmem_limit_bytes=40 * 2**20),
        cost_estimate=FREE,
        name="attend_back",
    )(qkv, qkv, qkv, dout, lse, docs.reshape(L, 1), docs.reshape(1, L))


def merge_rows(first, second):
    peak = jnp.maximum(first[0], second[0])
    total = first[1] * jnp.exp(first[0] - peak) + second[1] * jnp.exp(second[0] - peak)
    return (peak, total, first[2] + second[2])


def layer_forward(embedded, docs, small, weights):
    base = L + 2
    x0 = norm_rows(embedded, small[base], small[base + 1])
    act = x0.astype(jnp.bfloat16)
    bias = jnp.concatenate([small[base + 6], jnp.zeros((D,), jnp.float32), small[base + 7]])
    qkv = (matmul(act, weights[:, 0 : 3 * D]) + bias).astype(jnp.bfloat16)
    out, lse = attend(qkv, docs)
    rone = x0 + (matmul(out, weights[:, 3 * D : 4 * D]) + small[base + 8])
    hone = norm_rows(rone, small[base + 2], small[base + 3])
    fin = hone.astype(jnp.bfloat16)
    upper = matmul(fin, weights[:, 4 * D : 4 * D + FF]) + small[base + 10 :].reshape(FF)
    gated = gelu_exact(upper).astype(jnp.bfloat16)
    rtwo = hone + (matmul_nt(gated, weights[:, 4 * D + FF :]) + small[base + 9])
    htwo = norm_rows(rtwo, small[base + 4], small[base + 5])
    return (htwo, (embedded, act, qkv, lse, out, rone, fin, upper, gated, rtwo))


def layer_backward(dhtwo, kept, docs, small, weights):
    embedded, act, qkv, lse, out, rone, fin, upper, gated, rtwo = kept
    base = L + 2
    _, pull = jax.vjp(norm_rows, rtwo, small[base + 4], small[base + 5])
    drtwo, dgain_two, dshift_two = pull(dhtwo)
    dffn = drtwo.astype(jnp.bfloat16)
    down = WorkerPiece((dffn, gated))
    dgated = matmul(dffn, weights[:, 4 * D + FF :])
    _, pull = jax.vjp(gelu_exact, upper)
    dupper = pull(dgated)[0].astype(jnp.bfloat16)
    dupper = down.received(dupper)
    down.across()
    up = WorkerPiece((fin, dupper))
    dhone = drtwo + matmul_nt(dupper, weights[:, 4 * D : 4 * D + FF])
    _, pull = jax.vjp(norm_rows, rone, small[base + 2], small[base + 3])
    drone, dgain_one, dshift_one = pull(dhone)
    dattn = drone.astype(jnp.bfloat16)
    dout = matmul_nt(dattn, weights[:, 3 * D : 4 * D]).astype(jnp.bfloat16)
    dout = up.received(dout)
    up.across()
    dqkv = attend_back(qkv, dout, lse, docs)
    (dqkv,) = down.crossed(dqkv)
    down.finish()
    mixed = WorkerPiece((act, dqkv), (out, dattn))
    dxzero = drone + matmul_nt(dqkv, weights[:, 0 : 3 * D])
    _, pull = jax.vjp(norm_rows, embedded, small[base], small[base + 1])
    dembed, dgain_emb, dshift_emb = pull(dxzero)
    dembed = mixed.received(dembed)
    dembed, mixed.far = up.crossed(dembed, mixed.far) if up.paired else (dembed, None)
    up.finish()
    mixed.across()
    bias_qkv = jnp.sum(dqkv, axis=0, dtype=jnp.float32)
    vectors = jnp.stack(
        [
            dgain_emb,
            dshift_emb,
            dgain_one,
            dshift_one,
            dgain_two,
            dshift_two,
            bias_qkv[0:D],
            bias_qkv[2 * D : 3 * D],
            jnp.sum(dattn, axis=0, dtype=jnp.float32),
            jnp.sum(dffn, axis=0, dtype=jnp.float32),
        ]
    )
    bias_up = jnp.sum(dupper, axis=0, dtype=jnp.float32).reshape(FF // D, D)
    return (dembed, jnp.concatenate([vectors, bias_up], axis=0), (mixed, up, down))


def paired_mesh():
    return lax.axis_size("wide") == 8 and lax.axis_size("narrow") == 4


def together(*values):
    return lax.optimization_barrier(values)


def swap_pairs(size, bit):
    return [(place, place ^ bit) for place in range(size)]


def cycle(size, by):
    return [(place, (place + by) % size) for place in range(size)]


def summed_over(value, axis):
    size = lax.axis_size(axis)
    if size & (size - 1):
        return lax.psum(value, axis)
    bit = 1
    while bit < size:
        value = value + lax.ppermute(value, axis, swap_pairs(size, bit))
        bit *= 2
    return value


def gathered_near(value, beside=None):
    size = lax.axis_size("narrow")
    rows = value.shape[0]
    around = [value]
    for by in range(1, size):
        around.append(lax.ppermute(value, "narrow", cycle(size, size - by)))
    if beside is not None:
        *around, beside = together(*around, beside)
    twice = jnp.concatenate(around + around[:-1], axis=0)
    start = lax.rem(size - lax.axis_index("narrow"), size) * rows
    whole = lax.dynamic_slice_in_dim(twice, start, size * rows, 0)
    return whole if beside is None else (whole, beside)


def scattered_near(value):
    size = lax.axis_size("narrow")
    rows = value.shape[0] // size
    place = lax.axis_index("narrow")
    total = lax.dynamic_slice_in_dim(value, place * rows, rows, 0)
    for by in range(1, size):
        target = lax.rem(place + by, size)
        give = lax.dynamic_slice_in_dim(value, target * rows, rows, 0).astype(jnp.bfloat16)
        take = lax.ppermute(give, "narrow", cycle(size, by))
        total = total + take.astype(jnp.float32)
    return total


def sent_around(blocks):
    size = lax.axis_size("narrow")
    place = lax.axis_index("narrow")

    def block(by):
        return lax.dynamic_index_in_dim(blocks, lax.rem(place + by, size), 0, keepdims=False)

    moved = [lax.ppermute(block(by), "narrow", cycle(size, by)) for by in range(1, size)]
    return jnp.stack([block(0)] + moved)


class WorkerPiece:
    def __init__(self, *pairs):
        self.pairs = pairs
        self.paired = paired_mesh()
        if not self.paired:
            return
        self.core = lax.axis_index("wide") % 2
        self.pair, self.side = lax.axis_index("narrow") // 2, lax.axis_index("narrow") % 2
        cores = swap_pairs(lax.axis_size("wide"), 1)
        self.far = lax.ppermute(self.block(1 - self.core, 1 - self.side), "wide", cores)
        self.near = lax.ppermute(self.block(1 - self.core, self.side), "wide", cores)

    def block(self, core, side, *terms):
        rows = D // lax.axis_size("narrow")
        blocks, start = [], 0
        for left, right in self.pairs:
            part = lax.dynamic_slice_in_dim(left, (2 * core + side) * rows, rows, 1)
            total = matmul_tn(part, right)
            for term in terms:
                total = total + term[:, start : start + right.shape[1]].astype(jnp.float32)
            blocks.append(total.astype(jnp.bfloat16))
            start += right.shape[1]
        return blocks[0] if len(blocks) == 1 else jnp.concatenate(blocks, axis=1)

    def received(self, value):
        if self.paired:
            value, self.far, self.near = together(value, self.far, self.near)
        return value

    def across(self):
        if self.paired:
            sides = swap_pairs(lax.axis_size("narrow"), 1)
            away = self.block(self.core, 1 - self.side, self.far)
            self.away = lax.ppermute(away, "narrow", sides)

    def crossed(self, *values):
        if self.paired:
            *values, self.away = together(*values, self.away)
        return values

    def finish(self):
        if not self.paired:
            blocks = [matmul_tn(left, right).astype(jnp.bfloat16) for left, right in self.pairs]
            grad = jnp.concatenate(blocks, axis=1)
            self.result = lax.psum_scatter(grad, "narrow", scatter_dimension=0, tiled=True)
            return
        n_wide, n_narrow = lax.axis_size("wide"), lax.axis_size("narrow")
        total = self.block(self.core, self.side, self.near, self.away)
        moves = []
        for wide in range(n_wide):
            for narrow in range(n_narrow):
                if narrow // 2 != wide % 2:
                    target_wide = wide - wide % 2 + narrow // 2
                    target = target_wide * n_narrow + 2 * (wide % 2) + narrow % 2
                    moves.append((wide * n_narrow + narrow, target))
        moved = lax.ppermute(total, ("wide", "narrow"), moves)
        self.result = jnp.where(self.pair == self.core, total, moved)


def hosted_rows(token_ids, mlm_labels, mlm_valid, doc_ids, mlm_pos):
    n_wide, n_narrow = lax.axis_size("wide"), lax.axis_size("narrow")
    packed = jnp.concatenate([token_ids, mlm_labels, mlm_valid], axis=1)[None]
    for bit, place in zip((1, 2, 4), wide_places()):
        other = lax.ppermute(packed, "wide", swap_pairs(n_wide, bit))
        first, second = jnp.where(place == 0, packed, other), jnp.where(place == 0, other, packed)
        packed = jnp.concatenate([first, second], axis=0)
    width = packed.shape[2]
    hosted = packed.reshape(n_wide // 2, 2, 2, 2, width).transpose(1, 2, 0, 3, 4)
    hosted = hosted.reshape(n_narrow, n_wide, width)
    column = lax.dynamic_index_in_dim(hosted, lax.axis_index("wide"), 1, keepdims=False)
    moves = []
    for wide in range(n_wide):
        for row in range(n_narrow):
            target_wide = wide - wide % 2 + row % 2
            target_narrow = 2 * (wide % 2) + row // 2
            moves.append((wide * n_narrow + row, target_wide * n_narrow + target_narrow))
    own = lax.ppermute(jnp.concatenate([doc_ids, mlm_pos], axis=1), ("wide", "narrow"), moves)
    return (
        hosted[:, :, 0:L],
        column[:, L : L + MPS],
        column[:, L + MPS :],
        own[:, 0:L],
        own[:, L:],
    )


STREAMS = 2


class Owners:
    def __init__(self, tokens, vshard):
        size = lax.axis_size("narrow")
        place = lax.axis_index("narrow")
        count = tokens.shape[1]
        self.room = count * 7 // 16
        owner = tokens // vshard
        held = (owner[None] == jnp.arange(size)[:, None, None]).astype(jnp.bfloat16)
        tiles = held.reshape(-1, count // 128, 128)
        order = jnp.arange(128)
        within = jnp.einsum(
            "btl,lm->btm",
            tiles,
            (order[:, None] < order[None]).astype(jnp.bfloat16),
            preferred_element_type=jnp.float32,
        )
        sums = jnp.sum(tiles.astype(jnp.float32), axis=2)
        tile = jnp.arange(count // 128)
        before = jnp.sum(jnp.where(tile[:, None] < tile[None], sums[:, :, None], 0.0), axis=1)
        rank = (within + before[..., None]).reshape(size, size, count) * held.astype(jnp.float32)
        rank = jnp.sum(rank, axis=0).astype(jnp.int32)
        self.full = jnp.max(jnp.sum(sums, axis=1)) > self.room
        self.count, self.vshard = count, vshard
        own = lax.dynamic_index_in_dim(owner, place, 0, keepdims=False)
        self.rank = lax.dynamic_index_in_dim(rank, place, 0, keepdims=False)
        self.behind = lax.rem(place - own + size, size)
        self.slots = jnp.where(owner == place, tokens - place * vshard, vshard)

    def behind_slots(self, room):
        return self.behind * room + jnp.minimum(self.rank, room - 1)

    def packed(self, slots):
        base = self.vshard + 1
        order = jnp.arange(self.count) * base + slots
        order = jnp.where(slots < self.vshard, order, order + self.count * base)
        order = lax.sort(order)
        return order % base, order // base % self.count


def pack_kernel(ids_ref, table_ref, out_ref, held, *rows):
    step, count, size = pl.program_id(0), out_ref.shape[1], table_ref.shape[0]

    @pl.when(step == 0)
    def _():
        held[0:size, :] = table_ref[...]
        held[size:, :] = jnp.zeros((8, table_ref.shape[1]), jnp.float32)
        for part in rows:
            part[...] = jnp.zeros_like(part)

    base = [(step * len(rows) + index) * count for index in range(len(rows))]

    def some(turn, used):
        used = list(used)
        for by in range(8):
            for index, part in enumerate(rows):
                place = ids_ref[base[index] + turn * 8 + by]
                part[pl.ds(used[index], 1), :] = held[pl.ds(place, 1), :]
                used[index] = used[index] + jnp.where(place < size, 1, 0)
        return tuple(used)

    lax.fori_loop(0, count // 8, some, (0,) * len(rows))
    for index, part in enumerate(rows):
        out_ref[index] = part[0:count, :].astype(out_ref.dtype)


def packed_rows(ids, table):
    size, cols = table.shape
    places, count = ids.shape
    return pl.pallas_call(
        pack_kernel,
        grid_spec=pltpu.PrefetchScalarGridSpec(
            num_scalar_prefetch=1,
            grid=(places // STREAMS,),
            in_specs=[pl.BlockSpec((size, cols), lambda step, ids: (0, 0))],
            out_specs=pl.BlockSpec((STREAMS, count, cols), lambda step, ids: (step, 0, 0)),
            scratch_shapes=[pltpu.VMEM((size + 8, cols), jnp.float32)]
            + [pltpu.VMEM((count + 8, cols), jnp.float32)] * STREAMS,
        ),
        out_shape=jax.ShapeDtypeStruct((places, count, cols), jnp.bfloat16),
        compiler_params=pltpu.CompilerParams(vmem_limit_bytes=40 * 2**20),
        cost_estimate=pl.CostEstimate(flops=0, bytes_accessed=15 * 10**7, transcendentals=0),
        name="pack_rows",
    )(ids.reshape(-1), table)


def take_kernel(ids_ref, table_ref, out_ref, held, rows):
    held[...] = table_ref[...].astype(jnp.float32)

    @pl.loop(0, out_ref.shape[0], step=16)
    def _(first):
        for by in range(16):
            rows[pl.ds(first + by, 1), :] = held[pl.ds(ids_ref[first + by], 1), :]

    out_ref[...] = rows[...].astype(out_ref.dtype)


def taken_rows(ids, table):
    count, cols = ids.shape[0], table.shape[1]
    return pl.pallas_call(
        take_kernel,
        grid_spec=pltpu.PrefetchScalarGridSpec(
            num_scalar_prefetch=1,
            grid=(1,),
            in_specs=[pl.BlockSpec(table.shape, lambda step, ids: (0, 0))],
            out_specs=pl.BlockSpec((count, cols), lambda step, ids: (0, 0)),
            scratch_shapes=[
                pltpu.VMEM(table.shape, jnp.float32),
                pltpu.VMEM((count, cols), jnp.float32),
            ],
        ),
        out_shape=jax.ShapeDtypeStruct((count, cols), table.dtype),
        compiler_params=pltpu.CompilerParams(vmem_limit_bytes=40 * 2**20),
        cost_estimate=FREE,
        name="take_rows",
    )(ids, table)


def add_kernel(length, ids_ref, from_ref, rows_ref, out_ref, rows, *sums):
    size, each = out_ref.shape[0], rows_ref.shape[1]
    for part in sums:
        part[...] = jnp.zeros_like(part)
    rows[...] = rows_ref[...].astype(jnp.float32)

    @pl.loop(0, length, step=8)
    def _(first):
        for by in range(8):
            for index, part in enumerate(sums):
                place = ids_ref[index * each + first + by]
                row = from_ref[index * each + first + by]
                part[pl.ds(place, 1), :] += rows[index, pl.ds(row, 1), :]

    total = sums[0][0:size, :]
    for part in sums[1:]:
        total = total + part[0:size, :]
    out_ref[...] = total


def added_rows(ids, rows, values, size, length):
    places, count, cols = values.shape
    return pl.pallas_call(
        functools.partial(add_kernel, length),
        grid_spec=pltpu.PrefetchScalarGridSpec(
            num_scalar_prefetch=2,
            grid=(1,),
            in_specs=[pl.BlockSpec(values.shape, lambda step, ids, rows: (0, 0, 0))],
            out_specs=pl.BlockSpec((size, cols), lambda step, ids, rows: (0, 0)),
            scratch_shapes=[pltpu.VMEM(values.shape, jnp.float32)]
            + [pltpu.VMEM((size + 8, cols), jnp.float32)] * places,
        ),
        out_shape=jax.ShapeDtypeStruct((size, cols), jnp.float32),
        compiler_params=pltpu.CompilerParams(vmem_limit_bytes=56 * 2**20),
        cost_estimate=pl.CostEstimate(flops=0, bytes_accessed=5 * 10**7, transcendentals=0),
        name="add_rows",
    )(ids.reshape(-1), rows.reshape(-1), values)


def span_kernel(momentum_ref, grad_ref, error_ref, span_ref, sum_ref):
    grad = grad_ref[...].astype(jnp.float32)
    span = BETA * momentum_ref[...] + (1.0 - BETA) * grad + error_ref[0]
    span_ref[...] = span

    @pl.when(pl.program_id(0) == 0)
    def _():
        sum_ref[...] = jnp.zeros_like(sum_ref)

    sum_ref[...] += jnp.sum(jnp.abs(span), axis=0, keepdims=True)


def span_of(momentum, grad, error, start):
    rows, cols = grad.shape
    block = 1024
    first = start // block
    span, sums = pl.pallas_call(
        span_kernel,
        grid=(cols // block,),
        in_specs=[
            pl.BlockSpec((rows, block), lambda step: (0, first + step)),
            pl.BlockSpec((rows, block), lambda step: (0, step)),
            pl.BlockSpec((1, rows, block), lambda step: (0, 0, first + step)),
        ],
        out_specs=[
            pl.BlockSpec((rows, block), lambda step: (0, step)),
            pl.BlockSpec((1, block), lambda step: (0, 0)),
        ],
        out_shape=[
            jax.ShapeDtypeStruct((rows, cols), jnp.float32),
            jax.ShapeDtypeStruct((1, block), jnp.float32),
        ],
        compiler_params=pltpu.CompilerParams(vmem_limit_bytes=24 * 2**20),
        cost_estimate=FREE,
        name="span",
    )(momentum, grad, error)
    return span, jnp.sum(sums)


def press_kernel(steps, scale_ref, *refs):
    *span_refs, error_ref, sent_ref = refs
    step = pl.program_id(0)
    scale = scale_ref[0]
    inverse = scale_ref[1]
    for index, span_ref in enumerate(span_refs):

        @pl.when((step >= steps[index]) & (step < steps[index + 1]))
        def _():
            span = span_ref[...]
            sent = scale * jnp.tanh(span * inverse)
            error_ref[0] = span - sent
            sent_ref[0] = sent.astype(jnp.bfloat16)


def pressed(spans, scale, parts):
    rows = spans[0].shape[0]
    cols = sum(span.shape[1] for span in spans)
    block = 512
    each = cols // parts // block
    steps = [0]
    for span in spans:
        steps.append(steps[-1] + span.shape[1] // block)

    def of(index):
        low, count = steps[index], steps[index + 1] - steps[index]
        return pl.BlockSpec((rows, block), lambda step: (0, jnp.clip(step - low, 0, count - 1)))

    return pl.pallas_call(
        functools.partial(press_kernel, steps),
        grid=(steps[-1],),
        in_specs=[pl.BlockSpec(memory_space=pltpu.SMEM)] + [of(i) for i in range(len(spans))],
        out_specs=[
            pl.BlockSpec((1, rows, block), lambda step: (0, 0, step)),
            pl.BlockSpec((1, rows, block), lambda step: (step // each, 0, step % each)),
        ],
        out_shape=[
            jax.ShapeDtypeStruct((1, rows, cols), jnp.float32),
            jax.ShapeDtypeStruct((parts, rows, cols // parts), jnp.bfloat16),
        ],
        compiler_params=pltpu.CompilerParams(vmem_limit_bytes=24 * 2**20),
        cost_estimate=FREE,
        name="press",
    )(jnp.stack([scale, 1.0 / scale]), *spans)


def update_kernel(grad_ref, head_ref, table_ref, first_ref, second_ref, *out_refs):
    first_out, update_ref, weight_sum, update_sum = out_refs
    grad = grad_ref[...] + head_ref[...].astype(jnp.float32)
    first = BETA * first_ref[...] + (1.0 - BETA) * grad
    table = table_ref[...]
    update = first / (jnp.sqrt(second_ref[...]) + OPT_EPS) + DECAY * table
    first_out[...] = first
    update_ref[...] = update

    @pl.when(pl.program_id(0) == 0)
    def _():
        weight_sum[...] = jnp.zeros_like(weight_sum)
        update_sum[...] = jnp.zeros_like(update_sum)

    weight_sum[...] += jnp.sum(table * table, axis=0, keepdims=True)
    update_sum[...] += jnp.sum(update * update, axis=0, keepdims=True)


def table_update(grad, head, table, first, second):
    size, cols = table.shape
    block = size // 9 if size % 9 == 0 and size // 9 % 16 == 0 else size
    whole = pl.BlockSpec((block, cols), lambda step: (step, 0))
    line = pl.BlockSpec((1, cols), lambda step: (0, 0))
    moment, update, *sums = pl.pallas_call(
        update_kernel,
        grid=(size // block,),
        in_specs=[whole] * 5,
        out_specs=[whole, whole, line, line],
        out_shape=[jax.ShapeDtypeStruct((size, cols), jnp.float32)] * 2
        + [jax.ShapeDtypeStruct((1, cols), jnp.float32)] * 2,
        compiler_params=pltpu.CompilerParams(vmem_limit_bytes=56 * 2**20),
        cost_estimate=FREE,
        name="update",
    )(grad, head, table, first, second)
    return moment, update, tuple(jnp.sum(part)[None] for part in sums)


def wide_places():
    wide_me = lax.axis_index("wide")
    return wide_me % 2, wide_me // 2 % 2, wide_me // 4


def scattered_sum(sent):
    n_wide = lax.axis_size("wide")
    core, x, y = wide_places()

    def send(value, bit):
        return lax.ppermute(value.astype(jnp.bfloat16), "wide", swap_pairs(n_wide, bit))

    def pick(value, index):
        return lax.dynamic_index_in_dim(value, index, 0, keepdims=False)

    rows, cols = sent.shape[1:]
    by_core = sent.reshape(n_wide // 2, 2, rows, cols)
    give = lax.dynamic_index_in_dim(by_core, 1 - core, 1, keepdims=False)
    keep = lax.dynamic_index_in_dim(by_core, core, 1, keepdims=False)
    take = send(give, 1)
    half = rows // 2

    def chip(y_of, x_of, part):
        low, high = part * half, (part + 1) * half
        index = 2 * y_of + x_of
        own, other = pick(keep[:, low:high], index), pick(take[:, low:high], index)
        return own.astype(jnp.float32) + other.astype(jnp.float32)

    upper_far = send(chip(1 - y, 1 - x, 0), 2)
    lower_far = send(chip(1 - y, 1 - x, 1), 4)
    upper_near = send(chip(y, 1 - x, 0), 2)
    lower_near = send(chip(1 - y, x, 1), 4)
    upper_far = send(chip(1 - y, x, 0) + upper_far.astype(jnp.float32), 4)
    lower_far = send(chip(y, 1 - x, 1) + lower_far.astype(jnp.float32), 2)
    own_upper = chip(y, x, 0) + upper_near.astype(jnp.float32) + upper_far.astype(jnp.float32)
    own_lower = chip(y, x, 1) + lower_near.astype(jnp.float32) + lower_far.astype(jnp.float32)
    return jnp.concatenate([own_upper, own_lower], axis=0)


def small_halved(value):
    n_wide = lax.axis_size("wide")
    for bit, place in zip((1, 2, 4), wide_places()):
        half = value.shape[1] // 2
        give = lax.dynamic_slice_in_dim(value, (1 - place) * half, half, 1).astype(jnp.bfloat16)
        keep = lax.dynamic_slice_in_dim(value, place * half, half, 1)
        value = keep + lax.ppermute(give, "wide", swap_pairs(n_wide, bit)).astype(jnp.float32)
    return value


def small_total(value):
    n_wide, n_narrow = lax.axis_size("wide"), lax.axis_size("narrow")
    bit = 1
    while bit < n_narrow:
        low = value.astype(jnp.bfloat16)
        other = lax.ppermute(low, "narrow", swap_pairs(n_narrow, bit))
        value = low.astype(jnp.float32) + other.astype(jnp.float32)
        bit *= 2
    value = value.astype(jnp.bfloat16)
    for bit, place in reversed(list(zip((1, 2, 4), wide_places()))):
        other = lax.ppermute(value, "wide", swap_pairs(n_wide, bit))
        first, second = jnp.where(place == 0, value, other), jnp.where(place == 0, other, value)
        value = jnp.concatenate([first, second], axis=1)
    return value.astype(jnp.float32)


def shards(
    token_ids,
    doc_ids,
    mlm_pos,
    mlm_labels,
    mlm_valid,
    table,
    table_m,
    table_v,
    small,
    small_m,
    small_v,
    layer,
    layer_m,
    layer_v,
    worker_err,
    server_err,
):
    n_wide, n_narrow = lax.axis_size("wide"), lax.axis_size("narrow")
    narrow_me = lax.axis_index("narrow")
    wide_me = lax.axis_index("wide")
    seqs = doc_ids.shape[0]
    paired = paired_mesh()
    vshard = table.shape[0]
    count = summed_over(jnp.sum(mlm_valid.astype(jnp.float32)), "wide")
    table_low, layer_low = table.astype(jnp.bfloat16), layer.astype(jnp.bfloat16)
    if paired:
        token_ids, mlm_labels, mlm_valid, doc_ids, mlm_pos = hosted_rows(
            token_ids, mlm_labels, mlm_valid, doc_ids, mlm_pos
        )
        owners = Owners(token_ids.reshape(n_narrow, n_wide * L), vshard)
        picked = packed_rows(owners.slots, table)
        layer_rows, picked = gathered_near(layer_low, picked)
    else:
        layer_rows = lax.all_gather(layer_low, "narrow", axis=0, tiled=True)
    weights = lax.all_gather(layer_rows, "wide", axis=1, tiled=True)
    if paired:

        def looked_up(room):
            rows = sent_around(picked[:, 0:room])
            return taken_rows(owners.behind_slots(room), rows.reshape(n_narrow * room, -1))

        layer_rows, picked = together(layer_rows, picked)
        looked = looked_up(owners.room)
        looked = lax.cond(owners.full, lambda: looked_up(owners.count), lambda: looked)
        looked = lax.all_to_all(looked.reshape(n_wide, L, -1), "wide", 0, 0)
        looked = looked.transpose(1, 0, 2).reshape(1, L, D)
        looked, slots = together(looked, owners.slots)
        packed_ids, packed_rows_at = owners.packed(slots)
        table_low, weights, looked, packed_ids, packed_rows_at = together(
            table_low, weights, looked, packed_ids, packed_rows_at
        )
        table_cols = lax.all_gather(table_low, "wide", axis=1, tiled=True)
    else:
        local_ids = token_ids - narrow_me * vshard
        inside = (local_ids >= 0) & (local_ids < vshard)
        slots = jnp.where(inside, local_ids, vshard).reshape(-1)
        table_cols = lax.all_gather(table_low, "wide", axis=1, tiled=True)
        picked = jnp.take(table_cols, jnp.clip(local_ids, 0, vshard - 1), axis=0)
        picked = jnp.where(inside[..., None], picked, 0.0)
        looked = lax.psum_scatter(picked, "narrow", scatter_dimension=0, tiled=True)
    looked = looked.astype(jnp.float32)
    even_doc = (doc_ids % 2 == 0)[..., None]
    embedded = looked + small[0:L][None] + jnp.where(even_doc, small[L], small[L + 1])
    htwo, kept = layer_forward(embedded.reshape(seqs * L, D), doc_ids, small, weights)
    hmask = jnp.take_along_axis(htwo.reshape(seqs, L, D), mlm_pos[..., None], axis=1)
    hmask = hmask.reshape(seqs * MPS, D).astype(jnp.bfloat16)
    if paired:
        group_h = gathered_near(hmask)
    else:
        group_h = lax.all_gather(hmask, "narrow", axis=0, tiled=True)
    vocab = narrow_me * vshard + jnp.arange(vshard)
    logits = jnp.where((vocab < VREAL)[None], matmul_nt(group_h, table_cols), -1000000000.0)
    labels = mlm_labels.reshape(-1)
    hit = vocab[None] == labels[:, None]
    top = jnp.max(logits, axis=1)
    total = jnp.sum(jnp.exp(logits - top[:, None]), axis=1)
    target = jnp.sum(jnp.where(hit, logits, 0.0), axis=1)
    if paired:
        stats = gathered_near(jnp.stack([top, total, target])[None])
        top, total, target = stats[0]
        for place in range(1, stats.shape[0]):
            top, total, target = merge_rows((top, total, target), tuple(stats[place]))
    else:
        top, total, target = joined((top, total, target), "narrow", merge_rows)
    lse = top + jnp.log(total)
    flags = mlm_valid.reshape(-1).astype(jnp.float32)
    own = seqs * MPS
    own_loss = lax.dynamic_slice_in_dim(flags * (lse - target), narrow_me * own, own)
    dlogit = (
        (jnp.exp(logits - lse[:, None]) - hit.astype(jnp.float32)) * (flags / count)[:, None]
    ).astype(jnp.bfloat16)
    dhmask = matmul(dlogit, table_cols)
    if paired:
        dhmask = scattered_near(dhmask)
        blocks = group_h.reshape(-1, n_wide, D // n_wide)
        table_head = jnp.einsum("sv,swc->wvc", dlogit, blocks, preferred_element_type=jnp.float32)
        table_head, dhmask = together(table_head.astype(jnp.bfloat16), dhmask)
        table_head = lax.psum_scatter(table_head, "wide", scatter_dimension=0)
    else:
        dhmask = lax.psum_scatter(dhmask, "narrow", scatter_dimension=0, tiled=True)
    dhtwo = (
        jnp.zeros((seqs, L, D), jnp.float32)
        .at[jnp.arange(seqs)[:, None], mlm_pos]
        .add(dhmask.reshape(seqs, MPS, D))
    )
    dembed, vectors, pieces = layer_backward(
        dhtwo.reshape(seqs * L, D), kept, doc_ids, small, weights
    )
    dembed_rows = dembed.reshape(seqs, L, D)
    seg_even = jnp.sum(jnp.where(even_doc, dembed_rows, 0.0), axis=(0, 1))
    seg_odd = jnp.sum(jnp.where(even_doc, 0.0, dembed_rows), axis=(0, 1))
    small_grad = jnp.concatenate(
        [jnp.sum(dembed_rows, axis=0), seg_even[None], seg_odd[None], vectors], axis=0
    )
    mixed = pieces[0]
    if paired:
        cut = dembed.astype(jnp.bfloat16).reshape(L, n_wide, D // n_wide).transpose(1, 0, 2)
        cut = lax.all_to_all(cut, "wide", 0, 0).reshape(n_wide * L, D // n_wide)
        small_grad = small_total(small_halved(small_grad))
        down, up = pieces[2], pieces[1]
        cut, mixed.away, small_grad, down.result, up.result, table_head = together(
            cut, mixed.away, small_grad, down.result, up.result, table_head
        )
        mixed.finish()
        cut, mixed.result = together(cut, mixed.result)
        group_rows = lax.all_gather(cut, "narrow", axis=0)
    else:
        mixed.finish()
        group_rows = lax.all_gather(dembed_rows.astype(jnp.bfloat16), "narrow", axis=0, tiled=True)
        table_grad = matmul_tn(dlogit, group_h).at[slots].add(
            group_rows.reshape(-1, D).astype(jnp.float32), mode="drop"
        )
        cut = table_grad.astype(jnp.bfloat16).reshape(vshard, n_wide, D // n_wide)
        table_grad = lax.psum_scatter(cut.transpose(1, 0, 2), "wide", scatter_dimension=0)
        table_grad = table_grad.astype(jnp.float32)
    part_cols = layer.shape[1]
    if paired:
        spans, total, start = [], 0.0, [0, 4 * D, 8 * D]
        for piece, first in zip(pieces[::-1], start[::-1]):
            span, amount = span_of(layer_m, piece.result, worker_err, first)
            spans.insert(0, span)
            total = total + amount
        scale = total / (layer_m.shape[0] * layer_m.shape[1]) + MAG_EPS
        new_worker, sent = pressed(spans, scale, n_wide)
        server_in = scattered_sum(sent) / n_wide + server_err
    else:
        worker_grad = jnp.concatenate([piece.result for piece in pieces], axis=1)
        span = BETA * layer_m + (1.0 - BETA) * worker_grad.astype(jnp.float32) + worker_err[0]
        scale = jnp.mean(jnp.abs(span)) + MAG_EPS
        sent = scale * jnp.tanh(span / scale)
        new_worker = (span - sent)[None]
        summed = lax.psum(sent.astype(jnp.bfloat16), "wide").astype(jnp.float32)
        mixed = lax.dynamic_slice_in_dim(summed, wide_me * part_cols, part_cols, 1) / n_wide
        server_in = mixed + server_err
    sscale = jnp.mean(jnp.abs(server_in)) + MAG_EPS
    server_out = sscale * jnp.tanh(server_in / sscale)
    new_server = server_in - server_out
    server_low = server_out.astype(jnp.bfloat16)
    if paired:
        server_low, group_rows = together(server_low, group_rows)

        def added(length):
            return added_rows(packed_ids, packed_rows_at, group_rows, vshard, length)

        table_grad = lax.cond(
            owners.full, lambda: added(owners.count), lambda: added(owners.room)
        )
        table_mom, table_upd, table_norms = table_update(
            table_grad, table_head, table, table_m, table_v
        )
    else:
        small_grad = lax.psum(small_grad, ("wide", "narrow"))
        table_mom = BETA * table_m + (1.0 - BETA) * table_grad
        table_upd = table_mom / (jnp.sqrt(table_v) + OPT_EPS) + DECAY * table
        table_norms = (jnp.sum(table * table)[None], jnp.sum(table_upd * table_upd)[None])
    small_mom = BETA * small_m + (1.0 - BETA) * small_grad
    small_upd = small_mom / (jnp.sqrt(small_v) + OPT_EPS) + DECAY * small
    small_norms = (jnp.sum(small * small)[None], jnp.sum(small_upd * small_upd)[None])
    new_m = lax.all_gather(server_low, "wide", axis=1, tiled=True).astype(jnp.float32)
    layer_upd = server_out / (jnp.sqrt(layer_v) + OPT_EPS) + DECAY * layer
    column = wide_me * part_cols + jnp.arange(part_cols)
    which = (
        (column >= 3 * D).astype(jnp.int32)
        + (column >= 4 * D).astype(jnp.int32)
        + (column >= 4 * D + FF).astype(jnp.int32)
    )
    onehot = (which[:, None] == jnp.arange(4)[None]).astype(jnp.float32)
    wsq = jnp.sum(jnp.sum(layer * layer, axis=0)[:, None] * onehot, axis=0)
    usq = jnp.sum(jnp.sum(layer_upd * layer_upd, axis=0)[:, None] * onehot, axis=0)
    parts = jnp.concatenate([wsq, usq, *table_norms, jnp.sum(own_loss)[None]])
    sums = summed_over(summed_over(parts, "wide"), "narrow")
    loss_sum = sums[10]
    wnorm = jnp.sqrt(jnp.concatenate([sums[0:4], sums[8:9], small_norms[0]]))
    unorm = jnp.sqrt(jnp.concatenate([sums[4:8], sums[9:10], small_norms[1]]))
    ratio = wnorm / unorm
    new_layer = layer - RATE * jnp.sum(onehot * ratio[None, 0:4], axis=1)[None] * layer_upd
    new_table = table - RATE * ratio[4] * table_upd
    new_small = small - RATE * ratio[5] * small_upd
    return (
        jnp.stack([loss_sum, count]),
        new_table,
        table_mom,
        new_small,
        small_mom,
        new_layer,
        new_m,
        new_worker,
        new_server,
        jnp.stack([wnorm, unorm]),
    )


def solution(mesh):
    placed = (
        P("wide", None),
        P(("wide", "narrow"), None),
        P(("wide", "narrow"), None),
        P("wide", None),
        P("wide", None),
        P("narrow", "wide"),
        P("narrow", "wide"),
        P("narrow", "wide"),
        P(),
        P(),
        P(),
        P("narrow", "wide"),
        P("narrow", None),
        P("narrow", "wide"),
        P("wide", "narrow", None),
        P("narrow", "wide"),
    )
    return jax.shard_map(
        shards,
        mesh=mesh,
        in_specs=placed,
        out_specs=(
            P(),
            P("narrow", "wide"),
            P("narrow", "wide"),
            P(),
            P(),
            P("narrow", "wide"),
            P("narrow", None),
            P("wide", "narrow", None),
            P("narrow", "wide"),
            P(),
        ),
        check_vma=False,
    )
```

```python
import functools

import jax
import jax.numpy as jnp
from jax import lax
from jax.experimental import pallas as pl
from jax.experimental.pallas import tpu as pltpu
from jax.sharding import PartitionSpec as P

D = 1024
HEADS = 16
HEAD = 64
FF = 4096
VREAL = 30522
L = 512
MPS = 80


LN_EPS = 1e-12
BETA = 0.9
DECAY = 0.01
RATE = 0.25
OPT_EPS = 1e-06
MAG_EPS = 1e-08

FREE = pl.CostEstimate(flops=0, bytes_accessed=0, transcendentals=0)


def joined(value, axis, join):
    pieces = jax.tree.map(lambda part: lax.all_gather(part, axis), value)
    head = jax.tree.map(lambda part: part[0], pieces)
    tail = jax.tree.map(lambda part: part[1:], pieces)
    subtotal, _ = lax.scan(lambda subtotal, slab: (join(subtotal, slab), None), head, tail)
    return subtotal


def norm_rows(x, gain, shift):
    mean = jnp.mean(x, axis=-1, keepdims=True)
    cent = x - mean
    var = jnp.mean(cent * cent, axis=-1, keepdims=True)
    return cent * lax.rsqrt(var + LN_EPS) * gain + shift


def gelu_exact(upper):
    return jax.nn.gelu(upper, approximate=False)


def matmul(left, right):
    return jnp.dot(left, right, preferred_element_type=jnp.float32)


def matmul_tn(left, right):
    return lax.dot_general(
        left, right, (((0,), (0,)), ((), ())), preferred_element_type=jnp.float32
    )


def matmul_nt(left, right):
    return lax.dot_general(
        left, right, (((1,), (1,)), ((), ())), preferred_element_type=jnp.float32
    )


def attend_kernel(q_ref, k_ref, v_ref, key_doc_ref, query_doc_ref, out_ref, lse_ref):
    same = key_doc_ref[...] == query_doc_ref[...]
    lane = lax.broadcasted_iota(jnp.int32, (1, 2 * HEAD), 1)
    outs = []
    for head in range(2):
        mine = lane // HEAD == head
        query = jnp.where(mine, q_ref[...] * 0.125, 0).astype(jnp.bfloat16)
        scores = jnp.where(same, matmul_nt(k_ref[...], query), -1000000000.0)
        top = jnp.max(scores, axis=0, keepdims=True)
        power = jnp.exp(scores - top)
        total = jnp.sum(power, axis=0, keepdims=True)
        lse_ref[0, head : head + 1, :] = top + jnp.log(total)
        prob = (power * (1.0 / total)).astype(jnp.bfloat16)
        outs.append(matmul_tn(prob, v_ref[...]))
    out_ref[...] = jnp.where(lane < HEAD, outs[0], outs[1]).astype(jnp.bfloat16)


def head_pairs(offset):
    return pl.BlockSpec((L, 2 * HEAD), lambda pair: (0, offset * HEADS // 2 + pair))


def attend(qkv, docs):
    return pl.pallas_call(
        attend_kernel,
        grid=(HEADS // 2,),
        in_specs=[
            head_pairs(0),
            head_pairs(1),
            head_pairs(2),
            pl.BlockSpec((L, 1), lambda pair: (0, 0)),
            pl.BlockSpec((1, L), lambda pair: (0, 0)),
        ],
        out_specs=[head_pairs(0), pl.BlockSpec((1, 2, L), lambda pair: (pair, 0, 0))],
        out_shape=[
            jax.ShapeDtypeStruct((L, D), jnp.bfloat16),
            jax.ShapeDtypeStruct((HEADS // 2, 2, L), jnp.float32),
        ],
        compiler_params=pltpu.CompilerParams(vmem_limit_bytes=40 * 2**20),
        cost_estimate=FREE,
        name="attend",
    )(qkv, qkv, qkv, docs.reshape(L, 1), docs.reshape(1, L))


def attend_back_kernel(q_ref, k_ref, v_ref, do_ref, lse_ref, key_doc_ref, query_doc_ref, out_ref):
    pair = pl.program_id(0)
    same = key_doc_ref[...] == query_doc_ref[...]
    lane = lax.broadcasted_iota(jnp.int32, (1, 2 * HEAD), 1)
    both = []
    for head in range(2):
        mine = lane // HEAD == head
        query = jnp.where(mine, q_ref[...] * 0.125, 0).astype(jnp.bfloat16)
        dout = jnp.where(mine, do_ref[...], 0).astype(jnp.bfloat16)
        scores = jnp.where(same, matmul_nt(k_ref[...], query), -1000000000.0)
        prob = jnp.exp(scores - lse_ref[0, head : head + 1, :])
        dvalue = matmul(prob.astype(jnp.bfloat16), dout)
        dprob = matmul_nt(v_ref[...], dout)
        delta = jnp.sum(prob * dprob, axis=0, keepdims=True)
        dscore = (prob * (dprob - delta)).astype(jnp.bfloat16)
        both.append((matmul_tn(dscore, k_ref[...]) * 0.125, matmul(dscore, query), dvalue))
    for part in range(3):
        value = jnp.where(lane < HEAD, both[0][part], both[1][part]).astype(jnp.bfloat16)
        start = pl.multiple_of(part * D + pair * 2 * HEAD, 2 * HEAD)
        out_ref[:, pl.ds(start, 2 * HEAD)] = value


def attend_back(qkv, dout, lse, docs):
    return pl.pallas_call(
        attend_back_kernel,
        grid=(HEADS // 2,),
        in_specs=[
            head_pairs(0),
            head_pairs(1),
            head_pairs(2),
            head_pairs(0),
            pl.BlockSpec((1, 2, L), lambda pair: (pair, 0, 0)),
            pl.BlockSpec((L, 1), lambda pair: (0, 0)),
            pl.BlockSpec((1, L), lambda pair: (0, 0)),
        ],
        out_specs=pl.BlockSpec((L, 3 * D), lambda pair: (0, 0)),
        out_shape=jax.ShapeDtypeStruct((L, 3 * D), jnp.bfloat16),
        compiler_params=pltpu.CompilerParams(vmem_limit_bytes=40 * 2**20),
        cost_estimate=FREE,
        name="attend_back",
    )(qkv, qkv, qkv, dout, lse, docs.reshape(L, 1), docs.reshape(1, L))


def merge_rows(first, second):
    peak = jnp.maximum(first[0], second[0])
    total = first[1] * jnp.exp(first[0] - peak) + second[1] * jnp.exp(second[0] - peak)
    return (peak, total, first[2] + second[2])


def layer_forward(embedded, docs, small, weights):
    base = L + 2
    x0 = norm_rows(embedded, small[base], small[base + 1])
    act = x0.astype(jnp.bfloat16)
    bias = jnp.concatenate([small[base + 6], jnp.zeros((D,), jnp.float32), small[base + 7]])
    qkv = (matmul(act, weights[:, 0 : 3 * D]) + bias).astype(jnp.bfloat16)
    out, lse = attend(qkv, docs)
    rone = x0 + (matmul(out, weights[:, 3 * D : 4 * D]) + small[base + 8])
    hone = norm_rows(rone, small[base + 2], small[base + 3])
    fin = hone.astype(jnp.bfloat16)
    upper = matmul(fin, weights[:, 4 * D : 4 * D + FF]) + small[base + 10 :].reshape(FF)
    gated = gelu_exact(upper).astype(jnp.bfloat16)
    rtwo = hone + (matmul_nt(gated, weights[:, 4 * D + FF :]) + small[base + 9])
    htwo = norm_rows(rtwo, small[base + 4], small[base + 5])
    return (htwo, (embedded, act, qkv, lse, out, rone, fin, upper, gated, rtwo))


def layer_backward(dhtwo, kept, docs, small, weights):
    embedded, act, qkv, lse, out, rone, fin, upper, gated, rtwo = kept
    base = L + 2
    _, pull = jax.vjp(norm_rows, rtwo, small[base + 4], small[base + 5])
    drtwo, dgain_two, dshift_two = pull(dhtwo)
    dffn = drtwo.astype(jnp.bfloat16)
    down = WorkerPiece((dffn, gated))
    dgated = matmul(dffn, weights[:, 4 * D + FF :])
    _, pull = jax.vjp(gelu_exact, upper)
    dupper = pull(dgated)[0].astype(jnp.bfloat16)
    dupper = down.received(dupper)
    down.across()
    up = WorkerPiece((fin, dupper))
    dhone = drtwo + matmul_nt(dupper, weights[:, 4 * D : 4 * D + FF])
    _, pull = jax.vjp(norm_rows, rone, small[base + 2], small[base + 3])
    drone, dgain_one, dshift_one = pull(dhone)
    dattn = drone.astype(jnp.bfloat16)
    dout = matmul_nt(dattn, weights[:, 3 * D : 4 * D]).astype(jnp.bfloat16)
    dout = up.received(dout)
    up.across()
    dqkv = attend_back(qkv, dout, lse, docs)
    (dqkv,) = down.crossed(dqkv)
    down.finish()
    mixed = WorkerPiece((act, dqkv), (out, dattn))
    dxzero = drone + matmul_nt(dqkv, weights[:, 0 : 3 * D])
    _, pull = jax.vjp(norm_rows, embedded, small[base], small[base + 1])
    dembed, dgain_emb, dshift_emb = pull(dxzero)
    dembed = mixed.received(dembed)
    mixed.across()
    (dembed,) = up.crossed(dembed)
    up.finish()
    bias_qkv = jnp.sum(dqkv, axis=0, dtype=jnp.float32)
    vectors = jnp.stack(
        [
            dgain_emb,
            dshift_emb,
            dgain_one,
            dshift_one,
            dgain_two,
            dshift_two,
            bias_qkv[0:D],
            bias_qkv[2 * D : 3 * D],
            jnp.sum(dattn, axis=0, dtype=jnp.float32),
            jnp.sum(dffn, axis=0, dtype=jnp.float32),
        ]
    )
    bias_up = jnp.sum(dupper, axis=0, dtype=jnp.float32).reshape(FF // D, D)
    return (dembed, jnp.concatenate([vectors, bias_up], axis=0), (mixed, up, down))


def paired_mesh():
    return lax.axis_size("wide") == 8 and lax.axis_size("narrow") == 4


def together(*values):
    return lax.optimization_barrier(values)


def swap_pairs(size, bit):
    return [(place, place ^ bit) for place in range(size)]


def cycle(size, by):
    return [(place, (place + by) % size) for place in range(size)]


def summed_over(value, axis):
    size = lax.axis_size(axis)
    if size & (size - 1):
        return lax.psum(value, axis)
    bit = 1
    while bit < size:
        value = value + lax.ppermute(value, axis, swap_pairs(size, bit))
        bit *= 2
    return value


def gathered_near(value, beside=None):
    size = lax.axis_size("narrow")
    rows = value.shape[0]
    around = [value]
    for by in range(1, size):
        around.append(lax.ppermute(value, "narrow", cycle(size, size - by)))
    if beside is not None:
        *around, beside = together(*around, beside)
    twice = jnp.concatenate(around + around[:-1], axis=0)
    start = lax.rem(size - lax.axis_index("narrow"), size) * rows
    whole = lax.dynamic_slice_in_dim(twice, start, size * rows, 0)
    return whole if beside is None else (whole, beside)


def scattered_near(value):
    size = lax.axis_size("narrow")
    rows = value.shape[0] // size
    place = lax.axis_index("narrow")
    total = lax.dynamic_slice_in_dim(value, place * rows, rows, 0)
    for by in range(1, size):
        target = lax.rem(place + by, size)
        give = lax.dynamic_slice_in_dim(value, target * rows, rows, 0).astype(jnp.bfloat16)
        take = lax.ppermute(give, "narrow", cycle(size, by))
        total = total + take.astype(jnp.float32)
    return total


def sent_around(blocks):
    size = lax.axis_size("narrow")
    place = lax.axis_index("narrow")

    def block(by):
        return lax.dynamic_index_in_dim(blocks, lax.rem(place + by, size), 0, keepdims=False)

    return [block(0)] + [
        lax.ppermute(block(by), "narrow", cycle(size, by)) for by in range(1, size)
    ]


class WorkerPiece:
    def __init__(self, *pairs):
        self.pairs = pairs
        self.paired = paired_mesh()
        if not self.paired:
            return
        self.core = lax.axis_index("wide") % 2
        self.pair, self.side = lax.axis_index("narrow") // 2, lax.axis_index("narrow") % 2
        cores = swap_pairs(lax.axis_size("wide"), 1)
        self.far = lax.ppermute(self.block(1 - self.core, 1 - self.side), "wide", cores)
        self.near = lax.ppermute(self.block(1 - self.core, self.side), "wide", cores)

    def block(self, core, side, *terms):
        rows = D // lax.axis_size("narrow")
        blocks, start = [], 0
        for left, right in self.pairs:
            part = lax.dynamic_slice_in_dim(left, (2 * core + side) * rows, rows, 1)
            total = matmul_tn(part, right)
            for term in terms:
                total = total + term[:, start : start + right.shape[1]].astype(jnp.float32)
            blocks.append(total.astype(jnp.bfloat16))
            start += right.shape[1]
        return blocks[0] if len(blocks) == 1 else jnp.concatenate(blocks, axis=1)

    def received(self, value):
        if self.paired:
            value, self.far, self.near = together(value, self.far, self.near)
        return value

    def across(self):
        if self.paired:
            sides = swap_pairs(lax.axis_size("narrow"), 1)
            away = self.block(self.core, 1 - self.side, self.far)
            self.away = lax.ppermute(away, "narrow", sides)

    def crossed(self, *values):
        if self.paired:
            *values, self.away = together(*values, self.away)
        return values

    def finish(self):
        if not self.paired:
            blocks = [matmul_tn(left, right).astype(jnp.bfloat16) for left, right in self.pairs]
            grad = jnp.concatenate(blocks, axis=1)
            self.result = lax.psum_scatter(grad, "narrow", scatter_dimension=0, tiled=True)
            return
        n_wide, n_narrow = lax.axis_size("wide"), lax.axis_size("narrow")
        total = self.block(self.core, self.side, self.near, self.away)
        moves = []
        for wide in range(n_wide):
            for narrow in range(n_narrow):
                if narrow // 2 != wide % 2:
                    target_wide = wide - wide % 2 + narrow // 2
                    target = target_wide * n_narrow + 2 * (wide % 2) + narrow % 2
                    moves.append((wide * n_narrow + narrow, target))
        moved = lax.ppermute(total, ("wide", "narrow"), moves)
        self.result = jnp.where(self.pair == self.core, total, moved)


def hosted_rows(token_ids, mlm_labels, mlm_valid, doc_ids, mlm_pos):
    n_wide, n_narrow = lax.axis_size("wide"), lax.axis_size("narrow")
    packed = jnp.concatenate([token_ids, mlm_labels, mlm_valid], axis=1)[None]
    for bit, place in zip((1, 2, 4), wide_places()):
        other = lax.ppermute(packed, "wide", swap_pairs(n_wide, bit))
        first, second = jnp.where(place == 0, packed, other), jnp.where(place == 0, other, packed)
        packed = jnp.concatenate([first, second], axis=0)
    width = packed.shape[2]
    hosted = packed.reshape(n_wide // 2, 2, 2, 2, width).transpose(1, 2, 0, 3, 4)
    hosted = hosted.reshape(n_narrow, n_wide, width)
    column = lax.dynamic_index_in_dim(hosted, lax.axis_index("wide"), 1, keepdims=False)
    moves = []
    for wide in range(n_wide):
        for row in range(n_narrow):
            target_wide = wide - wide % 2 + row % 2
            target_narrow = 2 * (wide % 2) + row // 2
            moves.append((wide * n_narrow + row, target_wide * n_narrow + target_narrow))
    own = lax.ppermute(jnp.concatenate([doc_ids, mlm_pos], axis=1), ("wide", "narrow"), moves)
    return (
        hosted[:, :, 0:L],
        column[:, L : L + MPS],
        column[:, L + MPS :],
        own[:, 0:L],
        own[:, L:],
    )


STREAMS = 2


class Owners:
    def __init__(self, tokens, vshard):
        size = lax.axis_size("narrow")
        place = lax.axis_index("narrow")
        count = tokens.shape[1]
        self.room = count * 7 // 16
        owner = tokens // vshard
        held = (owner[None] == jnp.arange(size)[:, None, None]).astype(jnp.bfloat16)
        tiles = held.reshape(-1, count // 128, 128)
        order = jnp.arange(128)
        within = jnp.einsum(
            "btl,lm->btm",
            tiles,
            (order[:, None] < order[None]).astype(jnp.bfloat16),
            preferred_element_type=jnp.float32,
        )
        sums = jnp.sum(tiles.astype(jnp.float32), axis=2)
        tile = jnp.arange(count // 128)
        before = jnp.sum(jnp.where(tile[:, None] < tile[None], sums[:, :, None], 0.0), axis=1)
        rank = (within + before[..., None]).reshape(size, size, count) * held.astype(jnp.float32)
        rank = jnp.sum(rank, axis=0).astype(jnp.int32)
        self.full = jnp.max(jnp.sum(sums, axis=1)) > self.room
        self.count, self.vshard = count, vshard
        own = lax.dynamic_index_in_dim(owner, place, 0, keepdims=False)
        self.rank = lax.dynamic_index_in_dim(rank, place, 0, keepdims=False)
        self.owner = own
        self.behind = lax.rem(place - own + size, size)
        self.slots = jnp.where(owner == place, tokens - place * vshard, vshard)

    def behind_slots(self, room):
        return self.behind * room + jnp.minimum(self.rank, room - 1)

    def owner_slots(self):
        return self.owner * self.count + self.rank

    def packed(self, slots):
        size = lax.axis_size("narrow")
        base = self.vshard + 1
        order = jnp.arange(self.count) * base + slots
        order = jnp.where(slots < self.vshard, order, order + self.count * base)
        backward = (lax.sort(order) % base)[::-1]
        backward = jnp.concatenate([backward, backward], axis=0)
        start = size - 1 - lax.axis_index("narrow")
        return lax.dynamic_slice_in_dim(backward, start, size, 0)


def pack_kernel(ids_ref, table_ref, out_ref, held, *rows):
    step, count, size = pl.program_id(0), out_ref.shape[1], table_ref.shape[0]

    @pl.when(step == 0)
    def _():
        held[0:size, :] = table_ref[...]
        held[size:, :] = jnp.zeros((8, table_ref.shape[1]), jnp.float32)
        for part in rows:
            part[...] = jnp.zeros_like(part)

    base = [(step * len(rows) + index) * count for index in range(len(rows))]

    def some(turn, used):
        used = list(used)
        for by in range(8):
            for index, part in enumerate(rows):
                place = ids_ref[base[index] + turn * 8 + by]
                part[pl.ds(used[index], 1), :] = held[pl.ds(place, 1), :]
                used[index] = used[index] + jnp.where(place < size, 1, 0)
        return tuple(used)

    lax.fori_loop(0, count // 8, some, (0,) * len(rows))
    for index, part in enumerate(rows):
        out_ref[index] = part[0:count, :].astype(out_ref.dtype)


def packed_rows(ids, table):
    size, cols = table.shape
    places, count = ids.shape
    return pl.pallas_call(
        pack_kernel,
        grid_spec=pltpu.PrefetchScalarGridSpec(
            num_scalar_prefetch=1,
            grid=(places // STREAMS,),
            in_specs=[pl.BlockSpec((size, cols), lambda step, ids: (0, 0))],
            out_specs=pl.BlockSpec((STREAMS, count, cols), lambda step, ids: (step, 0, 0)),
            scratch_shapes=[pltpu.VMEM((size + 8, cols), jnp.float32)]
            + [pltpu.VMEM((count + 8, cols), jnp.float32)] * STREAMS,
        ),
        out_shape=jax.ShapeDtypeStruct((places, count, cols), jnp.bfloat16),
        compiler_params=pltpu.CompilerParams(vmem_limit_bytes=40 * 2**20),
        cost_estimate=pl.CostEstimate(flops=0, bytes_accessed=15 * 10**7, transcendentals=0),
        name="pack_rows",
    )(ids.reshape(-1), table)


def take_kernel(ids_ref, table_ref, out_ref, held, rows):
    held[...] = table_ref[...].astype(jnp.float32)

    @pl.loop(0, out_ref.shape[0], step=16)
    def _(first):
        for by in range(16):
            rows[pl.ds(first + by, 1), :] = held[pl.ds(ids_ref[first + by], 1), :]

    out_ref[...] = rows[...].astype(out_ref.dtype)


def taken_rows(ids, table):
    count, cols = ids.shape[0], table.shape[1]
    return pl.pallas_call(
        take_kernel,
        grid_spec=pltpu.PrefetchScalarGridSpec(
            num_scalar_prefetch=1,
            grid=(1,),
            in_specs=[pl.BlockSpec(table.shape, lambda step, ids: (0, 0))],
            out_specs=pl.BlockSpec((count, cols), lambda step, ids: (0, 0)),
            scratch_shapes=[
                pltpu.VMEM(table.shape, jnp.float32),
                pltpu.VMEM((count, cols), jnp.float32),
            ],
        ),
        out_shape=jax.ShapeDtypeStruct((count, cols), table.dtype),
        compiler_params=pltpu.CompilerParams(vmem_limit_bytes=40 * 2**20),
        cost_estimate=FREE,
        name="take_rows",
    )(ids, table)


def put_kernel(ids_ref, rows_ref, out_ref, rows, held):
    rows[...] = rows_ref[...].astype(jnp.float32)
    held[...] = jnp.zeros_like(held)

    @pl.loop(0, rows_ref.shape[0], step=16)
    def _(first):
        for by in range(16):
            held[pl.ds(ids_ref[first + by], 1), :] = rows[pl.ds(first + by, 1), :]

    out_ref[...] = held[...].astype(out_ref.dtype)


def put_rows(ids, values, size):
    cols = values.shape[1]
    return pl.pallas_call(
        put_kernel,
        grid_spec=pltpu.PrefetchScalarGridSpec(
            num_scalar_prefetch=1,
            grid=(1,),
            in_specs=[pl.BlockSpec(values.shape, lambda step, ids: (0, 0))],
            out_specs=pl.BlockSpec((size, cols), lambda step, ids: (0, 0)),
            scratch_shapes=[
                pltpu.VMEM(values.shape, jnp.float32),
                pltpu.VMEM((size, cols), jnp.float32),
            ],
        ),
        out_shape=jax.ShapeDtypeStruct((size, cols), values.dtype),
        compiler_params=pltpu.CompilerParams(vmem_limit_bytes=40 * 2**20),
        cost_estimate=FREE,
        name="put_rows",
    )(ids, values)


def add_kernel(ids_ref, *refs):
    count = (len(refs) - 1) // 3
    rows_refs, out_ref, rows, sums = refs[:count], refs[count], refs[count + 1 : 2 * count + 1], refs[2 * count + 1 :]
    size, length = out_ref.shape[0], rows_refs[0].shape[0]
    each = ids_ref.shape[0] // count
    for part, held, rows_ref in zip(sums, rows, rows_refs):
        part[...] = jnp.zeros_like(part)
        held[...] = rows_ref[...].astype(jnp.float32)

    @pl.loop(0, length, step=8)
    def _(first):
        for by in range(8):
            for index, part in enumerate(sums):
                place = ids_ref[index * each + first + by]
                part[pl.ds(place, 1), :] += rows[index][pl.ds(first + by, 1), :]

    total = sums[0][0:size, :]
    for part in sums[1:]:
        total = total + part[0:size, :]
    out_ref[...] = total


def added_rows(ids, values, size):
    length, cols = values[0].shape
    block = pl.BlockSpec((length, cols), lambda step, ids: (0, 0))
    return pl.pallas_call(
        add_kernel,
        grid_spec=pltpu.PrefetchScalarGridSpec(
            num_scalar_prefetch=1,
            grid=(1,),
            in_specs=[block] * len(values),
            out_specs=pl.BlockSpec((size, cols), lambda step, ids: (0, 0)),
            scratch_shapes=[pltpu.VMEM((length, cols), jnp.float32)] * len(values)
            + [pltpu.VMEM((size + 8, cols), jnp.float32)] * len(values),
        ),
        out_shape=jax.ShapeDtypeStruct((size, cols), jnp.float32),
        compiler_params=pltpu.CompilerParams(vmem_limit_bytes=56 * 2**20),
        cost_estimate=FREE,
        name="add_rows",
    )(ids.reshape(-1), *values)


def span_kernel(momentum_ref, grad_ref, error_ref, span_ref, sum_ref):
    grad = grad_ref[...].astype(jnp.float32)
    span = BETA * momentum_ref[...] + (1.0 - BETA) * grad + error_ref[0]
    span_ref[...] = span

    @pl.when(pl.program_id(0) == 0)
    def _():
        sum_ref[...] = jnp.zeros_like(sum_ref)

    sum_ref[...] += jnp.sum(jnp.abs(span), axis=0, keepdims=True)


def span_of(momentum, grad, error, start):
    rows, cols = grad.shape
    block = 1024
    first = start // block
    span, sums = pl.pallas_call(
        span_kernel,
        grid=(cols // block,),
        in_specs=[
            pl.BlockSpec((rows, block), lambda step: (0, first + step)),
            pl.BlockSpec((rows, block), lambda step: (0, step)),
            pl.BlockSpec((1, rows, block), lambda step: (0, 0, first + step)),
        ],
        out_specs=[
            pl.BlockSpec((rows, block), lambda step: (0, step)),
            pl.BlockSpec((1, block), lambda step: (0, 0)),
        ],
        out_shape=[
            jax.ShapeDtypeStruct((rows, cols), jnp.float32),
            jax.ShapeDtypeStruct((1, block), jnp.float32),
        ],
        compiler_params=pltpu.CompilerParams(vmem_limit_bytes=24 * 2**20),
        cost_estimate=FREE,
        name="span",
    )(momentum, grad, error)
    return span, jnp.sum(sums)


def press_kernel(steps, scale_ref, *refs):
    *span_refs, error_ref, sent_ref = refs
    step = pl.program_id(0)
    scale = scale_ref[0]
    inverse = scale_ref[1]
    for index, span_ref in enumerate(span_refs):

        @pl.when((step >= steps[index]) & (step < steps[index + 1]))
        def _():
            span = span_ref[...]
            sent = scale * jnp.tanh(span * inverse)
            error_ref[0] = span - sent
            sent_ref[0] = sent.astype(jnp.bfloat16)


def pressed(spans, scale, parts):
    rows = spans[0].shape[0]
    cols = sum(span.shape[1] for span in spans)
    block = 512
    each = cols // parts // block
    steps = [0]
    for span in spans:
        steps.append(steps[-1] + span.shape[1] // block)

    def of(index):
        low, count = steps[index], steps[index + 1] - steps[index]
        return pl.BlockSpec((rows, block), lambda step: (0, jnp.clip(step - low, 0, count - 1)))

    return pl.pallas_call(
        functools.partial(press_kernel, steps),
        grid=(steps[-1],),
        in_specs=[pl.BlockSpec(memory_space=pltpu.SMEM)] + [of(i) for i in range(len(spans))],
        out_specs=[
            pl.BlockSpec((1, rows, block), lambda step: (0, 0, step)),
            pl.BlockSpec((1, rows, block), lambda step: (step // each, 0, step % each)),
        ],
        out_shape=[
            jax.ShapeDtypeStruct((1, rows, cols), jnp.float32),
            jax.ShapeDtypeStruct((parts, rows, cols // parts), jnp.bfloat16),
        ],
        compiler_params=pltpu.CompilerParams(vmem_limit_bytes=24 * 2**20),
        cost_estimate=FREE,
        name="press",
    )(jnp.stack([scale, 1.0 / scale]), *spans)


def update_kernel(grad_ref, head_ref, table_ref, first_ref, second_ref, *out_refs):
    first_out, update_ref, weight_sum, update_sum = out_refs
    grad = grad_ref[...] + head_ref[...].astype(jnp.float32)
    first = BETA * first_ref[...] + (1.0 - BETA) * grad
    table = table_ref[...]
    update = first / (jnp.sqrt(second_ref[...]) + OPT_EPS) + DECAY * table
    first_out[...] = first
    update_ref[...] = update

    @pl.when(pl.program_id(0) == 0)
    def _():
        weight_sum[...] = jnp.zeros_like(weight_sum)
        update_sum[...] = jnp.zeros_like(update_sum)

    weight_sum[...] += jnp.sum(table * table, axis=0, keepdims=True)
    update_sum[...] += jnp.sum(update * update, axis=0, keepdims=True)


def table_update(grad, head, table, first, second):
    size, cols = table.shape
    block = size // 9 if size % 9 == 0 and size // 9 % 16 == 0 else size
    whole = pl.BlockSpec((block, cols), lambda step: (step, 0))
    line = pl.BlockSpec((1, cols), lambda step: (0, 0))
    moment, update, *sums = pl.pallas_call(
        update_kernel,
        grid=(size // block,),
        in_specs=[whole] * 5,
        out_specs=[whole, whole, line, line],
        out_shape=[jax.ShapeDtypeStruct((size, cols), jnp.float32)] * 2
        + [jax.ShapeDtypeStruct((1, cols), jnp.float32)] * 2,
        compiler_params=pltpu.CompilerParams(vmem_limit_bytes=56 * 2**20),
        cost_estimate=FREE,
        name="update",
    )(grad, head, table, first, second)
    return moment, update, tuple(jnp.sum(part)[None] for part in sums)


def wide_places():
    wide_me = lax.axis_index("wide")
    return wide_me % 2, wide_me // 2 % 2, wide_me // 4


def scattered_sum(sent):
    n_wide = lax.axis_size("wide")
    core, x, y = wide_places()

    def send(value, bit):
        return lax.ppermute(value.astype(jnp.bfloat16), "wide", swap_pairs(n_wide, bit))

    def pick(value, index):
        return lax.dynamic_index_in_dim(value, index, 0, keepdims=False)

    rows, cols = sent.shape[1:]
    by_core = sent.reshape(n_wide // 2, 2, rows, cols)
    give = lax.dynamic_index_in_dim(by_core, 1 - core, 1, keepdims=False)
    keep = lax.dynamic_index_in_dim(by_core, core, 1, keepdims=False)
    take = send(give, 1)
    half = rows // 2

    def chip(y_of, x_of, part):
        low, high = part * half, (part + 1) * half
        index = 2 * y_of + x_of
        own, other = pick(keep[:, low:high], index), pick(take[:, low:high], index)
        return own.astype(jnp.float32) + other.astype(jnp.float32)

    upper_far = send(chip(1 - y, 1 - x, 0), 2)
    lower_far = send(chip(1 - y, 1 - x, 1), 4)
    upper_near = send(chip(y, 1 - x, 0), 2)
    lower_near = send(chip(1 - y, x, 1), 4)
    upper_far = send(chip(1 - y, x, 0) + upper_far.astype(jnp.float32), 4)
    lower_far = send(chip(y, 1 - x, 1) + lower_far.astype(jnp.float32), 2)
    own_upper = chip(y, x, 0) + upper_near.astype(jnp.float32) + upper_far.astype(jnp.float32)
    own_lower = chip(y, x, 1) + lower_near.astype(jnp.float32) + lower_far.astype(jnp.float32)
    return jnp.concatenate([own_upper, own_lower], axis=0)


def small_halved(value):
    n_wide = lax.axis_size("wide")
    for bit, place in zip((1, 2, 4), wide_places()):
        half = value.shape[1] // 2
        give = lax.dynamic_slice_in_dim(value, (1 - place) * half, half, 1).astype(jnp.bfloat16)
        keep = lax.dynamic_slice_in_dim(value, place * half, half, 1)
        value = keep + lax.ppermute(give, "wide", swap_pairs(n_wide, bit)).astype(jnp.float32)
    return value


def small_total(parts):
    n_wide, n_narrow = lax.axis_size("wide"), lax.axis_size("narrow")
    parts = jnp.stack(parts + parts[:-1])
    start = lax.rem(lax.axis_index("narrow") + 1, n_narrow)
    parts = lax.dynamic_slice_in_dim(parts, start, n_narrow, 0).astype(jnp.float32)
    value = parts[0]
    for place in range(1, n_narrow):
        value = value + parts[place]
    value = value.astype(jnp.bfloat16)
    for bit, place in reversed(list(zip((1, 2, 4), wide_places()))):
        other = lax.ppermute(value, "wide", swap_pairs(n_wide, bit))
        first, second = jnp.where(place == 0, value, other), jnp.where(place == 0, other, value)
        value = jnp.concatenate([first, second], axis=1)
    return value.astype(jnp.float32)


def shards(
    token_ids,
    doc_ids,
    mlm_pos,
    mlm_labels,
    mlm_valid,
    table,
    table_m,
    table_v,
    small,
    small_m,
    small_v,
    layer,
    layer_m,
    layer_v,
    worker_err,
    server_err,
):
    n_wide, n_narrow = lax.axis_size("wide"), lax.axis_size("narrow")
    narrow_me = lax.axis_index("narrow")
    wide_me = lax.axis_index("wide")
    seqs = doc_ids.shape[0]
    paired = paired_mesh()
    vshard = table.shape[0]
    count = summed_over(jnp.sum(mlm_valid.astype(jnp.float32)), "wide")
    table_low, layer_low = table.astype(jnp.bfloat16), layer.astype(jnp.bfloat16)
    if paired:
        token_ids, mlm_labels, mlm_valid, doc_ids, mlm_pos = hosted_rows(
            token_ids, mlm_labels, mlm_valid, doc_ids, mlm_pos
        )
        owners = Owners(token_ids.reshape(n_narrow, n_wide * L), vshard)
        picked = packed_rows(owners.slots, table)
        layer_rows, picked = gathered_near(layer_low, picked)
    else:
        layer_rows = lax.all_gather(layer_low, "narrow", axis=0, tiled=True)
    weights = lax.all_gather(layer_rows, "wide", axis=1, tiled=True)
    if paired:

        def looked_up(room):
            rows = sent_around(picked[:, 0:room])
            return taken_rows(owners.behind_slots(room), jnp.concatenate(rows, axis=0))

        layer_rows, picked = together(layer_rows, picked)
        looked = looked_up(owners.room)
        looked = lax.cond(owners.full, lambda: looked_up(owners.count), lambda: looked)
        looked = lax.all_to_all(looked.reshape(n_wide, L, -1), "wide", 0, 0)
        looked = looked.transpose(1, 0, 2).reshape(1, L, D)
        table_low, weights, looked = together(table_low, weights, looked)
        table_cols = lax.all_gather(table_low, "wide", axis=1, tiled=True)
    else:
        local_ids = token_ids - narrow_me * vshard
        inside = (local_ids >= 0) & (local_ids < vshard)
        slots = jnp.where(inside, local_ids, vshard).reshape(-1)
        table_cols = lax.all_gather(table_low, "wide", axis=1, tiled=True)
        picked = jnp.take(table_cols, jnp.clip(local_ids, 0, vshard - 1), axis=0)
        picked = jnp.where(inside[..., None], picked, 0.0)
        looked = lax.psum_scatter(picked, "narrow", scatter_dimension=0, tiled=True)
    looked = looked.astype(jnp.float32)
    even_doc = (doc_ids % 2 == 0)[..., None]
    embedded = looked + small[0:L][None] + jnp.where(even_doc, small[L], small[L + 1])
    htwo, kept = layer_forward(embedded.reshape(seqs * L, D), doc_ids, small, weights)
    hmask = jnp.take_along_axis(htwo.reshape(seqs, L, D), mlm_pos[..., None], axis=1)
    hmask = hmask.reshape(seqs * MPS, D).astype(jnp.bfloat16)
    if paired:
        slots, hmask = together(owners.slots, hmask)
        packed_ids = owners.packed(slots)
        group_h = gathered_near(hmask)
    else:
        group_h = lax.all_gather(hmask, "narrow", axis=0, tiled=True)
    vocab = narrow_me * vshard + jnp.arange(vshard)
    logits = jnp.where((vocab < VREAL)[None], matmul_nt(group_h, table_cols), -1000000000.0)
    labels = mlm_labels.reshape(-1)
    hit = vocab[None] == labels[:, None]
    top = jnp.max(logits, axis=1)
    total = jnp.sum(jnp.exp(logits - top[:, None]), axis=1)
    target = jnp.sum(jnp.where(hit, logits, 0.0), axis=1)
    if paired:
        stats = gathered_near(jnp.stack([top, total, target])[None])
        top, total, target = stats[0]
        for place in range(1, stats.shape[0]):
            top, total, target = merge_rows((top, total, target), tuple(stats[place]))
    else:
        top, total, target = joined((top, total, target), "narrow", merge_rows)
    lse = top + jnp.log(total)
    flags = mlm_valid.reshape(-1).astype(jnp.float32)
    own = seqs * MPS
    own_loss = lax.dynamic_slice_in_dim(flags * (lse - target), narrow_me * own, own)
    dlogit = (
        (jnp.exp(logits - lse[:, None]) - hit.astype(jnp.float32)) * (flags / count)[:, None]
    ).astype(jnp.bfloat16)
    dhmask = matmul(dlogit, table_cols)
    if paired:
        dhmask = scattered_near(dhmask)
        blocks = group_h.reshape(-1, n_wide, D // n_wide)
        table_head = jnp.einsum("sv,swc->wvc", dlogit, blocks, preferred_element_type=jnp.float32)
        table_head, dhmask = together(table_head.astype(jnp.bfloat16), dhmask)
        table_head = lax.psum_scatter(table_head, "wide", scatter_dimension=0)
    else:
        dhmask = lax.psum_scatter(dhmask, "narrow", scatter_dimension=0, tiled=True)
    dhtwo = (
        jnp.zeros((seqs, L, D), jnp.float32)
        .at[jnp.arange(seqs)[:, None], mlm_pos]
        .add(dhmask.reshape(seqs, MPS, D))
    )
    dembed, vectors, pieces = layer_backward(
        dhtwo.reshape(seqs * L, D), kept, doc_ids, small, weights
    )
    dembed_rows = dembed.reshape(seqs, L, D)
    seg_even = jnp.sum(jnp.where(even_doc, dembed_rows, 0.0), axis=(0, 1))
    seg_odd = jnp.sum(jnp.where(even_doc, 0.0, dembed_rows), axis=(0, 1))
    small_grad = jnp.concatenate(
        [jnp.sum(dembed_rows, axis=0), seg_even[None], seg_odd[None], vectors], axis=0
    )
    mixed = pieces[0]
    if paired:
        cut = dembed.astype(jnp.bfloat16).reshape(L, n_wide, D // n_wide).transpose(1, 0, 2)
        cut = lax.all_to_all(cut, "wide", 0, 0).reshape(n_wide * L, D // n_wide)
        halved = small_halved(small_grad).astype(jnp.bfloat16)
        placed = put_rows(owners.owner_slots(), cut, n_narrow * owners.count)
        placed = placed.reshape(n_narrow, owners.count, -1)
        near = placed[:, 0 : owners.room]
        wider = jnp.broadcast_to(halved[None], (n_narrow,) + halved.shape)
        near = sent_around(jnp.concatenate([near, wider], axis=1))
        down, up = pieces[2], pieces[1]
        *near, mixed.away, down.result, up.result, table_head = together(
            *near, mixed.away, down.result, up.result, table_head
        )
        mixed.finish()
        table_grad = added_rows(packed_ids, [part[0 : owners.room] for part in near], vshard)
        table_grad = lax.cond(
            owners.full,
            lambda: added_rows(packed_ids, sent_around(placed), vshard),
            lambda: table_grad,
        )
        table_mom, table_upd, table_norms = table_update(
            table_grad, table_head, table, table_m, table_v
        )
        small_grad = small_total([part[owners.room :] for part in near])
        mixed.result, table_norms, small_grad = together(mixed.result, table_norms, small_grad)
    else:
        mixed.finish()
        group_rows = lax.all_gather(dembed_rows.astype(jnp.bfloat16), "narrow", axis=0, tiled=True)
        table_grad = matmul_tn(dlogit, group_h).at[slots].add(
            group_rows.reshape(-1, D).astype(jnp.float32), mode="drop"
        )
        cut = table_grad.astype(jnp.bfloat16).reshape(vshard, n_wide, D // n_wide)
        table_grad = lax.psum_scatter(cut.transpose(1, 0, 2), "wide", scatter_dimension=0)
        table_grad = table_grad.astype(jnp.float32)
    part_cols = layer.shape[1]
    if paired:
        spans, total, start = [], 0.0, [0, 4 * D, 8 * D]
        for piece, first in zip(pieces[::-1], start[::-1]):
            span, amount = span_of(layer_m, piece.result, worker_err, first)
            spans.insert(0, span)
            total = total + amount
        scale = total / (layer_m.shape[0] * layer_m.shape[1]) + MAG_EPS
        new_worker, sent = pressed(spans, scale, n_wide)
        server_in = scattered_sum(sent) / n_wide + server_err
    else:
        worker_grad = jnp.concatenate([piece.result for piece in pieces], axis=1)
        span = BETA * layer_m + (1.0 - BETA) * worker_grad.astype(jnp.float32) + worker_err[0]
        scale = jnp.mean(jnp.abs(span)) + MAG_EPS
        sent = scale * jnp.tanh(span / scale)
        new_worker = (span - sent)[None]
        summed = lax.psum(sent.astype(jnp.bfloat16), "wide").astype(jnp.float32)
        mixed = lax.dynamic_slice_in_dim(summed, wide_me * part_cols, part_cols, 1) / n_wide
        server_in = mixed + server_err
    sscale = jnp.mean(jnp.abs(server_in)) + MAG_EPS
    server_out = sscale * jnp.tanh(server_in / sscale)
    new_server = server_in - server_out
    server_low = server_out.astype(jnp.bfloat16)
    if not paired:
        small_grad = lax.psum(small_grad, ("wide", "narrow"))
        table_mom = BETA * table_m + (1.0 - BETA) * table_grad
        table_upd = table_mom / (jnp.sqrt(table_v) + OPT_EPS) + DECAY * table
        table_norms = (jnp.sum(table * table)[None], jnp.sum(table_upd * table_upd)[None])
    small_mom = BETA * small_m + (1.0 - BETA) * small_grad
    small_upd = small_mom / (jnp.sqrt(small_v) + OPT_EPS) + DECAY * small
    small_norms = (jnp.sum(small * small)[None], jnp.sum(small_upd * small_upd)[None])
    new_m = lax.all_gather(server_low, "wide", axis=1, tiled=True).astype(jnp.float32)
    layer_upd = server_out / (jnp.sqrt(layer_v) + OPT_EPS) + DECAY * layer
    column = wide_me * part_cols + jnp.arange(part_cols)
    which = (
        (column >= 3 * D).astype(jnp.int32)
        + (column >= 4 * D).astype(jnp.int32)
        + (column >= 4 * D + FF).astype(jnp.int32)
    )
    onehot = (which[:, None] == jnp.arange(4)[None]).astype(jnp.float32)
    wsq = jnp.sum(jnp.sum(layer * layer, axis=0)[:, None] * onehot, axis=0)
    usq = jnp.sum(jnp.sum(layer_upd * layer_upd, axis=0)[:, None] * onehot, axis=0)
    parts = jnp.concatenate([wsq, usq, *table_norms, jnp.sum(own_loss)[None]])
    sums = summed_over(summed_over(parts, "wide"), "narrow")
    loss_sum = sums[10]
    wnorm = jnp.sqrt(jnp.concatenate([sums[0:4], sums[8:9], small_norms[0]]))
    unorm = jnp.sqrt(jnp.concatenate([sums[4:8], sums[9:10], small_norms[1]]))
    ratio = wnorm / unorm
    new_layer = layer - RATE * jnp.sum(onehot * ratio[None, 0:4], axis=1)[None] * layer_upd
    new_table = table - RATE * ratio[4] * table_upd
    new_small = small - RATE * ratio[5] * small_upd
    return (
        jnp.stack([loss_sum, count]),
        new_table,
        table_mom,
        new_small,
        small_mom,
        new_layer,
        new_m,
        new_worker,
        new_server,
        jnp.stack([wnorm, unorm]),
    )


def solution(mesh):
    placed = (
        P("wide", None),
        P(("wide", "narrow"), None),
        P(("wide", "narrow"), None),
        P("wide", None),
        P("wide", None),
        P("narrow", "wide"),
        P("narrow", "wide"),
        P("narrow", "wide"),
        P(),
        P(),
        P(),
        P("narrow", "wide"),
        P("narrow", None),
        P("narrow", "wide"),
        P("wide", "narrow", None),
        P("narrow", "wide"),
    )
    return jax.shard_map(
        shards,
        mesh=mesh,
        in_specs=placed,
        out_specs=(
            P(),
            P("narrow", "wide"),
            P("narrow", "wide"),
            P(),
            P(),
            P("narrow", "wide"),
            P("narrow", None),
            P("wide", "narrow", None),
            P("narrow", "wide"),
            P(),
        ),
        check_vma=False,
    )
```

```python
import functools

import jax
import jax.numpy as jnp
from jax import lax
from jax.experimental import pallas as pl
from jax.experimental.pallas import tpu as pltpu
from jax.sharding import PartitionSpec as P

D = 1024
HEADS = 16
HEAD = 64
FF = 4096
VREAL = 30522
L = 512
MPS = 80


LN_EPS = 1e-12
BETA = 0.9
DECAY = 0.01
RATE = 0.25
OPT_EPS = 1e-06
MAG_EPS = 1e-08

FREE = pl.CostEstimate(flops=0, bytes_accessed=0, transcendentals=0)


def joined(value, axis, join):
    pieces = jax.tree.map(lambda part: lax.all_gather(part, axis), value)
    head = jax.tree.map(lambda part: part[0], pieces)
    tail = jax.tree.map(lambda part: part[1:], pieces)
    subtotal, _ = lax.scan(lambda subtotal, slab: (join(subtotal, slab), None), head, tail)
    return subtotal


def norm_rows(x, gain, shift):
    mean = jnp.mean(x, axis=-1, keepdims=True)
    cent = x - mean
    var = jnp.mean(cent * cent, axis=-1, keepdims=True)
    return cent * lax.rsqrt(var + LN_EPS) * gain + shift


def gelu_exact(upper):
    return jax.nn.gelu(upper, approximate=False)


def matmul(left, right):
    return jnp.dot(left, right, preferred_element_type=jnp.float32)


def matmul_tn(left, right):
    return lax.dot_general(
        left, right, (((0,), (0,)), ((), ())), preferred_element_type=jnp.float32
    )


def matmul_nt(left, right):
    return lax.dot_general(
        left, right, (((1,), (1,)), ((), ())), preferred_element_type=jnp.float32
    )


def attend_kernel(q_ref, k_ref, v_ref, key_doc_ref, query_doc_ref, out_ref, lse_ref):
    same = key_doc_ref[...] == query_doc_ref[...]
    lane = lax.broadcasted_iota(jnp.int32, (1, 2 * HEAD), 1)
    outs = []
    for head in range(2):
        mine = lane // HEAD == head
        query = jnp.where(mine, q_ref[...] * 0.125, 0).astype(jnp.bfloat16)
        scores = jnp.where(same, matmul_nt(k_ref[...], query), -1000000000.0)
        top = jnp.max(scores, axis=0, keepdims=True)
        power = jnp.exp(scores - top)
        total = jnp.sum(power, axis=0, keepdims=True)
        lse_ref[0, head : head + 1, :] = top + jnp.log(total)
        prob = (power * (1.0 / total)).astype(jnp.bfloat16)
        outs.append(matmul_tn(prob, v_ref[...]))
    out_ref[...] = jnp.where(lane < HEAD, outs[0], outs[1]).astype(jnp.bfloat16)


def head_pairs(offset):
    return pl.BlockSpec((L, 2 * HEAD), lambda pair: (0, offset * HEADS // 2 + pair))


def attend(qkv, docs):
    return pl.pallas_call(
        attend_kernel,
        grid=(HEADS // 2,),
        in_specs=[
            head_pairs(0),
            head_pairs(1),
            head_pairs(2),
            pl.BlockSpec((L, 1), lambda pair: (0, 0)),
            pl.BlockSpec((1, L), lambda pair: (0, 0)),
        ],
        out_specs=[head_pairs(0), pl.BlockSpec((1, 2, L), lambda pair: (pair, 0, 0))],
        out_shape=[
            jax.ShapeDtypeStruct((L, D), jnp.bfloat16),
            jax.ShapeDtypeStruct((HEADS // 2, 2, L), jnp.float32),
        ],
        compiler_params=pltpu.CompilerParams(vmem_limit_bytes=40 * 2**20),
        cost_estimate=FREE,
        name="attend",
    )(qkv, qkv, qkv, docs.reshape(L, 1), docs.reshape(1, L))


def attend_back_kernel(q_ref, k_ref, v_ref, do_ref, lse_ref, key_doc_ref, query_doc_ref, out_ref):
    pair = pl.program_id(0)
    same = key_doc_ref[...] == query_doc_ref[...]
    lane = lax.broadcasted_iota(jnp.int32, (1, 2 * HEAD), 1)
    both = []
    for head in range(2):
        mine = lane // HEAD == head
        query = jnp.where(mine, q_ref[...] * 0.125, 0).astype(jnp.bfloat16)
        dout = jnp.where(mine, do_ref[...], 0).astype(jnp.bfloat16)
        scores = jnp.where(same, matmul_nt(k_ref[...], query), -1000000000.0)
        prob = jnp.exp(scores - lse_ref[0, head : head + 1, :])
        dvalue = matmul(prob.astype(jnp.bfloat16), dout)
        dprob = matmul_nt(v_ref[...], dout)
        delta = jnp.sum(prob * dprob, axis=0, keepdims=True)
        dscore = (prob * (dprob - delta)).astype(jnp.bfloat16)
        both.append((matmul_tn(dscore, k_ref[...]) * 0.125, matmul(dscore, query), dvalue))
    for part in range(3):
        value = jnp.where(lane < HEAD, both[0][part], both[1][part]).astype(jnp.bfloat16)
        start = pl.multiple_of(part * D + pair * 2 * HEAD, 2 * HEAD)
        out_ref[:, pl.ds(start, 2 * HEAD)] = value


def attend_back(qkv, dout, lse, docs):
    return pl.pallas_call(
        attend_back_kernel,
        grid=(HEADS // 2,),
        in_specs=[
            head_pairs(0),
            head_pairs(1),
            head_pairs(2),
            head_pairs(0),
            pl.BlockSpec((1, 2, L), lambda pair: (pair, 0, 0)),
            pl.BlockSpec((L, 1), lambda pair: (0, 0)),
            pl.BlockSpec((1, L), lambda pair: (0, 0)),
        ],
        out_specs=pl.BlockSpec((L, 3 * D), lambda pair: (0, 0)),
        out_shape=jax.ShapeDtypeStruct((L, 3 * D), jnp.bfloat16),
        compiler_params=pltpu.CompilerParams(vmem_limit_bytes=40 * 2**20),
        cost_estimate=FREE,
        name="attend_back",
    )(qkv, qkv, qkv, dout, lse, docs.reshape(L, 1), docs.reshape(1, L))


def merge_rows(first, second):
    peak = jnp.maximum(first[0], second[0])
    total = first[1] * jnp.exp(first[0] - peak) + second[1] * jnp.exp(second[0] - peak)
    return (peak, total, first[2] + second[2])


def layer_forward(embedded, x0, act, docs, small, weights):
    base = L + 2
    bias = jnp.concatenate([small[base + 6], jnp.zeros((D,), jnp.float32), small[base + 7]])
    qkv = (matmul(act, weights[:, 0 : 3 * D]) + bias).astype(jnp.bfloat16)
    out, lse = attend(qkv, docs)
    rone = x0 + (matmul(out, weights[:, 3 * D : 4 * D]) + small[base + 8])
    hone = norm_rows(rone, small[base + 2], small[base + 3])
    fin = hone.astype(jnp.bfloat16)
    upper = matmul(fin, weights[:, 4 * D : 4 * D + FF]) + small[base + 10 :].reshape(FF)
    gated = gelu_exact(upper).astype(jnp.bfloat16)
    rtwo = hone + (matmul_nt(gated, weights[:, 4 * D + FF :]) + small[base + 9])
    htwo = norm_rows(rtwo, small[base + 4], small[base + 5])
    return (htwo, (embedded, act, qkv, lse, out, rone, fin, upper, gated, rtwo))


def layer_backward(dhtwo, kept, docs, small, weights):
    embedded, act, qkv, lse, out, rone, fin, upper, gated, rtwo = kept
    base = L + 2
    _, pull = jax.vjp(norm_rows, rtwo, small[base + 4], small[base + 5])
    drtwo, dgain_two, dshift_two = pull(dhtwo)
    dffn = drtwo.astype(jnp.bfloat16)
    down = WorkerPiece((dffn, gated))
    dgated = matmul(dffn, weights[:, 4 * D + FF :])
    _, pull = jax.vjp(gelu_exact, upper)
    dupper = pull(dgated)[0].astype(jnp.bfloat16)
    dupper = down.received(dupper)
    down.across()
    up = WorkerPiece((fin, dupper))
    dhone = drtwo + matmul_nt(dupper, weights[:, 4 * D : 4 * D + FF])
    _, pull = jax.vjp(norm_rows, rone, small[base + 2], small[base + 3])
    drone, dgain_one, dshift_one = pull(dhone)
    dattn = drone.astype(jnp.bfloat16)
    dout = matmul_nt(dattn, weights[:, 3 * D : 4 * D]).astype(jnp.bfloat16)
    dout = up.received(dout)
    up.across()
    dqkv = attend_back(qkv, dout, lse, docs)
    (dqkv,) = down.crossed(dqkv)
    down.finish()
    mixed = WorkerPiece((act, dqkv), (out, dattn))
    dxzero = drone + matmul_nt(dqkv, weights[:, 0 : 3 * D])
    _, pull = jax.vjp(norm_rows, embedded, small[base], small[base + 1])
    dembed, dgain_emb, dshift_emb = pull(dxzero)
    dembed = mixed.received(dembed)
    mixed.across(up)
    up.finish()
    bias_qkv = jnp.sum(dqkv, axis=0, dtype=jnp.float32)
    vectors = jnp.stack(
        [
            dgain_emb,
            dshift_emb,
            dgain_one,
            dshift_one,
            dgain_two,
            dshift_two,
            bias_qkv[0:D],
            bias_qkv[2 * D : 3 * D],
            jnp.sum(dattn, axis=0, dtype=jnp.float32),
            jnp.sum(dffn, axis=0, dtype=jnp.float32),
        ]
    )
    bias_up = jnp.sum(dupper, axis=0, dtype=jnp.float32).reshape(FF // D, D)
    return (dembed, jnp.concatenate([vectors, bias_up], axis=0), (mixed, up, down))


def paired_mesh():
    return lax.axis_size("wide") == 8 and lax.axis_size("narrow") == 4


def together(*values):
    return lax.optimization_barrier(values)


def swap_pairs(size, bit):
    return [(place, place ^ bit) for place in range(size)]


def cycle(size, by):
    return [(place, (place + by) % size) for place in range(size)]


def summed_over(value, axis):
    size = lax.axis_size(axis)
    if size & (size - 1):
        return lax.psum(value, axis)
    bit = 1
    while bit < size:
        value = value + lax.ppermute(value, axis, swap_pairs(size, bit))
        bit *= 2
    return value


def gathered_near(value, beside=None):
    size = lax.axis_size("narrow")
    rows = value.shape[0]
    around = [value]
    for by in range(1, size):
        around.append(lax.ppermute(value, "narrow", cycle(size, size - by)))
    if beside is not None:
        *around, beside = together(*around, beside)
    twice = jnp.concatenate(around + around[:-1], axis=0)
    start = lax.rem(size - lax.axis_index("narrow"), size) * rows
    whole = lax.dynamic_slice_in_dim(twice, start, size * rows, 0)
    return whole if beside is None else (whole, beside)


def scattered_near(value):
    size = lax.axis_size("narrow")
    rows = value.shape[0] // size
    place = lax.axis_index("narrow")
    total = lax.dynamic_slice_in_dim(value, place * rows, rows, 0)
    for by in range(1, size):
        target = lax.rem(place + by, size)
        give = lax.dynamic_slice_in_dim(value, target * rows, rows, 0).astype(jnp.bfloat16)
        take = lax.ppermute(give, "narrow", cycle(size, by))
        total = total + take.astype(jnp.float32)
    return total


def sent_around(blocks):
    size = lax.axis_size("narrow")
    place = lax.axis_index("narrow")

    def block(by):
        return lax.dynamic_index_in_dim(blocks, lax.rem(place + by, size), 0, keepdims=False)

    return [block(0)] + [
        lax.ppermute(block(by), "narrow", cycle(size, by)) for by in range(1, size)
    ]


class WorkerPiece:
    def __init__(self, *pairs):
        self.pairs = pairs
        self.paired = paired_mesh()
        if not self.paired:
            return
        self.core = lax.axis_index("wide") % 2
        self.pair, self.side = lax.axis_index("narrow") // 2, lax.axis_index("narrow") % 2
        cores = swap_pairs(lax.axis_size("wide"), 1)
        self.far = lax.ppermute(self.block(1 - self.core, 1 - self.side), "wide", cores)
        self.near = lax.ppermute(self.block(1 - self.core, self.side), "wide", cores)

    def block(self, core, side, *terms):
        rows = D // lax.axis_size("narrow")
        blocks, start = [], 0
        for left, right in self.pairs:
            part = lax.dynamic_slice_in_dim(left, (2 * core + side) * rows, rows, 1)
            total = matmul_tn(part, right)
            for term in terms:
                total = total + term[:, start : start + right.shape[1]].astype(jnp.float32)
            blocks.append(total.astype(jnp.bfloat16))
            start += right.shape[1]
        return blocks[0] if len(blocks) == 1 else jnp.concatenate(blocks, axis=1)

    def received(self, value):
        if self.paired:
            value, self.far, self.near = together(value, self.far, self.near)
        return value

    def across(self, before=None):
        if self.paired:
            sides = swap_pairs(lax.axis_size("narrow"), 1)
            away = self.block(self.core, 1 - self.side, self.far)
            if before is not None:
                away, before.near = together(away, before.near)
            self.away = lax.ppermute(away, "narrow", sides)

    def crossed(self, *values):
        if self.paired:
            *values, self.away = together(*values, self.away)
        return values

    def finish(self, *values):
        if not self.paired:
            blocks = [matmul_tn(left, right).astype(jnp.bfloat16) for left, right in self.pairs]
            grad = jnp.concatenate(blocks, axis=1)
            self.result = lax.psum_scatter(grad, "narrow", scatter_dimension=0, tiled=True)
            return values
        n_wide, n_narrow = lax.axis_size("wide"), lax.axis_size("narrow")
        total = self.block(self.core, self.side, self.near, self.away)
        moves = []
        for wide in range(n_wide):
            for narrow in range(n_narrow):
                if narrow // 2 != wide % 2:
                    target_wide = wide - wide % 2 + narrow // 2
                    target = target_wide * n_narrow + 2 * (wide % 2) + narrow % 2
                    moves.append((wide * n_narrow + narrow, target))
        total, *values = together(total, *values)
        moved = lax.ppermute(total, ("wide", "narrow"), moves)
        self.result = jnp.where(self.pair == self.core, total, moved)
        return values


def hosted_rows(token_ids, mlm_labels, mlm_valid, doc_ids, mlm_pos):
    n_wide, n_narrow = lax.axis_size("wide"), lax.axis_size("narrow")
    packed = jnp.concatenate([token_ids, mlm_labels, mlm_valid], axis=1)[None]
    for bit, place in zip((1, 2, 4), wide_places()):
        other = lax.ppermute(packed, "wide", swap_pairs(n_wide, bit))
        first, second = jnp.where(place == 0, packed, other), jnp.where(place == 0, other, packed)
        packed = jnp.concatenate([first, second], axis=0)
    width = packed.shape[2]
    hosted = packed.reshape(n_wide // 2, 2, 2, 2, width).transpose(1, 2, 0, 3, 4)
    hosted = hosted.reshape(n_narrow, n_wide, width)
    column = lax.dynamic_index_in_dim(hosted, lax.axis_index("wide"), 1, keepdims=False)
    moves = []
    for wide in range(n_wide):
        for row in range(n_narrow):
            target_wide = wide - wide % 2 + row % 2
            target_narrow = 2 * (wide % 2) + row // 2
            moves.append((wide * n_narrow + row, target_wide * n_narrow + target_narrow))
    own = lax.ppermute(jnp.concatenate([doc_ids, mlm_pos], axis=1), ("wide", "narrow"), moves)
    return (
        hosted[:, :, 0:L],
        column[:, L : L + MPS],
        column[:, L + MPS :],
        own[:, 0:L],
        own[:, L:],
    )


STREAMS = 2


class Owners:
    def __init__(self, tokens, vshard):
        size = lax.axis_size("narrow")
        place = lax.axis_index("narrow")
        count = tokens.shape[1]
        self.room = count * 7 // 16
        owner = tokens // vshard
        held = (owner[None] == jnp.arange(size)[:, None, None]).astype(jnp.bfloat16)
        tiles = held.reshape(-1, count // 128, 128)
        order = jnp.arange(128)
        within = jnp.einsum(
            "btl,lm->btm",
            tiles,
            (order[:, None] < order[None]).astype(jnp.bfloat16),
            preferred_element_type=jnp.float32,
        )
        sums = jnp.sum(tiles.astype(jnp.float32), axis=2)
        tile = jnp.arange(count // 128)
        before = jnp.sum(jnp.where(tile[:, None] < tile[None], sums[:, :, None], 0.0), axis=1)
        rank = (within + before[..., None]).reshape(size, size, count) * held.astype(jnp.float32)
        rank = jnp.sum(rank, axis=0).astype(jnp.int32)
        self.full = jnp.max(jnp.sum(sums, axis=1)) > self.room
        self.count, self.vshard = count, vshard
        own = lax.dynamic_index_in_dim(owner, place, 0, keepdims=False)
        self.rank = lax.dynamic_index_in_dim(rank, place, 0, keepdims=False)
        self.owner = own
        self.behind = lax.rem(place - own + size, size)
        self.slots = jnp.where(owner == place, tokens - place * vshard, vshard)

    def behind_slots(self, room):
        return self.behind * room + jnp.minimum(self.rank, room - 1)

    def owner_slots(self):
        return self.owner * self.count + self.rank

    def packed(self, slots):
        size = lax.axis_size("narrow")
        base = self.vshard + 1
        order = jnp.arange(self.count) * base + slots
        order = jnp.where(slots < self.vshard, order, order + self.count * base)
        backward = (lax.sort(order) % base)[::-1]
        backward = jnp.concatenate([backward, backward], axis=0)
        start = size - 1 - lax.axis_index("narrow")
        return lax.dynamic_slice_in_dim(backward, start, size, 0)


def pack_kernel(ids_ref, table_ref, out_ref, held, *rows):
    step, count, size = pl.program_id(0), out_ref.shape[1], table_ref.shape[0]

    @pl.when(step == 0)
    def _():
        held[0:size, :] = table_ref[...]
        held[size:, :] = jnp.zeros((8, table_ref.shape[1]), jnp.float32)
        for part in rows:
            part[...] = jnp.zeros_like(part)

    base = [(step * len(rows) + index) * count for index in range(len(rows))]

    def some(turn, used):
        used = list(used)
        for by in range(8):
            for index, part in enumerate(rows):
                place = ids_ref[base[index] + turn * 8 + by]
                part[pl.ds(used[index], 1), :] = held[pl.ds(place, 1), :]
                used[index] = used[index] + jnp.where(place < size, 1, 0)
        return tuple(used)

    lax.fori_loop(0, count // 8, some, (0,) * len(rows))
    for index, part in enumerate(rows):
        out_ref[index] = part[0:count, :].astype(out_ref.dtype)


def packed_rows(ids, table):
    size, cols = table.shape
    places, count = ids.shape
    return pl.pallas_call(
        pack_kernel,
        grid_spec=pltpu.PrefetchScalarGridSpec(
            num_scalar_prefetch=1,
            grid=(places // STREAMS,),
            in_specs=[pl.BlockSpec((size, cols), lambda step, ids: (0, 0))],
            out_specs=pl.BlockSpec((STREAMS, count, cols), lambda step, ids: (step, 0, 0)),
            scratch_shapes=[pltpu.VMEM((size + 8, cols), jnp.float32)]
            + [pltpu.VMEM((count + 8, cols), jnp.float32)] * STREAMS,
        ),
        out_shape=jax.ShapeDtypeStruct((places, count, cols), jnp.bfloat16),
        compiler_params=pltpu.CompilerParams(vmem_limit_bytes=40 * 2**20),
        cost_estimate=pl.CostEstimate(flops=0, bytes_accessed=15 * 10**7, transcendentals=0),
        name="pack_rows",
    )(ids.reshape(-1), table)


def take_kernel(ids_ref, table_ref, out_ref, held, rows):
    held[...] = table_ref[...].astype(jnp.float32)

    @pl.loop(0, out_ref.shape[0], step=16)
    def _(first):
        for by in range(16):
            rows[pl.ds(first + by, 1), :] = held[pl.ds(ids_ref[first + by], 1), :]

    out_ref[...] = rows[...].astype(out_ref.dtype)


def taken_rows(ids, table):
    count, cols = ids.shape[0], table.shape[1]
    return pl.pallas_call(
        take_kernel,
        grid_spec=pltpu.PrefetchScalarGridSpec(
            num_scalar_prefetch=1,
            grid=(1,),
            in_specs=[pl.BlockSpec(table.shape, lambda step, ids: (0, 0))],
            out_specs=pl.BlockSpec((count, cols), lambda step, ids: (0, 0)),
            scratch_shapes=[
                pltpu.VMEM(table.shape, jnp.float32),
                pltpu.VMEM((count, cols), jnp.float32),
            ],
        ),
        out_shape=jax.ShapeDtypeStruct((count, cols), table.dtype),
        compiler_params=pltpu.CompilerParams(vmem_limit_bytes=40 * 2**20),
        cost_estimate=FREE,
        name="take_rows",
    )(ids, table)


def put_kernel(ids_ref, rows_ref, out_ref, rows, held):
    rows[...] = rows_ref[...].astype(jnp.float32)
    held[...] = jnp.zeros_like(held)

    @pl.loop(0, rows_ref.shape[0], step=16)
    def _(first):
        for by in range(16):
            held[pl.ds(ids_ref[first + by], 1), :] = rows[pl.ds(first + by, 1), :]

    out_ref[...] = held[...].astype(out_ref.dtype)


def put_rows(ids, values, size):
    cols = values.shape[1]
    return pl.pallas_call(
        put_kernel,
        grid_spec=pltpu.PrefetchScalarGridSpec(
            num_scalar_prefetch=1,
            grid=(1,),
            in_specs=[pl.BlockSpec(values.shape, lambda step, ids: (0, 0))],
            out_specs=pl.BlockSpec((size, cols), lambda step, ids: (0, 0)),
            scratch_shapes=[
                pltpu.VMEM(values.shape, jnp.float32),
                pltpu.VMEM((size, cols), jnp.float32),
            ],
        ),
        out_shape=jax.ShapeDtypeStruct((size, cols), values.dtype),
        compiler_params=pltpu.CompilerParams(vmem_limit_bytes=40 * 2**20),
        cost_estimate=FREE,
        name="put_rows",
    )(ids, values)


def add_kernel(length, ids_ref, *refs):
    count = (len(refs) - 1) // 3
    rows_refs, out_ref, rows, sums = refs[:count], refs[count], refs[count + 1 : 2 * count + 1], refs[2 * count + 1 :]
    size = out_ref.shape[0]
    each = ids_ref.shape[0] // count
    for part, held, rows_ref in zip(sums, rows, rows_refs):
        part[...] = jnp.zeros_like(part)
        held[...] = rows_ref[0:length, :].astype(jnp.float32)

    @pl.loop(0, length, step=8)
    def _(first):
        for by in range(8):
            for index, part in enumerate(sums):
                place = ids_ref[index * each + first + by]
                part[pl.ds(place, 1), :] += rows[index][pl.ds(first + by, 1), :]

    total = sums[0][0:size, :]
    for part in sums[1:]:
        total = total + part[0:size, :]
    out_ref[...] = total


def added_rows(ids, values, size, length):
    cols = values[0].shape[1]
    block = pl.BlockSpec(values[0].shape, lambda step, ids: (0, 0))
    return pl.pallas_call(
        functools.partial(add_kernel, length),
        grid_spec=pltpu.PrefetchScalarGridSpec(
            num_scalar_prefetch=1,
            grid=(1,),
            in_specs=[block] * len(values),
            out_specs=pl.BlockSpec((size, cols), lambda step, ids: (0, 0)),
            scratch_shapes=[pltpu.VMEM((length, cols), jnp.float32)] * len(values)
            + [pltpu.VMEM((size + 8, cols), jnp.float32)] * len(values),
        ),
        out_shape=jax.ShapeDtypeStruct((size, cols), jnp.float32),
        compiler_params=pltpu.CompilerParams(vmem_limit_bytes=56 * 2**20),
        cost_estimate=FREE,
        name="add_rows",
    )(ids.reshape(-1), *values)


def span_kernel(momentum_ref, grad_ref, error_ref, span_ref, sum_ref):
    grad = grad_ref[...].astype(jnp.float32)
    span = BETA * momentum_ref[...] + (1.0 - BETA) * grad + error_ref[0]
    span_ref[...] = span

    @pl.when(pl.program_id(0) == 0)
    def _():
        sum_ref[...] = jnp.zeros_like(sum_ref)

    sum_ref[...] += jnp.sum(jnp.abs(span), axis=0, keepdims=True)


def span_of(momentum, grad, error, start):
    rows, cols = grad.shape
    block = 1024
    first = start // block
    span, sums = pl.pallas_call(
        span_kernel,
        grid=(cols // block,),
        in_specs=[
            pl.BlockSpec((rows, block), lambda step: (0, first + step)),
            pl.BlockSpec((rows, block), lambda step: (0, step)),
            pl.BlockSpec((1, rows, block), lambda step: (0, 0, first + step)),
        ],
        out_specs=[
            pl.BlockSpec((rows, block), lambda step: (0, step)),
            pl.BlockSpec((1, block), lambda step: (0, 0)),
        ],
        out_shape=[
            jax.ShapeDtypeStruct((rows, cols), jnp.float32),
            jax.ShapeDtypeStruct((1, block), jnp.float32),
        ],
        compiler_params=pltpu.CompilerParams(vmem_limit_bytes=60 * 2**20),
        cost_estimate=FREE,
        name="span",
    )(momentum, grad, error)
    return span, jnp.sum(sums)


def press_kernel(steps, scale_ref, *refs):
    *span_refs, error_ref, sent_ref = refs
    step = pl.program_id(0)
    scale = scale_ref[0]
    inverse = scale_ref[1]
    for index, span_ref in enumerate(span_refs):

        @pl.when((step >= steps[index]) & (step < steps[index + 1]))
        def _():
            span = span_ref[...]
            sent = scale * jnp.tanh(span * inverse)
            error_ref[0] = span - sent
            sent_ref[0] = sent.astype(jnp.bfloat16)


def pressed(spans, scale, parts):
    rows = spans[0].shape[0]
    cols = sum(span.shape[1] for span in spans)
    block = 512
    each = cols // parts // block
    steps = [0]
    for span in spans:
        steps.append(steps[-1] + span.shape[1] // block)

    def of(index):
        low, count = steps[index], steps[index + 1] - steps[index]
        return pl.BlockSpec((rows, block), lambda step: (0, jnp.clip(step - low, 0, count - 1)))

    return pl.pallas_call(
        functools.partial(press_kernel, steps),
        grid=(steps[-1],),
        in_specs=[pl.BlockSpec(memory_space=pltpu.SMEM)] + [of(i) for i in range(len(spans))],
        out_specs=[
            pl.BlockSpec((1, rows, block), lambda step: (0, 0, step)),
            pl.BlockSpec((1, rows, block), lambda step: (step // each, 0, step % each)),
        ],
        out_shape=[
            jax.ShapeDtypeStruct((1, rows, cols), jnp.float32),
            jax.ShapeDtypeStruct((parts, rows, cols // parts), jnp.bfloat16),
        ],
        compiler_params=pltpu.CompilerParams(vmem_limit_bytes=60 * 2**20),
        cost_estimate=FREE,
        name="press",
    )(jnp.stack([scale, 1.0 / scale]), *spans)


def update_kernel(grad_ref, head_ref, table_ref, first_ref, second_ref, *out_refs):
    first_out, update_ref, weight_sum, update_sum = out_refs
    grad = grad_ref[...] + head_ref[...].astype(jnp.float32)
    first = BETA * first_ref[...] + (1.0 - BETA) * grad
    table = table_ref[...]
    update = first / (jnp.sqrt(second_ref[...]) + OPT_EPS) + DECAY * table
    first_out[...] = first
    update_ref[...] = update

    @pl.when(pl.program_id(0) == 0)
    def _():
        weight_sum[...] = jnp.zeros_like(weight_sum)
        update_sum[...] = jnp.zeros_like(update_sum)

    weight_sum[...] += jnp.sum(table * table, axis=0, keepdims=True)
    update_sum[...] += jnp.sum(update * update, axis=0, keepdims=True)


def table_update(grad, head, table, first, second):
    size, cols = table.shape
    block = size // 9 if size % 9 == 0 and size // 9 % 16 == 0 else size
    whole = pl.BlockSpec((block, cols), lambda step: (step, 0))
    line = pl.BlockSpec((1, cols), lambda step: (0, 0))
    moment, update, *sums = pl.pallas_call(
        update_kernel,
        grid=(size // block,),
        in_specs=[whole] * 5,
        out_specs=[whole, whole, line, line],
        out_shape=[jax.ShapeDtypeStruct((size, cols), jnp.float32)] * 2
        + [jax.ShapeDtypeStruct((1, cols), jnp.float32)] * 2,
        compiler_params=pltpu.CompilerParams(vmem_limit_bytes=56 * 2**20),
        cost_estimate=FREE,
        name="update",
    )(grad, head, table, first, second)
    return moment, update, tuple(jnp.sum(part)[None] for part in sums)


def wide_places():
    wide_me = lax.axis_index("wide")
    return wide_me % 2, wide_me // 2 % 2, wide_me // 4


def scattered_sum(sent):
    n_wide = lax.axis_size("wide")
    core, x, y = wide_places()

    def send(value, bit):
        return lax.ppermute(value.astype(jnp.bfloat16), "wide", swap_pairs(n_wide, bit))

    def pick(value, index):
        return lax.dynamic_index_in_dim(value, index, 0, keepdims=False)

    rows, cols = sent.shape[1:]
    by_core = sent.reshape(n_wide // 2, 2, rows, cols)
    give = lax.dynamic_index_in_dim(by_core, 1 - core, 1, keepdims=False)
    keep = lax.dynamic_index_in_dim(by_core, core, 1, keepdims=False)
    take = send(give, 1)
    half = rows // 2

    def chip(y_of, x_of, part):
        low, high = part * half, (part + 1) * half
        index = 2 * y_of + x_of
        own, other = pick(keep[:, low:high], index), pick(take[:, low:high], index)
        return own.astype(jnp.float32) + other.astype(jnp.float32)

    upper_far = send(chip(1 - y, 1 - x, 0), 2)
    lower_far = send(chip(1 - y, 1 - x, 1), 4)
    upper_near = send(chip(y, 1 - x, 0), 2)
    lower_near = send(chip(1 - y, x, 1), 4)
    upper_far = send(chip(1 - y, x, 0) + upper_far.astype(jnp.float32), 4)
    lower_far = send(chip(y, 1 - x, 1) + lower_far.astype(jnp.float32), 2)
    own_upper = chip(y, x, 0) + upper_near.astype(jnp.float32) + upper_far.astype(jnp.float32)
    own_lower = chip(y, x, 1) + lower_near.astype(jnp.float32) + lower_far.astype(jnp.float32)
    return jnp.concatenate([own_upper, own_lower], axis=0)


def small_halved(value):
    n_wide = lax.axis_size("wide")
    for bit, place in zip((1, 2, 4), wide_places()):
        half = value.shape[1] // 2
        give = lax.dynamic_slice_in_dim(value, (1 - place) * half, half, 1).astype(jnp.bfloat16)
        keep = lax.dynamic_slice_in_dim(value, place * half, half, 1)
        value = keep + lax.ppermute(give, "wide", swap_pairs(n_wide, bit)).astype(jnp.float32)
    return value


def small_total(parts):
    n_wide, n_narrow = lax.axis_size("wide"), lax.axis_size("narrow")
    parts = jnp.stack(parts + parts[:-1])
    start = lax.rem(lax.axis_index("narrow") + 1, n_narrow)
    parts = lax.dynamic_slice_in_dim(parts, start, n_narrow, 0).astype(jnp.float32)
    value = parts[0]
    for place in range(1, n_narrow):
        value = value + parts[place]
    value = value.astype(jnp.bfloat16)
    for bit, place in reversed(list(zip((1, 2, 4), wide_places()))):
        other = lax.ppermute(value, "wide", swap_pairs(n_wide, bit))
        first, second = jnp.where(place == 0, value, other), jnp.where(place == 0, other, value)
        value = jnp.concatenate([first, second], axis=1)
    return value.astype(jnp.float32)


def shards(
    token_ids,
    doc_ids,
    mlm_pos,
    mlm_labels,
    mlm_valid,
    table,
    table_m,
    table_v,
    small,
    small_m,
    small_v,
    layer,
    layer_m,
    layer_v,
    worker_err,
    server_err,
):
    n_wide, n_narrow = lax.axis_size("wide"), lax.axis_size("narrow")
    narrow_me = lax.axis_index("narrow")
    wide_me = lax.axis_index("wide")
    seqs = doc_ids.shape[0]
    paired = paired_mesh()
    vshard = table.shape[0]
    count = summed_over(jnp.sum(mlm_valid.astype(jnp.float32)), "wide")
    table_low, layer_low = table.astype(jnp.bfloat16), layer.astype(jnp.bfloat16)
    if paired:
        token_ids, mlm_labels, mlm_valid, doc_ids, mlm_pos = hosted_rows(
            token_ids, mlm_labels, mlm_valid, doc_ids, mlm_pos
        )
        owners = Owners(token_ids.reshape(n_narrow, n_wide * L), vshard)
        picked = packed_rows(owners.slots, table)
        layer_rows, picked = gathered_near(layer_low, picked)
    else:
        layer_rows = lax.all_gather(layer_low, "narrow", axis=0, tiled=True)
    weights = lax.all_gather(layer_rows, "wide", axis=1, tiled=True)
    if paired:

        def looked_up(room):
            rows = sent_around(picked[:, 0:room])
            return taken_rows(owners.behind_slots(room), jnp.concatenate(rows, axis=0))

        layer_rows, picked = together(layer_rows, picked)
        looked = looked_up(owners.room)
        looked = lax.cond(owners.full, lambda: looked_up(owners.count), lambda: looked)
        looked = lax.all_to_all(looked.reshape(n_wide, L, -1), "wide", 0, 0)
        looked = looked.transpose(1, 0, 2).reshape(1, L, D)
        looked, count, doc_ids, mlm_pos = together(looked, count, doc_ids, mlm_pos)
    else:
        local_ids = token_ids - narrow_me * vshard
        inside = (local_ids >= 0) & (local_ids < vshard)
        slots = jnp.where(inside, local_ids, vshard).reshape(-1)
        table_cols = lax.all_gather(table_low, "wide", axis=1, tiled=True)
        picked = jnp.take(table_cols, jnp.clip(local_ids, 0, vshard - 1), axis=0)
        picked = jnp.where(inside[..., None], picked, 0.0)
        looked = lax.psum_scatter(picked, "narrow", scatter_dimension=0, tiled=True)
    looked = looked.astype(jnp.float32)
    even_doc = (doc_ids % 2 == 0)[..., None]
    embedded = looked + small[0:L][None] + jnp.where(even_doc, small[L], small[L + 1])
    embedded = embedded.reshape(seqs * L, D)
    x0 = norm_rows(embedded, small[L + 2], small[L + 3])
    act = x0.astype(jnp.bfloat16)
    if paired:
        table_low, weights, act = together(table_low, weights, act)
        table_cols = lax.all_gather(table_low, "wide", axis=1, tiled=True)
    htwo, kept = layer_forward(embedded, x0, act, doc_ids, small, weights)
    hmask = jnp.take_along_axis(htwo.reshape(seqs, L, D), mlm_pos[..., None], axis=1)
    hmask = hmask.reshape(seqs * MPS, D).astype(jnp.bfloat16)
    if paired:
        slots, hmask = together(owners.slots, hmask)
        packed_ids = owners.packed(slots)
        group_h = gathered_near(hmask)
    else:
        group_h = lax.all_gather(hmask, "narrow", axis=0, tiled=True)
    vocab = narrow_me * vshard + jnp.arange(vshard)
    logits = jnp.where((vocab < VREAL)[None], matmul_nt(group_h, table_cols), -1000000000.0)
    labels = mlm_labels.reshape(-1)
    hit = vocab[None] == labels[:, None]
    top = jnp.max(logits, axis=1)
    total = jnp.sum(jnp.exp(logits - top[:, None]), axis=1)
    target = jnp.sum(jnp.where(hit, logits, 0.0), axis=1)
    if paired:
        stats = gathered_near(jnp.stack([top, total, target])[None])
        top, total, target = stats[0]
        for place in range(1, stats.shape[0]):
            top, total, target = merge_rows((top, total, target), tuple(stats[place]))
    else:
        top, total, target = joined((top, total, target), "narrow", merge_rows)
    lse = top + jnp.log(total)
    flags = mlm_valid.reshape(-1).astype(jnp.float32)
    own = seqs * MPS
    own_loss = lax.dynamic_slice_in_dim(flags * (lse - target), narrow_me * own, own)
    dlogit = (
        (jnp.exp(logits - lse[:, None]) - hit.astype(jnp.float32)) * (flags / count)[:, None]
    ).astype(jnp.bfloat16)
    dhmask = matmul(dlogit, table_cols)
    if paired:
        dhmask = scattered_near(dhmask)
        blocks = group_h.reshape(-1, n_wide, D // n_wide)
        table_head = jnp.einsum("sv,swc->wvc", dlogit, blocks, preferred_element_type=jnp.float32)
        table_head, dhmask = together(table_head.astype(jnp.bfloat16), dhmask)
        table_head = lax.psum_scatter(table_head, "wide", scatter_dimension=0)
    else:
        dhmask = lax.psum_scatter(dhmask, "narrow", scatter_dimension=0, tiled=True)
    dhtwo = (
        jnp.zeros((seqs, L, D), jnp.float32)
        .at[jnp.arange(seqs)[:, None], mlm_pos]
        .add(dhmask.reshape(seqs, MPS, D))
    )
    dembed, vectors, pieces = layer_backward(
        dhtwo.reshape(seqs * L, D), kept, doc_ids, small, weights
    )
    dembed_rows = dembed.reshape(seqs, L, D)
    seg_even = jnp.sum(jnp.where(even_doc, dembed_rows, 0.0), axis=(0, 1))
    seg_odd = jnp.sum(jnp.where(even_doc, 0.0, dembed_rows), axis=(0, 1))
    small_grad = jnp.concatenate(
        [jnp.sum(dembed_rows, axis=0), seg_even[None], seg_odd[None], vectors], axis=0
    )
    mixed = pieces[0]
    if paired:
        cut = dembed.astype(jnp.bfloat16).reshape(L, n_wide, D // n_wide).transpose(1, 0, 2)
        cut = lax.all_to_all(cut, "wide", 0, 0).reshape(n_wide * L, D // n_wide)
        halved = small_halved(small_grad).astype(jnp.bfloat16)
        down, up = pieces[2], pieces[1]
        cut, mixed.away = together(cut, mixed.away)
        cut, halved = mixed.finish(cut, halved)
        placed = put_rows(owners.owner_slots(), cut, n_narrow * owners.count)
        placed = placed.reshape(n_narrow, owners.count, -1)
        wider = jnp.broadcast_to(halved[None], (n_narrow,) + halved.shape)
        near = sent_around(jnp.concatenate([placed[:, 0 : owners.room], wider], axis=1))
        table_grad = added_rows(packed_ids, near, vshard, owners.room)
        table_grad = lax.cond(
            owners.full,
            lambda: added_rows(packed_ids, sent_around(placed), vshard, owners.count),
            lambda: table_grad,
        )
        table_mom, table_upd, table_norms = table_update(
            table_grad, table_head, table, table_m, table_v
        )
        mixed.result, down.result, up.result, table_norms = together(
            mixed.result, down.result, up.result, table_norms
        )
    else:
        mixed.finish()
        group_rows = lax.all_gather(dembed_rows.astype(jnp.bfloat16), "narrow", axis=0, tiled=True)
        table_grad = matmul_tn(dlogit, group_h).at[slots].add(
            group_rows.reshape(-1, D).astype(jnp.float32), mode="drop"
        )
        cut = table_grad.astype(jnp.bfloat16).reshape(vshard, n_wide, D // n_wide)
        table_grad = lax.psum_scatter(cut.transpose(1, 0, 2), "wide", scatter_dimension=0)
        table_grad = table_grad.astype(jnp.float32)
    part_cols = layer.shape[1]
    if paired:
        spans, total, start = [], 0.0, [0, 4 * D, 8 * D]
        for piece, first in zip(pieces[::-1], start[::-1]):
            span, amount = span_of(layer_m, piece.result, worker_err, first)
            spans.insert(0, span)
            total = total + amount
        scale = total / (layer_m.shape[0] * layer_m.shape[1]) + MAG_EPS
        new_worker, sent = pressed(spans, scale, n_wide)
        sent, *near = together(sent, *[part[owners.room :] for part in near])
        small_grad = small_total(near)
        server_in = scattered_sum(sent) / n_wide + server_err
    else:
        worker_grad = jnp.concatenate([piece.result for piece in pieces], axis=1)
        span = BETA * layer_m + (1.0 - BETA) * worker_grad.astype(jnp.float32) + worker_err[0]
        scale = jnp.mean(jnp.abs(span)) + MAG_EPS
        sent = scale * jnp.tanh(span / scale)
        new_worker = (span - sent)[None]
        summed = lax.psum(sent.astype(jnp.bfloat16), "wide").astype(jnp.float32)
        mixed = lax.dynamic_slice_in_dim(summed, wide_me * part_cols, part_cols, 1) / n_wide
        server_in = mixed + server_err
    sscale = jnp.mean(jnp.abs(server_in)) + MAG_EPS
    server_out = sscale * jnp.tanh(server_in / sscale)
    new_server = server_in - server_out
    server_low = server_out.astype(jnp.bfloat16)
    if not paired:
        small_grad = lax.psum(small_grad, ("wide", "narrow"))
        table_mom = BETA * table_m + (1.0 - BETA) * table_grad
        table_upd = table_mom / (jnp.sqrt(table_v) + OPT_EPS) + DECAY * table
        table_norms = (jnp.sum(table * table)[None], jnp.sum(table_upd * table_upd)[None])
    small_mom = BETA * small_m + (1.0 - BETA) * small_grad
    small_upd = small_mom / (jnp.sqrt(small_v) + OPT_EPS) + DECAY * small
    small_norms = (jnp.sum(small * small)[None], jnp.sum(small_upd * small_upd)[None])
    new_m = lax.all_gather(server_low, "wide", axis=1, tiled=True).astype(jnp.float32)
    layer_upd = server_out / (jnp.sqrt(layer_v) + OPT_EPS) + DECAY * layer
    column = wide_me * part_cols + jnp.arange(part_cols)
    which = (
        (column >= 3 * D).astype(jnp.int32)
        + (column >= 4 * D).astype(jnp.int32)
        + (column >= 4 * D + FF).astype(jnp.int32)
    )
    onehot = (which[:, None] == jnp.arange(4)[None]).astype(jnp.float32)
    wsq = jnp.sum(jnp.sum(layer * layer, axis=0)[:, None] * onehot, axis=0)
    usq = jnp.sum(jnp.sum(layer_upd * layer_upd, axis=0)[:, None] * onehot, axis=0)
    parts = jnp.concatenate([wsq, usq, *table_norms, jnp.sum(own_loss)[None]])
    sums = summed_over(summed_over(parts, "wide"), "narrow")
    loss_sum = sums[10]
    wnorm = jnp.sqrt(jnp.concatenate([sums[0:4], sums[8:9], small_norms[0]]))
    unorm = jnp.sqrt(jnp.concatenate([sums[4:8], sums[9:10], small_norms[1]]))
    ratio = wnorm / unorm
    new_layer = layer - RATE * jnp.sum(onehot * ratio[None, 0:4], axis=1)[None] * layer_upd
    new_table = table - RATE * ratio[4] * table_upd
    new_small = small - RATE * ratio[5] * small_upd
    return (
        jnp.stack([loss_sum, count]),
        new_table,
        table_mom,
        new_small,
        small_mom,
        new_layer,
        new_m,
        new_worker,
        new_server,
        jnp.stack([wnorm, unorm]),
    )


def solution(mesh):
    placed = (
        P("wide", None),
        P(("wide", "narrow"), None),
        P(("wide", "narrow"), None),
        P("wide", None),
        P("wide", None),
        P("narrow", "wide"),
        P("narrow", "wide"),
        P("narrow", "wide"),
        P(),
        P(),
        P(),
        P("narrow", "wide"),
        P("narrow", None),
        P("narrow", "wide"),
        P("wide", "narrow", None),
        P("narrow", "wide"),
    )
    return jax.shard_map(
        shards,
        mesh=mesh,
        in_specs=placed,
        out_specs=(
            P(),
            P("narrow", "wide"),
            P("narrow", "wide"),
            P(),
            P(),
            P("narrow", "wide"),
            P("narrow", None),
            P("wide", "narrow", None),
            P("narrow", "wide"),
            P(),
        ),
        check_vma=False,
    )
```

```python
import functools

import jax
import jax.numpy as jnp
from jax import lax
from jax.experimental import pallas as pl
from jax.experimental.pallas import tpu as pltpu
from jax.sharding import PartitionSpec as P

D = 1024
HEADS = 16
HEAD = 64
FF = 4096
VREAL = 30522
L = 512
MPS = 80


LN_EPS = 1e-12
BETA = 0.9
DECAY = 0.01
RATE = 0.25
OPT_EPS = 1e-06
MAG_EPS = 1e-08

FREE = pl.CostEstimate(flops=0, bytes_accessed=0, transcendentals=0)


def joined(value, axis, join):
    pieces = jax.tree.map(lambda part: lax.all_gather(part, axis), value)
    head = jax.tree.map(lambda part: part[0], pieces)
    tail = jax.tree.map(lambda part: part[1:], pieces)
    subtotal, _ = lax.scan(lambda subtotal, slab: (join(subtotal, slab), None), head, tail)
    return subtotal


def norm_rows(x, gain, shift):
    mean = jnp.mean(x, axis=-1, keepdims=True)
    cent = x - mean
    var = jnp.mean(cent * cent, axis=-1, keepdims=True)
    return cent * lax.rsqrt(var + LN_EPS) * gain + shift


def gelu_exact(upper):
    return jax.nn.gelu(upper, approximate=False)


def matmul(left, right):
    return jnp.dot(left, right, preferred_element_type=jnp.float32)


def matmul_tn(left, right):
    return lax.dot_general(
        left, right, (((0,), (0,)), ((), ())), preferred_element_type=jnp.float32
    )


def matmul_nt(left, right):
    return lax.dot_general(
        left, right, (((1,), (1,)), ((), ())), preferred_element_type=jnp.float32
    )


def attend_kernel(q_ref, k_ref, v_ref, key_doc_ref, query_doc_ref, out_ref, lse_ref):
    same = key_doc_ref[...] == query_doc_ref[...]
    lane = lax.broadcasted_iota(jnp.int32, (1, 2 * HEAD), 1)
    outs = []
    for head in range(2):
        mine = lane // HEAD == head
        query = jnp.where(mine, q_ref[...] * 0.125, 0).astype(jnp.bfloat16)
        scores = jnp.where(same, matmul_nt(k_ref[...], query), -1000000000.0)
        top = jnp.max(scores, axis=0, keepdims=True)
        power = jnp.exp(scores - top)
        total = jnp.sum(power, axis=0, keepdims=True)
        lse_ref[0, head : head + 1, :] = top + jnp.log(total)
        prob = (power * (1.0 / total)).astype(jnp.bfloat16)
        outs.append(matmul_tn(prob, v_ref[...]))
    out_ref[...] = jnp.where(lane < HEAD, outs[0], outs[1]).astype(jnp.bfloat16)


def head_pairs(offset):
    return pl.BlockSpec((L, 2 * HEAD), lambda pair: (0, offset * HEADS // 2 + pair))


def attend(qkv, docs):
    return pl.pallas_call(
        attend_kernel,
        grid=(HEADS // 2,),
        in_specs=[
            head_pairs(0),
            head_pairs(1),
            head_pairs(2),
            pl.BlockSpec((L, 1), lambda pair: (0, 0)),
            pl.BlockSpec((1, L), lambda pair: (0, 0)),
        ],
        out_specs=[head_pairs(0), pl.BlockSpec((1, 2, L), lambda pair: (pair, 0, 0))],
        out_shape=[
            jax.ShapeDtypeStruct((L, D), jnp.bfloat16),
            jax.ShapeDtypeStruct((HEADS // 2, 2, L), jnp.float32),
        ],
        compiler_params=pltpu.CompilerParams(vmem_limit_bytes=40 * 2**20),
        cost_estimate=FREE,
        name="attend",
    )(qkv, qkv, qkv, docs.reshape(L, 1), docs.reshape(1, L))


def attend_back_kernel(q_ref, k_ref, v_ref, do_ref, lse_ref, key_doc_ref, query_doc_ref, out_ref):
    pair = pl.program_id(0)
    same = key_doc_ref[...] == query_doc_ref[...]
    lane = lax.broadcasted_iota(jnp.int32, (1, 2 * HEAD), 1)
    both = []
    for head in range(2):
        mine = lane // HEAD == head
        query = jnp.where(mine, q_ref[...] * 0.125, 0).astype(jnp.bfloat16)
        dout = jnp.where(mine, do_ref[...], 0).astype(jnp.bfloat16)
        scores = jnp.where(same, matmul_nt(k_ref[...], query), -1000000000.0)
        prob = jnp.exp(scores - lse_ref[0, head : head + 1, :])
        dvalue = matmul(prob.astype(jnp.bfloat16), dout)
        dprob = matmul_nt(v_ref[...], dout)
        delta = jnp.sum(prob * dprob, axis=0, keepdims=True)
        dscore = (prob * (dprob - delta)).astype(jnp.bfloat16)
        both.append((matmul_tn(dscore, k_ref[...]) * 0.125, matmul(dscore, query), dvalue))
    for part in range(3):
        value = jnp.where(lane < HEAD, both[0][part], both[1][part]).astype(jnp.bfloat16)
        start = pl.multiple_of(part * D + pair * 2 * HEAD, 2 * HEAD)
        out_ref[:, pl.ds(start, 2 * HEAD)] = value


def attend_back(qkv, dout, lse, docs):
    return pl.pallas_call(
        attend_back_kernel,
        grid=(HEADS // 2,),
        in_specs=[
            head_pairs(0),
            head_pairs(1),
            head_pairs(2),
            head_pairs(0),
            pl.BlockSpec((1, 2, L), lambda pair: (pair, 0, 0)),
            pl.BlockSpec((L, 1), lambda pair: (0, 0)),
            pl.BlockSpec((1, L), lambda pair: (0, 0)),
        ],
        out_specs=pl.BlockSpec((L, 3 * D), lambda pair: (0, 0)),
        out_shape=jax.ShapeDtypeStruct((L, 3 * D), jnp.bfloat16),
        compiler_params=pltpu.CompilerParams(vmem_limit_bytes=40 * 2**20),
        cost_estimate=FREE,
        name="attend_back",
    )(qkv, qkv, qkv, dout, lse, docs.reshape(L, 1), docs.reshape(1, L))


def merge_rows(first, second):
    peak = jnp.maximum(first[0], second[0])
    total = first[1] * jnp.exp(first[0] - peak) + second[1] * jnp.exp(second[0] - peak)
    return (peak, total, first[2] + second[2])


def layer_forward(embedded, x0, act, docs, small, weights):
    base = L + 2
    bias = jnp.concatenate([small[base + 6], jnp.zeros((D,), jnp.float32), small[base + 7]])
    qkv = (matmul(act, weights[:, 0 : 3 * D]) + bias).astype(jnp.bfloat16)
    out, lse = attend(qkv, docs)
    rone = x0 + (matmul(out, weights[:, 3 * D : 4 * D]) + small[base + 8])
    hone = norm_rows(rone, small[base + 2], small[base + 3])
    fin = hone.astype(jnp.bfloat16)
    upper = matmul(fin, weights[:, 4 * D : 4 * D + FF]) + small[base + 10 :].reshape(FF)
    gated = gelu_exact(upper).astype(jnp.bfloat16)
    rtwo = hone + (matmul_nt(gated, weights[:, 4 * D + FF :]) + small[base + 9])
    htwo = norm_rows(rtwo, small[base + 4], small[base + 5])
    return (htwo, (embedded, act, qkv, lse, out, rone, fin, upper, gated, rtwo))


def layer_backward(dhtwo, kept, docs, small, weights):
    embedded, act, qkv, lse, out, rone, fin, upper, gated, rtwo = kept
    base = L + 2
    _, pull = jax.vjp(norm_rows, rtwo, small[base + 4], small[base + 5])
    drtwo, dgain_two, dshift_two = pull(dhtwo)
    dffn = drtwo.astype(jnp.bfloat16)
    down = WorkerPiece((dffn, gated))
    dgated = matmul(dffn, weights[:, 4 * D + FF :])
    _, pull = jax.vjp(gelu_exact, upper)
    dupper = pull(dgated)[0].astype(jnp.bfloat16)
    dupper = down.received(dupper)
    dupper = down.across(dupper)
    up = WorkerPiece((fin, dupper))
    dhone = drtwo + matmul_nt(dupper, weights[:, 4 * D : 4 * D + FF])
    _, pull = jax.vjp(norm_rows, rone, small[base + 2], small[base + 3])
    drone, dgain_one, dshift_one = pull(dhone)
    dattn = drone.astype(jnp.bfloat16)
    dout = matmul_nt(dattn, weights[:, 3 * D : 4 * D]).astype(jnp.bfloat16)
    dout = up.received(dout)
    dout = up.across(dout)
    dqkv = attend_back(qkv, dout, lse, docs)
    (dqkv,) = down.crossed(dqkv)
    down.finish()
    mixed = WorkerPiece((act, dqkv), (out, dattn))
    dxzero = drone + matmul_nt(mixed.across(dqkv), weights[:, 0 : 3 * D])
    _, pull = jax.vjp(norm_rows, embedded, small[base], small[base + 1])
    dembed, dgain_emb, dshift_emb = pull(dxzero)
    (dembed,) = up.crossed(dembed)
    up.finish()
    bias_qkv = jnp.sum(dqkv, axis=0, dtype=jnp.float32)
    vectors = jnp.stack(
        [
            dgain_emb,
            dshift_emb,
            dgain_one,
            dshift_one,
            dgain_two,
            dshift_two,
            bias_qkv[0:D],
            bias_qkv[2 * D : 3 * D],
            jnp.sum(dattn, axis=0, dtype=jnp.float32),
            jnp.sum(dffn, axis=0, dtype=jnp.float32),
        ]
    )
    bias_up = jnp.sum(dupper, axis=0, dtype=jnp.float32).reshape(FF // D, D)
    return (dembed, jnp.concatenate([vectors, bias_up], axis=0), (mixed, up, down))


def paired_mesh():
    return lax.axis_size("wide") == 8 and lax.axis_size("narrow") == 4


def together(*values):
    return lax.optimization_barrier(values)


def swap_pairs(size, bit):
    return [(place, place ^ bit) for place in range(size)]


def cycle(size, by):
    return [(place, (place + by) % size) for place in range(size)]


def summed_over(value, axis):
    size = lax.axis_size(axis)
    if size & (size - 1):
        return lax.psum(value, axis)
    bit = 1
    while bit < size:
        value = value + lax.ppermute(value, axis, swap_pairs(size, bit))
        bit *= 2
    return value


def gathered_near(value, beside=None):
    size = lax.axis_size("narrow")
    rows = value.shape[0]
    around = [value]
    for by in range(1, size):
        around.append(lax.ppermute(value, "narrow", cycle(size, size - by)))
    if beside is not None:
        *around, beside = together(*around, beside)
    twice = jnp.concatenate(around + around[:-1], axis=0)
    start = lax.rem(size - lax.axis_index("narrow"), size) * rows
    whole = lax.dynamic_slice_in_dim(twice, start, size * rows, 0)
    return whole if beside is None else (whole, beside)


def scattered_near(value):
    size = lax.axis_size("narrow")
    rows = value.shape[0] // size
    place = lax.axis_index("narrow")
    total = lax.dynamic_slice_in_dim(value, place * rows, rows, 0)
    for by in range(1, size):
        target = lax.rem(place + by, size)
        give = lax.dynamic_slice_in_dim(value, target * rows, rows, 0).astype(jnp.bfloat16)
        take = lax.ppermute(give, "narrow", cycle(size, by))
        total = total + take.astype(jnp.float32)
    return total


def sent_around(blocks):
    size = lax.axis_size("narrow")
    place = lax.axis_index("narrow")

    def block(by):
        return lax.dynamic_index_in_dim(blocks, lax.rem(place + by, size), 0, keepdims=False)

    return [block(0)] + [
        lax.ppermute(block(by), "narrow", cycle(size, by)) for by in range(1, size)
    ]


def block_kernel(steps, place_ref, *refs):
    pairs = len(steps) - 1
    lefts, rights, terms, out_ref = refs[:pairs], refs[pairs : 2 * pairs], refs[2 * pairs : -1], refs[-1]
    step = pl.program_id(0)
    for index in range(pairs):

        @pl.when((step >= steps[index]) & (step < steps[index + 1]))
        def _():
            total = matmul_tn(lefts[index][...], rights[index][...])
            for term_ref in terms:
                total = total + term_ref[...].astype(jnp.float32)
            out_ref[...] = total.astype(jnp.bfloat16)


def gradient_block(pairs, place, terms):
    block = D
    size = D // lax.axis_size("narrow")
    steps = [0]
    for _, right in pairs:
        steps.append(steps[-1] + right.shape[1] // block)
    tokens = pairs[0][0].shape[0]

    def right_of(index):
        low, count = steps[index], steps[index + 1] - steps[index]
        return pl.BlockSpec(
            (tokens, block), lambda step, place: (0, jnp.clip(step - low, 0, count - 1))
        )

    piece = pl.BlockSpec((size, block), lambda step, place: (0, step))
    return pl.pallas_call(
        functools.partial(block_kernel, steps),
        grid_spec=pltpu.PrefetchScalarGridSpec(
            num_scalar_prefetch=1,
            grid=(steps[-1],),
            in_specs=[pl.BlockSpec((tokens, size), lambda step, place: (0, place[0]))] * len(pairs)
            + [right_of(index) for index in range(len(pairs))]
            + [piece] * len(terms),
            out_specs=piece,
        ),
        out_shape=jax.ShapeDtypeStruct((size, steps[-1] * block), jnp.bfloat16),
        compiler_params=pltpu.CompilerParams(vmem_limit_bytes=24 * 2**20),
        cost_estimate=FREE,
        name="gradient_block",
    )(place[None], *[left for left, _ in pairs], *[right for _, right in pairs], *terms)


class WorkerPiece:
    def __init__(self, *pairs):
        self.pairs = pairs
        self.paired = paired_mesh()
        if not self.paired:
            return
        self.core = lax.axis_index("wide") % 2
        self.pair, self.side = lax.axis_index("narrow") // 2, lax.axis_index("narrow") % 2
        cores = swap_pairs(lax.axis_size("wide"), 1)
        self.far = lax.ppermute(self.block(1 - self.core, 1 - self.side), "wide", cores)
        self.near = lax.ppermute(self.block(1 - self.core, self.side), "wide", cores)

    def block(self, core, side, *terms):
        return gradient_block(self.pairs, 2 * core + side, terms)

    def received(self, value):
        if self.paired:
            value, self.far, self.near = together(value, self.far, self.near)
        return value

    def across(self, value):
        if self.paired:
            sides = swap_pairs(lax.axis_size("narrow"), 1)
            away = self.block(self.core, 1 - self.side, self.far)
            away, value = together(away, value)
            self.away = lax.ppermute(away, "narrow", sides)
        return value

    def crossed(self, *values):
        if self.paired:
            *values, self.away = together(*values, self.away)
        return values

    def finish(self, *values):
        if not self.paired:
            blocks = [matmul_tn(left, right).astype(jnp.bfloat16) for left, right in self.pairs]
            grad = jnp.concatenate(blocks, axis=1)
            self.result = lax.psum_scatter(grad, "narrow", scatter_dimension=0, tiled=True)
            return values
        n_wide, n_narrow = lax.axis_size("wide"), lax.axis_size("narrow")
        total = self.block(self.core, self.side, self.near, self.away)
        moves = []
        for wide in range(n_wide):
            for narrow in range(n_narrow):
                if narrow // 2 != wide % 2:
                    target_wide = wide - wide % 2 + narrow // 2
                    target = target_wide * n_narrow + 2 * (wide % 2) + narrow % 2
                    moves.append((wide * n_narrow + narrow, target))
        total, *values = together(total, *values)
        moved = lax.ppermute(total, ("wide", "narrow"), moves)
        self.result = jnp.where(self.pair == self.core, total, moved)
        return values


def hosted_rows(token_ids, mlm_labels, mlm_valid, doc_ids, mlm_pos):
    n_wide, n_narrow = lax.axis_size("wide"), lax.axis_size("narrow")
    packed = jnp.concatenate([token_ids, mlm_labels, mlm_valid], axis=1)[None]
    for bit, place in zip((1, 2, 4), wide_places()):
        other = lax.ppermute(packed, "wide", swap_pairs(n_wide, bit))
        first, second = jnp.where(place == 0, packed, other), jnp.where(place == 0, other, packed)
        packed = jnp.concatenate([first, second], axis=0)
    width = packed.shape[2]
    hosted = packed.reshape(n_wide // 2, 2, 2, 2, width).transpose(1, 2, 0, 3, 4)
    hosted = hosted.reshape(n_narrow, n_wide, width)
    column = lax.dynamic_index_in_dim(hosted, lax.axis_index("wide"), 1, keepdims=False)
    moves = []
    for wide in range(n_wide):
        for row in range(n_narrow):
            target_wide = wide - wide % 2 + row % 2
            target_narrow = 2 * (wide % 2) + row // 2
            moves.append((wide * n_narrow + row, target_wide * n_narrow + target_narrow))
    own = lax.ppermute(jnp.concatenate([doc_ids, mlm_pos], axis=1), ("wide", "narrow"), moves)
    return (
        hosted[:, :, 0:L],
        column[:, L : L + MPS],
        column[:, L + MPS :],
        own[:, 0:L],
        own[:, L:],
    )


STREAMS = 2


class Owners:
    def __init__(self, tokens, vshard):
        size = lax.axis_size("narrow")
        place = lax.axis_index("narrow")
        count = tokens.shape[1]
        self.room = count * 7 // 16
        owner = tokens // vshard
        held = (owner[None] == jnp.arange(size)[:, None, None]).astype(jnp.bfloat16)
        tiles = held.reshape(-1, count // 128, 128)
        order = jnp.arange(128)
        within = jnp.einsum(
            "btl,lm->btm",
            tiles,
            (order[:, None] < order[None]).astype(jnp.bfloat16),
            preferred_element_type=jnp.float32,
        )
        sums = jnp.sum(tiles.astype(jnp.float32), axis=2)
        tile = jnp.arange(count // 128)
        before = jnp.sum(jnp.where(tile[:, None] < tile[None], sums[:, :, None], 0.0), axis=1)
        rank = (within + before[..., None]).reshape(size, size, count) * held.astype(jnp.float32)
        rank = jnp.sum(rank, axis=0).astype(jnp.int32)
        self.full = jnp.max(jnp.sum(sums, axis=1)) > self.room
        self.count, self.vshard = count, vshard
        own = lax.dynamic_index_in_dim(owner, place, 0, keepdims=False)
        self.rank = lax.dynamic_index_in_dim(rank, place, 0, keepdims=False)
        self.behind = lax.rem(place - own + size, size)
        self.slots = jnp.where(owner == place, tokens - place * vshard, vshard)

    def behind_slots(self, room):
        return self.behind * room + jnp.minimum(self.rank, room - 1)


def pack_kernel(ids_ref, table_ref, out_ref, held, *rows):
    step, count, size = pl.program_id(0), out_ref.shape[1], table_ref.shape[0]

    @pl.when(step == 0)
    def _():
        held[0:size, :] = table_ref[...]
        held[size:, :] = jnp.zeros((8, table_ref.shape[1]), jnp.float32)
        for part in rows:
            part[...] = jnp.zeros_like(part)

    base = [(step * len(rows) + index) * count for index in range(len(rows))]

    def some(turn, used):
        used = list(used)
        for by in range(8):
            for index, part in enumerate(rows):
                place = ids_ref[base[index] + turn * 8 + by]
                part[pl.ds(used[index], 1), :] = held[pl.ds(place, 1), :]
                used[index] = used[index] + jnp.where(place < size, 1, 0)
        return tuple(used)

    lax.fori_loop(0, count // 8, some, (0,) * len(rows))
    for index, part in enumerate(rows):
        out_ref[index] = part[0:count, :].astype(out_ref.dtype)


def packed_rows(ids, table):
    size, cols = table.shape
    places, count = ids.shape
    return pl.pallas_call(
        pack_kernel,
        grid_spec=pltpu.PrefetchScalarGridSpec(
            num_scalar_prefetch=1,
            grid=(places // STREAMS,),
            in_specs=[pl.BlockSpec((size, cols), lambda step, ids: (0, 0))],
            out_specs=pl.BlockSpec((STREAMS, count, cols), lambda step, ids: (step, 0, 0)),
            scratch_shapes=[pltpu.VMEM((size + 8, cols), jnp.float32)]
            + [pltpu.VMEM((count + 8, cols), jnp.float32)] * STREAMS,
        ),
        out_shape=jax.ShapeDtypeStruct((places, count, cols), jnp.bfloat16),
        compiler_params=pltpu.CompilerParams(vmem_limit_bytes=40 * 2**20),
        cost_estimate=pl.CostEstimate(flops=0, bytes_accessed=15 * 10**7, transcendentals=0),
        name="pack_rows",
    )(ids.reshape(-1), table)


def take_kernel(ids_ref, table_ref, out_ref, held, rows):
    held[...] = table_ref[...].astype(jnp.float32)

    @pl.loop(0, out_ref.shape[0], step=16)
    def _(first):
        for by in range(16):
            rows[pl.ds(first + by, 1), :] = held[pl.ds(ids_ref[first + by], 1), :]

    out_ref[...] = rows[...].astype(out_ref.dtype)


def taken_rows(ids, table):
    count, cols = ids.shape[0], table.shape[1]
    return pl.pallas_call(
        take_kernel,
        grid_spec=pltpu.PrefetchScalarGridSpec(
            num_scalar_prefetch=1,
            grid=(1,),
            in_specs=[pl.BlockSpec(table.shape, lambda step, ids: (0, 0))],
            out_specs=pl.BlockSpec((count, cols), lambda step, ids: (0, 0)),
            scratch_shapes=[
                pltpu.VMEM(table.shape, jnp.float32),
                pltpu.VMEM((count, cols), jnp.float32),
            ],
        ),
        out_shape=jax.ShapeDtypeStruct((count, cols), table.dtype),
        compiler_params=pltpu.CompilerParams(vmem_limit_bytes=40 * 2**20),
        cost_estimate=FREE,
        name="take_rows",
    )(ids, table)


def add_kernel(ids_ref, values_ref, out_ref, rows, *sums):
    size, length = out_ref.shape[0], rows.shape[1]
    for part in sums:
        part[...] = jnp.zeros_like(part)
    rows[...] = values_ref[:, 0:length, :].astype(jnp.float32)

    @pl.loop(0, length, step=8)
    def _(first):
        for by in range(8):
            for index, part in enumerate(sums):
                place = ids_ref[index * length + first + by]
                part[pl.ds(place, 1), :] += rows[index, pl.ds(first + by, 1), :]

    total = sums[0][0:size, :]
    for part in sums[1:]:
        total = total + part[0:size, :]
    out_ref[...] = total


def added_rows(ids, values, size):
    places, length = ids.shape
    cols = values.shape[2]
    return pl.pallas_call(
        add_kernel,
        grid_spec=pltpu.PrefetchScalarGridSpec(
            num_scalar_prefetch=1,
            grid=(1,),
            in_specs=[pl.BlockSpec(values.shape, lambda step, ids: (0, 0, 0))],
            out_specs=pl.BlockSpec((size, cols), lambda step, ids: (0, 0)),
            scratch_shapes=[pltpu.VMEM((places, length, cols), jnp.float32)]
            + [pltpu.VMEM((size + 8, cols), jnp.float32)] * places,
        ),
        out_shape=jax.ShapeDtypeStruct((size, cols), jnp.float32),
        compiler_params=pltpu.CompilerParams(vmem_limit_bytes=56 * 2**20),
        cost_estimate=FREE,
        name="add_rows",
    )(ids.reshape(-1), values)


def span_kernel(momentum_ref, grad_ref, error_ref, span_ref, sum_ref):
    grad = grad_ref[...].astype(jnp.float32)
    span = BETA * momentum_ref[...] + (1.0 - BETA) * grad + error_ref[0]
    span_ref[...] = span

    @pl.when(pl.program_id(0) == 0)
    def _():
        sum_ref[...] = jnp.zeros_like(sum_ref)

    sum_ref[...] += jnp.sum(jnp.abs(span), axis=0, keepdims=True)


def span_of(momentum, grad, error, start):
    rows, cols = grad.shape
    block = 1024
    first = start // block
    span, sums = pl.pallas_call(
        span_kernel,
        grid=(cols // block,),
        in_specs=[
            pl.BlockSpec((rows, block), lambda step: (0, first + step)),
            pl.BlockSpec((rows, block), lambda step: (0, step)),
            pl.BlockSpec((1, rows, block), lambda step: (0, 0, first + step)),
        ],
        out_specs=[
            pl.BlockSpec((rows, block), lambda step: (0, step)),
            pl.BlockSpec((1, block), lambda step: (0, 0)),
        ],
        out_shape=[
            jax.ShapeDtypeStruct((rows, cols), jnp.float32),
            jax.ShapeDtypeStruct((1, block), jnp.float32),
        ],
        compiler_params=pltpu.CompilerParams(vmem_limit_bytes=60 * 2**20),
        cost_estimate=FREE,
        name="span",
    )(momentum, grad, error)
    return span, jnp.sum(sums)


def press_kernel(steps, scale_ref, *refs):
    *span_refs, error_ref, sent_ref = refs
    step = pl.program_id(0)
    scale = scale_ref[0]
    inverse = scale_ref[1]
    for index, span_ref in enumerate(span_refs):

        @pl.when((step >= steps[index]) & (step < steps[index + 1]))
        def _():
            span = span_ref[...]
            sent = scale * jnp.tanh(span * inverse)
            error_ref[0] = span - sent
            sent_ref[0] = sent.astype(jnp.bfloat16)


def pressed(spans, scale, parts):
    rows = spans[0].shape[0]
    cols = sum(span.shape[1] for span in spans)
    block = 512
    each = cols // parts // block
    steps = [0]
    for span in spans:
        steps.append(steps[-1] + span.shape[1] // block)

    def of(index):
        low, count = steps[index], steps[index + 1] - steps[index]
        return pl.BlockSpec((rows, block), lambda step: (0, jnp.clip(step - low, 0, count - 1)))

    return pl.pallas_call(
        functools.partial(press_kernel, steps),
        grid=(steps[-1],),
        in_specs=[pl.BlockSpec(memory_space=pltpu.SMEM)] + [of(i) for i in range(len(spans))],
        out_specs=[
            pl.BlockSpec((1, rows, block), lambda step: (0, 0, step)),
            pl.BlockSpec((1, rows, block), lambda step: (step // each, 0, step % each)),
        ],
        out_shape=[
            jax.ShapeDtypeStruct((1, rows, cols), jnp.float32),
            jax.ShapeDtypeStruct((parts, rows, cols // parts), jnp.bfloat16),
        ],
        compiler_params=pltpu.CompilerParams(vmem_limit_bytes=60 * 2**20),
        cost_estimate=FREE,
        name="press",
    )(jnp.stack([scale, 1.0 / scale]), *spans)


def update_kernel(grad_ref, head_ref, table_ref, first_ref, second_ref, *out_refs):
    first_out, update_ref, weight_sum, update_sum = out_refs
    grad = grad_ref[...] + head_ref[...].astype(jnp.float32)
    first = BETA * first_ref[...] + (1.0 - BETA) * grad
    table = table_ref[...]
    update = first / (jnp.sqrt(second_ref[...]) + OPT_EPS) + DECAY * table
    first_out[...] = first
    update_ref[...] = update

    @pl.when(pl.program_id(0) == 0)
    def _():
        weight_sum[...] = jnp.zeros_like(weight_sum)
        update_sum[...] = jnp.zeros_like(update_sum)

    weight_sum[...] += jnp.sum(table * table, axis=0, keepdims=True)
    update_sum[...] += jnp.sum(update * update, axis=0, keepdims=True)


def table_update(grad, head, table, first, second):
    size, cols = table.shape
    block = size // 9 if size % 9 == 0 and size // 9 % 16 == 0 else size
    whole = pl.BlockSpec((block, cols), lambda step: (step, 0))
    line = pl.BlockSpec((1, cols), lambda step: (0, 0))
    moment, update, *sums = pl.pallas_call(
        update_kernel,
        grid=(size // block,),
        in_specs=[whole] * 5,
        out_specs=[whole, whole, line, line],
        out_shape=[jax.ShapeDtypeStruct((size, cols), jnp.float32)] * 2
        + [jax.ShapeDtypeStruct((1, cols), jnp.float32)] * 2,
        compiler_params=pltpu.CompilerParams(vmem_limit_bytes=56 * 2**20),
        cost_estimate=FREE,
        name="update",
    )(grad, head, table, first, second)
    return moment, update, tuple(jnp.sum(part)[None] for part in sums)


def wide_places():
    wide_me = lax.axis_index("wide")
    return wide_me % 2, wide_me // 2 % 2, wide_me // 4


def scattered_sum(sent):
    n_wide = lax.axis_size("wide")
    core, x, y = wide_places()

    def send(value, bit):
        return lax.ppermute(value.astype(jnp.bfloat16), "wide", swap_pairs(n_wide, bit))

    def pick(value, index):
        return lax.dynamic_index_in_dim(value, index, 0, keepdims=False)

    rows, cols = sent.shape[1:]
    by_core = sent.reshape(n_wide // 2, 2, rows, cols)
    give = lax.dynamic_index_in_dim(by_core, 1 - core, 1, keepdims=False)
    keep = lax.dynamic_index_in_dim(by_core, core, 1, keepdims=False)
    take = send(give, 1)
    half = rows // 2

    def chip(y_of, x_of, part):
        low, high = part * half, (part + 1) * half
        index = 2 * y_of + x_of
        own, other = pick(keep[:, low:high], index), pick(take[:, low:high], index)
        return own.astype(jnp.float32) + other.astype(jnp.float32)

    upper_far = send(chip(1 - y, 1 - x, 0), 2)
    lower_far = send(chip(1 - y, 1 - x, 1), 4)
    upper_near = send(chip(y, 1 - x, 0), 2)
    lower_near = send(chip(1 - y, x, 1), 4)
    upper_far = send(chip(1 - y, x, 0) + upper_far.astype(jnp.float32), 4)
    lower_far = send(chip(y, 1 - x, 1) + lower_far.astype(jnp.float32), 2)
    own_upper = chip(y, x, 0) + upper_near.astype(jnp.float32) + upper_far.astype(jnp.float32)
    own_lower = chip(y, x, 1) + lower_near.astype(jnp.float32) + lower_far.astype(jnp.float32)
    return jnp.concatenate([own_upper, own_lower], axis=0)


def small_halved(value):
    n_wide = lax.axis_size("wide")
    for bit, place in list(zip((1, 2, 4), wide_places()))[::-1]:
        half = value.shape[1] // 2
        give = lax.dynamic_slice_in_dim(value, (1 - place) * half, half, 1).astype(jnp.bfloat16)
        keep = lax.dynamic_slice_in_dim(value, place * half, half, 1)
        value = keep + lax.ppermute(give, "wide", swap_pairs(n_wide, bit)).astype(jnp.float32)
    return value


def small_update(grad, first, second, weight):
    first = BETA * first + (1.0 - BETA) * grad.astype(jnp.float32)
    return first, first / (jnp.sqrt(second) + OPT_EPS) + DECAY * weight


def shards(
    token_ids,
    doc_ids,
    mlm_pos,
    mlm_labels,
    mlm_valid,
    table,
    table_m,
    table_v,
    small,
    small_m,
    small_v,
    layer,
    layer_m,
    layer_v,
    worker_err,
    server_err,
):
    n_wide, n_narrow = lax.axis_size("wide"), lax.axis_size("narrow")
    narrow_me = lax.axis_index("narrow")
    wide_me = lax.axis_index("wide")
    seqs = doc_ids.shape[0]
    paired = paired_mesh()
    vshard = table.shape[0]
    count = summed_over(jnp.sum(mlm_valid.astype(jnp.float32)), "wide")
    table_low, layer_low = table.astype(jnp.bfloat16), layer.astype(jnp.bfloat16)
    if paired:
        token_ids, mlm_labels, mlm_valid, doc_ids, mlm_pos = hosted_rows(
            token_ids, mlm_labels, mlm_valid, doc_ids, mlm_pos
        )
        owners = Owners(token_ids.reshape(n_narrow, n_wide * L), vshard)
        picked = packed_rows(owners.slots, table)
        layer_rows, picked = gathered_near(layer_low, picked)
    else:
        layer_rows = lax.all_gather(layer_low, "narrow", axis=0, tiled=True)
    weights = lax.all_gather(layer_rows, "wide", axis=1, tiled=True)
    if paired:

        def looked_up(room):
            rows = sent_around(picked[:, 0:room])
            return taken_rows(owners.behind_slots(room), jnp.concatenate(rows, axis=0))

        layer_rows, picked = together(layer_rows, picked)
        looked = looked_up(owners.room)
        looked = lax.cond(owners.full, lambda: looked_up(owners.count), lambda: looked)
        looked = lax.all_to_all(looked.reshape(n_wide, L, -1), "wide", 0, 0)
        looked = looked.transpose(1, 0, 2).reshape(1, L, D)
        looked, count, doc_ids, mlm_pos = together(looked, count, doc_ids, mlm_pos)
    else:
        local_ids = token_ids - narrow_me * vshard
        inside = (local_ids >= 0) & (local_ids < vshard)
        slots = jnp.where(inside, local_ids, vshard).reshape(-1)
        table_cols = lax.all_gather(table_low, "wide", axis=1, tiled=True)
        picked = jnp.take(table_cols, jnp.clip(local_ids, 0, vshard - 1), axis=0)
        picked = jnp.where(inside[..., None], picked, 0.0)
        looked = lax.psum_scatter(picked, "narrow", scatter_dimension=0, tiled=True)
    looked = looked.astype(jnp.float32)
    even_doc = (doc_ids % 2 == 0)[..., None]
    embedded = looked + small[0:L][None] + jnp.where(even_doc, small[L], small[L + 1])
    embedded = embedded.reshape(seqs * L, D)
    x0 = norm_rows(embedded, small[L + 2], small[L + 3])
    act = x0.astype(jnp.bfloat16)
    if paired:
        table_low, weights, act = together(table_low, weights, act)
        table_cols = lax.all_gather(table_low, "wide", axis=1, tiled=True)
    htwo, kept = layer_forward(embedded, x0, act, doc_ids, small, weights)
    hmask = jnp.take_along_axis(htwo.reshape(seqs, L, D), mlm_pos[..., None], axis=1)
    hmask = hmask.reshape(seqs * MPS, D).astype(jnp.bfloat16)
    if paired:
        group_h = gathered_near(hmask)
    else:
        group_h = lax.all_gather(hmask, "narrow", axis=0, tiled=True)
    vocab = narrow_me * vshard + jnp.arange(vshard)
    logits = jnp.where((vocab < VREAL)[None], matmul_nt(group_h, table_cols), -1000000000.0)
    labels = mlm_labels.reshape(-1)
    hit = vocab[None] == labels[:, None]
    top = jnp.max(logits, axis=1)
    total = jnp.sum(jnp.exp(logits - top[:, None]), axis=1)
    target = jnp.sum(jnp.where(hit, logits, 0.0), axis=1)
    if paired:
        stats = gathered_near(jnp.stack([top, total, target])[None])
        top, total, target = stats[0]
        for place in range(1, stats.shape[0]):
            top, total, target = merge_rows((top, total, target), tuple(stats[place]))
    else:
        top, total, target = joined((top, total, target), "narrow", merge_rows)
    lse = top + jnp.log(total)
    flags = mlm_valid.reshape(-1).astype(jnp.float32)
    own = seqs * MPS
    own_loss = lax.dynamic_slice_in_dim(flags * (lse - target), narrow_me * own, own)
    dlogit = (
        (jnp.exp(logits - lse[:, None]) - hit.astype(jnp.float32)) * (flags / count)[:, None]
    ).astype(jnp.bfloat16)
    dhmask = matmul(dlogit, table_cols)
    if paired:
        dhmask = scattered_near(dhmask)
        blocks = group_h.reshape(-1, n_wide, D // n_wide)
        table_head = jnp.einsum("sv,swc->wvc", dlogit, blocks, preferred_element_type=jnp.float32)
        table_head, dhmask = together(table_head.astype(jnp.bfloat16), dhmask)
        table_head = lax.psum_scatter(table_head, "wide", scatter_dimension=0)
    else:
        dhmask = lax.psum_scatter(dhmask, "narrow", scatter_dimension=0, tiled=True)
    dhtwo = (
        jnp.zeros((seqs, L, D), jnp.float32)
        .at[jnp.arange(seqs)[:, None], mlm_pos]
        .add(dhmask.reshape(seqs, MPS, D))
    )
    dembed, vectors, pieces = layer_backward(
        dhtwo.reshape(seqs * L, D), kept, doc_ids, small, weights
    )
    dembed_rows = dembed.reshape(seqs, L, D)
    seg_even = jnp.sum(jnp.where(even_doc, dembed_rows, 0.0), axis=(0, 1))
    seg_odd = jnp.sum(jnp.where(even_doc, 0.0, dembed_rows), axis=(0, 1))
    small_grad = jnp.concatenate(
        [jnp.sum(dembed_rows, axis=0), seg_even[None], seg_odd[None], vectors], axis=0
    )
    mixed = pieces[0]
    if paired:
        cut = dembed.astype(jnp.bfloat16).reshape(L, n_wide, D // n_wide).transpose(1, 0, 2)
        cut = lax.all_to_all(cut, "wide", 0, 0).reshape(n_wide * L, D // n_wide)
        halved = small_halved(small_grad).astype(jnp.bfloat16)
        down, up = pieces[2], pieces[1]
        cut, mixed.away, halved, down.result, up.result, table_head = together(
            cut, mixed.away, halved, down.result, up.result, table_head
        )
        mixed.finish()
        cut, mixed.result = together(jnp.concatenate([cut, halved]), mixed.result)
        group_rows = lax.all_gather(cut, "narrow", axis=0)
    else:
        mixed.finish()
        group_rows = lax.all_gather(dembed_rows.astype(jnp.bfloat16), "narrow", axis=0, tiled=True)
        table_grad = matmul_tn(dlogit, group_h).at[slots].add(
            group_rows.reshape(-1, D).astype(jnp.float32), mode="drop"
        )
        cut = table_grad.astype(jnp.bfloat16).reshape(vshard, n_wide, D // n_wide)
        table_grad = lax.psum_scatter(cut.transpose(1, 0, 2), "wide", scatter_dimension=0)
        table_grad = table_grad.astype(jnp.float32)
    part_cols = layer.shape[1]
    if paired:
        spans, total, start = [], 0.0, [0, 4 * D, 8 * D]
        for piece, first in zip(pieces[::-1], start[::-1]):
            span, amount = span_of(layer_m, piece.result, worker_err, first)
            spans.insert(0, span)
            total = total + amount
        scale = total / (layer_m.shape[0] * layer_m.shape[1]) + MAG_EPS
        new_worker, sent = pressed(spans, scale, n_wide)
        server_in = scattered_sum(sent) / n_wide + server_err
    else:
        worker_grad = jnp.concatenate([piece.result for piece in pieces], axis=1)
        span = BETA * layer_m + (1.0 - BETA) * worker_grad.astype(jnp.float32) + worker_err[0]
        scale = jnp.mean(jnp.abs(span)) + MAG_EPS
        sent = scale * jnp.tanh(span / scale)
        new_worker = (span - sent)[None]
        summed = lax.psum(sent.astype(jnp.bfloat16), "wide").astype(jnp.float32)
        mixed = lax.dynamic_slice_in_dim(summed, wide_me * part_cols, part_cols, 1) / n_wide
        server_in = mixed + server_err
    sscale = jnp.mean(jnp.abs(server_in)) + MAG_EPS
    server_out = sscale * jnp.tanh(server_in / sscale)
    new_server = server_in - server_out
    server_low = server_out.astype(jnp.bfloat16)
    if paired:
        server_low, group_rows = together(server_low, group_rows)
        table_grad = added_rows(owners.slots, group_rows, vshard)
        table_mom, table_upd, table_norms = table_update(
            table_grad, table_head, table, table_m, table_v
        )
        eighth = D // n_wide
        small_grad = jnp.sum(group_rows[:, n_wide * L :].astype(jnp.float32), axis=0)
        small_grad = small_grad.astype(jnp.bfloat16)

        def own(value):
            return lax.dynamic_slice_in_dim(value, wide_me * eighth, eighth, 1)

        _, own_upd = small_update(small_grad, own(small_m), own(small_v), own(small))
        small_norm = jnp.where(narrow_me == 0, jnp.sum(own_upd * own_upd), 0.0)
    else:
        small_grad = lax.psum(small_grad, ("wide", "narrow"))
        table_mom = BETA * table_m + (1.0 - BETA) * table_grad
        table_upd = table_mom / (jnp.sqrt(table_v) + OPT_EPS) + DECAY * table
        table_norms = (jnp.sum(table * table)[None], jnp.sum(table_upd * table_upd)[None])
    new_m = lax.all_gather(server_low, "wide", axis=1, tiled=True).astype(jnp.float32)
    if paired:
        small_grad = lax.all_gather(small_grad, "wide", axis=1, tiled=True)
    small_mom, small_upd = small_update(small_grad, small_m, small_v, small)
    if not paired:
        small_norm = jnp.where((wide_me == 0) & (narrow_me == 0), jnp.sum(small_upd * small_upd), 0.0)
    layer_upd = server_out / (jnp.sqrt(layer_v) + OPT_EPS) + DECAY * layer
    column = wide_me * part_cols + jnp.arange(part_cols)
    which = (
        (column >= 3 * D).astype(jnp.int32)
        + (column >= 4 * D).astype(jnp.int32)
        + (column >= 4 * D + FF).astype(jnp.int32)
    )
    onehot = (which[:, None] == jnp.arange(4)[None]).astype(jnp.float32)
    wsq = jnp.sum(jnp.sum(layer * layer, axis=0)[:, None] * onehot, axis=0)
    usq = jnp.sum(jnp.sum(layer_upd * layer_upd, axis=0)[:, None] * onehot, axis=0)
    parts = jnp.concatenate([wsq, usq, *table_norms, jnp.sum(own_loss)[None], small_norm[None]])
    sums = summed_over(summed_over(parts, "wide"), "narrow")
    loss_sum = sums[10]
    wnorm = jnp.sqrt(jnp.concatenate([sums[0:4], sums[8:9], jnp.sum(small * small)[None]]))
    unorm = jnp.sqrt(jnp.concatenate([sums[4:8], sums[9:10], sums[11:12]]))
    ratio = wnorm / unorm
    new_layer = layer - RATE * jnp.sum(onehot * ratio[None, 0:4], axis=1)[None] * layer_upd
    new_table = table - RATE * ratio[4] * table_upd
    new_small = small - RATE * ratio[5] * small_upd
    return (
        jnp.stack([loss_sum, count]),
        new_table,
        table_mom,
        new_small,
        small_mom,
        new_layer,
        new_m,
        new_worker,
        new_server,
        jnp.stack([wnorm, unorm]),
    )


def solution(mesh):
    placed = (
        P("wide", None),
        P(("wide", "narrow"), None),
        P(("wide", "narrow"), None),
        P("wide", None),
        P("wide", None),
        P("narrow", "wide"),
        P("narrow", "wide"),
        P("narrow", "wide"),
        P(),
        P(),
        P(),
        P("narrow", "wide"),
        P("narrow", None),
        P("narrow", "wide"),
        P("wide", "narrow", None),
        P("narrow", "wide"),
    )
    return jax.shard_map(
        shards,
        mesh=mesh,
        in_specs=placed,
        out_specs=(
            P(),
            P("narrow", "wide"),
            P("narrow", "wide"),
            P(),
            P(),
            P("narrow", "wide"),
            P("narrow", None),
            P("wide", "narrow", None),
            P("narrow", "wide"),
            P(),
        ),
        check_vma=False,
    )
```

```python
import functools

import jax
import jax.numpy as jnp
from jax import lax
from jax.experimental import pallas as pl
from jax.experimental.pallas import tpu as pltpu
from jax.sharding import PartitionSpec as P

D = 1024
HEADS = 16
HEAD = 64
FF = 4096
VREAL = 30522
L = 512
MPS = 80


LN_EPS = 1e-12
BETA = 0.9
DECAY = 0.01
RATE = 0.25
OPT_EPS = 1e-06
MAG_EPS = 1e-08

FREE = pl.CostEstimate(flops=0, bytes_accessed=0, transcendentals=0)


def joined(value, axis, join):
    pieces = jax.tree.map(lambda part: lax.all_gather(part, axis), value)
    head = jax.tree.map(lambda part: part[0], pieces)
    tail = jax.tree.map(lambda part: part[1:], pieces)
    subtotal, _ = lax.scan(lambda subtotal, slab: (join(subtotal, slab), None), head, tail)
    return subtotal


def norm_rows(x, gain, shift):
    mean = jnp.mean(x, axis=-1, keepdims=True)
    cent = x - mean
    var = jnp.mean(cent * cent, axis=-1, keepdims=True)
    return cent * lax.rsqrt(var + LN_EPS) * gain + shift


def gelu_exact(upper):
    return jax.nn.gelu(upper, approximate=False)


def matmul(left, right):
    return jnp.dot(left, right, preferred_element_type=jnp.float32)


def matmul_tn(left, right):
    return lax.dot_general(
        left, right, (((0,), (0,)), ((), ())), preferred_element_type=jnp.float32
    )


def matmul_nt(left, right):
    return lax.dot_general(
        left, right, (((1,), (1,)), ((), ())), preferred_element_type=jnp.float32
    )


def attend_kernel(q_ref, k_ref, v_ref, key_doc_ref, query_doc_ref, out_ref, lse_ref):
    same = key_doc_ref[...] == query_doc_ref[...]
    lane = lax.broadcasted_iota(jnp.int32, (1, 2 * HEAD), 1)
    outs = []
    for head in range(2):
        mine = lane // HEAD == head
        query = jnp.where(mine, q_ref[...] * 0.125, 0).astype(jnp.bfloat16)
        scores = jnp.where(same, matmul_nt(k_ref[...], query), -1000000000.0)
        top = jnp.max(scores, axis=0, keepdims=True)
        power = jnp.exp(scores - top)
        total = jnp.sum(power, axis=0, keepdims=True)
        lse_ref[0, head : head + 1, :] = top + jnp.log(total)
        prob = (power * (1.0 / total)).astype(jnp.bfloat16)
        outs.append(matmul_tn(prob, v_ref[...]))
    out_ref[...] = jnp.where(lane < HEAD, outs[0], outs[1]).astype(jnp.bfloat16)


def head_pairs(offset):
    return pl.BlockSpec((L, 2 * HEAD), lambda pair: (0, offset * HEADS // 2 + pair))


def attend(qkv, docs):
    return pl.pallas_call(
        attend_kernel,
        grid=(HEADS // 2,),
        in_specs=[
            head_pairs(0),
            head_pairs(1),
            head_pairs(2),
            pl.BlockSpec((L, 1), lambda pair: (0, 0)),
            pl.BlockSpec((1, L), lambda pair: (0, 0)),
        ],
        out_specs=[head_pairs(0), pl.BlockSpec((1, 2, L), lambda pair: (pair, 0, 0))],
        out_shape=[
            jax.ShapeDtypeStruct((L, D), jnp.bfloat16),
            jax.ShapeDtypeStruct((HEADS // 2, 2, L), jnp.float32),
        ],
        compiler_params=pltpu.CompilerParams(vmem_limit_bytes=40 * 2**20),
        cost_estimate=FREE,
        name="attend",
    )(qkv, qkv, qkv, docs.reshape(L, 1), docs.reshape(1, L))


def attend_back_kernel(q_ref, k_ref, v_ref, do_ref, lse_ref, key_doc_ref, query_doc_ref, out_ref):
    pair = pl.program_id(0)
    same = key_doc_ref[...] == query_doc_ref[...]
    lane = lax.broadcasted_iota(jnp.int32, (1, 2 * HEAD), 1)
    both = []
    for head in range(2):
        mine = lane // HEAD == head
        query = jnp.where(mine, q_ref[...] * 0.125, 0).astype(jnp.bfloat16)
        dout = jnp.where(mine, do_ref[...], 0).astype(jnp.bfloat16)
        scores = jnp.where(same, matmul_nt(k_ref[...], query), -1000000000.0)
        prob = jnp.exp(scores - lse_ref[0, head : head + 1, :])
        dvalue = matmul(prob.astype(jnp.bfloat16), dout)
        dprob = matmul_nt(v_ref[...], dout)
        delta = jnp.sum(prob * dprob, axis=0, keepdims=True)
        dscore = (prob * (dprob - delta)).astype(jnp.bfloat16)
        both.append((matmul_tn(dscore, k_ref[...]) * 0.125, matmul(dscore, query), dvalue))
    for part in range(3):
        value = jnp.where(lane < HEAD, both[0][part], both[1][part]).astype(jnp.bfloat16)
        start = pl.multiple_of(part * D + pair * 2 * HEAD, 2 * HEAD)
        out_ref[:, pl.ds(start, 2 * HEAD)] = value


def attend_back(qkv, dout, lse, docs):
    return pl.pallas_call(
        attend_back_kernel,
        grid=(HEADS // 2,),
        in_specs=[
            head_pairs(0),
            head_pairs(1),
            head_pairs(2),
            head_pairs(0),
            pl.BlockSpec((1, 2, L), lambda pair: (pair, 0, 0)),
            pl.BlockSpec((L, 1), lambda pair: (0, 0)),
            pl.BlockSpec((1, L), lambda pair: (0, 0)),
        ],
        out_specs=pl.BlockSpec((L, 3 * D), lambda pair: (0, 0)),
        out_shape=jax.ShapeDtypeStruct((L, 3 * D), jnp.bfloat16),
        compiler_params=pltpu.CompilerParams(vmem_limit_bytes=40 * 2**20),
        cost_estimate=FREE,
        name="attend_back",
    )(qkv, qkv, qkv, dout, lse, docs.reshape(L, 1), docs.reshape(1, L))


def merge_rows(first, second):
    peak = jnp.maximum(first[0], second[0])
    total = first[1] * jnp.exp(first[0] - peak) + second[1] * jnp.exp(second[0] - peak)
    return (peak, total, first[2] + second[2])


def embed_back_kernel(dqkv_ref, weight_ref, drone_ref, embedded_ref, gain_ref, even_ref, *refs):
    dembed_ref, rows_ref, sums_ref, total = refs
    step = pl.program_id(0)
    dqkv = dqkv_ref[...]
    part = matmul_nt(dqkv, weight_ref[...])
    sums_ref[...] = jnp.sum(dqkv.astype(jnp.float32), axis=0, keepdims=True)

    @pl.when(step == 0)
    def _():
        total[...] = drone_ref[...] + part

    @pl.when(step > 0)
    def _():
        total[...] += part

    @pl.when(step == pl.num_programs(0) - 1)
    def _():
        grad = total[...]
        embedded = embedded_ref[...]
        cent = embedded - jnp.mean(embedded, axis=1, keepdims=True)
        scale = lax.rsqrt(jnp.mean(cent * cent, axis=1, keepdims=True) + LN_EPS)
        normed = cent * scale
        inner = grad * gain_ref[...]
        inner_mean = jnp.mean(inner, axis=1, keepdims=True)
        along = jnp.mean(inner * normed, axis=1, keepdims=True)
        dembed = scale * (inner - inner_mean - normed * along)
        dembed_ref[...] = dembed
        even = even_ref[...]
        rows_ref[0:1, :] = jnp.sum(grad * normed, axis=0, keepdims=True)
        rows_ref[1:2, :] = jnp.sum(grad, axis=0, keepdims=True)
        rows_ref[2:3, :] = jnp.sum(dembed * even, axis=0, keepdims=True)
        rows_ref[3:4, :] = jnp.sum(dembed * (1.0 - even), axis=0, keepdims=True)
        rows_ref[4:8, :] = jnp.zeros((4, D), jnp.float32)


def embed_back(dqkv, weights, drone, embedded, gain, even):
    tokens = dqkv.shape[0]
    whole = pl.BlockSpec((tokens, D), lambda step: (0, 0))
    return pl.pallas_call(
        embed_back_kernel,
        grid=(3,),
        in_specs=[
            pl.BlockSpec((tokens, D), lambda step: (0, step)),
            pl.BlockSpec((D, D), lambda step: (0, step)),
            whole,
            whole,
            pl.BlockSpec((1, D), lambda step: (0, 0)),
            pl.BlockSpec((tokens, 1), lambda step: (0, 0)),
        ],
        out_specs=[
            whole,
            pl.BlockSpec((8, D), lambda step: (0, 0)),
            pl.BlockSpec((1, D), lambda step: (0, step)),
        ],
        out_shape=[
            jax.ShapeDtypeStruct((tokens, D), jnp.float32),
            jax.ShapeDtypeStruct((8, D), jnp.float32),
            jax.ShapeDtypeStruct((1, 3 * D), jnp.float32),
        ],
        scratch_shapes=[pltpu.VMEM((tokens, D), jnp.float32)],
        compiler_params=pltpu.CompilerParams(vmem_limit_bytes=40 * 2**20),
        cost_estimate=FREE,
        name="embed_back",
    )(dqkv, weights, drone, embedded, gain[None], even)


def layer_forward(embedded, x0, act, docs, small, weights):
    base = L + 2
    bias = jnp.concatenate([small[base + 6], jnp.zeros((D,), jnp.float32), small[base + 7]])
    qkv = (matmul(act, weights[:, 0 : 3 * D]) + bias).astype(jnp.bfloat16)
    out, lse = attend(qkv, docs)
    rone = x0 + (matmul(out, weights[:, 3 * D : 4 * D]) + small[base + 8])
    hone = norm_rows(rone, small[base + 2], small[base + 3])
    fin = hone.astype(jnp.bfloat16)
    upper = matmul(fin, weights[:, 4 * D : 4 * D + FF]) + small[base + 10 :].reshape(FF)
    gated = gelu_exact(upper).astype(jnp.bfloat16)
    rtwo = hone + (matmul_nt(gated, weights[:, 4 * D + FF :]) + small[base + 9])
    htwo = norm_rows(rtwo, small[base + 4], small[base + 5])
    return (htwo, (embedded, act, qkv, lse, out, rone, fin, upper, gated, rtwo))


def layer_backward(dhtwo, kept, docs, small, weights):
    embedded, act, qkv, lse, out, rone, fin, upper, gated, rtwo = kept
    base = L + 2
    _, pull = jax.vjp(norm_rows, rtwo, small[base + 4], small[base + 5])
    drtwo, dgain_two, dshift_two = pull(dhtwo)
    dffn = drtwo.astype(jnp.bfloat16)
    down = WorkerPiece((dffn, gated))
    dgated = matmul(dffn, weights[:, 4 * D + FF :])
    _, pull = jax.vjp(gelu_exact, upper)
    dupper = pull(dgated)[0].astype(jnp.bfloat16)
    dupper = down.received(dupper)
    dupper = down.across(dupper)
    up = WorkerPiece((fin, dupper))
    dhone = drtwo + matmul_nt(dupper, weights[:, 4 * D : 4 * D + FF])
    _, pull = jax.vjp(norm_rows, rone, small[base + 2], small[base + 3])
    drone, dgain_one, dshift_one = pull(dhone)
    dattn = drone.astype(jnp.bfloat16)
    dout = matmul_nt(dattn, weights[:, 3 * D : 4 * D]).astype(jnp.bfloat16)
    dout = up.received(dout)
    dout = up.across(dout)
    dqkv = attend_back(qkv, dout, lse, docs)
    (dqkv,) = down.crossed(dqkv)
    down.finish()
    mixed = WorkerPiece((act, dqkv), (out, dattn))
    even = (docs.reshape(L, 1) % 2 == 0).astype(jnp.float32)
    dembed, embed_rows, bias_qkv = embed_back(
        mixed.across(dqkv), weights, drone, embedded, small[base], even
    )
    (dembed,) = up.crossed(dembed)
    up.finish()
    vectors = jnp.stack(
        [
            embed_rows[0],
            embed_rows[1],
            dgain_one,
            dshift_one,
            dgain_two,
            dshift_two,
            bias_qkv[0, 0:D],
            bias_qkv[0, 2 * D : 3 * D],
            jnp.sum(dattn, axis=0, dtype=jnp.float32),
            jnp.sum(dffn, axis=0, dtype=jnp.float32),
        ]
    )
    bias_up = jnp.sum(dupper, axis=0, dtype=jnp.float32).reshape(FF // D, D)
    vectors = jnp.concatenate([embed_rows[2:4], vectors, bias_up], axis=0)
    return (dembed, vectors, (mixed, up, down))


def paired_mesh():
    return lax.axis_size("wide") == 8 and lax.axis_size("narrow") == 4


def together(*values):
    return lax.optimization_barrier(values)


def swap_pairs(size, bit):
    return [(place, place ^ bit) for place in range(size)]


def cycle(size, by):
    return [(place, (place + by) % size) for place in range(size)]


def summed_over(value, axis):
    size = lax.axis_size(axis)
    if size & (size - 1):
        return lax.psum(value, axis)
    bit = 1
    while bit < size:
        value = value + lax.ppermute(value, axis, swap_pairs(size, bit))
        bit *= 2
    return value


def gathered_near(value, beside=None):
    size = lax.axis_size("narrow")
    rows = value.shape[0]
    around = [value]
    for by in range(1, size):
        around.append(lax.ppermute(value, "narrow", cycle(size, size - by)))
    if beside is not None:
        *around, beside = together(*around, beside)
    twice = jnp.concatenate(around + around[:-1], axis=0)
    start = lax.rem(size - lax.axis_index("narrow"), size) * rows
    whole = lax.dynamic_slice_in_dim(twice, start, size * rows, 0)
    return whole if beside is None else (whole, beside)


def scattered_near(value):
    size = lax.axis_size("narrow")
    rows = value.shape[0] // size
    place = lax.axis_index("narrow")
    total = lax.dynamic_slice_in_dim(value, place * rows, rows, 0)
    for by in range(1, size):
        target = lax.rem(place + by, size)
        give = lax.dynamic_slice_in_dim(value, target * rows, rows, 0).astype(jnp.bfloat16)
        take = lax.ppermute(give, "narrow", cycle(size, by))
        total = total + take.astype(jnp.float32)
    return total


def sent_around(blocks):
    size = lax.axis_size("narrow")
    place = lax.axis_index("narrow")

    def block(by):
        return lax.dynamic_index_in_dim(blocks, lax.rem(place + by, size), 0, keepdims=False)

    return [block(0)] + [
        lax.ppermute(block(by), "narrow", cycle(size, by)) for by in range(1, size)
    ]


def block_kernel(steps, place_ref, *refs):
    pairs = len(steps) - 1
    lefts, rights, terms, out_ref = refs[:pairs], refs[pairs : 2 * pairs], refs[2 * pairs : -1], refs[-1]
    step = pl.program_id(0)
    for index in range(pairs):

        @pl.when((step >= steps[index]) & (step < steps[index + 1]))
        def _():
            total = matmul_tn(lefts[index][...], rights[index][...])
            for term_ref in terms:
                total = total + term_ref[...].astype(jnp.float32)
            out_ref[...] = total.astype(jnp.bfloat16)


def gradient_block(pairs, place, terms):
    block = D
    size = D // lax.axis_size("narrow")
    steps = [0]
    for _, right in pairs:
        steps.append(steps[-1] + right.shape[1] // block)
    tokens = pairs[0][0].shape[0]

    def right_of(index):
        low, count = steps[index], steps[index + 1] - steps[index]
        return pl.BlockSpec(
            (tokens, block), lambda step, place: (0, jnp.clip(step - low, 0, count - 1))
        )

    piece = pl.BlockSpec((size, block), lambda step, place: (0, step))
    return pl.pallas_call(
        functools.partial(block_kernel, steps),
        grid_spec=pltpu.PrefetchScalarGridSpec(
            num_scalar_prefetch=1,
            grid=(steps[-1],),
            in_specs=[pl.BlockSpec((tokens, size), lambda step, place: (0, place[0]))] * len(pairs)
            + [right_of(index) for index in range(len(pairs))]
            + [piece] * len(terms),
            out_specs=piece,
        ),
        out_shape=jax.ShapeDtypeStruct((size, steps[-1] * block), jnp.bfloat16),
        compiler_params=pltpu.CompilerParams(vmem_limit_bytes=24 * 2**20),
        cost_estimate=FREE,
        name="gradient_block",
    )(place[None], *[left for left, _ in pairs], *[right for _, right in pairs], *terms)


class WorkerPiece:
    def __init__(self, *pairs):
        self.pairs = pairs
        self.paired = paired_mesh()
        if not self.paired:
            return
        self.core = lax.axis_index("wide") % 2
        self.pair, self.side = lax.axis_index("narrow") // 2, lax.axis_index("narrow") % 2
        cores = swap_pairs(lax.axis_size("wide"), 1)
        self.far = lax.ppermute(self.block(1 - self.core, 1 - self.side), "wide", cores)
        self.near = lax.ppermute(self.block(1 - self.core, self.side), "wide", cores)

    def block(self, core, side, *terms):
        return gradient_block(self.pairs, 2 * core + side, terms)

    def received(self, value):
        if self.paired:
            value, self.far, self.near = together(value, self.far, self.near)
        return value

    def across(self, value):
        if self.paired:
            sides = swap_pairs(lax.axis_size("narrow"), 1)
            away = self.block(self.core, 1 - self.side, self.far)
            away, value = together(away, value)
            self.away = lax.ppermute(away, "narrow", sides)
        return value

    def crossed(self, *values):
        if self.paired:
            *values, self.away = together(*values, self.away)
        return values

    def finish(self, *values):
        if not self.paired:
            blocks = [matmul_tn(left, right).astype(jnp.bfloat16) for left, right in self.pairs]
            grad = jnp.concatenate(blocks, axis=1)
            self.result = lax.psum_scatter(grad, "narrow", scatter_dimension=0, tiled=True)
            return values
        n_wide, n_narrow = lax.axis_size("wide"), lax.axis_size("narrow")
        total = self.block(self.core, self.side, self.near, self.away)
        moves = []
        for wide in range(n_wide):
            for narrow in range(n_narrow):
                if narrow // 2 != wide % 2:
                    target_wide = wide - wide % 2 + narrow // 2
                    target = target_wide * n_narrow + 2 * (wide % 2) + narrow % 2
                    moves.append((wide * n_narrow + narrow, target))
        total, *values = together(total, *values)
        moved = lax.ppermute(total, ("wide", "narrow"), moves)
        self.result = jnp.where(self.pair == self.core, total, moved)
        return values


def hosted_rows(token_ids, mlm_labels, mlm_valid, doc_ids, mlm_pos):
    n_wide, n_narrow = lax.axis_size("wide"), lax.axis_size("narrow")
    packed = jnp.concatenate([token_ids, mlm_labels, mlm_valid], axis=1)[None]
    for bit, place in zip((1, 2, 4), wide_places()):
        other = lax.ppermute(packed, "wide", swap_pairs(n_wide, bit))
        first, second = jnp.where(place == 0, packed, other), jnp.where(place == 0, other, packed)
        packed = jnp.concatenate([first, second], axis=0)
    width = packed.shape[2]
    hosted = packed.reshape(n_wide // 2, 2, 2, 2, width).transpose(1, 2, 0, 3, 4)
    hosted = hosted.reshape(n_narrow, n_wide, width)
    column = lax.dynamic_index_in_dim(hosted, lax.axis_index("wide"), 1, keepdims=False)
    moves = []
    for wide in range(n_wide):
        for row in range(n_narrow):
            target_wide = wide - wide % 2 + row % 2
            target_narrow = 2 * (wide % 2) + row // 2
            moves.append((wide * n_narrow + row, target_wide * n_narrow + target_narrow))
    own = lax.ppermute(jnp.concatenate([doc_ids, mlm_pos], axis=1), ("wide", "narrow"), moves)
    return (
        hosted[:, :, 0:L],
        column[:, L : L + MPS],
        column[:, L + MPS :],
        own[:, 0:L],
        own[:, L:],
    )


STREAMS = 2


class Owners:
    def __init__(self, tokens, vshard):
        size = lax.axis_size("narrow")
        place = lax.axis_index("narrow")
        count = tokens.shape[1]
        self.room = count * 7 // 16
        owner = tokens // vshard
        held = (owner[None] == jnp.arange(size)[:, None, None]).astype(jnp.bfloat16)
        tiles = held.reshape(-1, count // 128, 128)
        order = jnp.arange(128)
        within = jnp.einsum(
            "btl,lm->btm",
            tiles,
            (order[:, None] < order[None]).astype(jnp.bfloat16),
            preferred_element_type=jnp.float32,
        )
        sums = jnp.sum(tiles.astype(jnp.float32), axis=2)
        tile = jnp.arange(count // 128)
        before = jnp.sum(jnp.where(tile[:, None] < tile[None], sums[:, :, None], 0.0), axis=1)
        rank = (within + before[..., None]).reshape(size, size, count) * held.astype(jnp.float32)
        rank = jnp.sum(rank, axis=0).astype(jnp.int32)
        self.full = jnp.max(jnp.sum(sums, axis=1)) > self.room
        self.count, self.vshard = count, vshard
        own = lax.dynamic_index_in_dim(owner, place, 0, keepdims=False)
        self.rank = lax.dynamic_index_in_dim(rank, place, 0, keepdims=False)
        self.behind = lax.rem(place - own + size, size)
        self.slots = jnp.where(owner == place, tokens - place * vshard, vshard)

    def behind_slots(self, room):
        return self.behind * room + jnp.minimum(self.rank, room - 1)


def pack_kernel(ids_ref, table_ref, out_ref, held, *rows):
    step, count, size = pl.program_id(0), out_ref.shape[1], table_ref.shape[0]

    @pl.when(step == 0)
    def _():
        held[0:size, :] = table_ref[...]
        held[size:, :] = jnp.zeros((8, table_ref.shape[1]), jnp.float32)
        for part in rows:
            part[...] = jnp.zeros_like(part)

    base = [(step * len(rows) + index) * count for index in range(len(rows))]

    def some(turn, used):
        used = list(used)
        for by in range(8):
            for index, part in enumerate(rows):
                place = ids_ref[base[index] + turn * 8 + by]
                part[pl.ds(used[index], 1), :] = held[pl.ds(place, 1), :]
                used[index] = used[index] + jnp.where(place < size, 1, 0)
        return tuple(used)

    lax.fori_loop(0, count // 8, some, (0,) * len(rows))
    for index, part in enumerate(rows):
        out_ref[index] = part[0:count, :].astype(out_ref.dtype)


def packed_rows(ids, table):
    size, cols = table.shape
    places, count = ids.shape
    return pl.pallas_call(
        pack_kernel,
        grid_spec=pltpu.PrefetchScalarGridSpec(
            num_scalar_prefetch=1,
            grid=(places // STREAMS,),
            in_specs=[pl.BlockSpec((size, cols), lambda step, ids: (0, 0))],
            out_specs=pl.BlockSpec((STREAMS, count, cols), lambda step, ids: (step, 0, 0)),
            scratch_shapes=[pltpu.VMEM((size + 8, cols), jnp.float32)]
            + [pltpu.VMEM((count + 8, cols), jnp.float32)] * STREAMS,
        ),
        out_shape=jax.ShapeDtypeStruct((places, count, cols), jnp.bfloat16),
        compiler_params=pltpu.CompilerParams(vmem_limit_bytes=40 * 2**20),
        cost_estimate=pl.CostEstimate(flops=0, bytes_accessed=15 * 10**7, transcendentals=0),
        name="pack_rows",
    )(ids.reshape(-1), table)


def take_kernel(ids_ref, table_ref, out_ref, held, rows):
    held[...] = table_ref[...].astype(jnp.float32)

    @pl.loop(0, out_ref.shape[0], step=16)
    def _(first):
        for by in range(16):
            rows[pl.ds(first + by, 1), :] = held[pl.ds(ids_ref[first + by], 1), :]

    out_ref[...] = rows[...].astype(out_ref.dtype)


def taken_rows(ids, table):
    count, cols = ids.shape[0], table.shape[1]
    return pl.pallas_call(
        take_kernel,
        grid_spec=pltpu.PrefetchScalarGridSpec(
            num_scalar_prefetch=1,
            grid=(1,),
            in_specs=[pl.BlockSpec(table.shape, lambda step, ids: (0, 0))],
            out_specs=pl.BlockSpec((count, cols), lambda step, ids: (0, 0)),
            scratch_shapes=[
                pltpu.VMEM(table.shape, jnp.float32),
                pltpu.VMEM((count, cols), jnp.float32),
            ],
        ),
        out_shape=jax.ShapeDtypeStruct((count, cols), table.dtype),
        compiler_params=pltpu.CompilerParams(vmem_limit_bytes=40 * 2**20),
        cost_estimate=FREE,
        name="take_rows",
    )(ids, table)


def add_kernel(ids_ref, values_ref, out_ref, rows, *sums):
    size, length = out_ref.shape[0], rows.shape[1]
    for part in sums:
        part[...] = jnp.zeros_like(part)
    rows[...] = values_ref[:, 0:length, :].astype(jnp.float32)

    @pl.loop(0, length, step=8)
    def _(first):
        for by in range(8):
            for index, part in enumerate(sums):
                place = ids_ref[index * length + first + by]
                part[pl.ds(place, 1), :] += rows[index, pl.ds(first + by, 1), :]

    total = sums[0][0:size, :]
    for part in sums[1:]:
        total = total + part[0:size, :]
    out_ref[...] = total


def added_rows(ids, values, size):
    places, length = ids.shape
    cols = values.shape[2]
    return pl.pallas_call(
        add_kernel,
        grid_spec=pltpu.PrefetchScalarGridSpec(
            num_scalar_prefetch=1,
            grid=(1,),
            in_specs=[pl.BlockSpec(values.shape, lambda step, ids: (0, 0, 0))],
            out_specs=pl.BlockSpec((size, cols), lambda step, ids: (0, 0)),
            scratch_shapes=[pltpu.VMEM((places, length, cols), jnp.float32)]
            + [pltpu.VMEM((size + 8, cols), jnp.float32)] * places,
        ),
        out_shape=jax.ShapeDtypeStruct((size, cols), jnp.float32),
        compiler_params=pltpu.CompilerParams(vmem_limit_bytes=56 * 2**20),
        cost_estimate=FREE,
        name="add_rows",
    )(ids.reshape(-1), values)


def span_kernel(momentum_ref, grad_ref, error_ref, span_ref, sum_ref):
    grad = grad_ref[...].astype(jnp.float32)
    span = BETA * momentum_ref[...] + (1.0 - BETA) * grad + error_ref[0]
    span_ref[...] = span

    @pl.when(pl.program_id(0) == 0)
    def _():
        sum_ref[...] = jnp.zeros_like(sum_ref)

    sum_ref[...] += jnp.sum(jnp.abs(span), axis=0, keepdims=True)


def span_of(momentum, grad, error, start):
    rows, cols = grad.shape
    block = 1024
    first = start // block
    span, sums = pl.pallas_call(
        span_kernel,
        grid=(cols // block,),
        in_specs=[
            pl.BlockSpec((rows, block), lambda step: (0, first + step)),
            pl.BlockSpec((rows, block), lambda step: (0, step)),
            pl.BlockSpec((1, rows, block), lambda step: (0, 0, first + step)),
        ],
        out_specs=[
            pl.BlockSpec((rows, block), lambda step: (0, step)),
            pl.BlockSpec((1, block), lambda step: (0, 0)),
        ],
        out_shape=[
            jax.ShapeDtypeStruct((rows, cols), jnp.float32),
            jax.ShapeDtypeStruct((1, block), jnp.float32),
        ],
        compiler_params=pltpu.CompilerParams(vmem_limit_bytes=60 * 2**20),
        cost_estimate=FREE,
        name="span",
    )(momentum, grad, error)
    return span, jnp.sum(sums)


def press_kernel(steps, core_ref, scale_ref, *refs):
    *span_refs, error_ref, give_ref, keep_ref = refs
    core = pl.program_id(2)
    step = pressed_step(pl.program_id(0), pl.program_id(1), core)
    scale = scale_ref[0]
    inverse = scale_ref[1]
    for index, span_ref in enumerate(span_refs):

        @pl.when((step >= steps[index]) & (step < steps[index + 1]))
        def _():
            span = span_ref[...]
            sent = scale * jnp.tanh(span * inverse)
            error_ref[0] = span - sent
            low = sent.astype(jnp.bfloat16)

            @pl.when(core == core_ref[0])
            def _():
                keep_ref[0] = low

            @pl.when(core != core_ref[0])
            def _():
                give_ref[0] = low


def pressed_step(chip, column, core):
    return (2 * chip + core) * 3 + column


def pressed(spans, scale, parts):
    rows = spans[0].shape[0]
    cols = sum(span.shape[1] for span in spans)
    block = cols // parts // 3
    steps = [0]
    for span in spans:
        steps.append(steps[-1] + span.shape[1] // block)

    def of(index):
        low, count = steps[index], steps[index + 1] - steps[index]

        def place(chip, column, core, _):
            return (0, jnp.clip(pressed_step(chip, column, core) - low, 0, count - 1))

        return pl.BlockSpec((rows, block), place)

    half = pl.BlockSpec((1, rows, block), lambda chip, column, core, _: (chip, 0, column))
    half_shape = jax.ShapeDtypeStruct((parts // 2, rows, cols // parts), jnp.bfloat16)
    return pl.pallas_call(
        functools.partial(press_kernel, steps),
        grid_spec=pltpu.PrefetchScalarGridSpec(
            num_scalar_prefetch=1,
            grid=(parts // 2, 3, 2),
            in_specs=[pl.BlockSpec(memory_space=pltpu.SMEM)] + [of(i) for i in range(len(spans))],
            out_specs=[
                pl.BlockSpec(
                    (1, rows, block),
                    lambda chip, column, core, _: (0, 0, pressed_step(chip, column, core)),
                ),
                half,
                half,
            ],
        ),
        out_shape=[jax.ShapeDtypeStruct((1, rows, cols), jnp.float32), half_shape, half_shape],
        compiler_params=pltpu.CompilerParams(vmem_limit_bytes=60 * 2**20),
        cost_estimate=FREE,
        name="press",
    )(wide_places()[0][None], jnp.stack([scale, 1.0 / scale]), *spans)


def update_kernel(grad_ref, head_ref, table_ref, first_ref, second_ref, *out_refs):
    first_out, update_ref, weight_sum, update_sum = out_refs
    grad = grad_ref[...] + head_ref[...].astype(jnp.float32)
    first = BETA * first_ref[...] + (1.0 - BETA) * grad
    table = table_ref[...]
    update = first / (jnp.sqrt(second_ref[...]) + OPT_EPS) + DECAY * table
    first_out[...] = first
    update_ref[...] = update

    @pl.when(pl.program_id(0) == 0)
    def _():
        weight_sum[...] = jnp.zeros_like(weight_sum)
        update_sum[...] = jnp.zeros_like(update_sum)

    weight_sum[...] += jnp.sum(table * table, axis=0, keepdims=True)
    update_sum[...] += jnp.sum(update * update, axis=0, keepdims=True)


def table_update(grad, head, table, first, second):
    size, cols = table.shape
    block = size // 9 if size % 9 == 0 and size // 9 % 16 == 0 else size
    whole = pl.BlockSpec((block, cols), lambda step: (step, 0))
    line = pl.BlockSpec((1, cols), lambda step: (0, 0))
    moment, update, *sums = pl.pallas_call(
        update_kernel,
        grid=(size // block,),
        in_specs=[whole] * 5,
        out_specs=[whole, whole, line, line],
        out_shape=[jax.ShapeDtypeStruct((size, cols), jnp.float32)] * 2
        + [jax.ShapeDtypeStruct((1, cols), jnp.float32)] * 2,
        compiler_params=pltpu.CompilerParams(vmem_limit_bytes=56 * 2**20),
        cost_estimate=FREE,
        name="update",
    )(grad, head, table, first, second)
    return moment, update, tuple(jnp.sum(part)[None] for part in sums)


def wide_places():
    wide_me = lax.axis_index("wide")
    return wide_me % 2, wide_me // 2 % 2, wide_me // 4


def scattered_sum(give, keep):
    n_wide = lax.axis_size("wide")
    _, x, y = wide_places()

    def send(value, bit):
        return lax.ppermute(value.astype(jnp.bfloat16), "wide", swap_pairs(n_wide, bit))

    take = send(give, 1)
    half = keep.shape[1] // 2

    def chip(y_of, x_of, part):
        start, size = (2 * y_of + x_of, part * half, 0), (1, half, keep.shape[2])
        own, other = lax.dynamic_slice(keep, start, size), lax.dynamic_slice(take, start, size)
        return own[0].astype(jnp.float32) + other[0].astype(jnp.float32)

    upper_far = send(chip(1 - y, 1 - x, 0), 2)
    lower_far = send(chip(1 - y, 1 - x, 1), 4)
    upper_near = send(chip(y, 1 - x, 0), 2)
    lower_near = send(chip(1 - y, x, 1), 4)
    upper_far = send(chip(1 - y, x, 0) + upper_far.astype(jnp.float32), 4)
    lower_far = send(chip(y, 1 - x, 1) + lower_far.astype(jnp.float32), 2)
    own_upper = chip(y, x, 0) + upper_near.astype(jnp.float32) + upper_far.astype(jnp.float32)
    own_lower = chip(y, x, 1) + lower_near.astype(jnp.float32) + lower_far.astype(jnp.float32)
    return jnp.concatenate([own_upper, own_lower], axis=0)


def small_halved(value):
    n_wide = lax.axis_size("wide")
    for bit, place in list(zip((1, 2, 4), wide_places()))[::-1]:
        half = value.shape[1] // 2
        give = lax.dynamic_slice_in_dim(value, (1 - place) * half, half, 1).astype(jnp.bfloat16)
        keep = lax.dynamic_slice_in_dim(value, place * half, half, 1)
        value = keep + lax.ppermute(give, "wide", swap_pairs(n_wide, bit)).astype(jnp.float32)
    return value


def small_update(grad, first, second, weight):
    first = BETA * first + (1.0 - BETA) * grad.astype(jnp.float32)
    return first, first / (jnp.sqrt(second) + OPT_EPS) + DECAY * weight


def shards(
    token_ids,
    doc_ids,
    mlm_pos,
    mlm_labels,
    mlm_valid,
    table,
    table_m,
    table_v,
    small,
    small_m,
    small_v,
    layer,
    layer_m,
    layer_v,
    worker_err,
    server_err,
):
    n_wide, n_narrow = lax.axis_size("wide"), lax.axis_size("narrow")
    narrow_me = lax.axis_index("narrow")
    wide_me = lax.axis_index("wide")
    seqs = doc_ids.shape[0]
    paired = paired_mesh()
    vshard = table.shape[0]
    count = summed_over(jnp.sum(mlm_valid.astype(jnp.float32)), "wide")
    table_low, layer_low = table.astype(jnp.bfloat16), layer.astype(jnp.bfloat16)
    if paired:
        token_ids, mlm_labels, mlm_valid, doc_ids, mlm_pos = hosted_rows(
            token_ids, mlm_labels, mlm_valid, doc_ids, mlm_pos
        )
        owners = Owners(token_ids.reshape(n_narrow, n_wide * L), vshard)
        picked = packed_rows(owners.slots, table)
        layer_rows, picked = gathered_near(layer_low, picked)
    else:
        layer_rows = lax.all_gather(layer_low, "narrow", axis=0, tiled=True)
    weights = lax.all_gather(layer_rows, "wide", axis=1, tiled=True)
    if paired:

        def looked_up(room):
            rows = sent_around(picked[:, 0:room])
            return taken_rows(owners.behind_slots(room), jnp.concatenate(rows, axis=0))

        layer_rows, picked = together(layer_rows, picked)
        looked = looked_up(owners.room)
        looked = lax.cond(owners.full, lambda: looked_up(owners.count), lambda: looked)
        looked = lax.all_to_all(looked.reshape(n_wide, L, -1), "wide", 0, 0)
        looked = looked.transpose(1, 0, 2).reshape(1, L, D)
        looked, count, doc_ids, mlm_pos = together(looked, count, doc_ids, mlm_pos)
    else:
        local_ids = token_ids - narrow_me * vshard
        inside = (local_ids >= 0) & (local_ids < vshard)
        slots = jnp.where(inside, local_ids, vshard).reshape(-1)
        table_cols = lax.all_gather(table_low, "wide", axis=1, tiled=True)
        picked = jnp.take(table_cols, jnp.clip(local_ids, 0, vshard - 1), axis=0)
        picked = jnp.where(inside[..., None], picked, 0.0)
        looked = lax.psum_scatter(picked, "narrow", scatter_dimension=0, tiled=True)
    looked = looked.astype(jnp.float32)
    even_doc = (doc_ids % 2 == 0)[..., None]
    embedded = looked + small[0:L][None] + jnp.where(even_doc, small[L], small[L + 1])
    embedded = embedded.reshape(seqs * L, D)
    x0 = norm_rows(embedded, small[L + 2], small[L + 3])
    act = x0.astype(jnp.bfloat16)
    if paired:
        table_low, weights, act = together(table_low, weights, act)
        table_cols = lax.all_gather(table_low, "wide", axis=1, tiled=True)
    htwo, kept = layer_forward(embedded, x0, act, doc_ids, small, weights)
    hmask = jnp.take_along_axis(htwo.reshape(seqs, L, D), mlm_pos[..., None], axis=1)
    hmask = hmask.reshape(seqs * MPS, D).astype(jnp.bfloat16)
    if paired:
        group_h = gathered_near(hmask)
    else:
        group_h = lax.all_gather(hmask, "narrow", axis=0, tiled=True)
    vocab = narrow_me * vshard + jnp.arange(vshard)
    logits = jnp.where((vocab < VREAL)[None], matmul_nt(group_h, table_cols), -1000000000.0)
    labels = mlm_labels.reshape(-1)
    hit = vocab[None] == labels[:, None]
    top = jnp.max(logits, axis=1)
    total = jnp.sum(jnp.exp(logits - top[:, None]), axis=1)
    target = jnp.sum(jnp.where(hit, logits, 0.0), axis=1)
    if paired:
        stats = gathered_near(jnp.stack([top, total, target])[None])
        top, total, target = stats[0]
        for place in range(1, stats.shape[0]):
            top, total, target = merge_rows((top, total, target), tuple(stats[place]))
    else:
        top, total, target = joined((top, total, target), "narrow", merge_rows)
    lse = top + jnp.log(total)
    flags = mlm_valid.reshape(-1).astype(jnp.float32)
    own = seqs * MPS
    own_loss = lax.dynamic_slice_in_dim(flags * (lse - target), narrow_me * own, own)
    dlogit = (
        (jnp.exp(logits - lse[:, None]) - hit.astype(jnp.float32)) * (flags / count)[:, None]
    ).astype(jnp.bfloat16)
    dhmask = matmul(dlogit, table_cols)
    if paired:
        dhmask = scattered_near(dhmask)
        blocks = group_h.reshape(-1, n_wide, D // n_wide)
        table_head = jnp.einsum("sv,swc->wvc", dlogit, blocks, preferred_element_type=jnp.float32)
        table_head, dhmask = together(table_head.astype(jnp.bfloat16), dhmask)
        table_head = lax.psum_scatter(table_head, "wide", scatter_dimension=0)
    else:
        dhmask = lax.psum_scatter(dhmask, "narrow", scatter_dimension=0, tiled=True)
    dhtwo = (
        jnp.zeros((seqs, L, D), jnp.float32)
        .at[jnp.arange(seqs)[:, None], mlm_pos]
        .add(dhmask.reshape(seqs, MPS, D))
    )
    dembed, vectors, pieces = layer_backward(
        dhtwo.reshape(seqs * L, D), kept, doc_ids, small, weights
    )
    dembed_rows = dembed.reshape(seqs, L, D)
    small_grad = jnp.concatenate([jnp.sum(dembed_rows, axis=0), vectors], axis=0)
    mixed = pieces[0]
    if paired:
        cut = dembed.astype(jnp.bfloat16).reshape(L, n_wide, D // n_wide).transpose(1, 0, 2)
        cut = lax.all_to_all(cut, "wide", 0, 0).reshape(n_wide * L, D // n_wide)
        halved = small_halved(small_grad).astype(jnp.bfloat16)
        down, up = pieces[2], pieces[1]
        mixed.finish()
        cut, mixed.result, down.result, up.result, table_head = together(
            jnp.concatenate([cut, halved]), mixed.result, down.result, up.result, table_head
        )
        group_rows = lax.all_gather(cut, "narrow", axis=0)
    else:
        mixed.finish()
        group_rows = lax.all_gather(dembed_rows.astype(jnp.bfloat16), "narrow", axis=0, tiled=True)
        table_grad = matmul_tn(dlogit, group_h).at[slots].add(
            group_rows.reshape(-1, D).astype(jnp.float32), mode="drop"
        )
        cut = table_grad.astype(jnp.bfloat16).reshape(vshard, n_wide, D // n_wide)
        table_grad = lax.psum_scatter(cut.transpose(1, 0, 2), "wide", scatter_dimension=0)
        table_grad = table_grad.astype(jnp.float32)
    part_cols = layer.shape[1]
    if paired:
        spans, total, start = [], 0.0, [0, 4 * D, 8 * D]
        for piece, first in zip(pieces[::-1], start[::-1]):
            span, amount = span_of(layer_m, piece.result, worker_err, first)
            spans.insert(0, span)
            total = total + amount
        scale = total / (layer_m.shape[0] * layer_m.shape[1]) + MAG_EPS
        new_worker, give, keep = pressed(spans, scale, n_wide)
        server_in = scattered_sum(give, keep) / n_wide + server_err
    else:
        worker_grad = jnp.concatenate([piece.result for piece in pieces], axis=1)
        span = BETA * layer_m + (1.0 - BETA) * worker_grad.astype(jnp.float32) + worker_err[0]
        scale = jnp.mean(jnp.abs(span)) + MAG_EPS
        sent = scale * jnp.tanh(span / scale)
        new_worker = (span - sent)[None]
        summed = lax.psum(sent.astype(jnp.bfloat16), "wide").astype(jnp.float32)
        mixed = lax.dynamic_slice_in_dim(summed, wide_me * part_cols, part_cols, 1) / n_wide
        server_in = mixed + server_err
    sscale = jnp.mean(jnp.abs(server_in)) + MAG_EPS
    server_out = sscale * jnp.tanh(server_in / sscale)
    new_server = server_in - server_out
    server_low = server_out.astype(jnp.bfloat16)
    if paired:
        server_out, group_rows = together(server_out, group_rows)
        table_grad = added_rows(owners.slots, group_rows, vshard)
        table_mom, table_upd, table_norms = table_update(
            table_grad, table_head, table, table_m, table_v
        )
        eighth = D // n_wide
        small_grad = jnp.sum(group_rows[:, n_wide * L :].astype(jnp.float32), axis=0)
        small_grad = small_grad.astype(jnp.bfloat16)

        def own(value):
            return lax.dynamic_slice_in_dim(value, wide_me * eighth, eighth, 1)

        _, own_upd = small_update(small_grad, own(small_m), own(small_v), own(small))
        small_norm = jnp.where(narrow_me == 0, jnp.sum(own_upd * own_upd), 0.0)
    else:
        small_grad = lax.psum(small_grad, ("wide", "narrow"))
        table_mom = BETA * table_m + (1.0 - BETA) * table_grad
        table_upd = table_mom / (jnp.sqrt(table_v) + OPT_EPS) + DECAY * table
        table_norms = (jnp.sum(table * table)[None], jnp.sum(table_upd * table_upd)[None])
    new_m = lax.all_gather(server_low, "wide", axis=1, tiled=True).astype(jnp.float32)
    if paired:
        small_grad = lax.all_gather(small_grad, "wide", axis=1, tiled=True)
    small_mom, small_upd = small_update(small_grad, small_m, small_v, small)
    if not paired:
        small_norm = jnp.where((wide_me == 0) & (narrow_me == 0), jnp.sum(small_upd * small_upd), 0.0)
    layer_upd = server_out / (jnp.sqrt(layer_v) + OPT_EPS) + DECAY * layer
    column = wide_me * part_cols + jnp.arange(part_cols)
    which = (
        (column >= 3 * D).astype(jnp.int32)
        + (column >= 4 * D).astype(jnp.int32)
        + (column >= 4 * D + FF).astype(jnp.int32)
    )
    onehot = (which[:, None] == jnp.arange(4)[None]).astype(jnp.float32)
    wsq = jnp.sum(jnp.sum(layer * layer, axis=0)[:, None] * onehot, axis=0)
    usq = jnp.sum(jnp.sum(layer_upd * layer_upd, axis=0)[:, None] * onehot, axis=0)
    parts = jnp.concatenate([wsq, usq, *table_norms, jnp.sum(own_loss)[None], small_norm[None]])
    sums = summed_over(summed_over(parts, "wide"), "narrow")
    loss_sum = sums[10]
    wnorm = jnp.sqrt(jnp.concatenate([sums[0:4], sums[8:9], jnp.sum(small * small)[None]]))
    unorm = jnp.sqrt(jnp.concatenate([sums[4:8], sums[9:10], sums[11:12]]))
    ratio = wnorm / unorm
    new_layer = layer - RATE * jnp.sum(onehot * ratio[None, 0:4], axis=1)[None] * layer_upd
    new_table = table - RATE * ratio[4] * table_upd
    new_small = small - RATE * ratio[5] * small_upd
    return (
        jnp.stack([loss_sum, count]),
        new_table,
        table_mom,
        new_small,
        small_mom,
        new_layer,
        new_m,
        new_worker,
        new_server,
        jnp.stack([wnorm, unorm]),
    )


def solution(mesh):
    placed = (
        P("wide", None),
        P(("wide", "narrow"), None),
        P(("wide", "narrow"), None),
        P("wide", None),
        P("wide", None),
        P("narrow", "wide"),
        P("narrow", "wide"),
        P("narrow", "wide"),
        P(),
        P(),
        P(),
        P("narrow", "wide"),
        P("narrow", None),
        P("narrow", "wide"),
        P("wide", "narrow", None),
        P("narrow", "wide"),
    )
    return jax.shard_map(
        shards,
        mesh=mesh,
        in_specs=placed,
        out_specs=(
            P(),
            P("narrow", "wide"),
            P("narrow", "wide"),
            P(),
            P(),
            P("narrow", "wide"),
            P("narrow", None),
            P("wide", "narrow", None),
            P("narrow", "wide"),
            P(),
        ),
        check_vma=False,
    )
```

```python
import functools

import jax
import jax.numpy as jnp
from jax import lax
from jax.experimental import pallas as pl
from jax.experimental.pallas import tpu as pltpu
from jax.sharding import PartitionSpec as P

D = 1024
HEADS = 16
HEAD = 64
FF = 4096
VREAL = 30522
L = 512
MPS = 80


LN_EPS = 1e-12
BETA = 0.9
DECAY = 0.01
RATE = 0.25
OPT_EPS = 1e-06
MAG_EPS = 1e-08

FREE = pl.CostEstimate(flops=0, bytes_accessed=0, transcendentals=0)


def joined(value, axis, join):
    pieces = jax.tree.map(lambda part: lax.all_gather(part, axis), value)
    head = jax.tree.map(lambda part: part[0], pieces)
    tail = jax.tree.map(lambda part: part[1:], pieces)
    subtotal, _ = lax.scan(lambda subtotal, slab: (join(subtotal, slab), None), head, tail)
    return subtotal


def norm_rows(x, gain, shift):
    mean = jnp.mean(x, axis=-1, keepdims=True)
    cent = x - mean
    var = jnp.mean(cent * cent, axis=-1, keepdims=True)
    return cent * lax.rsqrt(var + LN_EPS) * gain + shift


def matmul(left, right):
    return jnp.dot(left, right, preferred_element_type=jnp.float32)


def matmul_tn(left, right):
    return lax.dot_general(
        left, right, (((0,), (0,)), ((), ())), preferred_element_type=jnp.float32
    )


def matmul_nt(left, right):
    return lax.dot_general(
        left, right, (((1,), (1,)), ((), ())), preferred_element_type=jnp.float32
    )


def attend_kernel(q_ref, k_ref, v_ref, key_doc_ref, query_doc_ref, out_ref, lse_ref):
    same = key_doc_ref[...] == query_doc_ref[...]
    lane = lax.broadcasted_iota(jnp.int32, (1, 2 * HEAD), 1)
    outs = []
    for head in range(2):
        mine = lane // HEAD == head
        query = jnp.where(mine, q_ref[...] * 0.125, 0).astype(jnp.bfloat16)
        scores = jnp.where(same, matmul_nt(k_ref[...], query), -1000000000.0)
        top = jnp.max(scores, axis=0, keepdims=True)
        power = jnp.exp(scores - top)
        total = jnp.sum(power, axis=0, keepdims=True)
        lse_ref[0, head : head + 1, :] = top + jnp.log(total)
        prob = (power * (1.0 / total)).astype(jnp.bfloat16)
        outs.append(matmul_tn(prob, v_ref[...]))
    out_ref[...] = jnp.where(lane < HEAD, outs[0], outs[1]).astype(jnp.bfloat16)


def head_pairs(offset):
    return pl.BlockSpec((L, 2 * HEAD), lambda pair: (0, offset * HEADS // 2 + pair))


def attend(qkv, docs):
    return pl.pallas_call(
        attend_kernel,
        grid=(HEADS // 2,),
        in_specs=[
            head_pairs(0),
            head_pairs(1),
            head_pairs(2),
            pl.BlockSpec((L, 1), lambda pair: (0, 0)),
            pl.BlockSpec((1, L), lambda pair: (0, 0)),
        ],
        out_specs=[head_pairs(0), pl.BlockSpec((1, 2, L), lambda pair: (pair, 0, 0))],
        out_shape=[
            jax.ShapeDtypeStruct((L, D), jnp.bfloat16),
            jax.ShapeDtypeStruct((HEADS // 2, 2, L), jnp.float32),
        ],
        compiler_params=pltpu.CompilerParams(vmem_limit_bytes=40 * 2**20),
        cost_estimate=FREE,
        name="attend",
    )(qkv, qkv, qkv, docs.reshape(L, 1), docs.reshape(1, L))


def attend_back_kernel(q_ref, k_ref, v_ref, do_ref, lse_ref, key_doc_ref, query_doc_ref, out_ref):
    pair = pl.program_id(0)
    same = key_doc_ref[...] == query_doc_ref[...]
    lane = lax.broadcasted_iota(jnp.int32, (1, 2 * HEAD), 1)
    both = []
    for head in range(2):
        mine = lane // HEAD == head
        query = jnp.where(mine, q_ref[...] * 0.125, 0).astype(jnp.bfloat16)
        dout = jnp.where(mine, do_ref[...], 0).astype(jnp.bfloat16)
        scores = jnp.where(same, matmul_nt(k_ref[...], query), -1000000000.0)
        prob = jnp.exp(scores - lse_ref[0, head : head + 1, :])
        dvalue = matmul(prob.astype(jnp.bfloat16), dout)
        dprob = matmul_nt(v_ref[...], dout)
        delta = jnp.sum(prob * dprob, axis=0, keepdims=True)
        dscore = (prob * (dprob - delta)).astype(jnp.bfloat16)
        both.append((matmul_tn(dscore, k_ref[...]) * 0.125, matmul(dscore, query), dvalue))
    for part in range(3):
        value = jnp.where(lane < HEAD, both[0][part], both[1][part]).astype(jnp.bfloat16)
        start = pl.multiple_of(part * D + pair * 2 * HEAD, 2 * HEAD)
        out_ref[:, pl.ds(start, 2 * HEAD)] = value


def attend_back(qkv, dout, lse, docs):
    return pl.pallas_call(
        attend_back_kernel,
        grid=(HEADS // 2,),
        in_specs=[
            head_pairs(0),
            head_pairs(1),
            head_pairs(2),
            head_pairs(0),
            pl.BlockSpec((1, 2, L), lambda pair: (pair, 0, 0)),
            pl.BlockSpec((L, 1), lambda pair: (0, 0)),
            pl.BlockSpec((1, L), lambda pair: (0, 0)),
        ],
        out_specs=pl.BlockSpec((L, 3 * D), lambda pair: (0, 0)),
        out_shape=jax.ShapeDtypeStruct((L, 3 * D), jnp.bfloat16),
        compiler_params=pltpu.CompilerParams(vmem_limit_bytes=40 * 2**20),
        cost_estimate=FREE,
        name="attend_back",
    )(qkv, qkv, qkv, dout, lse, docs.reshape(L, 1), docs.reshape(1, L))


def merge_rows(first, second):
    peak = jnp.maximum(first[0], second[0])
    total = first[1] * jnp.exp(first[0] - peak) + second[1] * jnp.exp(second[0] - peak)
    return (peak, total, first[2] + second[2])


def embed_back_kernel(dqkv_ref, weight_ref, drone_ref, embedded_ref, gain_ref, even_ref, *refs):
    dembed_ref, rows_ref, sums_ref, total = refs
    step = pl.program_id(0)
    dqkv = dqkv_ref[...]
    part = matmul_nt(dqkv, weight_ref[...])
    sums_ref[...] = jnp.sum(dqkv.astype(jnp.float32), axis=0, keepdims=True)

    @pl.when(step == 0)
    def _():
        total[...] = drone_ref[...] + part

    @pl.when(step > 0)
    def _():
        total[...] += part

    @pl.when(step == pl.num_programs(0) - 1)
    def _():
        grad = total[...]
        embedded = embedded_ref[...]
        cent = embedded - jnp.mean(embedded, axis=1, keepdims=True)
        scale = lax.rsqrt(jnp.mean(cent * cent, axis=1, keepdims=True) + LN_EPS)
        normed = cent * scale
        inner = grad * gain_ref[...]
        inner_mean = jnp.mean(inner, axis=1, keepdims=True)
        along = jnp.mean(inner * normed, axis=1, keepdims=True)
        dembed = scale * (inner - inner_mean - normed * along)
        dembed_ref[...] = dembed
        even = even_ref[...]
        rows_ref[0:1, :] = jnp.sum(grad * normed, axis=0, keepdims=True)
        rows_ref[1:2, :] = jnp.sum(grad, axis=0, keepdims=True)
        rows_ref[2:3, :] = jnp.sum(dembed * even, axis=0, keepdims=True)
        rows_ref[3:4, :] = jnp.sum(dembed * (1.0 - even), axis=0, keepdims=True)
        rows_ref[4:8, :] = jnp.zeros((4, D), jnp.float32)


def embed_back(dqkv, weights, drone, embedded, gain, even):
    tokens = dqkv.shape[0]
    whole = pl.BlockSpec((tokens, D), lambda step: (0, 0))
    return pl.pallas_call(
        embed_back_kernel,
        grid=(3,),
        in_specs=[
            pl.BlockSpec((tokens, D), lambda step: (0, step)),
            pl.BlockSpec((D, D), lambda step: (0, step)),
            whole,
            whole,
            pl.BlockSpec((1, D), lambda step: (0, 0)),
            pl.BlockSpec((tokens, 1), lambda step: (0, 0)),
        ],
        out_specs=[
            whole,
            pl.BlockSpec((8, D), lambda step: (0, 0)),
            pl.BlockSpec((1, D), lambda step: (0, step)),
        ],
        out_shape=[
            jax.ShapeDtypeStruct((tokens, D), jnp.float32),
            jax.ShapeDtypeStruct((8, D), jnp.float32),
            jax.ShapeDtypeStruct((1, 3 * D), jnp.float32),
        ],
        scratch_shapes=[pltpu.VMEM((tokens, D), jnp.float32)],
        compiler_params=pltpu.CompilerParams(vmem_limit_bytes=40 * 2**20),
        cost_estimate=FREE,
        name="embed_back",
    )(dqkv, weights, drone, embedded, gain[None], even)


def ffn_kernel(fin_ref, weight_ref, bias_ref, gated_ref, slope_ref):
    upper = matmul(fin_ref[...], weight_ref[...]) + bias_ref[...]
    below = 0.5 + 0.5 * lax.erf(upper * 0.7071067811865476)
    gated_ref[...] = (upper * below).astype(jnp.bfloat16)
    density = 0.3989422804014327 * jnp.exp(-0.5 * upper * upper)
    slope_ref[...] = (below + upper * density).astype(jnp.bfloat16)


def ffn_up(fin, weights, bias):
    tokens = fin.shape[0]
    block = 512
    first = 4 * D // block
    out = pl.BlockSpec((tokens, block), lambda step: (0, step))
    return pl.pallas_call(
        ffn_kernel,
        grid=(FF // block,),
        in_specs=[
            pl.BlockSpec((tokens, D), lambda step: (0, 0)),
            pl.BlockSpec((D, block), lambda step: (0, first + step)),
            pl.BlockSpec((1, block), lambda step: (0, step)),
        ],
        out_specs=[out, out],
        out_shape=[jax.ShapeDtypeStruct((tokens, FF), jnp.bfloat16)] * 2,
        compiler_params=pltpu.CompilerParams(vmem_limit_bytes=32 * 2**20),
        cost_estimate=pl.CostEstimate(flops=2 * tokens * D * FF, bytes_accessed=0, transcendentals=0),
        name="ffn_up",
    )(fin, weights, bias)


def layer_forward(embedded, x0, act, docs, small, weights):
    base = L + 2
    bias = jnp.concatenate([small[base + 6], jnp.zeros((D,), jnp.float32), small[base + 7]])
    qkv = (matmul(act, weights[:, 0 : 3 * D]) + bias).astype(jnp.bfloat16)
    out, lse = attend(qkv, docs)
    rone = x0 + (matmul(out, weights[:, 3 * D : 4 * D]) + small[base + 8])
    hone = norm_rows(rone, small[base + 2], small[base + 3])
    fin = hone.astype(jnp.bfloat16)
    gated, slope = ffn_up(fin, weights, small[base + 10 :].reshape(1, FF))
    rtwo = hone + (matmul_nt(gated, weights[:, 4 * D + FF :]) + small[base + 9])
    htwo = norm_rows(rtwo, small[base + 4], small[base + 5])
    return (htwo, (embedded, act, qkv, lse, out, rone, fin, slope, gated, rtwo))


def layer_backward(dhtwo, kept, docs, small, weights):
    embedded, act, qkv, lse, out, rone, fin, slope, gated, rtwo = kept
    base = L + 2
    _, pull = jax.vjp(norm_rows, rtwo, small[base + 4], small[base + 5])
    drtwo, dgain_two, dshift_two = pull(dhtwo)
    dffn = drtwo.astype(jnp.bfloat16)
    down = WorkerPiece((dffn, gated))
    dgated = matmul(dffn, weights[:, 4 * D + FF :])
    dupper = (dgated * slope.astype(jnp.float32)).astype(jnp.bfloat16)
    dupper = down.received(dupper)
    dupper = down.across(dupper)
    up = WorkerPiece((fin, dupper))
    dhone = drtwo + matmul_nt(dupper, weights[:, 4 * D : 4 * D + FF])
    _, pull = jax.vjp(norm_rows, rone, small[base + 2], small[base + 3])
    drone, dgain_one, dshift_one = pull(dhone)
    dattn = drone.astype(jnp.bfloat16)
    dout = matmul_nt(dattn, weights[:, 3 * D : 4 * D]).astype(jnp.bfloat16)
    dout = up.received(dout)
    dout = up.across(dout)
    dqkv = attend_back(qkv, dout, lse, docs)
    (dqkv,) = down.crossed(dqkv)
    down.finish()
    mixed = WorkerPiece((act, dqkv), (out, dattn))
    even = (docs.reshape(L, 1) % 2 == 0).astype(jnp.float32)
    dembed, embed_rows, bias_qkv = embed_back(
        mixed.across(dqkv), weights, drone, embedded, small[base], even
    )
    (dembed,) = up.crossed(dembed)
    up.finish()
    vectors = jnp.stack(
        [
            embed_rows[0],
            embed_rows[1],
            dgain_one,
            dshift_one,
            dgain_two,
            dshift_two,
            bias_qkv[0, 0:D],
            bias_qkv[0, 2 * D : 3 * D],
            jnp.sum(dattn, axis=0, dtype=jnp.float32),
            jnp.sum(dffn, axis=0, dtype=jnp.float32),
        ]
    )
    bias_up = jnp.sum(dupper, axis=0, dtype=jnp.float32).reshape(FF // D, D)
    vectors = jnp.concatenate([embed_rows[2:4], vectors, bias_up], axis=0)
    return (dembed, vectors, (mixed, up, down))


def paired_mesh():
    return lax.axis_size("wide") == 8 and lax.axis_size("narrow") == 4


def together(*values):
    return lax.optimization_barrier(values)


def swap_pairs(size, bit):
    return [(place, place ^ bit) for place in range(size)]


def cycle(size, by):
    return [(place, (place + by) % size) for place in range(size)]


def summed_over(value, axis):
    size = lax.axis_size(axis)
    if size & (size - 1):
        return lax.psum(value, axis)
    bit = 1
    while bit < size:
        value = value + lax.ppermute(value, axis, swap_pairs(size, bit))
        bit *= 2
    return value


def gathered_near(value, beside=None):
    size = lax.axis_size("narrow")
    rows = value.shape[0]
    around = [value]
    for by in range(1, size):
        around.append(lax.ppermute(value, "narrow", cycle(size, size - by)))
    if beside is not None:
        *around, beside = together(*around, beside)
    place = lax.axis_index("narrow")
    whole = jnp.zeros((size * rows,) + value.shape[1:], value.dtype)
    for by, part in enumerate(around):
        start = lax.rem(place + by, size) * rows
        whole = lax.dynamic_update_slice_in_dim(whole, part, start, 0)
    return whole if beside is None else (whole, beside)


def scattered_near(value):
    size = lax.axis_size("narrow")
    rows = value.shape[0] // size
    place = lax.axis_index("narrow")
    total = lax.dynamic_slice_in_dim(value, place * rows, rows, 0)
    for by in range(1, size):
        target = lax.rem(place + by, size)
        give = lax.dynamic_slice_in_dim(value, target * rows, rows, 0).astype(jnp.bfloat16)
        take = lax.ppermute(give, "narrow", cycle(size, by))
        total = total + take.astype(jnp.float32)
    return total


def sent_around(blocks):
    size = lax.axis_size("narrow")
    place = lax.axis_index("narrow")

    def block(by):
        return lax.dynamic_index_in_dim(blocks, lax.rem(place + by, size), 0, keepdims=False)

    return [block(0)] + [
        lax.ppermute(block(by), "narrow", cycle(size, by)) for by in range(1, size)
    ]


def block_kernel(steps, place_ref, *refs):
    pairs = len(steps) - 1
    lefts, rights, terms, out_ref = refs[:pairs], refs[pairs : 2 * pairs], refs[2 * pairs : -1], refs[-1]
    step = pl.program_id(0)
    for index in range(pairs):

        @pl.when((step >= steps[index]) & (step < steps[index + 1]))
        def _():
            total = matmul_tn(lefts[index][...], rights[index][...])
            for term_ref in terms:
                total = total + term_ref[...].astype(jnp.float32)
            out_ref[...] = total.astype(jnp.bfloat16)


def gradient_block(pairs, place, terms):
    block = D
    size = D // lax.axis_size("narrow")
    steps = [0]
    for _, right in pairs:
        steps.append(steps[-1] + right.shape[1] // block)
    tokens = pairs[0][0].shape[0]

    def right_of(index):
        low, count = steps[index], steps[index + 1] - steps[index]
        return pl.BlockSpec(
            (tokens, block), lambda step, place: (0, jnp.clip(step - low, 0, count - 1))
        )

    piece = pl.BlockSpec((size, block), lambda step, place: (0, step))
    return pl.pallas_call(
        functools.partial(block_kernel, steps),
        grid_spec=pltpu.PrefetchScalarGridSpec(
            num_scalar_prefetch=1,
            grid=(steps[-1],),
            in_specs=[pl.BlockSpec((tokens, size), lambda step, place: (0, place[0]))] * len(pairs)
            + [right_of(index) for index in range(len(pairs))]
            + [piece] * len(terms),
            out_specs=piece,
        ),
        out_shape=jax.ShapeDtypeStruct((size, steps[-1] * block), jnp.bfloat16),
        compiler_params=pltpu.CompilerParams(vmem_limit_bytes=24 * 2**20),
        cost_estimate=FREE,
        name="gradient_block",
    )(place[None], *[left for left, _ in pairs], *[right for _, right in pairs], *terms)


class WorkerPiece:
    def __init__(self, *pairs):
        self.pairs = pairs
        self.paired = paired_mesh()
        if not self.paired:
            return
        self.core = lax.axis_index("wide") % 2
        self.pair, self.side = lax.axis_index("narrow") // 2, lax.axis_index("narrow") % 2
        cores = swap_pairs(lax.axis_size("wide"), 1)
        self.far = lax.ppermute(self.block(1 - self.core, 1 - self.side), "wide", cores)
        self.near = lax.ppermute(self.block(1 - self.core, self.side), "wide", cores)

    def block(self, core, side, *terms):
        return gradient_block(self.pairs, 2 * core + side, terms)

    def received(self, value):
        if self.paired:
            value, self.far, self.near = together(value, self.far, self.near)
        return value

    def across(self, value):
        if self.paired:
            sides = swap_pairs(lax.axis_size("narrow"), 1)
            away = self.block(self.core, 1 - self.side, self.far)
            away, value = together(away, value)
            self.away = lax.ppermute(away, "narrow", sides)
        return value

    def crossed(self, *values):
        if self.paired:
            *values, self.away = together(*values, self.away)
        return values

    def finish(self, *values):
        if not self.paired:
            blocks = [matmul_tn(left, right).astype(jnp.bfloat16) for left, right in self.pairs]
            grad = jnp.concatenate(blocks, axis=1)
            self.result = lax.psum_scatter(grad, "narrow", scatter_dimension=0, tiled=True)
            return values
        n_wide, n_narrow = lax.axis_size("wide"), lax.axis_size("narrow")
        total = self.block(self.core, self.side, self.near, self.away)
        moves = []
        for wide in range(n_wide):
            for narrow in range(n_narrow):
                if narrow // 2 != wide % 2:
                    target_wide = wide - wide % 2 + narrow // 2
                    target = target_wide * n_narrow + 2 * (wide % 2) + narrow % 2
                    moves.append((wide * n_narrow + narrow, target))
        total, *values = together(total, *values)
        moved = lax.ppermute(total, ("wide", "narrow"), moves)
        self.result = jnp.where(self.pair == self.core, total, moved)
        return values


def hosted_rows(token_ids, mlm_labels, mlm_valid, doc_ids, mlm_pos):
    n_wide, n_narrow = lax.axis_size("wide"), lax.axis_size("narrow")
    packed = jnp.concatenate([token_ids, mlm_labels, mlm_valid], axis=1)[None]
    for bit, place in zip((1, 2, 4), wide_places()):
        other = lax.ppermute(packed, "wide", swap_pairs(n_wide, bit))
        first, second = jnp.where(place == 0, packed, other), jnp.where(place == 0, other, packed)
        packed = jnp.concatenate([first, second], axis=0)
    width = packed.shape[2]
    hosted = packed.reshape(n_wide // 2, 2, 2, 2, width).transpose(1, 2, 0, 3, 4)
    hosted = hosted.reshape(n_narrow, n_wide, width)
    column = lax.dynamic_index_in_dim(hosted, lax.axis_index("wide"), 1, keepdims=False)
    moves = []
    for wide in range(n_wide):
        for row in range(n_narrow):
            target_wide = wide - wide % 2 + row % 2
            target_narrow = 2 * (wide % 2) + row // 2
            moves.append((wide * n_narrow + row, target_wide * n_narrow + target_narrow))
    own = lax.ppermute(jnp.concatenate([doc_ids, mlm_pos], axis=1), ("wide", "narrow"), moves)
    return (
        hosted[:, :, 0:L],
        column[:, L : L + MPS],
        column[:, L + MPS :],
        own[:, 0:L],
        own[:, L:],
    )


STREAMS = 2


class Owners:
    def __init__(self, tokens, vshard):
        size = lax.axis_size("narrow")
        place = lax.axis_index("narrow")
        count = tokens.shape[1]
        self.room = count * 7 // 16
        owner = tokens // vshard
        held = (owner[None] == jnp.arange(size)[:, None, None]).astype(jnp.bfloat16)
        tiles = held.reshape(-1, count // 128, 128)
        order = jnp.arange(128)
        within = jnp.einsum(
            "btl,lm->btm",
            tiles,
            (order[:, None] < order[None]).astype(jnp.bfloat16),
            preferred_element_type=jnp.float32,
        )
        sums = jnp.sum(tiles.astype(jnp.float32), axis=2)
        tile = jnp.arange(count // 128)
        before = jnp.sum(jnp.where(tile[:, None] < tile[None], sums[:, :, None], 0.0), axis=1)
        rank = (within + before[..., None]).reshape(size, size, count) * held.astype(jnp.float32)
        rank = jnp.sum(rank, axis=0).astype(jnp.int32)
        self.full = jnp.max(jnp.sum(sums, axis=1)) > self.room
        self.count, self.vshard = count, vshard
        own = lax.dynamic_index_in_dim(owner, place, 0, keepdims=False)
        self.rank = lax.dynamic_index_in_dim(rank, place, 0, keepdims=False)
        self.behind = lax.rem(place - own + size, size)
        self.slots = jnp.where(owner == place, tokens - place * vshard, vshard)

    def behind_slots(self, room):
        return self.behind * room + jnp.minimum(self.rank, room - 1)


def pack_kernel(ids_ref, table_ref, out_ref, held, *rows):
    step, count, size = pl.program_id(0), out_ref.shape[1], table_ref.shape[0]

    @pl.when(step == 0)
    def _():
        held[0:size, :] = table_ref[...]
        held[size:, :] = jnp.zeros((8, table_ref.shape[1]), jnp.float32)
        for part in rows:
            part[...] = jnp.zeros_like(part)

    base = [(step * len(rows) + index) * count for index in range(len(rows))]

    def some(turn, used):
        used = list(used)
        for by in range(8):
            for index, part in enumerate(rows):
                place = ids_ref[base[index] + turn * 8 + by]
                part[pl.ds(used[index], 1), :] = held[pl.ds(place, 1), :]
                used[index] = used[index] + jnp.where(place < size, 1, 0)
        return tuple(used)

    lax.fori_loop(0, count // 8, some, (0,) * len(rows))
    for index, part in enumerate(rows):
        out_ref[index] = part[0:count, :].astype(out_ref.dtype)


def packed_rows(ids, table):
    size, cols = table.shape
    places, count = ids.shape
    return pl.pallas_call(
        pack_kernel,
        grid_spec=pltpu.PrefetchScalarGridSpec(
            num_scalar_prefetch=1,
            grid=(places // STREAMS,),
            in_specs=[pl.BlockSpec((size, cols), lambda step, ids: (0, 0))],
            out_specs=pl.BlockSpec((STREAMS, count, cols), lambda step, ids: (step, 0, 0)),
            scratch_shapes=[pltpu.VMEM((size + 8, cols), jnp.float32)]
            + [pltpu.VMEM((count + 8, cols), jnp.float32)] * STREAMS,
        ),
        out_shape=jax.ShapeDtypeStruct((places, count, cols), jnp.bfloat16),
        compiler_params=pltpu.CompilerParams(vmem_limit_bytes=40 * 2**20),
        cost_estimate=pl.CostEstimate(flops=0, bytes_accessed=15 * 10**7, transcendentals=0),
        name="pack_rows",
    )(ids.reshape(-1), table)


def take_kernel(ids_ref, table_ref, out_ref, held, rows):
    held[...] = table_ref[...].astype(jnp.float32)

    @pl.loop(0, out_ref.shape[0], step=16)
    def _(first):
        for by in range(16):
            rows[pl.ds(first + by, 1), :] = held[pl.ds(ids_ref[first + by], 1), :]

    out_ref[...] = rows[...].astype(out_ref.dtype)


def taken_rows(ids, table):
    count, cols = ids.shape[0], table.shape[1]
    return pl.pallas_call(
        take_kernel,
        grid_spec=pltpu.PrefetchScalarGridSpec(
            num_scalar_prefetch=1,
            grid=(1,),
            in_specs=[pl.BlockSpec(table.shape, lambda step, ids: (0, 0))],
            out_specs=pl.BlockSpec((count, cols), lambda step, ids: (0, 0)),
            scratch_shapes=[
                pltpu.VMEM(table.shape, jnp.float32),
                pltpu.VMEM((count, cols), jnp.float32),
            ],
        ),
        out_shape=jax.ShapeDtypeStruct((count, cols), table.dtype),
        compiler_params=pltpu.CompilerParams(vmem_limit_bytes=40 * 2**20),
        cost_estimate=FREE,
        name="take_rows",
    )(ids, table)


def add_kernel(ids_ref, values_ref, out_ref, rows, *sums):
    size, length = out_ref.shape[0], rows.shape[1]
    for part in sums:
        part[...] = jnp.zeros_like(part)
    rows[...] = values_ref[:, 0:length, :].astype(jnp.float32)

    @pl.loop(0, length, step=8)
    def _(first):
        for by in range(8):
            for index, part in enumerate(sums):
                place = ids_ref[index * length + first + by]
                part[pl.ds(place, 1), :] += rows[index, pl.ds(first + by, 1), :]

    total = sums[0][0:size, :]
    for part in sums[1:]:
        total = total + part[0:size, :]
    out_ref[...] = total


def added_rows(ids, values, size):
    places, length = ids.shape
    cols = values.shape[2]
    return pl.pallas_call(
        add_kernel,
        grid_spec=pltpu.PrefetchScalarGridSpec(
            num_scalar_prefetch=1,
            grid=(1,),
            in_specs=[pl.BlockSpec(values.shape, lambda step, ids: (0, 0, 0))],
            out_specs=pl.BlockSpec((size, cols), lambda step, ids: (0, 0)),
            scratch_shapes=[pltpu.VMEM((places, length, cols), jnp.float32)]
            + [pltpu.VMEM((size + 8, cols), jnp.float32)] * places,
        ),
        out_shape=jax.ShapeDtypeStruct((size, cols), jnp.float32),
        compiler_params=pltpu.CompilerParams(vmem_limit_bytes=56 * 2**20),
        cost_estimate=FREE,
        name="add_rows",
    )(ids.reshape(-1), values)


def span_kernel(momentum_ref, grad_ref, error_ref, span_ref, sum_ref):
    grad = grad_ref[...].astype(jnp.float32)
    span = BETA * momentum_ref[...] + (1.0 - BETA) * grad + error_ref[0]
    span_ref[...] = span

    @pl.when(pl.program_id(0) == 0)
    def _():
        sum_ref[...] = jnp.zeros_like(sum_ref)

    sum_ref[...] += jnp.sum(jnp.abs(span), axis=0, keepdims=True)


def span_of(momentum, grad, error, start):
    rows, cols = grad.shape
    block = 1024
    first = start // block
    span, sums = pl.pallas_call(
        span_kernel,
        grid=(cols // block,),
        in_specs=[
            pl.BlockSpec((rows, block), lambda step: (0, first + step)),
            pl.BlockSpec((rows, block), lambda step: (0, step)),
            pl.BlockSpec((1, rows, block), lambda step: (0, 0, first + step)),
        ],
        out_specs=[
            pl.BlockSpec((rows, block), lambda step: (0, step)),
            pl.BlockSpec((1, block), lambda step: (0, 0)),
        ],
        out_shape=[
            jax.ShapeDtypeStruct((rows, cols), jnp.float32),
            jax.ShapeDtypeStruct((1, block), jnp.float32),
        ],
        compiler_params=pltpu.CompilerParams(vmem_limit_bytes=60 * 2**20),
        cost_estimate=pl.CostEstimate(flops=0, bytes_accessed=2 * 10**7, transcendentals=0),
        name="span",
    )(momentum, grad, error)
    return span, jnp.sum(sums)


def press_kernel(steps, core_ref, scale_ref, *refs):
    *span_refs, error_ref, give_ref, keep_ref = refs
    core = pl.program_id(2)
    step = pressed_step(pl.program_id(0), pl.program_id(1), core)
    scale = scale_ref[0]
    inverse = scale_ref[1]
    for index, span_ref in enumerate(span_refs):

        @pl.when((step >= steps[index]) & (step < steps[index + 1]))
        def _():
            span = span_ref[...]
            sent = scale * jnp.tanh(span * inverse)
            error_ref[0] = span - sent
            low = sent.astype(jnp.bfloat16)

            @pl.when(core == core_ref[0])
            def _():
                keep_ref[0] = low

            @pl.when(core != core_ref[0])
            def _():
                give_ref[0] = low


def pressed_step(chip, column, core):
    return (2 * chip + core) * 3 + column


def pressed(spans, scale, parts):
    rows = spans[0].shape[0]
    cols = sum(span.shape[1] for span in spans)
    block = cols // parts // 3
    steps = [0]
    for span in spans:
        steps.append(steps[-1] + span.shape[1] // block)

    def of(index):
        low, count = steps[index], steps[index + 1] - steps[index]

        def place(chip, column, core, _):
            return (0, jnp.clip(pressed_step(chip, column, core) - low, 0, count - 1))

        return pl.BlockSpec((rows, block), place)

    half = pl.BlockSpec((1, rows, block), lambda chip, column, core, _: (chip, 0, column))
    half_shape = jax.ShapeDtypeStruct((parts // 2, rows, cols // parts), jnp.bfloat16)
    return pl.pallas_call(
        functools.partial(press_kernel, steps),
        grid_spec=pltpu.PrefetchScalarGridSpec(
            num_scalar_prefetch=1,
            grid=(parts // 2, 3, 2),
            in_specs=[pl.BlockSpec(memory_space=pltpu.SMEM)] + [of(i) for i in range(len(spans))],
            out_specs=[
                pl.BlockSpec(
                    (1, rows, block),
                    lambda chip, column, core, _: (0, 0, pressed_step(chip, column, core)),
                ),
                half,
                half,
            ],
        ),
        out_shape=[jax.ShapeDtypeStruct((1, rows, cols), jnp.float32), half_shape, half_shape],
        compiler_params=pltpu.CompilerParams(vmem_limit_bytes=60 * 2**20),
        cost_estimate=FREE,
        name="press",
    )(wide_places()[0][None], jnp.stack([scale, 1.0 / scale]), *spans)


def update_kernel(grad_ref, head_ref, table_ref, first_ref, second_ref, *out_refs):
    first_out, update_ref, weight_sum, update_sum = out_refs
    grad = grad_ref[...] + head_ref[...].astype(jnp.float32)
    first = BETA * first_ref[...] + (1.0 - BETA) * grad
    table = table_ref[...]
    update = first / (jnp.sqrt(second_ref[...]) + OPT_EPS) + DECAY * table
    first_out[...] = first
    update_ref[...] = update

    @pl.when(pl.program_id(0) == 0)
    def _():
        weight_sum[...] = jnp.zeros_like(weight_sum)
        update_sum[...] = jnp.zeros_like(update_sum)

    weight_sum[...] += jnp.sum(table * table, axis=0, keepdims=True)
    update_sum[...] += jnp.sum(update * update, axis=0, keepdims=True)


def table_update(grad, head, table, first, second):
    size, cols = table.shape
    block = size // 9 if size % 9 == 0 and size // 9 % 16 == 0 else size
    whole = pl.BlockSpec((block, cols), lambda step: (step, 0))
    line = pl.BlockSpec((1, cols), lambda step: (0, 0))
    moment, update, *sums = pl.pallas_call(
        update_kernel,
        grid=(size // block,),
        in_specs=[whole] * 5,
        out_specs=[whole, whole, line, line],
        out_shape=[jax.ShapeDtypeStruct((size, cols), jnp.float32)] * 2
        + [jax.ShapeDtypeStruct((1, cols), jnp.float32)] * 2,
        compiler_params=pltpu.CompilerParams(vmem_limit_bytes=56 * 2**20),
        cost_estimate=FREE,
        name="update",
    )(grad, head, table, first, second)
    return moment, update, tuple(jnp.sum(part)[None] for part in sums)


def wide_places():
    wide_me = lax.axis_index("wide")
    return wide_me % 2, wide_me // 2 % 2, wide_me // 4


def scattered_sum(give, keep):
    n_wide = lax.axis_size("wide")
    _, x, y = wide_places()

    def send(value, bit):
        return lax.ppermute(value.astype(jnp.bfloat16), "wide", swap_pairs(n_wide, bit))

    take = send(give, 1)
    half = keep.shape[1] // 2

    def chip(y_of, x_of, part):
        start, size = (2 * y_of + x_of, part * half, 0), (1, half, keep.shape[2])
        own, other = lax.dynamic_slice(keep, start, size), lax.dynamic_slice(take, start, size)
        return own[0].astype(jnp.float32) + other[0].astype(jnp.float32)

    upper_far = send(chip(1 - y, 1 - x, 0), 2)
    lower_far = send(chip(1 - y, 1 - x, 1), 4)
    upper_near = send(chip(y, 1 - x, 0), 2)
    lower_near = send(chip(1 - y, x, 1), 4)
    upper_far = send(chip(1 - y, x, 0) + upper_far.astype(jnp.float32), 4)
    lower_far = send(chip(y, 1 - x, 1) + lower_far.astype(jnp.float32), 2)
    own_upper = chip(y, x, 0) + upper_near.astype(jnp.float32) + upper_far.astype(jnp.float32)
    own_lower = chip(y, x, 1) + lower_near.astype(jnp.float32) + lower_far.astype(jnp.float32)
    return jnp.concatenate([own_upper, own_lower], axis=0)


def small_halved(value):
    n_wide = lax.axis_size("wide")
    for bit, place in list(zip((1, 2, 4), wide_places()))[::-1]:
        half = value.shape[1] // 2
        give = lax.dynamic_slice_in_dim(value, (1 - place) * half, half, 1).astype(jnp.bfloat16)
        keep = lax.dynamic_slice_in_dim(value, place * half, half, 1)
        value = keep + lax.ppermute(give, "wide", swap_pairs(n_wide, bit)).astype(jnp.float32)
    return value


def small_update(grad, first, second, weight):
    first = BETA * first + (1.0 - BETA) * grad.astype(jnp.float32)
    return first, first / (jnp.sqrt(second) + OPT_EPS) + DECAY * weight


def shards(
    token_ids,
    doc_ids,
    mlm_pos,
    mlm_labels,
    mlm_valid,
    table,
    table_m,
    table_v,
    small,
    small_m,
    small_v,
    layer,
    layer_m,
    layer_v,
    worker_err,
    server_err,
):
    n_wide, n_narrow = lax.axis_size("wide"), lax.axis_size("narrow")
    narrow_me = lax.axis_index("narrow")
    wide_me = lax.axis_index("wide")
    seqs = doc_ids.shape[0]
    paired = paired_mesh()
    vshard = table.shape[0]
    count = summed_over(jnp.sum(mlm_valid.astype(jnp.float32)), "wide")
    table_low, layer_low = table.astype(jnp.bfloat16), layer.astype(jnp.bfloat16)
    if paired:
        token_ids, mlm_labels, mlm_valid, doc_ids, mlm_pos = hosted_rows(
            token_ids, mlm_labels, mlm_valid, doc_ids, mlm_pos
        )
        owners = Owners(token_ids.reshape(n_narrow, n_wide * L), vshard)
        picked = packed_rows(owners.slots, table)
        layer_rows, picked = gathered_near(layer_low, picked)
    else:
        layer_rows = lax.all_gather(layer_low, "narrow", axis=0, tiled=True)
    weights = lax.all_gather(layer_rows, "wide", axis=1, tiled=True)
    if paired:

        def looked_up(room):
            rows = sent_around(picked[:, 0:room])
            return taken_rows(owners.behind_slots(room), jnp.concatenate(rows, axis=0))

        layer_rows, picked = together(layer_rows, picked)
        looked = looked_up(owners.room)
        looked = lax.cond(owners.full, lambda: looked_up(owners.count), lambda: looked)
        looked = lax.all_to_all(looked.reshape(n_wide, L, -1), "wide", 0, 0)
        looked = looked.transpose(1, 0, 2).reshape(1, L, D)
        looked, count, doc_ids, mlm_pos = together(looked, count, doc_ids, mlm_pos)
    else:
        local_ids = token_ids - narrow_me * vshard
        inside = (local_ids >= 0) & (local_ids < vshard)
        slots = jnp.where(inside, local_ids, vshard).reshape(-1)
        table_cols = lax.all_gather(table_low, "wide", axis=1, tiled=True)
        picked = jnp.take(table_cols, jnp.clip(local_ids, 0, vshard - 1), axis=0)
        picked = jnp.where(inside[..., None], picked, 0.0)
        looked = lax.psum_scatter(picked, "narrow", scatter_dimension=0, tiled=True)
    looked = looked.astype(jnp.float32)
    even_doc = (doc_ids % 2 == 0)[..., None]
    embedded = looked + small[0:L][None] + jnp.where(even_doc, small[L], small[L + 1])
    embedded = embedded.reshape(seqs * L, D)
    x0 = norm_rows(embedded, small[L + 2], small[L + 3])
    act = x0.astype(jnp.bfloat16)
    if paired:
        table_low, weights, act = together(table_low, weights, act)
        table_cols = lax.all_gather(table_low, "wide", axis=1, tiled=True)
    htwo, kept = layer_forward(embedded, x0, act, doc_ids, small, weights)
    hmask = jnp.take_along_axis(htwo.reshape(seqs, L, D), mlm_pos[..., None], axis=1)
    hmask = hmask.reshape(seqs * MPS, D).astype(jnp.bfloat16)
    if paired:
        group_h = gathered_near(hmask)
    else:
        group_h = lax.all_gather(hmask, "narrow", axis=0, tiled=True)
    vocab = narrow_me * vshard + jnp.arange(vshard)
    logits = jnp.where((vocab < VREAL)[None], matmul_nt(group_h, table_cols), -1000000000.0)
    labels = mlm_labels.reshape(-1)
    hit = vocab[None] == labels[:, None]
    top = jnp.max(logits, axis=1)
    total = jnp.sum(jnp.exp(logits - top[:, None]), axis=1)
    target = jnp.sum(jnp.where(hit, logits, 0.0), axis=1)
    if paired:
        stats = gathered_near(jnp.stack([top, total, target])[None])
        top, total, target = stats[0]
        for place in range(1, stats.shape[0]):
            top, total, target = merge_rows((top, total, target), tuple(stats[place]))
    else:
        top, total, target = joined((top, total, target), "narrow", merge_rows)
    lse = top + jnp.log(total)
    flags = mlm_valid.reshape(-1).astype(jnp.float32)
    own = seqs * MPS
    own_loss = lax.dynamic_slice_in_dim(flags * (lse - target), narrow_me * own, own)
    dlogit = (
        (jnp.exp(logits - lse[:, None]) - hit.astype(jnp.float32)) * (flags / count)[:, None]
    ).astype(jnp.bfloat16)
    dhmask = matmul(dlogit, table_cols)
    if paired:
        dhmask = scattered_near(dhmask)
        blocks = group_h.reshape(-1, n_wide, D // n_wide)
        table_head = jnp.einsum("sv,swc->wvc", dlogit, blocks, preferred_element_type=jnp.float32)
        table_head, dhmask = together(table_head.astype(jnp.bfloat16), dhmask)
        table_head = lax.psum_scatter(table_head, "wide", scatter_dimension=0)
    else:
        dhmask = lax.psum_scatter(dhmask, "narrow", scatter_dimension=0, tiled=True)
    dhtwo = (
        jnp.zeros((seqs, L, D), jnp.float32)
        .at[jnp.arange(seqs)[:, None], mlm_pos]
        .add(dhmask.reshape(seqs, MPS, D))
    )
    dembed, vectors, pieces = layer_backward(
        dhtwo.reshape(seqs * L, D), kept, doc_ids, small, weights
    )
    dembed_rows = dembed.reshape(seqs, L, D)
    small_grad = jnp.concatenate([jnp.sum(dembed_rows, axis=0), vectors], axis=0)
    mixed = pieces[0]
    if paired:
        cut = dembed.astype(jnp.bfloat16).reshape(L, n_wide, D // n_wide).transpose(1, 0, 2)
        cut = lax.all_to_all(cut, "wide", 0, 0).reshape(n_wide * L, D // n_wide)
        halved = small_halved(small_grad).astype(jnp.bfloat16)
        down, up = pieces[2], pieces[1]
        mixed.finish()
        spans = [span_of(layer_m, up.result, worker_err, 4 * D)]
        spans.append(span_of(layer_m, down.result, worker_err, 8 * D))
        cut, mixed.result, spans, table_head = together(
            jnp.concatenate([cut, halved]), mixed.result, spans, table_head
        )
        group_rows = lax.all_gather(cut, "narrow", axis=0)
    else:
        mixed.finish()
        group_rows = lax.all_gather(dembed_rows.astype(jnp.bfloat16), "narrow", axis=0, tiled=True)
        table_grad = matmul_tn(dlogit, group_h).at[slots].add(
            group_rows.reshape(-1, D).astype(jnp.float32), mode="drop"
        )
        cut = table_grad.astype(jnp.bfloat16).reshape(vshard, n_wide, D // n_wide)
        table_grad = lax.psum_scatter(cut.transpose(1, 0, 2), "wide", scatter_dimension=0)
        table_grad = table_grad.astype(jnp.float32)
    part_cols = layer.shape[1]
    if paired:
        spans.insert(0, span_of(layer_m, mixed.result, worker_err, 0))
        total = sum(amount for _, amount in spans)
        spans = [span for span, _ in spans]
        scale = total / (layer_m.shape[0] * layer_m.shape[1]) + MAG_EPS
        new_worker, give, keep = pressed(spans, scale, n_wide)
        server_in = scattered_sum(give, keep) / n_wide + server_err
    else:
        worker_grad = jnp.concatenate([piece.result for piece in pieces], axis=1)
        span = BETA * layer_m + (1.0 - BETA) * worker_grad.astype(jnp.float32) + worker_err[0]
        scale = jnp.mean(jnp.abs(span)) + MAG_EPS
        sent = scale * jnp.tanh(span / scale)
        new_worker = (span - sent)[None]
        summed = lax.psum(sent.astype(jnp.bfloat16), "wide").astype(jnp.float32)
        mixed = lax.dynamic_slice_in_dim(summed, wide_me * part_cols, part_cols, 1) / n_wide
        server_in = mixed + server_err
    sscale = jnp.mean(jnp.abs(server_in)) + MAG_EPS
    server_out = sscale * jnp.tanh(server_in / sscale)
    new_server = server_in - server_out
    server_low = server_out.astype(jnp.bfloat16)
    if paired:
        server_out, group_rows = together(server_out, group_rows)
        table_grad = added_rows(owners.slots, group_rows, vshard)
        table_mom, table_upd, table_norms = table_update(
            table_grad, table_head, table, table_m, table_v
        )
        eighth = D // n_wide
        small_grad = jnp.sum(group_rows[:, n_wide * L :].astype(jnp.float32), axis=0)
        small_grad = small_grad.astype(jnp.bfloat16)

        def own(value):
            return lax.dynamic_slice_in_dim(value, wide_me * eighth, eighth, 1)

        _, own_upd = small_update(small_grad, own(small_m), own(small_v), own(small))
        small_norm = jnp.where(narrow_me == 0, jnp.sum(own_upd * own_upd), 0.0)
    else:
        small_grad = lax.psum(small_grad, ("wide", "narrow"))
        table_mom = BETA * table_m + (1.0 - BETA) * table_grad
        table_upd = table_mom / (jnp.sqrt(table_v) + OPT_EPS) + DECAY * table
        table_norms = (jnp.sum(table * table)[None], jnp.sum(table_upd * table_upd)[None])
    new_m = lax.all_gather(server_low, "wide", axis=1, tiled=True)
    if paired:
        small_grad, new_m = together(small_grad, new_m)
        small_grad = lax.all_gather(small_grad, "wide", axis=1, tiled=True)
    small_mom, small_upd = small_update(small_grad, small_m, small_v, small)
    if not paired:
        small_norm = jnp.where((wide_me == 0) & (narrow_me == 0), jnp.sum(small_upd * small_upd), 0.0)
    layer_upd = server_out / (jnp.sqrt(layer_v) + OPT_EPS) + DECAY * layer
    column = wide_me * part_cols + jnp.arange(part_cols)
    which = (
        (column >= 3 * D).astype(jnp.int32)
        + (column >= 4 * D).astype(jnp.int32)
        + (column >= 4 * D + FF).astype(jnp.int32)
    )
    onehot = (which[:, None] == jnp.arange(4)[None]).astype(jnp.float32)
    wsq = jnp.sum(jnp.sum(layer * layer, axis=0)[:, None] * onehot, axis=0)
    usq = jnp.sum(jnp.sum(layer_upd * layer_upd, axis=0)[:, None] * onehot, axis=0)
    parts = jnp.concatenate([wsq, usq, *table_norms, jnp.sum(own_loss)[None], small_norm[None]])
    sums = summed_over(summed_over(parts, "wide"), "narrow")
    loss_sum = sums[10]
    wnorm = jnp.sqrt(jnp.concatenate([sums[0:4], sums[8:9], jnp.sum(small * small)[None]]))
    unorm = jnp.sqrt(jnp.concatenate([sums[4:8], sums[9:10], sums[11:12]]))
    ratio = wnorm / unorm
    new_layer = layer - RATE * jnp.sum(onehot * ratio[None, 0:4], axis=1)[None] * layer_upd
    new_table = table - RATE * ratio[4] * table_upd
    new_small = small - RATE * ratio[5] * small_upd
    return (
        jnp.stack([loss_sum, count]),
        new_table,
        table_mom,
        new_small,
        small_mom,
        new_layer,
        new_m.astype(jnp.float32),
        new_worker,
        new_server,
        jnp.stack([wnorm, unorm]),
    )


def solution(mesh):
    placed = (
        P("wide", None),
        P(("wide", "narrow"), None),
        P(("wide", "narrow"), None),
        P("wide", None),
        P("wide", None),
        P("narrow", "wide"),
        P("narrow", "wide"),
        P("narrow", "wide"),
        P(),
        P(),
        P(),
        P("narrow", "wide"),
        P("narrow", None),
        P("narrow", "wide"),
        P("wide", "narrow", None),
        P("narrow", "wide"),
    )
    return jax.shard_map(
        shards,
        mesh=mesh,
        in_specs=placed,
        out_specs=(
            P(),
            P("narrow", "wide"),
            P("narrow", "wide"),
            P(),
            P(),
            P("narrow", "wide"),
            P("narrow", None),
            P("wide", "narrow", None),
            P("narrow", "wide"),
            P(),
        ),
        check_vma=False,
    )
```

```python
import functools

import jax
import jax.numpy as jnp
from jax import lax
from jax.experimental import pallas as pl
from jax.experimental.pallas import tpu as pltpu
from jax.sharding import PartitionSpec as P

D = 1024
HEADS = 16
HEAD = 64
FF = 4096
VREAL = 30522
L = 512
MPS = 80


LN_EPS = 1e-12
BETA = 0.9
DECAY = 0.01
RATE = 0.25
OPT_EPS = 1e-06
MAG_EPS = 1e-08

FREE = pl.CostEstimate(flops=0, bytes_accessed=0, transcendentals=0)


def joined(value, axis, join):
    pieces = jax.tree.map(lambda part: lax.all_gather(part, axis), value)
    head = jax.tree.map(lambda part: part[0], pieces)
    tail = jax.tree.map(lambda part: part[1:], pieces)
    subtotal, _ = lax.scan(lambda subtotal, slab: (join(subtotal, slab), None), head, tail)
    return subtotal


def norm_rows(x, gain, shift):
    mean = jnp.mean(x, axis=-1, keepdims=True)
    cent = x - mean
    var = jnp.mean(cent * cent, axis=-1, keepdims=True)
    return cent * lax.rsqrt(var + LN_EPS) * gain + shift


def matmul(left, right):
    return jnp.dot(left, right, preferred_element_type=jnp.float32)


def matmul_tn(left, right):
    return lax.dot_general(
        left, right, (((0,), (0,)), ((), ())), preferred_element_type=jnp.float32
    )


def matmul_nt(left, right):
    return lax.dot_general(
        left, right, (((1,), (1,)), ((), ())), preferred_element_type=jnp.float32
    )


def attend_kernel(q_ref, k_ref, v_ref, key_doc_ref, query_doc_ref, out_ref, lse_ref):
    same = key_doc_ref[...] == query_doc_ref[...]
    lane = lax.broadcasted_iota(jnp.int32, (1, 2 * HEAD), 1)
    outs = []
    for head in range(2):
        mine = lane // HEAD == head
        query = jnp.where(mine, q_ref[...] * 0.125, 0).astype(jnp.bfloat16)
        scores = jnp.where(same, matmul_nt(k_ref[...], query), -1000000000.0)
        top = jnp.max(scores, axis=0, keepdims=True)
        power = jnp.exp(scores - top)
        total = jnp.sum(power, axis=0, keepdims=True)
        lse_ref[0, head : head + 1, :] = top + jnp.log(total)
        prob = (power * (1.0 / total)).astype(jnp.bfloat16)
        outs.append(matmul_tn(prob, v_ref[...]))
    out_ref[...] = jnp.where(lane < HEAD, outs[0], outs[1]).astype(jnp.bfloat16)


def head_pairs(offset):
    return pl.BlockSpec((L, 2 * HEAD), lambda pair: (0, offset * HEADS // 2 + pair))


def attend(qkv, docs):
    return pl.pallas_call(
        attend_kernel,
        grid=(HEADS // 2,),
        in_specs=[
            head_pairs(0),
            head_pairs(1),
            head_pairs(2),
            pl.BlockSpec((L, 1), lambda pair: (0, 0)),
            pl.BlockSpec((1, L), lambda pair: (0, 0)),
        ],
        out_specs=[head_pairs(0), pl.BlockSpec((1, 2, L), lambda pair: (pair, 0, 0))],
        out_shape=[
            jax.ShapeDtypeStruct((L, D), jnp.bfloat16),
            jax.ShapeDtypeStruct((HEADS // 2, 2, L), jnp.float32),
        ],
        compiler_params=pltpu.CompilerParams(vmem_limit_bytes=40 * 2**20),
        cost_estimate=FREE,
        name="attend",
    )(qkv, qkv, qkv, docs.reshape(L, 1), docs.reshape(1, L))


def attend_back_kernel(q_ref, k_ref, v_ref, do_ref, lse_ref, key_doc_ref, query_doc_ref, out_ref):
    pair = pl.program_id(0)
    same = key_doc_ref[...] == query_doc_ref[...]
    lane = lax.broadcasted_iota(jnp.int32, (1, 2 * HEAD), 1)
    both = []
    for head in range(2):
        mine = lane // HEAD == head
        query = jnp.where(mine, q_ref[...] * 0.125, 0).astype(jnp.bfloat16)
        dout = jnp.where(mine, do_ref[...], 0).astype(jnp.bfloat16)
        scores = jnp.where(same, matmul_nt(k_ref[...], query), -1000000000.0)
        prob = jnp.exp(scores - lse_ref[0, head : head + 1, :])
        dvalue = matmul(prob.astype(jnp.bfloat16), dout)
        dprob = matmul_nt(v_ref[...], dout)
        delta = jnp.sum(prob * dprob, axis=0, keepdims=True)
        dscore = (prob * (dprob - delta)).astype(jnp.bfloat16)
        both.append((matmul_tn(dscore, k_ref[...]) * 0.125, matmul(dscore, query), dvalue))
    for part in range(3):
        value = jnp.where(lane < HEAD, both[0][part], both[1][part]).astype(jnp.bfloat16)
        start = pl.multiple_of(part * D + pair * 2 * HEAD, 2 * HEAD)
        out_ref[:, pl.ds(start, 2 * HEAD)] = value


def attend_back(qkv, dout, lse, docs):
    return pl.pallas_call(
        attend_back_kernel,
        grid=(HEADS // 2,),
        in_specs=[
            head_pairs(0),
            head_pairs(1),
            head_pairs(2),
            head_pairs(0),
            pl.BlockSpec((1, 2, L), lambda pair: (pair, 0, 0)),
            pl.BlockSpec((L, 1), lambda pair: (0, 0)),
            pl.BlockSpec((1, L), lambda pair: (0, 0)),
        ],
        out_specs=pl.BlockSpec((L, 3 * D), lambda pair: (0, 0)),
        out_shape=jax.ShapeDtypeStruct((L, 3 * D), jnp.bfloat16),
        compiler_params=pltpu.CompilerParams(vmem_limit_bytes=40 * 2**20),
        cost_estimate=FREE,
        name="attend_back",
    )(qkv, qkv, qkv, dout, lse, docs.reshape(L, 1), docs.reshape(1, L))


def merge_rows(first, second):
    peak = jnp.maximum(first[0], second[0])
    total = first[1] * jnp.exp(first[0] - peak) + second[1] * jnp.exp(second[0] - peak)
    return (peak, total, first[2] + second[2])


def embed_back_kernel(dqkv_ref, weight_ref, drone_ref, embedded_ref, gain_ref, even_ref, *refs):
    dembed_ref, rows_ref, sums_ref, total = refs
    step = pl.program_id(0)
    dqkv = dqkv_ref[...]
    part = matmul_nt(dqkv, weight_ref[...])
    sums_ref[...] = jnp.sum(dqkv.astype(jnp.float32), axis=0, keepdims=True)

    @pl.when(step == 0)
    def _():
        total[...] = drone_ref[...] + part

    @pl.when(step > 0)
    def _():
        total[...] += part

    @pl.when(step == pl.num_programs(0) - 1)
    def _():
        grad = total[...]
        embedded = embedded_ref[...]
        cent = embedded - jnp.mean(embedded, axis=1, keepdims=True)
        scale = lax.rsqrt(jnp.mean(cent * cent, axis=1, keepdims=True) + LN_EPS)
        normed = cent * scale
        inner = grad * gain_ref[...]
        inner_mean = jnp.mean(inner, axis=1, keepdims=True)
        along = jnp.mean(inner * normed, axis=1, keepdims=True)
        dembed = scale * (inner - inner_mean - normed * along)
        dembed_ref[...] = dembed
        even = even_ref[...]
        rows_ref[0:1, :] = jnp.sum(grad * normed, axis=0, keepdims=True)
        rows_ref[1:2, :] = jnp.sum(grad, axis=0, keepdims=True)
        rows_ref[2:3, :] = jnp.sum(dembed * even, axis=0, keepdims=True)
        rows_ref[3:4, :] = jnp.sum(dembed * (1.0 - even), axis=0, keepdims=True)
        rows_ref[4:8, :] = jnp.zeros((4, D), jnp.float32)


def embed_back(dqkv, weights, drone, embedded, gain, even):
    tokens = dqkv.shape[0]
    whole = pl.BlockSpec((tokens, D), lambda step: (0, 0))
    return pl.pallas_call(
        embed_back_kernel,
        grid=(3,),
        in_specs=[
            pl.BlockSpec((tokens, D), lambda step: (0, step)),
            pl.BlockSpec((D, D), lambda step: (0, step)),
            whole,
            whole,
            pl.BlockSpec((1, D), lambda step: (0, 0)),
            pl.BlockSpec((tokens, 1), lambda step: (0, 0)),
        ],
        out_specs=[
            whole,
            pl.BlockSpec((8, D), lambda step: (0, 0)),
            pl.BlockSpec((1, D), lambda step: (0, step)),
        ],
        out_shape=[
            jax.ShapeDtypeStruct((tokens, D), jnp.float32),
            jax.ShapeDtypeStruct((8, D), jnp.float32),
            jax.ShapeDtypeStruct((1, 3 * D), jnp.float32),
        ],
        scratch_shapes=[pltpu.VMEM((tokens, D), jnp.float32)],
        compiler_params=pltpu.CompilerParams(vmem_limit_bytes=40 * 2**20),
        cost_estimate=FREE,
        name="embed_back",
    )(dqkv, weights, drone, embedded, gain[None], even)


def ffn_kernel(fin_ref, weight_ref, bias_ref, gated_ref, slope_ref):
    upper = matmul(fin_ref[...], weight_ref[...]) + bias_ref[...]
    below = 0.5 + 0.5 * lax.erf(upper * 0.7071067811865476)
    gated_ref[...] = (upper * below).astype(jnp.bfloat16)
    density = 0.3989422804014327 * jnp.exp(-0.5 * upper * upper)
    slope_ref[...] = (below + upper * density).astype(jnp.bfloat16)


def ffn_up(fin, weights, bias):
    tokens = fin.shape[0]
    block = 512
    first = 4 * D // block
    out = pl.BlockSpec((tokens, block), lambda step: (0, step))
    return pl.pallas_call(
        ffn_kernel,
        grid=(FF // block,),
        in_specs=[
            pl.BlockSpec((tokens, D), lambda step: (0, 0)),
            pl.BlockSpec((D, block), lambda step: (0, first + step)),
            pl.BlockSpec((1, block), lambda step: (0, step)),
        ],
        out_specs=[out, out],
        out_shape=[jax.ShapeDtypeStruct((tokens, FF), jnp.bfloat16)] * 2,
        compiler_params=pltpu.CompilerParams(vmem_limit_bytes=32 * 2**20),
        cost_estimate=pl.CostEstimate(flops=2 * tokens * D * FF, bytes_accessed=0, transcendentals=0),
        name="ffn_up",
    )(fin, weights, bias)


def layer_forward(embedded, x0, act, docs, small, weights):
    base = L + 2
    bias = jnp.concatenate([small[base + 6], jnp.zeros((D,), jnp.float32), small[base + 7]])
    qkv = (matmul(act, weights[:, 0 : 3 * D]) + bias).astype(jnp.bfloat16)
    out, lse = attend(qkv, docs)
    rone = x0 + (matmul(out, weights[:, 3 * D : 4 * D]) + small[base + 8])
    hone = norm_rows(rone, small[base + 2], small[base + 3])
    fin = hone.astype(jnp.bfloat16)
    gated, slope = ffn_up(fin, weights, small[base + 10 :].reshape(1, FF))
    rtwo = hone + (matmul_nt(gated, weights[:, 4 * D + FF :]) + small[base + 9])
    htwo = norm_rows(rtwo, small[base + 4], small[base + 5])
    return (htwo, (embedded, act, qkv, lse, out, rone, fin, slope, gated, rtwo))


def layer_backward(dhtwo, kept, docs, small, weights):
    embedded, act, qkv, lse, out, rone, fin, slope, gated, rtwo = kept
    base = L + 2
    _, pull = jax.vjp(norm_rows, rtwo, small[base + 4], small[base + 5])
    drtwo, dgain_two, dshift_two = pull(dhtwo)
    dffn = drtwo.astype(jnp.bfloat16)
    down = WorkerPiece((dffn, gated))
    dgated = matmul(dffn, weights[:, 4 * D + FF :])
    dupper = (dgated * slope.astype(jnp.float32)).astype(jnp.bfloat16)
    dupper = down.received(dupper)
    dupper = down.across(dupper)
    up = WorkerPiece((fin, dupper))
    dhone = drtwo + matmul_nt(dupper, weights[:, 4 * D : 4 * D + FF])
    _, pull = jax.vjp(norm_rows, rone, small[base + 2], small[base + 3])
    drone, dgain_one, dshift_one = pull(dhone)
    dattn = drone.astype(jnp.bfloat16)
    dout = matmul_nt(dattn, weights[:, 3 * D : 4 * D]).astype(jnp.bfloat16)
    dout = up.received(dout)
    dout = up.across(dout)
    dqkv = attend_back(qkv, dout, lse, docs)
    (dqkv,) = down.crossed(dqkv)
    down.finish()
    mixed = WorkerPiece((act, dqkv), (out, dattn))
    even = (docs.reshape(L, 1) % 2 == 0).astype(jnp.float32)
    dembed, embed_rows, bias_qkv = embed_back(
        mixed.across(dqkv), weights, drone, embedded, small[base], even
    )
    (dembed,) = up.crossed(dembed)
    up.finish()
    vectors = jnp.stack(
        [
            embed_rows[0],
            embed_rows[1],
            dgain_one,
            dshift_one,
            dgain_two,
            dshift_two,
            bias_qkv[0, 0:D],
            bias_qkv[0, 2 * D : 3 * D],
            jnp.sum(dattn, axis=0, dtype=jnp.float32),
            jnp.sum(dffn, axis=0, dtype=jnp.float32),
        ]
    )
    bias_up = jnp.sum(dupper, axis=0, dtype=jnp.float32).reshape(FF // D, D)
    vectors = jnp.concatenate([embed_rows[2:4], vectors, bias_up], axis=0)
    return (dembed, vectors, (mixed, up, down))


def paired_mesh():
    return lax.axis_size("wide") == 8 and lax.axis_size("narrow") == 4


def together(*values):
    return lax.optimization_barrier(values)


def swap_pairs(size, bit):
    return [(place, place ^ bit) for place in range(size)]


def cycle(size, by):
    return [(place, (place + by) % size) for place in range(size)]


def summed_over(value, axis):
    size = lax.axis_size(axis)
    if size & (size - 1):
        return lax.psum(value, axis)
    bit = 1
    while bit < size:
        value = value + lax.ppermute(value, axis, swap_pairs(size, bit))
        bit *= 2
    return value


def gathered_near(value, beside=None):
    size = lax.axis_size("narrow")
    rows = value.shape[0]
    around = [value]
    for by in range(1, size):
        around.append(lax.ppermute(value, "narrow", cycle(size, size - by)))
    if beside is not None:
        *around, beside = together(*around, beside)
    place = lax.axis_index("narrow")
    whole = jnp.zeros((size * rows,) + value.shape[1:], value.dtype)
    for by, part in enumerate(around):
        start = lax.rem(place + by, size) * rows
        whole = lax.dynamic_update_slice_in_dim(whole, part, start, 0)
    return whole if beside is None else (whole, beside)


def scattered_near(value):
    size = lax.axis_size("narrow")
    rows = value.shape[0] // size
    place = lax.axis_index("narrow")
    total = lax.dynamic_slice_in_dim(value, place * rows, rows, 0)
    for by in range(1, size):
        target = lax.rem(place + by, size)
        give = lax.dynamic_slice_in_dim(value, target * rows, rows, 0).astype(jnp.bfloat16)
        take = lax.ppermute(give, "narrow", cycle(size, by))
        total = total + take.astype(jnp.float32)
    return total


def sent_around(blocks):
    size = lax.axis_size("narrow")
    place = lax.axis_index("narrow")

    def block(by):
        return lax.dynamic_index_in_dim(blocks, lax.rem(place + by, size), 0, keepdims=False)

    return [block(0)] + [
        lax.ppermute(block(by), "narrow", cycle(size, by)) for by in range(1, size)
    ]


def block_kernel(steps, place_ref, *refs):
    pairs = len(steps) - 1
    lefts, rights, terms, out_ref = refs[:pairs], refs[pairs : 2 * pairs], refs[2 * pairs : -1], refs[-1]
    step = pl.program_id(0)
    for index in range(pairs):

        @pl.when((step >= steps[index]) & (step < steps[index + 1]))
        def _():
            total = matmul_tn(lefts[index][...], rights[index][...])
            for term_ref in terms:
                total = total + term_ref[...].astype(jnp.float32)
            out_ref[...] = total.astype(jnp.bfloat16)


def gradient_block(pairs, place, terms):
    block = D
    size = D // lax.axis_size("narrow")
    steps = [0]
    for _, right in pairs:
        steps.append(steps[-1] + right.shape[1] // block)
    tokens = pairs[0][0].shape[0]

    def right_of(index):
        low, count = steps[index], steps[index + 1] - steps[index]
        return pl.BlockSpec(
            (tokens, block), lambda step, place: (0, jnp.clip(step - low, 0, count - 1))
        )

    piece = pl.BlockSpec((size, block), lambda step, place: (0, step))
    return pl.pallas_call(
        functools.partial(block_kernel, steps),
        grid_spec=pltpu.PrefetchScalarGridSpec(
            num_scalar_prefetch=1,
            grid=(steps[-1],),
            in_specs=[pl.BlockSpec((tokens, size), lambda step, place: (0, place[0]))] * len(pairs)
            + [right_of(index) for index in range(len(pairs))]
            + [piece] * len(terms),
            out_specs=piece,
        ),
        out_shape=jax.ShapeDtypeStruct((size, steps[-1] * block), jnp.bfloat16),
        compiler_params=pltpu.CompilerParams(vmem_limit_bytes=24 * 2**20),
        cost_estimate=FREE,
        name="gradient_block",
    )(place[None], *[left for left, _ in pairs], *[right for _, right in pairs], *terms)


class WorkerPiece:
    def __init__(self, *pairs):
        self.pairs = pairs
        self.paired = paired_mesh()
        if not self.paired:
            return
        self.core = lax.axis_index("wide") % 2
        self.pair, self.side = lax.axis_index("narrow") // 2, lax.axis_index("narrow") % 2
        cores = swap_pairs(lax.axis_size("wide"), 1)
        self.far = lax.ppermute(self.block(1 - self.core, 1 - self.side), "wide", cores)
        self.near = lax.ppermute(self.block(1 - self.core, self.side), "wide", cores)

    def block(self, core, side, *terms):
        return gradient_block(self.pairs, 2 * core + side, terms)

    def received(self, value):
        if self.paired:
            value, self.far, self.near = together(value, self.far, self.near)
        return value

    def across(self, value):
        if self.paired:
            sides = swap_pairs(lax.axis_size("narrow"), 1)
            away = self.block(self.core, 1 - self.side, self.far)
            away, value = together(away, value)
            self.away = lax.ppermute(away, "narrow", sides)
        return value

    def crossed(self, *values):
        if self.paired:
            *values, self.away = together(*values, self.away)
        return values

    def finish(self, *values):
        if not self.paired:
            blocks = [matmul_tn(left, right).astype(jnp.bfloat16) for left, right in self.pairs]
            grad = jnp.concatenate(blocks, axis=1)
            self.result = lax.psum_scatter(grad, "narrow", scatter_dimension=0, tiled=True)
            return values
        n_wide, n_narrow = lax.axis_size("wide"), lax.axis_size("narrow")
        total = self.block(self.core, self.side, self.near, self.away)
        moves = []
        for wide in range(n_wide):
            for narrow in range(n_narrow):
                if narrow // 2 != wide % 2:
                    target_wide = wide - wide % 2 + narrow // 2
                    target = target_wide * n_narrow + 2 * (wide % 2) + narrow % 2
                    moves.append((wide * n_narrow + narrow, target))
        total, *values = together(total, *values)
        moved = lax.ppermute(total, ("wide", "narrow"), moves)
        self.result = jnp.where(self.pair == self.core, total, moved)
        return values


def hosted_rows(token_ids, mlm_labels, mlm_valid, doc_ids, mlm_pos):
    n_wide, n_narrow = lax.axis_size("wide"), lax.axis_size("narrow")
    packed = jnp.concatenate([token_ids, mlm_labels, mlm_valid], axis=1)[None]
    for bit, place in zip((1, 2, 4), wide_places()):
        other = lax.ppermute(packed, "wide", swap_pairs(n_wide, bit))
        first, second = jnp.where(place == 0, packed, other), jnp.where(place == 0, other, packed)
        packed = jnp.concatenate([first, second], axis=0)
    width = packed.shape[2]
    hosted = packed.reshape(n_wide // 2, 2, 2, 2, width).transpose(1, 2, 0, 3, 4)
    hosted = hosted.reshape(n_narrow, n_wide, width)
    column = lax.dynamic_index_in_dim(hosted, lax.axis_index("wide"), 1, keepdims=False)
    moves = []
    for wide in range(n_wide):
        for row in range(n_narrow):
            target_wide = wide - wide % 2 + row % 2
            target_narrow = 2 * (wide % 2) + row // 2
            moves.append((wide * n_narrow + row, target_wide * n_narrow + target_narrow))
    own = lax.ppermute(jnp.concatenate([doc_ids, mlm_pos], axis=1), ("wide", "narrow"), moves)
    return (
        hosted[:, :, 0:L],
        column[:, L : L + MPS],
        column[:, L + MPS :],
        own[:, 0:L],
        own[:, L:],
    )


STREAMS = 2


class Owners:
    def __init__(self, tokens, vshard):
        size = lax.axis_size("narrow")
        place = lax.axis_index("narrow")
        count = tokens.shape[1]
        self.room = count * 7 // 16
        owner = tokens // vshard
        held = (owner[None] == jnp.arange(size)[:, None, None]).astype(jnp.bfloat16)
        tiles = held.reshape(-1, count // 128, 128)
        order = jnp.arange(128)
        within = jnp.einsum(
            "btl,lm->btm",
            tiles,
            (order[:, None] < order[None]).astype(jnp.bfloat16),
            preferred_element_type=jnp.float32,
        )
        sums = jnp.sum(tiles.astype(jnp.float32), axis=2)
        tile = jnp.arange(count // 128)
        before = jnp.sum(jnp.where(tile[:, None] < tile[None], sums[:, :, None], 0.0), axis=1)
        rank = (within + before[..., None]).reshape(size, size, count) * held.astype(jnp.float32)
        rank = jnp.sum(rank, axis=0).astype(jnp.int32)
        self.full = jnp.max(jnp.sum(sums, axis=1)) > self.room
        self.count, self.vshard = count, vshard
        own = lax.dynamic_index_in_dim(owner, place, 0, keepdims=False)
        self.rank = lax.dynamic_index_in_dim(rank, place, 0, keepdims=False)
        self.behind = lax.rem(place - own + size, size)
        self.slots = jnp.where(owner == place, tokens - place * vshard, vshard)

    def behind_slots(self, room):
        return self.behind * room + jnp.minimum(self.rank, room - 1)


def pack_kernel(ids_ref, table_ref, out_ref, held, *rows):
    step, count, size = pl.program_id(0), out_ref.shape[1], table_ref.shape[0]

    @pl.when(step == 0)
    def _():
        held[0:size, :] = table_ref[...]
        held[size:, :] = jnp.zeros((8, table_ref.shape[1]), jnp.float32)
        for part in rows:
            part[...] = jnp.zeros_like(part)

    base = [(step * len(rows) + index) * count for index in range(len(rows))]

    def some(turn, used):
        used = list(used)
        for by in range(8):
            for index, part in enumerate(rows):
                place = ids_ref[base[index] + turn * 8 + by]
                part[pl.ds(used[index], 1), :] = held[pl.ds(place, 1), :]
                used[index] = used[index] + jnp.where(place < size, 1, 0)
        return tuple(used)

    lax.fori_loop(0, count // 8, some, (0,) * len(rows))
    for index, part in enumerate(rows):
        out_ref[index] = part[0:count, :].astype(out_ref.dtype)


def packed_rows(ids, table):
    size, cols = table.shape
    places, count = ids.shape
    return pl.pallas_call(
        pack_kernel,
        grid_spec=pltpu.PrefetchScalarGridSpec(
            num_scalar_prefetch=1,
            grid=(places // STREAMS,),
            in_specs=[pl.BlockSpec((size, cols), lambda step, ids: (0, 0))],
            out_specs=pl.BlockSpec((STREAMS, count, cols), lambda step, ids: (step, 0, 0)),
            scratch_shapes=[pltpu.VMEM((size + 8, cols), jnp.float32)]
            + [pltpu.VMEM((count + 8, cols), jnp.float32)] * STREAMS,
        ),
        out_shape=jax.ShapeDtypeStruct((places, count, cols), jnp.bfloat16),
        compiler_params=pltpu.CompilerParams(vmem_limit_bytes=40 * 2**20),
        cost_estimate=pl.CostEstimate(flops=0, bytes_accessed=0, transcendentals=0),
        name="pack_rows",
    )(ids.reshape(-1), table)


def take_kernel(ids_ref, table_ref, out_ref, held, rows):
    held[...] = table_ref[...].astype(jnp.float32)

    @pl.loop(0, out_ref.shape[0], step=16)
    def _(first):
        for by in range(16):
            rows[pl.ds(first + by, 1), :] = held[pl.ds(ids_ref[first + by], 1), :]

    out_ref[...] = rows[...].astype(out_ref.dtype)


def taken_rows(ids, table):
    count, cols = ids.shape[0], table.shape[1]
    return pl.pallas_call(
        take_kernel,
        grid_spec=pltpu.PrefetchScalarGridSpec(
            num_scalar_prefetch=1,
            grid=(1,),
            in_specs=[pl.BlockSpec(table.shape, lambda step, ids: (0, 0))],
            out_specs=pl.BlockSpec((count, cols), lambda step, ids: (0, 0)),
            scratch_shapes=[
                pltpu.VMEM(table.shape, jnp.float32),
                pltpu.VMEM((count, cols), jnp.float32),
            ],
        ),
        out_shape=jax.ShapeDtypeStruct((count, cols), table.dtype),
        compiler_params=pltpu.CompilerParams(vmem_limit_bytes=40 * 2**20),
        cost_estimate=FREE,
        name="take_rows",
    )(ids, table)


def add_kernel(ids_ref, values_ref, out_ref, rows, *sums):
    size, length = out_ref.shape[0], rows.shape[1]
    for part in sums:
        part[...] = jnp.zeros_like(part)
    rows[...] = values_ref[:, 0:length, :].astype(jnp.float32)

    @pl.loop(0, length, step=8)
    def _(first):
        for by in range(8):
            for index, part in enumerate(sums):
                place = ids_ref[index * length + first + by]
                part[pl.ds(place, 1), :] += rows[index, pl.ds(first + by, 1), :]

    total = sums[0][0:size, :]
    for part in sums[1:]:
        total = total + part[0:size, :]
    out_ref[...] = total


def added_rows(ids, values, size):
    places, length = ids.shape
    cols = values.shape[2]
    return pl.pallas_call(
        add_kernel,
        grid_spec=pltpu.PrefetchScalarGridSpec(
            num_scalar_prefetch=1,
            grid=(1,),
            in_specs=[pl.BlockSpec(values.shape, lambda step, ids: (0, 0, 0))],
            out_specs=pl.BlockSpec((size, cols), lambda step, ids: (0, 0)),
            scratch_shapes=[pltpu.VMEM((places, length, cols), jnp.float32)]
            + [pltpu.VMEM((size + 8, cols), jnp.float32)] * places,
        ),
        out_shape=jax.ShapeDtypeStruct((size, cols), jnp.float32),
        compiler_params=pltpu.CompilerParams(vmem_limit_bytes=56 * 2**20),
        cost_estimate=FREE,
        name="add_rows",
    )(ids.reshape(-1), values)


def span_kernel(momentum_ref, grad_ref, error_ref, span_ref, sum_ref):
    grad = grad_ref[...].astype(jnp.float32)
    span = BETA * momentum_ref[...] + (1.0 - BETA) * grad + error_ref[0]
    span_ref[...] = span

    @pl.when(pl.program_id(0) == 0)
    def _():
        sum_ref[...] = jnp.zeros_like(sum_ref)

    sum_ref[...] += jnp.sum(jnp.abs(span), axis=0, keepdims=True)


def span_of(momentum, grad, error, start):
    rows, cols = grad.shape
    block = 1024
    first = start // block
    span, sums = pl.pallas_call(
        span_kernel,
        grid=(cols // block,),
        in_specs=[
            pl.BlockSpec((rows, block), lambda step: (0, first + step)),
            pl.BlockSpec((rows, block), lambda step: (0, step)),
            pl.BlockSpec((1, rows, block), lambda step: (0, 0, first + step)),
        ],
        out_specs=[
            pl.BlockSpec((rows, block), lambda step: (0, step)),
            pl.BlockSpec((1, block), lambda step: (0, 0)),
        ],
        out_shape=[
            jax.ShapeDtypeStruct((rows, cols), jnp.float32),
            jax.ShapeDtypeStruct((1, block), jnp.float32),
        ],
        compiler_params=pltpu.CompilerParams(vmem_limit_bytes=60 * 2**20),
        cost_estimate=pl.CostEstimate(flops=0, bytes_accessed=2 * 10**7, transcendentals=0),
        name="span",
    )(momentum, grad, error)
    return span, jnp.sum(sums)


def press_kernel(steps, core_ref, scale_ref, *refs):
    *span_refs, error_ref, give_ref, keep_ref = refs
    core = pl.program_id(2)
    step = pressed_step(pl.program_id(0), pl.program_id(1), core)
    scale = scale_ref[0]
    inverse = scale_ref[1]
    for index, span_ref in enumerate(span_refs):

        @pl.when((step >= steps[index]) & (step < steps[index + 1]))
        def _():
            span = span_ref[...]
            sent = scale * jnp.tanh(span * inverse)
            error_ref[0] = span - sent
            low = sent.astype(jnp.bfloat16)

            @pl.when(core == core_ref[0])
            def _():
                keep_ref[0] = low

            @pl.when(core != core_ref[0])
            def _():
                give_ref[0] = low


def pressed_step(chip, column, core):
    return (2 * chip + core) * 3 + column


def pressed(spans, scale, parts):
    rows = spans[0].shape[0]
    cols = sum(span.shape[1] for span in spans)
    block = cols // parts // 3
    steps = [0]
    for span in spans:
        steps.append(steps[-1] + span.shape[1] // block)

    def of(index):
        low, count = steps[index], steps[index + 1] - steps[index]

        def place(chip, column, core, _):
            return (0, jnp.clip(pressed_step(chip, column, core) - low, 0, count - 1))

        return pl.BlockSpec((rows, block), place)

    half = pl.BlockSpec((1, rows, block), lambda chip, column, core, _: (chip, 0, column))
    half_shape = jax.ShapeDtypeStruct((parts // 2, rows, cols // parts), jnp.bfloat16)
    return pl.pallas_call(
        functools.partial(press_kernel, steps),
        grid_spec=pltpu.PrefetchScalarGridSpec(
            num_scalar_prefetch=1,
            grid=(parts // 2, 3, 2),
            in_specs=[pl.BlockSpec(memory_space=pltpu.SMEM)] + [of(i) for i in range(len(spans))],
            out_specs=[
                pl.BlockSpec(
                    (1, rows, block),
                    lambda chip, column, core, _: (0, 0, pressed_step(chip, column, core)),
                ),
                half,
                half,
            ],
        ),
        out_shape=[jax.ShapeDtypeStruct((1, rows, cols), jnp.float32), half_shape, half_shape],
        compiler_params=pltpu.CompilerParams(vmem_limit_bytes=60 * 2**20),
        cost_estimate=FREE,
        name="press",
    )(wide_places()[0][None], jnp.stack([scale, 1.0 / scale]), *spans)


def update_kernel(grad_ref, head_ref, table_ref, first_ref, second_ref, *out_refs):
    first_out, update_ref, weight_sum, update_sum = out_refs
    grad = grad_ref[...] + head_ref[...].astype(jnp.float32)
    first = BETA * first_ref[...] + (1.0 - BETA) * grad
    table = table_ref[...]
    update = first / (jnp.sqrt(second_ref[...]) + OPT_EPS) + DECAY * table
    first_out[...] = first
    update_ref[...] = update

    @pl.when(pl.program_id(0) == 0)
    def _():
        weight_sum[...] = jnp.zeros_like(weight_sum)
        update_sum[...] = jnp.zeros_like(update_sum)

    weight_sum[...] += jnp.sum(table * table, axis=0, keepdims=True)
    update_sum[...] += jnp.sum(update * update, axis=0, keepdims=True)


def table_update(grad, head, table, first, second):
    size, cols = table.shape
    block = size // 9 if size % 9 == 0 and size // 9 % 16 == 0 else size
    whole = pl.BlockSpec((block, cols), lambda step: (step, 0))
    line = pl.BlockSpec((1, cols), lambda step: (0, 0))
    moment, update, *sums = pl.pallas_call(
        update_kernel,
        grid=(size // block,),
        in_specs=[whole] * 5,
        out_specs=[whole, whole, line, line],
        out_shape=[jax.ShapeDtypeStruct((size, cols), jnp.float32)] * 2
        + [jax.ShapeDtypeStruct((1, cols), jnp.float32)] * 2,
        compiler_params=pltpu.CompilerParams(vmem_limit_bytes=56 * 2**20),
        cost_estimate=FREE,
        name="update",
    )(grad, head, table, first, second)
    return moment, update, tuple(jnp.sum(part)[None] for part in sums)


def wide_places():
    wide_me = lax.axis_index("wide")
    return wide_me % 2, wide_me // 2 % 2, wide_me // 4


def scattered_sum(give, keep):
    n_wide = lax.axis_size("wide")
    _, x, y = wide_places()

    def send(value, bit):
        return lax.ppermute(value.astype(jnp.bfloat16), "wide", swap_pairs(n_wide, bit))

    take = send(give, 1)
    half = keep.shape[1] // 2

    def chip(y_of, x_of, part):
        start, size = (2 * y_of + x_of, part * half, 0), (1, half, keep.shape[2])
        own, other = lax.dynamic_slice(keep, start, size), lax.dynamic_slice(take, start, size)
        return own[0].astype(jnp.float32) + other[0].astype(jnp.float32)

    upper_far = send(chip(1 - y, 1 - x, 0), 2)
    lower_far = send(chip(1 - y, 1 - x, 1), 4)
    upper_near = send(chip(y, 1 - x, 0), 2)
    lower_near = send(chip(1 - y, x, 1), 4)
    upper_far = send(chip(1 - y, x, 0) + upper_far.astype(jnp.float32), 4)
    lower_far = send(chip(y, 1 - x, 1) + lower_far.astype(jnp.float32), 2)
    own_upper = chip(y, x, 0) + upper_near.astype(jnp.float32) + upper_far.astype(jnp.float32)
    own_lower = chip(y, x, 1) + lower_near.astype(jnp.float32) + lower_far.astype(jnp.float32)
    return jnp.concatenate([own_upper, own_lower], axis=0)


def small_halved(value):
    n_wide = lax.axis_size("wide")
    for bit, place in list(zip((1, 2, 4), wide_places()))[::-1]:
        half = value.shape[1] // 2
        give = lax.dynamic_slice_in_dim(value, (1 - place) * half, half, 1).astype(jnp.bfloat16)
        keep = lax.dynamic_slice_in_dim(value, place * half, half, 1)
        value = keep + lax.ppermute(give, "wide", swap_pairs(n_wide, bit)).astype(jnp.float32)
    return value


def small_update(grad, first, second, weight):
    first = BETA * first + (1.0 - BETA) * grad.astype(jnp.float32)
    return first, first / (jnp.sqrt(second) + OPT_EPS) + DECAY * weight


def shards(
    token_ids,
    doc_ids,
    mlm_pos,
    mlm_labels,
    mlm_valid,
    table,
    table_m,
    table_v,
    small,
    small_m,
    small_v,
    layer,
    layer_m,
    layer_v,
    worker_err,
    server_err,
):
    n_wide, n_narrow = lax.axis_size("wide"), lax.axis_size("narrow")
    narrow_me = lax.axis_index("narrow")
    wide_me = lax.axis_index("wide")
    seqs = doc_ids.shape[0]
    paired = paired_mesh()
    vshard = table.shape[0]
    count = summed_over(jnp.sum(mlm_valid.astype(jnp.float32)), "wide")
    table_low, layer_low = table.astype(jnp.bfloat16), layer.astype(jnp.bfloat16)
    if paired:
        token_ids, mlm_labels, mlm_valid, doc_ids, mlm_pos = hosted_rows(
            token_ids, mlm_labels, mlm_valid, doc_ids, mlm_pos
        )
        owners = Owners(token_ids.reshape(n_narrow, n_wide * L), vshard)
        picked = packed_rows(owners.slots, table)
        layer_rows, picked = gathered_near(layer_low, picked)
    else:
        layer_rows = lax.all_gather(layer_low, "narrow", axis=0, tiled=True)
    weights = lax.all_gather(layer_rows, "wide", axis=1, tiled=True)
    if paired:

        def looked_up(room):
            rows = sent_around(picked[:, 0:room])
            return taken_rows(owners.behind_slots(room), jnp.concatenate(rows, axis=0))

        layer_rows, picked = together(layer_rows, picked)
        looked = looked_up(owners.room)
        looked = lax.cond(owners.full, lambda: looked_up(owners.count), lambda: looked)
        looked = lax.all_to_all(looked.reshape(n_wide, L, -1), "wide", 0, 0)
        looked = looked.transpose(1, 0, 2).reshape(1, L, D)
        looked, count, doc_ids, mlm_pos = together(looked, count, doc_ids, mlm_pos)
    else:
        local_ids = token_ids - narrow_me * vshard
        inside = (local_ids >= 0) & (local_ids < vshard)
        slots = jnp.where(inside, local_ids, vshard).reshape(-1)
        table_cols = lax.all_gather(table_low, "wide", axis=1, tiled=True)
        picked = jnp.take(table_cols, jnp.clip(local_ids, 0, vshard - 1), axis=0)
        picked = jnp.where(inside[..., None], picked, 0.0)
        looked = lax.psum_scatter(picked, "narrow", scatter_dimension=0, tiled=True)
    looked = looked.astype(jnp.float32)
    even_doc = (doc_ids % 2 == 0)[..., None]
    embedded = looked + small[0:L][None] + jnp.where(even_doc, small[L], small[L + 1])
    embedded = embedded.reshape(seqs * L, D)
    x0 = norm_rows(embedded, small[L + 2], small[L + 3])
    act = x0.astype(jnp.bfloat16)
    if paired:
        table_low, weights, act = together(table_low, weights, act)
        table_cols = lax.all_gather(table_low, "wide", axis=1, tiled=True)
    htwo, kept = layer_forward(embedded, x0, act, doc_ids, small, weights)
    hmask = jnp.take_along_axis(htwo.reshape(seqs, L, D), mlm_pos[..., None], axis=1)
    hmask = hmask.reshape(seqs * MPS, D).astype(jnp.bfloat16)
    if paired:
        group_h = gathered_near(hmask)
    else:
        group_h = lax.all_gather(hmask, "narrow", axis=0, tiled=True)
    vocab = narrow_me * vshard + jnp.arange(vshard)
    logits = jnp.where((vocab < VREAL)[None], matmul_nt(group_h, table_cols), -1000000000.0)
    labels = mlm_labels.reshape(-1)
    hit = vocab[None] == labels[:, None]
    top = jnp.max(logits, axis=1)
    total = jnp.sum(jnp.exp(logits - top[:, None]), axis=1)
    target = jnp.sum(jnp.where(hit, logits, 0.0), axis=1)
    if paired:
        stats = gathered_near(jnp.stack([top, total, target])[None])
        top, total, target = stats[0]
        for place in range(1, stats.shape[0]):
            top, total, target = merge_rows((top, total, target), tuple(stats[place]))
    else:
        top, total, target = joined((top, total, target), "narrow", merge_rows)
    lse = top + jnp.log(total)
    flags = mlm_valid.reshape(-1).astype(jnp.float32)
    own = seqs * MPS
    own_loss = lax.dynamic_slice_in_dim(flags * (lse - target), narrow_me * own, own)
    dlogit = (
        (jnp.exp(logits - lse[:, None]) - hit.astype(jnp.float32)) * (flags / count)[:, None]
    ).astype(jnp.bfloat16)
    dhmask = matmul(dlogit, table_cols)
    if paired:
        dhmask = scattered_near(dhmask)
        blocks = group_h.reshape(-1, n_wide, D // n_wide)
        table_head = jnp.einsum("sv,swc->wvc", dlogit, blocks, preferred_element_type=jnp.float32)
        table_head, dhmask = together(table_head.astype(jnp.bfloat16), dhmask)
        table_head = lax.psum_scatter(table_head, "wide", scatter_dimension=0)
    else:
        dhmask = lax.psum_scatter(dhmask, "narrow", scatter_dimension=0, tiled=True)
    dhtwo = (
        jnp.zeros((seqs, L, D), jnp.float32)
        .at[jnp.arange(seqs)[:, None], mlm_pos]
        .add(dhmask.reshape(seqs, MPS, D))
    )
    dembed, vectors, pieces = layer_backward(
        dhtwo.reshape(seqs * L, D), kept, doc_ids, small, weights
    )
    dembed_rows = dembed.reshape(seqs, L, D)
    small_grad = jnp.concatenate([jnp.sum(dembed_rows, axis=0), vectors], axis=0)
    mixed = pieces[0]
    if paired:
        cut = dembed.astype(jnp.bfloat16).reshape(L, n_wide, D // n_wide).transpose(1, 0, 2)
        cut = lax.all_to_all(cut, "wide", 0, 0).reshape(n_wide * L, D // n_wide)
        halved = small_halved(small_grad).astype(jnp.bfloat16)
        down, up = pieces[2], pieces[1]
        mixed.away, down.result = together(mixed.away, down.result)
        mixed.finish()
        spans = [span_of(layer_m, up.result, worker_err, 4 * D)]
        spans.append(span_of(layer_m, down.result, worker_err, 8 * D))
        cut, mixed.result, spans, table_head = together(
            jnp.concatenate([cut, halved]), mixed.result, spans, table_head
        )
        group_rows = lax.all_gather(cut, "narrow", axis=0)
    else:
        mixed.finish()
        group_rows = lax.all_gather(dembed_rows.astype(jnp.bfloat16), "narrow", axis=0, tiled=True)
        table_grad = matmul_tn(dlogit, group_h).at[slots].add(
            group_rows.reshape(-1, D).astype(jnp.float32), mode="drop"
        )
        cut = table_grad.astype(jnp.bfloat16).reshape(vshard, n_wide, D // n_wide)
        table_grad = lax.psum_scatter(cut.transpose(1, 0, 2), "wide", scatter_dimension=0)
        table_grad = table_grad.astype(jnp.float32)
    part_cols = layer.shape[1]
    if paired:
        spans.insert(0, span_of(layer_m, mixed.result, worker_err, 0))
        total = sum(amount for _, amount in spans)
        spans = [span for span, _ in spans]
        scale = total / (layer_m.shape[0] * layer_m.shape[1]) + MAG_EPS
        new_worker, give, keep = pressed(spans, scale, n_wide)
        server_in = scattered_sum(give, keep) / n_wide + server_err
    else:
        worker_grad = jnp.concatenate([piece.result for piece in pieces], axis=1)
        span = BETA * layer_m + (1.0 - BETA) * worker_grad.astype(jnp.float32) + worker_err[0]
        scale = jnp.mean(jnp.abs(span)) + MAG_EPS
        sent = scale * jnp.tanh(span / scale)
        new_worker = (span - sent)[None]
        summed = lax.psum(sent.astype(jnp.bfloat16), "wide").astype(jnp.float32)
        mixed = lax.dynamic_slice_in_dim(summed, wide_me * part_cols, part_cols, 1) / n_wide
        server_in = mixed + server_err
    sscale = jnp.mean(jnp.abs(server_in)) + MAG_EPS
    server_out = sscale * jnp.tanh(server_in / sscale)
    new_server = server_in - server_out
    server_low = server_out.astype(jnp.bfloat16)
    if paired:
        server_out, group_rows = together(server_out, group_rows)
        table_grad = added_rows(owners.slots, group_rows, vshard)
        table_mom, table_upd, table_norms = table_update(
            table_grad, table_head, table, table_m, table_v
        )
        eighth = D // n_wide
        small_grad = jnp.sum(group_rows[:, n_wide * L :].astype(jnp.float32), axis=0)
        small_grad = small_grad.astype(jnp.bfloat16)

        def own(value):
            return lax.dynamic_slice_in_dim(value, wide_me * eighth, eighth, 1)

        _, own_upd = small_update(small_grad, own(small_m), own(small_v), own(small))
        small_norm = jnp.where(narrow_me == 0, jnp.sum(own_upd * own_upd), 0.0)
    else:
        small_grad = lax.psum(small_grad, ("wide", "narrow"))
        table_mom = BETA * table_m + (1.0 - BETA) * table_grad
        table_upd = table_mom / (jnp.sqrt(table_v) + OPT_EPS) + DECAY * table
        table_norms = (jnp.sum(table * table)[None], jnp.sum(table_upd * table_upd)[None])
    new_m = lax.all_gather(server_low, "wide", axis=1, tiled=True)
    if paired:
        small_grad, new_m, table_norms = together(small_grad, new_m, table_norms)
        small_grad = lax.all_gather(small_grad, "wide", axis=1, tiled=True)
    if not paired:
        _, small_upd = small_update(small_grad, small_m, small_v, small)
        small_norm = jnp.where((wide_me == 0) & (narrow_me == 0), jnp.sum(small_upd * small_upd), 0.0)
    layer_upd = server_out / (jnp.sqrt(layer_v) + OPT_EPS) + DECAY * layer
    column = wide_me * part_cols + jnp.arange(part_cols)
    which = (
        (column >= 3 * D).astype(jnp.int32)
        + (column >= 4 * D).astype(jnp.int32)
        + (column >= 4 * D + FF).astype(jnp.int32)
    )
    onehot = (which[:, None] == jnp.arange(4)[None]).astype(jnp.float32)
    wsq = jnp.sum(jnp.sum(layer * layer, axis=0)[:, None] * onehot, axis=0)
    usq = jnp.sum(jnp.sum(layer_upd * layer_upd, axis=0)[:, None] * onehot, axis=0)
    parts = jnp.concatenate([wsq, usq, *table_norms, jnp.sum(own_loss)[None], small_norm[None]])
    sums = summed_over(summed_over(parts, "wide"), "narrow")
    if paired:
        sums, small_grad = together(sums, small_grad)
    small_mom, small_upd = small_update(small_grad, small_m, small_v, small)
    loss_sum = sums[10]
    wnorm = jnp.sqrt(jnp.concatenate([sums[0:4], sums[8:9], jnp.sum(small * small)[None]]))
    unorm = jnp.sqrt(jnp.concatenate([sums[4:8], sums[9:10], sums[11:12]]))
    ratio = wnorm / unorm
    new_layer = layer - RATE * jnp.sum(onehot * ratio[None, 0:4], axis=1)[None] * layer_upd
    new_table = table - RATE * ratio[4] * table_upd
    new_small = small - RATE * ratio[5] * small_upd
    return (
        jnp.stack([loss_sum, count]),
        new_table,
        table_mom,
        new_small,
        small_mom,
        new_layer,
        new_m.astype(jnp.float32),
        new_worker,
        new_server,
        jnp.stack([wnorm, unorm]),
    )


def solution(mesh):
    placed = (
        P("wide", None),
        P(("wide", "narrow"), None),
        P(("wide", "narrow"), None),
        P("wide", None),
        P("wide", None),
        P("narrow", "wide"),
        P("narrow", "wide"),
        P("narrow", "wide"),
        P(),
        P(),
        P(),
        P("narrow", "wide"),
        P("narrow", None),
        P("narrow", "wide"),
        P("wide", "narrow", None),
        P("narrow", "wide"),
    )
    return jax.shard_map(
        shards,
        mesh=mesh,
        in_specs=placed,
        out_specs=(
            P(),
            P("narrow", "wide"),
            P("narrow", "wide"),
            P(),
            P(),
            P("narrow", "wide"),
            P("narrow", None),
            P("wide", "narrow", None),
            P("narrow", "wide"),
            P(),
        ),
        check_vma=False,
    )
```

```python
import functools

import jax
import jax.numpy as jnp
from jax import lax
from jax.experimental import pallas as pl
from jax.experimental.pallas import tpu as pltpu
from jax.sharding import PartitionSpec as P

D = 1024
HEADS = 16
HEAD = 64
FF = 4096
VREAL = 30522
L = 512
MPS = 80


LN_EPS = 1e-12
BETA = 0.9
DECAY = 0.01
RATE = 0.25
OPT_EPS = 1e-06
MAG_EPS = 1e-08

FREE = pl.CostEstimate(flops=0, bytes_accessed=0, transcendentals=0)


def joined(value, axis, join):
    pieces = jax.tree.map(lambda part: lax.all_gather(part, axis), value)
    head = jax.tree.map(lambda part: part[0], pieces)
    tail = jax.tree.map(lambda part: part[1:], pieces)
    subtotal, _ = lax.scan(lambda subtotal, slab: (join(subtotal, slab), None), head, tail)
    return subtotal


def norm_rows(x, gain, shift):
    mean = jnp.mean(x, axis=-1, keepdims=True)
    cent = x - mean
    var = jnp.mean(cent * cent, axis=-1, keepdims=True)
    return cent * lax.rsqrt(var + LN_EPS) * gain + shift


def matmul(left, right):
    return jnp.dot(left, right, preferred_element_type=jnp.float32)


def matmul_tn(left, right):
    return lax.dot_general(
        left, right, (((0,), (0,)), ((), ())), preferred_element_type=jnp.float32
    )


def matmul_nt(left, right):
    return lax.dot_general(
        left, right, (((1,), (1,)), ((), ())), preferred_element_type=jnp.float32
    )


def attend_kernel(q_ref, k_ref, v_ref, key_doc_ref, query_doc_ref, out_ref, lse_ref):
    same = key_doc_ref[...] == query_doc_ref[...]
    lane = lax.broadcasted_iota(jnp.int32, (1, 2 * HEAD), 1)
    outs = []
    for head in range(2):
        mine = lane // HEAD == head
        query = jnp.where(mine, q_ref[...] * 0.125, 0).astype(jnp.bfloat16)
        scores = jnp.where(same, matmul_nt(k_ref[...], query), -1000000000.0)
        top = jnp.max(scores, axis=0, keepdims=True)
        power = jnp.exp(scores - top)
        total = jnp.sum(power, axis=0, keepdims=True)
        lse_ref[0, head : head + 1, :] = top + jnp.log(total)
        prob = (power * (1.0 / total)).astype(jnp.bfloat16)
        outs.append(matmul_tn(prob, v_ref[...]))
    out_ref[...] = jnp.where(lane < HEAD, outs[0], outs[1]).astype(jnp.bfloat16)


def head_pairs(offset):
    return pl.BlockSpec((L, 2 * HEAD), lambda pair: (0, offset * HEADS // 2 + pair))


def attend(qkv, docs):
    return pl.pallas_call(
        attend_kernel,
        grid=(HEADS // 2,),
        in_specs=[
            head_pairs(0),
            head_pairs(1),
            head_pairs(2),
            pl.BlockSpec((L, 1), lambda pair: (0, 0)),
            pl.BlockSpec((1, L), lambda pair: (0, 0)),
        ],
        out_specs=[head_pairs(0), pl.BlockSpec((1, 2, L), lambda pair: (pair, 0, 0))],
        out_shape=[
            jax.ShapeDtypeStruct((L, D), jnp.bfloat16),
            jax.ShapeDtypeStruct((HEADS // 2, 2, L), jnp.float32),
        ],
        compiler_params=pltpu.CompilerParams(vmem_limit_bytes=40 * 2**20),
        cost_estimate=FREE,
        name="attend",
    )(qkv, qkv, qkv, docs.reshape(L, 1), docs.reshape(1, L))


def attend_back_kernel(q_ref, k_ref, v_ref, do_ref, lse_ref, key_doc_ref, query_doc_ref, out_ref):
    pair = pl.program_id(0)
    same = key_doc_ref[...] == query_doc_ref[...]
    lane = lax.broadcasted_iota(jnp.int32, (1, 2 * HEAD), 1)
    both = []
    for head in range(2):
        mine = lane // HEAD == head
        query = jnp.where(mine, q_ref[...] * 0.125, 0).astype(jnp.bfloat16)
        dout = jnp.where(mine, do_ref[...], 0).astype(jnp.bfloat16)
        scores = jnp.where(same, matmul_nt(k_ref[...], query), -1000000000.0)
        prob = jnp.exp(scores - lse_ref[0, head : head + 1, :])
        dvalue = matmul(prob.astype(jnp.bfloat16), dout)
        dprob = matmul_nt(v_ref[...], dout)
        delta = jnp.sum(prob * dprob, axis=0, keepdims=True)
        dscore = (prob * (dprob - delta)).astype(jnp.bfloat16)
        both.append((matmul_tn(dscore, k_ref[...]) * 0.125, matmul(dscore, query), dvalue))
    for part in range(3):
        value = jnp.where(lane < HEAD, both[0][part], both[1][part]).astype(jnp.bfloat16)
        start = pl.multiple_of(part * D + pair * 2 * HEAD, 2 * HEAD)
        out_ref[:, pl.ds(start, 2 * HEAD)] = value


def attend_back(qkv, dout, lse, docs):
    return pl.pallas_call(
        attend_back_kernel,
        grid=(HEADS // 2,),
        in_specs=[
            head_pairs(0),
            head_pairs(1),
            head_pairs(2),
            head_pairs(0),
            pl.BlockSpec((1, 2, L), lambda pair: (pair, 0, 0)),
            pl.BlockSpec((L, 1), lambda pair: (0, 0)),
            pl.BlockSpec((1, L), lambda pair: (0, 0)),
        ],
        out_specs=pl.BlockSpec((L, 3 * D), lambda pair: (0, 0)),
        out_shape=jax.ShapeDtypeStruct((L, 3 * D), jnp.bfloat16),
        compiler_params=pltpu.CompilerParams(vmem_limit_bytes=40 * 2**20),
        cost_estimate=FREE,
        name="attend_back",
    )(qkv, qkv, qkv, dout, lse, docs.reshape(L, 1), docs.reshape(1, L))


def merge_rows(first, second):
    peak = jnp.maximum(first[0], second[0])
    total = first[1] * jnp.exp(first[0] - peak) + second[1] * jnp.exp(second[0] - peak)
    return (peak, total, first[2] + second[2])


def embed_back_kernel(dqkv_ref, weight_ref, drone_ref, embedded_ref, gain_ref, even_ref, *refs):
    dembed_ref, rows_ref, sums_ref, total = refs
    step = pl.program_id(0)
    dqkv = dqkv_ref[...]
    part = matmul_nt(dqkv, weight_ref[...])
    sums_ref[...] = jnp.sum(dqkv.astype(jnp.float32), axis=0, keepdims=True)

    @pl.when(step == 0)
    def _():
        total[...] = drone_ref[...] + part

    @pl.when(step > 0)
    def _():
        total[...] += part

    @pl.when(step == pl.num_programs(0) - 1)
    def _():
        grad = total[...]
        embedded = embedded_ref[...]
        cent = embedded - jnp.mean(embedded, axis=1, keepdims=True)
        scale = lax.rsqrt(jnp.mean(cent * cent, axis=1, keepdims=True) + LN_EPS)
        normed = cent * scale
        inner = grad * gain_ref[...]
        inner_mean = jnp.mean(inner, axis=1, keepdims=True)
        along = jnp.mean(inner * normed, axis=1, keepdims=True)
        dembed = scale * (inner - inner_mean - normed * along)
        dembed_ref[...] = dembed
        even = even_ref[...]
        rows_ref[0:1, :] = jnp.sum(grad * normed, axis=0, keepdims=True)
        rows_ref[1:2, :] = jnp.sum(grad, axis=0, keepdims=True)
        rows_ref[2:3, :] = jnp.sum(dembed * even, axis=0, keepdims=True)
        rows_ref[3:4, :] = jnp.sum(dembed * (1.0 - even), axis=0, keepdims=True)
        rows_ref[4:8, :] = jnp.zeros((4, D), jnp.float32)


def embed_back(dqkv, weights, drone, embedded, gain, even):
    tokens = dqkv.shape[0]
    whole = pl.BlockSpec((tokens, D), lambda step: (0, 0))
    return pl.pallas_call(
        embed_back_kernel,
        grid=(3,),
        in_specs=[
            pl.BlockSpec((tokens, D), lambda step: (0, step)),
            pl.BlockSpec((D, D), lambda step: (0, step)),
            whole,
            whole,
            pl.BlockSpec((1, D), lambda step: (0, 0)),
            pl.BlockSpec((tokens, 1), lambda step: (0, 0)),
        ],
        out_specs=[
            whole,
            pl.BlockSpec((8, D), lambda step: (0, 0)),
            pl.BlockSpec((1, D), lambda step: (0, step)),
        ],
        out_shape=[
            jax.ShapeDtypeStruct((tokens, D), jnp.float32),
            jax.ShapeDtypeStruct((8, D), jnp.float32),
            jax.ShapeDtypeStruct((1, 3 * D), jnp.float32),
        ],
        scratch_shapes=[pltpu.VMEM((tokens, D), jnp.float32)],
        compiler_params=pltpu.CompilerParams(vmem_limit_bytes=40 * 2**20),
        cost_estimate=FREE,
        name="embed_back",
    )(dqkv, weights, drone, embedded, gain[None], even)


def ffn_kernel(fin_ref, weight_ref, bias_ref, gated_ref, slope_ref):
    upper = matmul(fin_ref[...], weight_ref[...]) + bias_ref[...]
    below = 0.5 + 0.5 * lax.erf(upper * 0.7071067811865476)
    gated_ref[...] = (upper * below).astype(jnp.bfloat16)
    density = 0.3989422804014327 * jnp.exp(-0.5 * upper * upper)
    slope_ref[...] = (below + upper * density).astype(jnp.bfloat16)


def ffn_up(fin, weights, bias):
    tokens = fin.shape[0]
    block = 512
    first = 4 * D // block
    out = pl.BlockSpec((tokens, block), lambda step: (0, step))
    return pl.pallas_call(
        ffn_kernel,
        grid=(FF // block,),
        in_specs=[
            pl.BlockSpec((tokens, D), lambda step: (0, 0)),
            pl.BlockSpec((D, block), lambda step: (0, first + step)),
            pl.BlockSpec((1, block), lambda step: (0, step)),
        ],
        out_specs=[out, out],
        out_shape=[jax.ShapeDtypeStruct((tokens, FF), jnp.bfloat16)] * 2,
        compiler_params=pltpu.CompilerParams(vmem_limit_bytes=32 * 2**20),
        cost_estimate=pl.CostEstimate(flops=2 * tokens * D * FF, bytes_accessed=0, transcendentals=0),
        name="ffn_up",
    )(fin, weights, bias)


def layer_forward(embedded, x0, act, docs, small, weights):
    base = L + 2
    bias = jnp.concatenate([small[base + 6], jnp.zeros((D,), jnp.float32), small[base + 7]])
    qkv = (matmul(act, weights[:, 0 : 3 * D]) + bias).astype(jnp.bfloat16)
    out, lse = attend(qkv, docs)
    rone = x0 + (matmul(out, weights[:, 3 * D : 4 * D]) + small[base + 8])
    hone = norm_rows(rone, small[base + 2], small[base + 3])
    fin = hone.astype(jnp.bfloat16)
    gated, slope = ffn_up(fin, weights, small[base + 10 :].reshape(1, FF))
    rtwo = hone + (matmul_nt(gated, weights[:, 4 * D + FF :]) + small[base + 9])
    htwo = norm_rows(rtwo, small[base + 4], small[base + 5])
    return (htwo, (embedded, act, qkv, lse, out, rone, fin, slope, gated, rtwo))


def layer_backward(dhtwo, kept, docs, small, weights):
    embedded, act, qkv, lse, out, rone, fin, slope, gated, rtwo = kept
    base = L + 2
    _, pull = jax.vjp(norm_rows, rtwo, small[base + 4], small[base + 5])
    drtwo, dgain_two, dshift_two = pull(dhtwo)
    dffn = drtwo.astype(jnp.bfloat16)
    down = WorkerPiece((dffn, gated))
    dgated = matmul(dffn, weights[:, 4 * D + FF :])
    dupper = (dgated * slope.astype(jnp.float32)).astype(jnp.bfloat16)
    dupper = down.received(dupper)
    dupper = down.across(dupper)
    up = WorkerPiece((fin, dupper))
    dhone = drtwo + matmul_nt(dupper, weights[:, 4 * D : 4 * D + FF])
    _, pull = jax.vjp(norm_rows, rone, small[base + 2], small[base + 3])
    drone, dgain_one, dshift_one = pull(dhone)
    dattn = drone.astype(jnp.bfloat16)
    dout = matmul_nt(dattn, weights[:, 3 * D : 4 * D]).astype(jnp.bfloat16)
    dout = up.received(dout)
    dout = up.across(dout)
    dqkv = attend_back(qkv, dout, lse, docs)
    (dqkv,) = down.crossed(dqkv)
    down.finish()
    mixed = WorkerPiece((act, dqkv), (out, dattn))
    even = (docs.reshape(L, 1) % 2 == 0).astype(jnp.float32)
    dembed, embed_rows, bias_qkv = embed_back(
        mixed.across(dqkv), weights, drone, embedded, small[base], even
    )
    (dembed,) = up.crossed(dembed)
    up.finish()
    vectors = jnp.stack(
        [
            embed_rows[0],
            embed_rows[1],
            dgain_one,
            dshift_one,
            dgain_two,
            dshift_two,
            bias_qkv[0, 0:D],
            bias_qkv[0, 2 * D : 3 * D],
            jnp.sum(dattn, axis=0, dtype=jnp.float32),
            jnp.sum(dffn, axis=0, dtype=jnp.float32),
        ]
    )
    bias_up = jnp.sum(dupper, axis=0, dtype=jnp.float32).reshape(FF // D, D)
    vectors = jnp.concatenate([embed_rows[2:4], vectors, bias_up], axis=0)
    return (dembed, vectors, (mixed, up, down))


def paired_mesh():
    return lax.axis_size("wide") == 8 and lax.axis_size("narrow") == 4


def together(*values):
    return lax.optimization_barrier(values)


def swap_pairs(size, bit):
    return [(place, place ^ bit) for place in range(size)]


def cycle(size, by):
    return [(place, (place + by) % size) for place in range(size)]


def summed_over(value, axis):
    size = lax.axis_size(axis)
    if size & (size - 1):
        return lax.psum(value, axis)
    bit = 1
    while bit < size:
        value = value + lax.ppermute(value, axis, swap_pairs(size, bit))
        bit *= 2
    return value


def gathered_near(value, beside=None):
    size = lax.axis_size("narrow")
    rows = value.shape[0]
    around = [value]
    for by in range(1, size):
        around.append(lax.ppermute(value, "narrow", cycle(size, size - by)))
    if beside is not None:
        *around, beside = together(*around, beside)
    place = lax.axis_index("narrow")
    whole = jnp.zeros((size * rows,) + value.shape[1:], value.dtype)
    for by, part in enumerate(around):
        start = lax.rem(place + by, size) * rows
        whole = lax.dynamic_update_slice_in_dim(whole, part, start, 0)
    return whole if beside is None else (whole, beside)


def scattered_near(value):
    size = lax.axis_size("narrow")
    rows = value.shape[0] // size
    place = lax.axis_index("narrow")
    total = lax.dynamic_slice_in_dim(value, place * rows, rows, 0)
    for by in range(1, size):
        target = lax.rem(place + by, size)
        give = lax.dynamic_slice_in_dim(value, target * rows, rows, 0).astype(jnp.bfloat16)
        take = lax.ppermute(give, "narrow", cycle(size, by))
        total = total + take.astype(jnp.float32)
    return total


def sent_around(blocks):
    size = lax.axis_size("narrow")
    place = lax.axis_index("narrow")

    def block(by):
        return lax.dynamic_index_in_dim(blocks, lax.rem(place + by, size), 0, keepdims=False)

    return [block(0)] + [
        lax.ppermute(block(by), "narrow", cycle(size, by)) for by in range(1, size)
    ]


def block_kernel(steps, place_ref, *refs):
    pairs = len(steps) - 1
    lefts, rights, terms, out_ref = refs[:pairs], refs[pairs : 2 * pairs], refs[2 * pairs : -1], refs[-1]
    step = pl.program_id(0)
    for index in range(pairs):

        @pl.when((step >= steps[index]) & (step < steps[index + 1]))
        def _():
            total = matmul_tn(lefts[index][...], rights[index][...])
            for term_ref in terms:
                total = total + term_ref[...].astype(jnp.float32)
            out_ref[...] = total.astype(jnp.bfloat16)


def gradient_block(pairs, place, terms):
    block = D
    size = D // lax.axis_size("narrow")
    steps = [0]
    for _, right in pairs:
        steps.append(steps[-1] + right.shape[1] // block)
    tokens = pairs[0][0].shape[0]

    def right_of(index):
        low, count = steps[index], steps[index + 1] - steps[index]
        return pl.BlockSpec(
            (tokens, block), lambda step, place: (0, jnp.clip(step - low, 0, count - 1))
        )

    piece = pl.BlockSpec((size, block), lambda step, place: (0, step))
    return pl.pallas_call(
        functools.partial(block_kernel, steps),
        grid_spec=pltpu.PrefetchScalarGridSpec(
            num_scalar_prefetch=1,
            grid=(steps[-1],),
            in_specs=[pl.BlockSpec((tokens, size), lambda step, place: (0, place[0]))] * len(pairs)
            + [right_of(index) for index in range(len(pairs))]
            + [piece] * len(terms),
            out_specs=piece,
        ),
        out_shape=jax.ShapeDtypeStruct((size, steps[-1] * block), jnp.bfloat16),
        compiler_params=pltpu.CompilerParams(vmem_limit_bytes=24 * 2**20),
        cost_estimate=FREE,
        name="gradient_block",
    )(place[None], *[left for left, _ in pairs], *[right for _, right in pairs], *terms)


class WorkerPiece:
    def __init__(self, *pairs):
        self.pairs = pairs
        self.paired = paired_mesh()
        if not self.paired:
            return
        self.core = lax.axis_index("wide") % 2
        self.pair, self.side = lax.axis_index("narrow") // 2, lax.axis_index("narrow") % 2
        cores = swap_pairs(lax.axis_size("wide"), 1)
        self.far = lax.ppermute(self.block(1 - self.core, 1 - self.side), "wide", cores)
        self.near = lax.ppermute(self.block(1 - self.core, self.side), "wide", cores)

    def block(self, core, side, *terms):
        return gradient_block(self.pairs, 2 * core + side, terms)

    def received(self, value):
        if self.paired:
            value, self.far, self.near = together(value, self.far, self.near)
        return value

    def across(self, value):
        if self.paired:
            sides = swap_pairs(lax.axis_size("narrow"), 1)
            away = self.block(self.core, 1 - self.side, self.far)
            away, value = together(away, value)
            self.away = lax.ppermute(away, "narrow", sides)
        return value

    def crossed(self, *values):
        if self.paired:
            *values, self.away = together(*values, self.away)
        return values

    def finish(self, *values):
        if not self.paired:
            blocks = [matmul_tn(left, right).astype(jnp.bfloat16) for left, right in self.pairs]
            grad = jnp.concatenate(blocks, axis=1)
            self.result = lax.psum_scatter(grad, "narrow", scatter_dimension=0, tiled=True)
            return values
        n_wide, n_narrow = lax.axis_size("wide"), lax.axis_size("narrow")
        total = self.block(self.core, self.side, self.near, self.away)
        moves = []
        for wide in range(n_wide):
            for narrow in range(n_narrow):
                if narrow // 2 != wide % 2:
                    target_wide = wide - wide % 2 + narrow // 2
                    target = target_wide * n_narrow + 2 * (wide % 2) + narrow % 2
                    moves.append((wide * n_narrow + narrow, target))
        total, *values = together(total, *values)
        moved = lax.ppermute(total, ("wide", "narrow"), moves)
        self.result = jnp.where(self.pair == self.core, total, moved)
        return values


def hosted_rows(token_ids, mlm_labels, mlm_valid, doc_ids, mlm_pos):
    n_wide, n_narrow = lax.axis_size("wide"), lax.axis_size("narrow")
    packed = jnp.concatenate([token_ids, mlm_labels, mlm_valid], axis=1)[None]
    for bit, place in zip((1, 2, 4), wide_places()):
        other = lax.ppermute(packed, "wide", swap_pairs(n_wide, bit))
        first, second = jnp.where(place == 0, packed, other), jnp.where(place == 0, other, packed)
        packed = jnp.concatenate([first, second], axis=0)
    width = packed.shape[2]
    hosted = packed.reshape(n_wide // 2, 2, 2, 2, width).transpose(1, 2, 0, 3, 4)
    hosted = hosted.reshape(n_narrow, n_wide, width)
    column = lax.dynamic_index_in_dim(hosted, lax.axis_index("wide"), 1, keepdims=False)
    moves = []
    for wide in range(n_wide):
        for row in range(n_narrow):
            target_wide = wide - wide % 2 + row % 2
            target_narrow = 2 * (wide % 2) + row // 2
            moves.append((wide * n_narrow + row, target_wide * n_narrow + target_narrow))
    own = lax.ppermute(jnp.concatenate([doc_ids, mlm_pos], axis=1), ("wide", "narrow"), moves)
    return (
        hosted[:, :, 0:L],
        column[:, L : L + MPS],
        column[:, L + MPS :],
        own[:, 0:L],
        own[:, L:],
    )


STREAMS = 2


class Owners:
    def __init__(self, tokens, vshard):
        size = lax.axis_size("narrow")
        place = lax.axis_index("narrow")
        count = tokens.shape[1]
        self.room = count * 7 // 16
        owner = tokens // vshard
        held = (owner[None] == jnp.arange(size)[:, None, None]).astype(jnp.bfloat16)
        tiles = held.reshape(-1, count // 128, 128)
        order = jnp.arange(128)
        within = jnp.einsum(
            "btl,lm->btm",
            tiles,
            (order[:, None] < order[None]).astype(jnp.bfloat16),
            preferred_element_type=jnp.float32,
        )
        sums = jnp.sum(tiles.astype(jnp.float32), axis=2)
        tile = jnp.arange(count // 128)
        before = jnp.sum(jnp.where(tile[:, None] < tile[None], sums[:, :, None], 0.0), axis=1)
        rank = (within + before[..., None]).reshape(size, size, count) * held.astype(jnp.float32)
        rank = jnp.sum(rank, axis=0).astype(jnp.int32)
        self.full = jnp.max(jnp.sum(sums, axis=1)) > self.room
        self.count, self.vshard = count, vshard
        own = lax.dynamic_index_in_dim(owner, place, 0, keepdims=False)
        self.rank = lax.dynamic_index_in_dim(rank, place, 0, keepdims=False)
        self.behind = lax.rem(place - own + size, size)
        self.slots = jnp.where(owner == place, tokens - place * vshard, vshard)

    def behind_slots(self, room):
        return self.behind * room + jnp.minimum(self.rank, room - 1)


def pack_kernel(ids_ref, table_ref, out_ref, held, *rows):
    step, count, size = pl.program_id(0), out_ref.shape[1], table_ref.shape[0]

    @pl.when(step == 0)
    def _():
        held[0:size, :] = table_ref[...]
        held[size:, :] = jnp.zeros((8, table_ref.shape[1]), jnp.float32)
        for part in rows:
            part[...] = jnp.zeros_like(part)

    base = [(step * len(rows) + index) * count for index in range(len(rows))]

    def some(turn, used):
        used = list(used)
        for by in range(8):
            for index, part in enumerate(rows):
                place = ids_ref[base[index] + turn * 8 + by]
                part[pl.ds(used[index], 1), :] = held[pl.ds(place, 1), :]
                used[index] = used[index] + jnp.where(place < size, 1, 0)
        return tuple(used)

    lax.fori_loop(0, count // 8, some, (0,) * len(rows))
    for index, part in enumerate(rows):
        out_ref[index] = part[0:count, :].astype(out_ref.dtype)


def packed_rows(ids, table):
    size, cols = table.shape
    places, count = ids.shape
    return pl.pallas_call(
        pack_kernel,
        grid_spec=pltpu.PrefetchScalarGridSpec(
            num_scalar_prefetch=1,
            grid=(places // STREAMS,),
            in_specs=[pl.BlockSpec((size, cols), lambda step, ids: (0, 0))],
            out_specs=pl.BlockSpec((STREAMS, count, cols), lambda step, ids: (step, 0, 0)),
            scratch_shapes=[pltpu.VMEM((size + 8, cols), jnp.float32)]
            + [pltpu.VMEM((count + 8, cols), jnp.float32)] * STREAMS,
        ),
        out_shape=jax.ShapeDtypeStruct((places, count, cols), jnp.bfloat16),
        compiler_params=pltpu.CompilerParams(vmem_limit_bytes=40 * 2**20),
        cost_estimate=pl.CostEstimate(flops=0, bytes_accessed=0, transcendentals=0),
        name="pack_rows",
    )(ids.reshape(-1), table)


def take_kernel(ids_ref, table_ref, out_ref, held, rows):
    held[...] = table_ref[...].astype(jnp.float32)

    @pl.loop(0, out_ref.shape[0], step=16)
    def _(first):
        for by in range(16):
            rows[pl.ds(first + by, 1), :] = held[pl.ds(ids_ref[first + by], 1), :]

    out_ref[...] = rows[...].astype(out_ref.dtype)


def taken_rows(ids, table):
    count, cols = ids.shape[0], table.shape[1]
    return pl.pallas_call(
        take_kernel,
        grid_spec=pltpu.PrefetchScalarGridSpec(
            num_scalar_prefetch=1,
            grid=(1,),
            in_specs=[pl.BlockSpec(table.shape, lambda step, ids: (0, 0))],
            out_specs=pl.BlockSpec((count, cols), lambda step, ids: (0, 0)),
            scratch_shapes=[
                pltpu.VMEM(table.shape, jnp.float32),
                pltpu.VMEM((count, cols), jnp.float32),
            ],
        ),
        out_shape=jax.ShapeDtypeStruct((count, cols), table.dtype),
        compiler_params=pltpu.CompilerParams(vmem_limit_bytes=40 * 2**20),
        cost_estimate=FREE,
        name="take_rows",
    )(ids, table)


def add_kernel(ids_ref, values_ref, out_ref, rows, *sums):
    size, length = out_ref.shape[0], rows.shape[1]
    for part in sums:
        part[...] = jnp.zeros_like(part)
    rows[...] = values_ref[:, 0:length, :].astype(jnp.float32)

    @pl.loop(0, length, step=8)
    def _(first):
        for by in range(8):
            for index, part in enumerate(sums):
                place = ids_ref[index * length + first + by]
                part[pl.ds(place, 1), :] += rows[index, pl.ds(first + by, 1), :]

    total = sums[0][0:size, :]
    for part in sums[1:]:
        total = total + part[0:size, :]
    out_ref[...] = total


def added_rows(ids, values, size):
    places, length = ids.shape
    cols = values.shape[2]
    return pl.pallas_call(
        add_kernel,
        grid_spec=pltpu.PrefetchScalarGridSpec(
            num_scalar_prefetch=1,
            grid=(1,),
            in_specs=[pl.BlockSpec(values.shape, lambda step, ids: (0, 0, 0))],
            out_specs=pl.BlockSpec((size, cols), lambda step, ids: (0, 0)),
            scratch_shapes=[pltpu.VMEM((places, length, cols), jnp.float32)]
            + [pltpu.VMEM((size + 8, cols), jnp.float32)] * places,
        ),
        out_shape=jax.ShapeDtypeStruct((size, cols), jnp.float32),
        compiler_params=pltpu.CompilerParams(vmem_limit_bytes=56 * 2**20),
        cost_estimate=FREE,
        name="add_rows",
    )(ids.reshape(-1), values)


def span_kernel(momentum_ref, grad_ref, error_ref, span_ref, sum_ref):
    grad = grad_ref[...].astype(jnp.float32)
    span = BETA * momentum_ref[...] + (1.0 - BETA) * grad + error_ref[0]
    span_ref[...] = span

    @pl.when(pl.program_id(0) == 0)
    def _():
        sum_ref[...] = jnp.zeros_like(sum_ref)

    sum_ref[...] += jnp.sum(jnp.abs(span), axis=0, keepdims=True)


def span_of(momentum, grad, error, start):
    rows, cols = grad.shape
    block = 1024
    first = start // block
    span, sums = pl.pallas_call(
        span_kernel,
        grid=(cols // block,),
        in_specs=[
            pl.BlockSpec((rows, block), lambda step: (0, first + step)),
            pl.BlockSpec((rows, block), lambda step: (0, step)),
            pl.BlockSpec((1, rows, block), lambda step: (0, 0, first + step)),
        ],
        out_specs=[
            pl.BlockSpec((rows, block), lambda step: (0, step)),
            pl.BlockSpec((1, block), lambda step: (0, 0)),
        ],
        out_shape=[
            jax.ShapeDtypeStruct((rows, cols), jnp.float32),
            jax.ShapeDtypeStruct((1, block), jnp.float32),
        ],
        compiler_params=pltpu.CompilerParams(vmem_limit_bytes=60 * 2**20),
        cost_estimate=pl.CostEstimate(flops=0, bytes_accessed=2 * 10**7, transcendentals=0),
        name="span",
    )(momentum, grad, error)
    return span, jnp.sum(sums)


def press_kernel(steps, core_ref, scale_ref, *refs):
    *span_refs, error_ref, give_ref, keep_ref = refs
    core = pl.program_id(2)
    step = pressed_step(pl.program_id(0), pl.program_id(1), core)
    scale = scale_ref[0]
    inverse = scale_ref[1]
    for index, span_ref in enumerate(span_refs):

        @pl.when((step >= steps[index]) & (step < steps[index + 1]))
        def _():
            span = span_ref[...]
            sent = scale * jnp.tanh(span * inverse)
            error_ref[0] = span - sent
            low = sent.astype(jnp.bfloat16)

            @pl.when(core == core_ref[0])
            def _():
                keep_ref[0] = low

            @pl.when(core != core_ref[0])
            def _():
                give_ref[0] = low


def pressed_step(chip, column, core):
    return (2 * chip + core) * 3 + column


def pressed(spans, scale, parts):
    rows = spans[0].shape[0]
    cols = sum(span.shape[1] for span in spans)
    block = cols // parts // 3
    steps = [0]
    for span in spans:
        steps.append(steps[-1] + span.shape[1] // block)

    def of(index):
        low, count = steps[index], steps[index + 1] - steps[index]

        def place(chip, column, core, _):
            return (0, jnp.clip(pressed_step(chip, column, core) - low, 0, count - 1))

        return pl.BlockSpec((rows, block), place)

    half = pl.BlockSpec((1, rows, block), lambda chip, column, core, _: (chip, 0, column))
    half_shape = jax.ShapeDtypeStruct((parts // 2, rows, cols // parts), jnp.bfloat16)
    return pl.pallas_call(
        functools.partial(press_kernel, steps),
        grid_spec=pltpu.PrefetchScalarGridSpec(
            num_scalar_prefetch=1,
            grid=(parts // 2, 3, 2),
            in_specs=[pl.BlockSpec(memory_space=pltpu.SMEM)] + [of(i) for i in range(len(spans))],
            out_specs=[
                pl.BlockSpec(
                    (1, rows, block),
                    lambda chip, column, core, _: (0, 0, pressed_step(chip, column, core)),
                ),
                half,
                half,
            ],
        ),
        out_shape=[jax.ShapeDtypeStruct((1, rows, cols), jnp.float32), half_shape, half_shape],
        compiler_params=pltpu.CompilerParams(vmem_limit_bytes=60 * 2**20),
        cost_estimate=FREE,
        name="press",
    )(wide_places()[0][None], jnp.stack([scale, 1.0 / scale]), *spans)


def update_kernel(grad_ref, head_ref, table_ref, first_ref, second_ref, *out_refs):
    first_out, update_ref, weight_sum, update_sum = out_refs
    grad = grad_ref[...] + head_ref[...].astype(jnp.float32)
    first = BETA * first_ref[...] + (1.0 - BETA) * grad
    table = table_ref[...]
    update = first / (jnp.sqrt(second_ref[...]) + OPT_EPS) + DECAY * table
    first_out[...] = first
    update_ref[...] = update

    @pl.when(pl.program_id(0) == 0)
    def _():
        weight_sum[...] = jnp.zeros_like(weight_sum)
        update_sum[...] = jnp.zeros_like(update_sum)

    weight_sum[...] += jnp.sum(table * table, axis=0, keepdims=True)
    update_sum[...] += jnp.sum(update * update, axis=0, keepdims=True)


def table_update(grad, head, table, first, second):
    size, cols = table.shape
    block = size // 9 if size % 9 == 0 and size // 9 % 16 == 0 else size
    whole = pl.BlockSpec((block, cols), lambda step: (step, 0))
    line = pl.BlockSpec((1, cols), lambda step: (0, 0))
    moment, update, *sums = pl.pallas_call(
        update_kernel,
        grid=(size // block,),
        in_specs=[whole] * 5,
        out_specs=[whole, whole, line, line],
        out_shape=[jax.ShapeDtypeStruct((size, cols), jnp.float32)] * 2
        + [jax.ShapeDtypeStruct((1, cols), jnp.float32)] * 2,
        compiler_params=pltpu.CompilerParams(vmem_limit_bytes=56 * 2**20),
        cost_estimate=FREE,
        name="update",
    )(grad, head, table, first, second)
    return moment, update, tuple(jnp.sum(part)[None] for part in sums)


def wide_places():
    wide_me = lax.axis_index("wide")
    return wide_me % 2, wide_me // 2 % 2, wide_me // 4


def scattered_sum(give, keep):
    n_wide = lax.axis_size("wide")
    _, x, y = wide_places()

    def send(value, bit):
        return lax.ppermute(value.astype(jnp.bfloat16), "wide", swap_pairs(n_wide, bit))

    take = send(give, 1)
    half = keep.shape[1] // 2

    def chip(y_of, x_of, part):
        start, size = (2 * y_of + x_of, part * half, 0), (1, half, keep.shape[2])
        own, other = lax.dynamic_slice(keep, start, size), lax.dynamic_slice(take, start, size)
        return own[0].astype(jnp.float32) + other[0].astype(jnp.float32)

    upper_far = send(chip(1 - y, 1 - x, 0), 2)
    lower_far = send(chip(1 - y, 1 - x, 1), 4)
    upper_near = send(chip(y, 1 - x, 0), 2)
    lower_near = send(chip(1 - y, x, 1), 4)
    upper_far = send(chip(1 - y, x, 0) + upper_far.astype(jnp.float32), 4)
    lower_far = send(chip(y, 1 - x, 1) + lower_far.astype(jnp.float32), 2)
    own_upper = chip(y, x, 0) + upper_near.astype(jnp.float32) + upper_far.astype(jnp.float32)
    own_lower = chip(y, x, 1) + lower_near.astype(jnp.float32) + lower_far.astype(jnp.float32)
    return jnp.concatenate([own_upper, own_lower], axis=0)


def small_halved(value):
    n_wide = lax.axis_size("wide")
    for bit, place in list(zip((1, 2, 4), wide_places()))[::-1]:
        half = value.shape[1] // 2
        give = lax.dynamic_slice_in_dim(value, (1 - place) * half, half, 1).astype(jnp.bfloat16)
        keep = lax.dynamic_slice_in_dim(value, place * half, half, 1)
        value = keep + lax.ppermute(give, "wide", swap_pairs(n_wide, bit)).astype(jnp.float32)
    return value


def small_update(grad, first, second, weight):
    first = BETA * first + (1.0 - BETA) * grad.astype(jnp.float32)
    return first, first / (jnp.sqrt(second) + OPT_EPS) + DECAY * weight


def shards(
    token_ids,
    doc_ids,
    mlm_pos,
    mlm_labels,
    mlm_valid,
    table,
    table_m,
    table_v,
    small,
    small_m,
    small_v,
    layer,
    layer_m,
    layer_v,
    worker_err,
    server_err,
):
    n_wide, n_narrow = lax.axis_size("wide"), lax.axis_size("narrow")
    narrow_me = lax.axis_index("narrow")
    wide_me = lax.axis_index("wide")
    seqs = doc_ids.shape[0]
    paired = paired_mesh()
    vshard = table.shape[0]
    count = summed_over(jnp.sum(mlm_valid.astype(jnp.float32)), "wide")
    table_low, layer_low = table.astype(jnp.bfloat16), layer.astype(jnp.bfloat16)
    if paired:
        token_ids, mlm_labels, mlm_valid, doc_ids, mlm_pos = hosted_rows(
            token_ids, mlm_labels, mlm_valid, doc_ids, mlm_pos
        )
        owners = Owners(token_ids.reshape(n_narrow, n_wide * L), vshard)
        table_cut = vshard // 2 // 16 * 16
        table_first = lax.all_gather(table_low[0:table_cut], "wide", axis=1, tiled=True)
        half = layer_low.shape[0] // 2
        first_rows = gathered_near(layer_low[0:half])
        first_rows, table_first = together(first_rows, table_first)
        slots, first_rows = together(owners.slots, first_rows)
        first_weights = lax.all_gather(first_rows, "wide", axis=1, tiled=True)
        picked = packed_rows(slots, table)
        last_rows, picked = gathered_near(layer_low[half:], picked)
        last_weights = lax.all_gather(last_rows, "wide", axis=1, tiled=True)
    else:
        layer_rows = lax.all_gather(layer_low, "narrow", axis=0, tiled=True)
        weights = lax.all_gather(layer_rows, "wide", axis=1, tiled=True)
    if paired:

        def looked_up(room):
            rows = sent_around(picked[:, 0:room])
            return taken_rows(owners.behind_slots(room), jnp.concatenate(rows, axis=0))

        looked = looked_up(owners.room)
        looked = lax.cond(owners.full, lambda: looked_up(owners.count), lambda: looked)
        looked = lax.all_to_all(looked.reshape(n_wide, L, -1), "wide", 0, 0)
        looked = looked.transpose(1, 0, 2).reshape(1, L, D)
        looked, count, doc_ids, mlm_pos = together(looked, count, doc_ids, mlm_pos)
    else:
        local_ids = token_ids - narrow_me * vshard
        inside = (local_ids >= 0) & (local_ids < vshard)
        slots = jnp.where(inside, local_ids, vshard).reshape(-1)
        table_cols = lax.all_gather(table_low, "wide", axis=1, tiled=True)
        picked = jnp.take(table_cols, jnp.clip(local_ids, 0, vshard - 1), axis=0)
        picked = jnp.where(inside[..., None], picked, 0.0)
        looked = lax.psum_scatter(picked, "narrow", scatter_dimension=0, tiled=True)
    looked = looked.astype(jnp.float32)
    even_doc = (doc_ids % 2 == 0)[..., None]
    embedded = looked + small[0:L][None] + jnp.where(even_doc, small[L], small[L + 1])
    embedded = embedded.reshape(seqs * L, D)
    x0 = norm_rows(embedded, small[L + 2], small[L + 3])
    act = x0.astype(jnp.bfloat16)
    if paired:
        whole = jnp.zeros((n_narrow, 2, half, last_weights.shape[1]), jnp.bfloat16)
        cut_shape = (n_narrow, 1, half, last_weights.shape[1])
        whole = lax.dynamic_update_slice(whole, first_weights.reshape(cut_shape), (0, 0, 0, 0))
        last_weights, act, whole = together(last_weights, act, whole)
        whole = lax.dynamic_update_slice(whole, last_weights.reshape(cut_shape), (0, 1, 0, 0))
        weights = whole.reshape(D, -1)
        table_last, last_weights = together(table_low[table_cut:], last_weights)
        table_last = lax.all_gather(table_last, "wide", axis=1, tiled=True)
        table_cols = lax.dynamic_update_slice(
            jnp.zeros((vshard, D), jnp.bfloat16), table_first, (0, 0)
        )
        table_cols = lax.dynamic_update_slice(table_cols, table_last, (table_cut, 0))
    htwo, kept = layer_forward(embedded, x0, act, doc_ids, small, weights)
    hmask = jnp.take_along_axis(htwo.reshape(seqs, L, D), mlm_pos[..., None], axis=1)
    hmask = hmask.reshape(seqs * MPS, D).astype(jnp.bfloat16)
    if paired:
        group_h = gathered_near(hmask)
    else:
        group_h = lax.all_gather(hmask, "narrow", axis=0, tiled=True)
    vocab = narrow_me * vshard + jnp.arange(vshard)
    logits = jnp.where((vocab < VREAL)[None], matmul_nt(group_h, table_cols), -1000000000.0)
    labels = mlm_labels.reshape(-1)
    hit = vocab[None] == labels[:, None]
    top = jnp.max(logits, axis=1)
    total = jnp.sum(jnp.exp(logits - top[:, None]), axis=1)
    target = jnp.sum(jnp.where(hit, logits, 0.0), axis=1)
    if paired:
        stats = gathered_near(jnp.stack([top, total, target])[None])
        top, total, target = stats[0]
        for place in range(1, stats.shape[0]):
            top, total, target = merge_rows((top, total, target), tuple(stats[place]))
    else:
        top, total, target = joined((top, total, target), "narrow", merge_rows)
    lse = top + jnp.log(total)
    flags = mlm_valid.reshape(-1).astype(jnp.float32)
    own = seqs * MPS
    own_loss = lax.dynamic_slice_in_dim(flags * (lse - target), narrow_me * own, own)
    dlogit = (
        (jnp.exp(logits - lse[:, None]) - hit.astype(jnp.float32)) * (flags / count)[:, None]
    ).astype(jnp.bfloat16)
    dhmask = matmul(dlogit, table_cols)
    if paired:
        dhmask = scattered_near(dhmask)
        blocks = group_h.reshape(-1, n_wide, D // n_wide)
        table_head = jnp.einsum("sv,swc->wvc", dlogit, blocks, preferred_element_type=jnp.float32)
        table_head, dhmask = together(table_head.astype(jnp.bfloat16), dhmask)
        table_head = lax.psum_scatter(table_head, "wide", scatter_dimension=0)
    else:
        dhmask = lax.psum_scatter(dhmask, "narrow", scatter_dimension=0, tiled=True)
    dhtwo = (
        jnp.zeros((seqs, L, D), jnp.float32)
        .at[jnp.arange(seqs)[:, None], mlm_pos]
        .add(dhmask.reshape(seqs, MPS, D))
    )
    dembed, vectors, pieces = layer_backward(
        dhtwo.reshape(seqs * L, D), kept, doc_ids, small, weights
    )
    dembed_rows = dembed.reshape(seqs, L, D)
    small_grad = jnp.concatenate([jnp.sum(dembed_rows, axis=0), vectors], axis=0)
    mixed = pieces[0]
    if paired:
        cut = dembed.astype(jnp.bfloat16).reshape(L, n_wide, D // n_wide).transpose(1, 0, 2)
        cut = lax.all_to_all(cut, "wide", 0, 0).reshape(n_wide * L, D // n_wide)
        halved = small_halved(small_grad).astype(jnp.bfloat16)
        down, up = pieces[2], pieces[1]
        mixed.away, down.result = together(mixed.away, down.result)
        mixed.finish()
        spans = [span_of(layer_m, up.result, worker_err, 4 * D)]
        spans.append(span_of(layer_m, down.result, worker_err, 8 * D))
        cut, mixed.result, spans, table_head = together(
            jnp.concatenate([cut, halved]), mixed.result, spans, table_head
        )
        group_rows = lax.all_gather(cut, "narrow", axis=0)
    else:
        mixed.finish()
        group_rows = lax.all_gather(dembed_rows.astype(jnp.bfloat16), "narrow", axis=0, tiled=True)
        table_grad = matmul_tn(dlogit, group_h).at[slots].add(
            group_rows.reshape(-1, D).astype(jnp.float32), mode="drop"
        )
        cut = table_grad.astype(jnp.bfloat16).reshape(vshard, n_wide, D // n_wide)
        table_grad = lax.psum_scatter(cut.transpose(1, 0, 2), "wide", scatter_dimension=0)
        table_grad = table_grad.astype(jnp.float32)
    part_cols = layer.shape[1]
    if paired:
        spans.insert(0, span_of(layer_m, mixed.result, worker_err, 0))
        total = sum(amount for _, amount in spans)
        spans = [span for span, _ in spans]
        scale = total / (layer_m.shape[0] * layer_m.shape[1]) + MAG_EPS
        new_worker, give, keep = pressed(spans, scale, n_wide)
        server_in = scattered_sum(give, keep) / n_wide + server_err
    else:
        worker_grad = jnp.concatenate([piece.result for piece in pieces], axis=1)
        span = BETA * layer_m + (1.0 - BETA) * worker_grad.astype(jnp.float32) + worker_err[0]
        scale = jnp.mean(jnp.abs(span)) + MAG_EPS
        sent = scale * jnp.tanh(span / scale)
        new_worker = (span - sent)[None]
        summed = lax.psum(sent.astype(jnp.bfloat16), "wide").astype(jnp.float32)
        mixed = lax.dynamic_slice_in_dim(summed, wide_me * part_cols, part_cols, 1) / n_wide
        server_in = mixed + server_err
    sscale = jnp.mean(jnp.abs(server_in)) + MAG_EPS
    server_out = sscale * jnp.tanh(server_in / sscale)
    new_server = server_in - server_out
    server_low = server_out.astype(jnp.bfloat16)
    if paired:
        server_out, group_rows = together(server_out, group_rows)
        table_grad = added_rows(owners.slots, group_rows, vshard)
        table_mom, table_upd, table_norms = table_update(
            table_grad, table_head, table, table_m, table_v
        )
        eighth = D // n_wide
        small_grad = jnp.sum(group_rows[:, n_wide * L :].astype(jnp.float32), axis=0)
        small_grad = small_grad.astype(jnp.bfloat16)

        def own(value):
            return lax.dynamic_slice_in_dim(value, wide_me * eighth, eighth, 1)

        _, own_upd = small_update(small_grad, own(small_m), own(small_v), own(small))
        small_norm = jnp.where(narrow_me == 0, jnp.sum(own_upd * own_upd), 0.0)
    else:
        small_grad = lax.psum(small_grad, ("wide", "narrow"))
        table_mom = BETA * table_m + (1.0 - BETA) * table_grad
        table_upd = table_mom / (jnp.sqrt(table_v) + OPT_EPS) + DECAY * table
        table_norms = (jnp.sum(table * table)[None], jnp.sum(table_upd * table_upd)[None])
    new_m = lax.all_gather(server_low, "wide", axis=1, tiled=True)
    if paired:
        small_grad, new_m, table_norms = together(small_grad, new_m, table_norms)
        small_grad = lax.all_gather(small_grad, "wide", axis=1, tiled=True)
    if not paired:
        _, small_upd = small_update(small_grad, small_m, small_v, small)
        small_norm = jnp.where((wide_me == 0) & (narrow_me == 0), jnp.sum(small_upd * small_upd), 0.0)
    layer_upd = server_out / (jnp.sqrt(layer_v) + OPT_EPS) + DECAY * layer
    column = wide_me * part_cols + jnp.arange(part_cols)
    which = (
        (column >= 3 * D).astype(jnp.int32)
        + (column >= 4 * D).astype(jnp.int32)
        + (column >= 4 * D + FF).astype(jnp.int32)
    )
    onehot = (which[:, None] == jnp.arange(4)[None]).astype(jnp.float32)
    wsq = jnp.sum(jnp.sum(layer * layer, axis=0)[:, None] * onehot, axis=0)
    usq = jnp.sum(jnp.sum(layer_upd * layer_upd, axis=0)[:, None] * onehot, axis=0)
    parts = jnp.concatenate([wsq, usq, *table_norms, jnp.sum(own_loss)[None], small_norm[None]])
    sums = summed_over(summed_over(parts, "wide"), "narrow")
    if paired:
        sums, small_grad = together(sums, small_grad)
    small_mom, small_upd = small_update(small_grad, small_m, small_v, small)
    loss_sum = sums[10]
    wnorm = jnp.sqrt(jnp.concatenate([sums[0:4], sums[8:9], jnp.sum(small * small)[None]]))
    unorm = jnp.sqrt(jnp.concatenate([sums[4:8], sums[9:10], sums[11:12]]))
    ratio = wnorm / unorm
    new_layer = layer - RATE * jnp.sum(onehot * ratio[None, 0:4], axis=1)[None] * layer_upd
    new_table = table - RATE * ratio[4] * table_upd
    new_small = small - RATE * ratio[5] * small_upd
    return (
        jnp.stack([loss_sum, count]),
        new_table,
        table_mom,
        new_small,
        small_mom,
        new_layer,
        new_m.astype(jnp.float32),
        new_worker,
        new_server,
        jnp.stack([wnorm, unorm]),
    )


def solution(mesh):
    placed = (
        P("wide", None),
        P(("wide", "narrow"), None),
        P(("wide", "narrow"), None),
        P("wide", None),
        P("wide", None),
        P("narrow", "wide"),
        P("narrow", "wide"),
        P("narrow", "wide"),
        P(),
        P(),
        P(),
        P("narrow", "wide"),
        P("narrow", None),
        P("narrow", "wide"),
        P("wide", "narrow", None),
        P("narrow", "wide"),
    )
    return jax.shard_map(
        shards,
        mesh=mesh,
        in_specs=placed,
        out_specs=(
            P(),
            P("narrow", "wide"),
            P("narrow", "wide"),
            P(),
            P(),
            P("narrow", "wide"),
            P("narrow", None),
            P("wide", "narrow", None),
            P("narrow", "wide"),
            P(),
        ),
        check_vma=False,
    )
```

```python
import functools

import jax
import jax.numpy as jnp
from jax import lax
from jax.experimental import pallas as pl
from jax.experimental.pallas import tpu as pltpu
from jax.sharding import PartitionSpec as P

D = 1024
HEADS = 16
HEAD = 64
FF = 4096
VREAL = 30522
L = 512
MPS = 80


LN_EPS = 1e-12
BETA = 0.9
DECAY = 0.01
RATE = 0.25
OPT_EPS = 1e-06
MAG_EPS = 1e-08

FREE = pl.CostEstimate(flops=0, bytes_accessed=0, transcendentals=0)


def joined(value, axis, join):
    pieces = jax.tree.map(lambda part: lax.all_gather(part, axis), value)
    head = jax.tree.map(lambda part: part[0], pieces)
    tail = jax.tree.map(lambda part: part[1:], pieces)
    subtotal, _ = lax.scan(lambda subtotal, slab: (join(subtotal, slab), None), head, tail)
    return subtotal


def norm_rows(x, gain, shift):
    mean = jnp.mean(x, axis=-1, keepdims=True)
    cent = x - mean
    var = jnp.mean(cent * cent, axis=-1, keepdims=True)
    return cent * lax.rsqrt(var + LN_EPS) * gain + shift


def matmul(left, right):
    return jnp.dot(left, right, preferred_element_type=jnp.float32)


def matmul_tn(left, right):
    return lax.dot_general(
        left, right, (((0,), (0,)), ((), ())), preferred_element_type=jnp.float32
    )


def matmul_nt(left, right):
    return lax.dot_general(
        left, right, (((1,), (1,)), ((), ())), preferred_element_type=jnp.float32
    )


def attend_kernel(q_ref, k_ref, v_ref, key_doc_ref, query_doc_ref, out_ref, lse_ref):
    same = key_doc_ref[...] == query_doc_ref[...]
    lane = lax.broadcasted_iota(jnp.int32, (1, 2 * HEAD), 1)
    outs = []
    for head in range(2):
        mine = lane // HEAD == head
        query = jnp.where(mine, q_ref[...] * 0.125, 0).astype(jnp.bfloat16)
        scores = jnp.where(same, matmul_nt(k_ref[...], query), -1000000000.0)
        top = jnp.max(scores, axis=0, keepdims=True)
        power = jnp.exp(scores - top)
        total = jnp.sum(power, axis=0, keepdims=True)
        lse_ref[0, head : head + 1, :] = top + jnp.log(total)
        prob = (power * (1.0 / total)).astype(jnp.bfloat16)
        outs.append(matmul_tn(prob, v_ref[...]))
    out_ref[...] = jnp.where(lane < HEAD, outs[0], outs[1]).astype(jnp.bfloat16)


def head_pairs(offset):
    return pl.BlockSpec((L, 2 * HEAD), lambda pair: (0, offset * HEADS // 2 + pair))


def attend(qkv, docs):
    return pl.pallas_call(
        attend_kernel,
        grid=(HEADS // 2,),
        in_specs=[
            head_pairs(0),
            head_pairs(1),
            head_pairs(2),
            pl.BlockSpec((L, 1), lambda pair: (0, 0)),
            pl.BlockSpec((1, L), lambda pair: (0, 0)),
        ],
        out_specs=[head_pairs(0), pl.BlockSpec((1, 2, L), lambda pair: (pair, 0, 0))],
        out_shape=[
            jax.ShapeDtypeStruct((L, D), jnp.bfloat16),
            jax.ShapeDtypeStruct((HEADS // 2, 2, L), jnp.float32),
        ],
        compiler_params=pltpu.CompilerParams(vmem_limit_bytes=40 * 2**20),
        cost_estimate=FREE,
        name="attend",
    )(qkv, qkv, qkv, docs.reshape(L, 1), docs.reshape(1, L))


def attend_back_kernel(q_ref, k_ref, v_ref, do_ref, lse_ref, key_doc_ref, query_doc_ref, out_ref):
    pair = pl.program_id(0)
    same = key_doc_ref[...] == query_doc_ref[...]
    lane = lax.broadcasted_iota(jnp.int32, (1, 2 * HEAD), 1)
    both = []
    for head in range(2):
        mine = lane // HEAD == head
        query = jnp.where(mine, q_ref[...] * 0.125, 0).astype(jnp.bfloat16)
        dout = jnp.where(mine, do_ref[...], 0).astype(jnp.bfloat16)
        scores = jnp.where(same, matmul_nt(k_ref[...], query), -1000000000.0)
        prob = jnp.exp(scores - lse_ref[0, head : head + 1, :])
        dvalue = matmul(prob.astype(jnp.bfloat16), dout)
        dprob = matmul_nt(v_ref[...], dout)
        delta = jnp.sum(prob * dprob, axis=0, keepdims=True)
        dscore = (prob * (dprob - delta)).astype(jnp.bfloat16)
        both.append((matmul_tn(dscore, k_ref[...]) * 0.125, matmul(dscore, query), dvalue))
    for part in range(3):
        value = jnp.where(lane < HEAD, both[0][part], both[1][part]).astype(jnp.bfloat16)
        start = pl.multiple_of(part * D + pair * 2 * HEAD, 2 * HEAD)
        out_ref[:, pl.ds(start, 2 * HEAD)] = value


def attend_back(qkv, dout, lse, docs):
    return pl.pallas_call(
        attend_back_kernel,
        grid=(HEADS // 2,),
        in_specs=[
            head_pairs(0),
            head_pairs(1),
            head_pairs(2),
            head_pairs(0),
            pl.BlockSpec((1, 2, L), lambda pair: (pair, 0, 0)),
            pl.BlockSpec((L, 1), lambda pair: (0, 0)),
            pl.BlockSpec((1, L), lambda pair: (0, 0)),
        ],
        out_specs=pl.BlockSpec((L, 3 * D), lambda pair: (0, 0)),
        out_shape=jax.ShapeDtypeStruct((L, 3 * D), jnp.bfloat16),
        compiler_params=pltpu.CompilerParams(vmem_limit_bytes=40 * 2**20),
        cost_estimate=FREE,
        name="attend_back",
    )(qkv, qkv, qkv, dout, lse, docs.reshape(L, 1), docs.reshape(1, L))


def merge_rows(first, second):
    peak = jnp.maximum(first[0], second[0])
    total = first[1] * jnp.exp(first[0] - peak) + second[1] * jnp.exp(second[0] - peak)
    return (peak, total, first[2] + second[2])


def embed_back_kernel(dqkv_ref, weight_ref, drone_ref, embedded_ref, gain_ref, even_ref, *refs):
    dembed_ref, rows_ref, sums_ref, total = refs
    step = pl.program_id(0)
    dqkv = dqkv_ref[...]
    part = matmul_nt(dqkv, weight_ref[...])
    sums_ref[...] = jnp.sum(dqkv.astype(jnp.float32), axis=0, keepdims=True)

    @pl.when(step == 0)
    def _():
        total[...] = drone_ref[...] + part

    @pl.when(step > 0)
    def _():
        total[...] += part

    @pl.when(step == pl.num_programs(0) - 1)
    def _():
        grad = total[...]
        embedded = embedded_ref[...]
        cent = embedded - jnp.mean(embedded, axis=1, keepdims=True)
        scale = lax.rsqrt(jnp.mean(cent * cent, axis=1, keepdims=True) + LN_EPS)
        normed = cent * scale
        inner = grad * gain_ref[...]
        inner_mean = jnp.mean(inner, axis=1, keepdims=True)
        along = jnp.mean(inner * normed, axis=1, keepdims=True)
        dembed = scale * (inner - inner_mean - normed * along)
        dembed_ref[...] = dembed
        even = even_ref[...]
        rows_ref[0:1, :] = jnp.sum(grad * normed, axis=0, keepdims=True)
        rows_ref[1:2, :] = jnp.sum(grad, axis=0, keepdims=True)
        rows_ref[2:3, :] = jnp.sum(dembed * even, axis=0, keepdims=True)
        rows_ref[3:4, :] = jnp.sum(dembed * (1.0 - even), axis=0, keepdims=True)
        rows_ref[4:8, :] = jnp.zeros((4, D), jnp.float32)


def embed_back(dqkv, weights, drone, embedded, gain, even):
    tokens = dqkv.shape[0]
    whole = pl.BlockSpec((tokens, D), lambda step: (0, 0))
    return pl.pallas_call(
        embed_back_kernel,
        grid=(3,),
        in_specs=[
            pl.BlockSpec((tokens, D), lambda step: (0, step)),
            pl.BlockSpec((D, D), lambda step: (0, step)),
            whole,
            whole,
            pl.BlockSpec((1, D), lambda step: (0, 0)),
            pl.BlockSpec((tokens, 1), lambda step: (0, 0)),
        ],
        out_specs=[
            whole,
            pl.BlockSpec((8, D), lambda step: (0, 0)),
            pl.BlockSpec((1, D), lambda step: (0, step)),
        ],
        out_shape=[
            jax.ShapeDtypeStruct((tokens, D), jnp.float32),
            jax.ShapeDtypeStruct((8, D), jnp.float32),
            jax.ShapeDtypeStruct((1, 3 * D), jnp.float32),
        ],
        scratch_shapes=[pltpu.VMEM((tokens, D), jnp.float32)],
        compiler_params=pltpu.CompilerParams(vmem_limit_bytes=40 * 2**20),
        cost_estimate=FREE,
        name="embed_back",
    )(dqkv, weights, drone, embedded, gain[None], even)


def ffn_kernel(fin_ref, weight_ref, bias_ref, gated_ref, slope_ref):
    upper = matmul(fin_ref[...], weight_ref[...]) + bias_ref[...]
    below = 0.5 + 0.5 * lax.erf(upper * 0.7071067811865476)
    gated_ref[...] = (upper * below).astype(jnp.bfloat16)
    density = 0.3989422804014327 * jnp.exp(-0.5 * upper * upper)
    slope_ref[...] = (below + upper * density).astype(jnp.bfloat16)


def ffn_up(fin, weights, bias):
    tokens = fin.shape[0]
    block = 512
    first = 4 * D // block
    out = pl.BlockSpec((tokens, block), lambda step: (0, step))
    return pl.pallas_call(
        ffn_kernel,
        grid=(FF // block,),
        in_specs=[
            pl.BlockSpec((tokens, D), lambda step: (0, 0)),
            pl.BlockSpec((D, block), lambda step: (0, first + step)),
            pl.BlockSpec((1, block), lambda step: (0, step)),
        ],
        out_specs=[out, out],
        out_shape=[jax.ShapeDtypeStruct((tokens, FF), jnp.bfloat16)] * 2,
        compiler_params=pltpu.CompilerParams(vmem_limit_bytes=32 * 2**20),
        cost_estimate=pl.CostEstimate(flops=2 * tokens * D * FF, bytes_accessed=0, transcendentals=0),
        name="ffn_up",
    )(fin, weights, bias)


def layer_forward(embedded, x0, act, docs, small, weights):
    base = L + 2
    bias = jnp.concatenate([small[base + 6], jnp.zeros((D,), jnp.float32), small[base + 7]])
    qkv = (matmul(act, weights[:, 0 : 3 * D]) + bias).astype(jnp.bfloat16)
    out, lse = attend(qkv, docs)
    rone = x0 + (matmul(out, weights[:, 3 * D : 4 * D]) + small[base + 8])
    hone = norm_rows(rone, small[base + 2], small[base + 3])
    fin = hone.astype(jnp.bfloat16)
    gated, slope = ffn_up(fin, weights, small[base + 10 :].reshape(1, FF))
    rtwo = hone + (matmul_nt(gated, weights[:, 4 * D + FF :]) + small[base + 9])
    htwo = norm_rows(rtwo, small[base + 4], small[base + 5])
    return (htwo, (embedded, act, qkv, lse, out, rone, fin, slope, gated, rtwo))


def layer_backward(dhtwo, kept, docs, small, weights):
    embedded, act, qkv, lse, out, rone, fin, slope, gated, rtwo = kept
    base = L + 2
    _, pull = jax.vjp(norm_rows, rtwo, small[base + 4], small[base + 5])
    drtwo, dgain_two, dshift_two = pull(dhtwo)
    dffn = drtwo.astype(jnp.bfloat16)
    down = WorkerPiece((dffn, gated))
    dgated = matmul(dffn, weights[:, 4 * D + FF :])
    dupper = (dgated * slope.astype(jnp.float32)).astype(jnp.bfloat16)
    dupper = down.received(dupper)
    dupper = down.across(dupper)
    up = WorkerPiece((fin, dupper))
    dhone = drtwo + matmul_nt(dupper, weights[:, 4 * D : 4 * D + FF])
    _, pull = jax.vjp(norm_rows, rone, small[base + 2], small[base + 3])
    drone, dgain_one, dshift_one = pull(dhone)
    dattn = drone.astype(jnp.bfloat16)
    dout = matmul_nt(dattn, weights[:, 3 * D : 4 * D]).astype(jnp.bfloat16)
    dout = up.received(dout)
    dout = up.across(dout)
    dqkv = attend_back(qkv, dout, lse, docs)
    (dqkv,) = down.crossed(dqkv)
    down.finish()
    mixed = WorkerPiece((act, dqkv), (out, dattn))
    even = (docs.reshape(L, 1) % 2 == 0).astype(jnp.float32)
    dembed, embed_rows, bias_qkv = embed_back(
        mixed.across(dqkv), weights, drone, embedded, small[base], even
    )
    (dembed,) = up.crossed(dembed)
    up.finish()
    vectors = jnp.stack(
        [
            embed_rows[0],
            embed_rows[1],
            dgain_one,
            dshift_one,
            dgain_two,
            dshift_two,
            bias_qkv[0, 0:D],
            bias_qkv[0, 2 * D : 3 * D],
            jnp.sum(dattn, axis=0, dtype=jnp.float32),
            jnp.sum(dffn, axis=0, dtype=jnp.float32),
        ]
    )
    bias_up = jnp.sum(dupper, axis=0, dtype=jnp.float32).reshape(FF // D, D)
    vectors = jnp.concatenate([embed_rows[2:4], vectors, bias_up], axis=0)
    return (dembed, vectors, (mixed, up, down))


def paired_mesh():
    return lax.axis_size("wide") == 8 and lax.axis_size("narrow") == 4


def together(*values):
    return lax.optimization_barrier(values)


def swap_pairs(size, bit):
    return [(place, place ^ bit) for place in range(size)]


def cycle(size, by):
    return [(place, (place + by) % size) for place in range(size)]


def summed_over(value, axis):
    size = lax.axis_size(axis)
    if size & (size - 1):
        return lax.psum(value, axis)
    bit = 1
    while bit < size:
        value = value + lax.ppermute(value, axis, swap_pairs(size, bit))
        bit *= 2
    return value


def gathered_near(value, beside=None):
    size = lax.axis_size("narrow")
    rows = value.shape[0]
    around = [value]
    for by in range(1, size):
        around.append(lax.ppermute(value, "narrow", cycle(size, size - by)))
    if beside is not None:
        *around, beside = together(*around, beside)
    place = lax.axis_index("narrow")
    whole = jnp.zeros((size * rows,) + value.shape[1:], value.dtype)
    for by, part in enumerate(around):
        start = lax.rem(place + by, size) * rows
        whole = lax.dynamic_update_slice_in_dim(whole, part, start, 0)
    return whole if beside is None else (whole, beside)


def scattered_near(value):
    size = lax.axis_size("narrow")
    rows = value.shape[0] // size
    place = lax.axis_index("narrow")
    total = lax.dynamic_slice_in_dim(value, place * rows, rows, 0)
    for by in range(1, size):
        target = lax.rem(place + by, size)
        give = lax.dynamic_slice_in_dim(value, target * rows, rows, 0).astype(jnp.bfloat16)
        take = lax.ppermute(give, "narrow", cycle(size, by))
        total = total + take.astype(jnp.float32)
    return total


def sent_around(blocks):
    size = lax.axis_size("narrow")
    place = lax.axis_index("narrow")

    def block(by):
        return lax.dynamic_index_in_dim(blocks, lax.rem(place + by, size), 0, keepdims=False)

    return [block(0)] + [
        lax.ppermute(block(by), "narrow", cycle(size, by)) for by in range(1, size)
    ]


def block_kernel(steps, place_ref, *refs):
    pairs = len(steps) - 1
    lefts, rights, terms, out_ref = refs[:pairs], refs[pairs : 2 * pairs], refs[2 * pairs : -1], refs[-1]
    step = pl.program_id(0)
    for index in range(pairs):

        @pl.when((step >= steps[index]) & (step < steps[index + 1]))
        def _():
            total = matmul_tn(lefts[index][...], rights[index][...])
            for term_ref in terms:
                total = total + term_ref[...].astype(jnp.float32)
            out_ref[...] = total.astype(jnp.bfloat16)


def gradient_block(pairs, place, terms):
    block = D
    size = D // lax.axis_size("narrow")
    steps = [0]
    for _, right in pairs:
        steps.append(steps[-1] + right.shape[1] // block)
    tokens = pairs[0][0].shape[0]

    def right_of(index):
        low, count = steps[index], steps[index + 1] - steps[index]
        return pl.BlockSpec(
            (tokens, block), lambda step, place: (0, jnp.clip(step - low, 0, count - 1))
        )

    piece = pl.BlockSpec((size, block), lambda step, place: (0, step))
    return pl.pallas_call(
        functools.partial(block_kernel, steps),
        grid_spec=pltpu.PrefetchScalarGridSpec(
            num_scalar_prefetch=1,
            grid=(steps[-1],),
            in_specs=[pl.BlockSpec((tokens, size), lambda step, place: (0, place[0]))] * len(pairs)
            + [right_of(index) for index in range(len(pairs))]
            + [piece] * len(terms),
            out_specs=piece,
        ),
        out_shape=jax.ShapeDtypeStruct((size, steps[-1] * block), jnp.bfloat16),
        compiler_params=pltpu.CompilerParams(vmem_limit_bytes=24 * 2**20),
        cost_estimate=FREE,
        name="gradient_block",
    )(place[None], *[left for left, _ in pairs], *[right for _, right in pairs], *terms)


class WorkerPiece:
    def __init__(self, *pairs):
        self.pairs = pairs
        self.paired = paired_mesh()
        if not self.paired:
            return
        self.core = lax.axis_index("wide") % 2
        self.pair, self.side = lax.axis_index("narrow") // 2, lax.axis_index("narrow") % 2
        cores = swap_pairs(lax.axis_size("wide"), 1)
        self.far = lax.ppermute(self.block(1 - self.core, 1 - self.side), "wide", cores)
        self.near = lax.ppermute(self.block(1 - self.core, self.side), "wide", cores)

    def block(self, core, side, *terms):
        return gradient_block(self.pairs, 2 * core + side, terms)

    def received(self, value):
        if self.paired:
            value, self.far, self.near = together(value, self.far, self.near)
        return value

    def across(self, value):
        if self.paired:
            sides = swap_pairs(lax.axis_size("narrow"), 1)
            away = self.block(self.core, 1 - self.side, self.far)
            away, value = together(away, value)
            self.away = lax.ppermute(away, "narrow", sides)
        return value

    def crossed(self, *values):
        if self.paired:
            *values, self.away = together(*values, self.away)
        return values

    def finish(self, *values):
        if not self.paired:
            blocks = [matmul_tn(left, right).astype(jnp.bfloat16) for left, right in self.pairs]
            grad = jnp.concatenate(blocks, axis=1)
            self.result = lax.psum_scatter(grad, "narrow", scatter_dimension=0, tiled=True)
            return values
        n_wide, n_narrow = lax.axis_size("wide"), lax.axis_size("narrow")
        total = self.block(self.core, self.side, self.near, self.away)
        moves = []
        for wide in range(n_wide):
            for narrow in range(n_narrow):
                if narrow // 2 != wide % 2:
                    target_wide = wide - wide % 2 + narrow // 2
                    target = target_wide * n_narrow + 2 * (wide % 2) + narrow % 2
                    moves.append((wide * n_narrow + narrow, target))
        total, *values = together(total, *values)
        moved = lax.ppermute(total, ("wide", "narrow"), moves)
        self.result = jnp.where(self.pair == self.core, total, moved)
        return values


def hosted_rows(token_ids, mlm_labels, mlm_valid, doc_ids, mlm_pos):
    n_wide, n_narrow = lax.axis_size("wide"), lax.axis_size("narrow")
    packed = jnp.concatenate([token_ids, mlm_labels, mlm_valid], axis=1)[None]
    for bit, place in zip((1, 2, 4), wide_places()):
        other = lax.ppermute(packed, "wide", swap_pairs(n_wide, bit))
        first, second = jnp.where(place == 0, packed, other), jnp.where(place == 0, other, packed)
        packed = jnp.concatenate([first, second], axis=0)
    width = packed.shape[2]
    hosted = packed.reshape(n_wide // 2, 2, 2, 2, width).transpose(1, 2, 0, 3, 4)
    hosted = hosted.reshape(n_narrow, n_wide, width)
    column = lax.dynamic_index_in_dim(hosted, lax.axis_index("wide"), 1, keepdims=False)
    moves = []
    for wide in range(n_wide):
        for row in range(n_narrow):
            target_wide = wide - wide % 2 + row % 2
            target_narrow = 2 * (wide % 2) + row // 2
            moves.append((wide * n_narrow + row, target_wide * n_narrow + target_narrow))
    own = lax.ppermute(jnp.concatenate([doc_ids, mlm_pos], axis=1), ("wide", "narrow"), moves)
    return (
        hosted[:, :, 0:L],
        column[:, L : L + MPS],
        column[:, L + MPS :],
        own[:, 0:L],
        own[:, L:],
    )


STREAMS = 2


class Owners:
    def __init__(self, tokens, vshard):
        size = lax.axis_size("narrow")
        place = lax.axis_index("narrow")
        count = tokens.shape[1]
        self.room = count * 7 // 16
        owner = tokens // vshard
        held = (owner[None] == jnp.arange(size)[:, None, None]).astype(jnp.bfloat16)
        tiles = held.reshape(-1, count // 128, 128)
        order = jnp.arange(128)
        within = jnp.einsum(
            "btl,lm->btm",
            tiles,
            (order[:, None] < order[None]).astype(jnp.bfloat16),
            preferred_element_type=jnp.float32,
        )
        sums = jnp.sum(tiles.astype(jnp.float32), axis=2)
        tile = jnp.arange(count // 128)
        before = jnp.sum(jnp.where(tile[:, None] < tile[None], sums[:, :, None], 0.0), axis=1)
        rank = (within + before[..., None]).reshape(size, size, count) * held.astype(jnp.float32)
        rank = jnp.sum(rank, axis=0).astype(jnp.int32)
        self.full = jnp.max(jnp.sum(sums, axis=1)) > self.room
        self.count, self.vshard = count, vshard
        own = lax.dynamic_index_in_dim(owner, place, 0, keepdims=False)
        self.rank = lax.dynamic_index_in_dim(rank, place, 0, keepdims=False)
        self.behind = lax.rem(place - own + size, size)
        self.slots = jnp.where(owner == place, tokens - place * vshard, vshard)

    def behind_slots(self, room):
        return self.behind * room + jnp.minimum(self.rank, room - 1)


def pack_kernel(ids_ref, table_ref, out_ref, held, *rows):
    step, count, size = pl.program_id(0), out_ref.shape[1], table_ref.shape[0]

    @pl.when(step == 0)
    def _():
        held[0:size, :] = table_ref[...]
        held[size:, :] = jnp.zeros((8, table_ref.shape[1]), jnp.float32)
        for part in rows:
            part[...] = jnp.zeros_like(part)

    base = [(step * len(rows) + index) * count for index in range(len(rows))]

    def some(turn, used):
        used = list(used)
        for by in range(8):
            for index, part in enumerate(rows):
                place = ids_ref[base[index] + turn * 8 + by]
                part[pl.ds(used[index], 1), :] = held[pl.ds(place, 1), :]
                used[index] = used[index] + jnp.where(place < size, 1, 0)
        return tuple(used)

    lax.fori_loop(0, count // 8, some, (0,) * len(rows))
    for index, part in enumerate(rows):
        out_ref[index] = part[0:count, :].astype(out_ref.dtype)


def packed_rows(ids, table):
    size, cols = table.shape
    places, count = ids.shape
    return pl.pallas_call(
        pack_kernel,
        grid_spec=pltpu.PrefetchScalarGridSpec(
            num_scalar_prefetch=1,
            grid=(places // STREAMS,),
            in_specs=[pl.BlockSpec((size, cols), lambda step, ids: (0, 0))],
            out_specs=pl.BlockSpec((STREAMS, count, cols), lambda step, ids: (step, 0, 0)),
            scratch_shapes=[pltpu.VMEM((size + 8, cols), jnp.float32)]
            + [pltpu.VMEM((count + 8, cols), jnp.float32)] * STREAMS,
        ),
        out_shape=jax.ShapeDtypeStruct((places, count, cols), jnp.bfloat16),
        compiler_params=pltpu.CompilerParams(vmem_limit_bytes=40 * 2**20),
        cost_estimate=pl.CostEstimate(flops=0, bytes_accessed=0, transcendentals=0),
        name="pack_rows",
    )(ids.reshape(-1), table)


def take_kernel(ids_ref, table_ref, out_ref, held, rows):
    held[...] = table_ref[...].astype(jnp.float32)

    @pl.loop(0, out_ref.shape[0], step=16)
    def _(first):
        for by in range(16):
            rows[pl.ds(first + by, 1), :] = held[pl.ds(ids_ref[first + by], 1), :]

    out_ref[...] = rows[...].astype(out_ref.dtype)


def taken_rows(ids, table):
    count, cols = ids.shape[0], table.shape[1]
    return pl.pallas_call(
        take_kernel,
        grid_spec=pltpu.PrefetchScalarGridSpec(
            num_scalar_prefetch=1,
            grid=(1,),
            in_specs=[pl.BlockSpec(table.shape, lambda step, ids: (0, 0))],
            out_specs=pl.BlockSpec((count, cols), lambda step, ids: (0, 0)),
            scratch_shapes=[
                pltpu.VMEM(table.shape, jnp.float32),
                pltpu.VMEM((count, cols), jnp.float32),
            ],
        ),
        out_shape=jax.ShapeDtypeStruct((count, cols), table.dtype),
        compiler_params=pltpu.CompilerParams(vmem_limit_bytes=40 * 2**20),
        cost_estimate=FREE,
        name="take_rows",
    )(ids, table)


def add_kernel(ids_ref, values_ref, out_ref, rows, *sums):
    size = out_ref.shape[0]
    places, length = rows.shape[0:2]
    split = len(sums) // places
    each = length // split
    for part in sums:
        part[...] = jnp.zeros_like(part)
    rows[...] = values_ref[:, 0:length, :].astype(jnp.float32)

    @pl.loop(0, each, step=8)
    def _(first):
        for by in range(8):
            for index, part in enumerate(sums):
                at = index % split * each + first + by
                place = ids_ref[index // split * length + at]
                part[pl.ds(place, 1), :] += rows[index // split, pl.ds(at, 1), :]

    total = sums[0][0:size, :]
    for part in sums[1:]:
        total = total + part[0:size, :]
    out_ref[...] = total


def added_rows(ids, values, size):
    places, length = ids.shape
    cols = values.shape[2]
    return pl.pallas_call(
        add_kernel,
        grid_spec=pltpu.PrefetchScalarGridSpec(
            num_scalar_prefetch=1,
            grid=(1,),
            in_specs=[pl.BlockSpec(values.shape, lambda step, ids: (0, 0, 0))],
            out_specs=pl.BlockSpec((size, cols), lambda step, ids: (0, 0)),
            scratch_shapes=[pltpu.VMEM((places, length, cols), jnp.float32)]
            + [pltpu.VMEM((size + 8, cols), jnp.float32)] * (2 * places),
        ),
        out_shape=jax.ShapeDtypeStruct((size, cols), jnp.float32),
        compiler_params=pltpu.CompilerParams(vmem_limit_bytes=62 * 2**20),
        cost_estimate=FREE,
        name="add_rows",
    )(ids.reshape(-1), values)


def span_kernel(momentum_ref, grad_ref, error_ref, span_ref, sum_ref):
    grad = grad_ref[...].astype(jnp.float32)
    span = BETA * momentum_ref[...] + (1.0 - BETA) * grad + error_ref[0]
    span_ref[...] = span

    @pl.when(pl.program_id(0) == 0)
    def _():
        sum_ref[...] = jnp.zeros_like(sum_ref)

    sum_ref[...] += jnp.sum(jnp.abs(span), axis=0, keepdims=True)


def span_of(momentum, grad, error, start):
    rows, cols = grad.shape
    block = 1024
    first = start // block
    span, sums = pl.pallas_call(
        span_kernel,
        grid=(cols // block,),
        in_specs=[
            pl.BlockSpec((rows, block), lambda step: (0, first + step)),
            pl.BlockSpec((rows, block), lambda step: (0, step)),
            pl.BlockSpec((1, rows, block), lambda step: (0, 0, first + step)),
        ],
        out_specs=[
            pl.BlockSpec((rows, block), lambda step: (0, step)),
            pl.BlockSpec((1, block), lambda step: (0, 0)),
        ],
        out_shape=[
            jax.ShapeDtypeStruct((rows, cols), jnp.float32),
            jax.ShapeDtypeStruct((1, block), jnp.float32),
        ],
        compiler_params=pltpu.CompilerParams(vmem_limit_bytes=60 * 2**20),
        cost_estimate=pl.CostEstimate(flops=0, bytes_accessed=2 * 10**7, transcendentals=0),
        name="span",
    )(momentum, grad, error)
    return span, jnp.sum(sums)


def press_kernel(steps, core_ref, scale_ref, *refs):
    *span_refs, error_ref, give_ref, keep_ref = refs
    core = pl.program_id(2)
    step = pressed_step(pl.program_id(0), pl.program_id(1), core)
    scale = scale_ref[0]
    inverse = scale_ref[1]
    for index, span_ref in enumerate(span_refs):

        @pl.when((step >= steps[index]) & (step < steps[index + 1]))
        def _():
            span = span_ref[...]
            sent = scale * jnp.tanh(span * inverse)
            error_ref[0] = span - sent
            low = sent.astype(jnp.bfloat16)

            @pl.when(core == core_ref[0])
            def _():
                keep_ref[0] = low

            @pl.when(core != core_ref[0])
            def _():
                give_ref[0] = low


def pressed_step(chip, column, core):
    return (2 * chip + core) * 3 + column


def pressed(spans, scale, parts):
    rows = spans[0].shape[0]
    cols = sum(span.shape[1] for span in spans)
    block = cols // parts // 3
    steps = [0]
    for span in spans:
        steps.append(steps[-1] + span.shape[1] // block)

    def of(index):
        low, count = steps[index], steps[index + 1] - steps[index]

        def place(chip, column, core, _):
            return (0, jnp.clip(pressed_step(chip, column, core) - low, 0, count - 1))

        return pl.BlockSpec((rows, block), place)

    half = pl.BlockSpec((1, rows, block), lambda chip, column, core, _: (chip, 0, column))
    half_shape = jax.ShapeDtypeStruct((parts // 2, rows, cols // parts), jnp.bfloat16)
    return pl.pallas_call(
        functools.partial(press_kernel, steps),
        grid_spec=pltpu.PrefetchScalarGridSpec(
            num_scalar_prefetch=1,
            grid=(parts // 2, 3, 2),
            in_specs=[pl.BlockSpec(memory_space=pltpu.SMEM)] + [of(i) for i in range(len(spans))],
            out_specs=[
                pl.BlockSpec(
                    (1, rows, block),
                    lambda chip, column, core, _: (0, 0, pressed_step(chip, column, core)),
                ),
                half,
                half,
            ],
        ),
        out_shape=[jax.ShapeDtypeStruct((1, rows, cols), jnp.float32), half_shape, half_shape],
        compiler_params=pltpu.CompilerParams(vmem_limit_bytes=60 * 2**20),
        cost_estimate=FREE,
        name="press",
    )(wide_places()[0][None], jnp.stack([scale, 1.0 / scale]), *spans)


def update_kernel(grad_ref, head_ref, table_ref, first_ref, second_ref, *out_refs):
    first_out, update_ref, weight_sum, update_sum = out_refs
    grad = grad_ref[...] + head_ref[...].astype(jnp.float32)
    first = BETA * first_ref[...] + (1.0 - BETA) * grad
    table = table_ref[...]
    update = first / (jnp.sqrt(second_ref[...]) + OPT_EPS) + DECAY * table
    first_out[...] = first
    update_ref[...] = update

    @pl.when(pl.program_id(0) == 0)
    def _():
        weight_sum[...] = jnp.zeros_like(weight_sum)
        update_sum[...] = jnp.zeros_like(update_sum)

    weight_sum[...] += jnp.sum(table * table, axis=0, keepdims=True)
    update_sum[...] += jnp.sum(update * update, axis=0, keepdims=True)


def table_update(grad, head, table, first, second):
    size, cols = table.shape
    block = size // 9 if size % 9 == 0 and size // 9 % 16 == 0 else size
    whole = pl.BlockSpec((block, cols), lambda step: (step, 0))
    line = pl.BlockSpec((1, cols), lambda step: (0, 0))
    moment, update, *sums = pl.pallas_call(
        update_kernel,
        grid=(size // block,),
        in_specs=[whole] * 5,
        out_specs=[whole, whole, line, line],
        out_shape=[jax.ShapeDtypeStruct((size, cols), jnp.float32)] * 2
        + [jax.ShapeDtypeStruct((1, cols), jnp.float32)] * 2,
        compiler_params=pltpu.CompilerParams(vmem_limit_bytes=56 * 2**20),
        cost_estimate=FREE,
        name="update",
    )(grad, head, table, first, second)
    return moment, update, tuple(jnp.sum(part)[None] for part in sums)


def wide_places():
    wide_me = lax.axis_index("wide")
    return wide_me % 2, wide_me // 2 % 2, wide_me // 4


def scattered_sum(give, keep):
    n_wide = lax.axis_size("wide")
    _, x, y = wide_places()

    def send(value, bit):
        return lax.ppermute(value.astype(jnp.bfloat16), "wide", swap_pairs(n_wide, bit))

    take = send(give, 1)
    half = keep.shape[1] // 2

    def chip(y_of, x_of, part):
        start, size = (2 * y_of + x_of, part * half, 0), (1, half, keep.shape[2])
        own, other = lax.dynamic_slice(keep, start, size), lax.dynamic_slice(take, start, size)
        return own[0].astype(jnp.float32) + other[0].astype(jnp.float32)

    upper_far = send(chip(1 - y, 1 - x, 0), 2)
    lower_far = send(chip(1 - y, 1 - x, 1), 4)
    upper_near = send(chip(y, 1 - x, 0), 2)
    lower_near = send(chip(1 - y, x, 1), 4)
    upper_far = send(chip(1 - y, x, 0) + upper_far.astype(jnp.float32), 4)
    lower_far = send(chip(y, 1 - x, 1) + lower_far.astype(jnp.float32), 2)
    own_upper = chip(y, x, 0) + upper_near.astype(jnp.float32) + upper_far.astype(jnp.float32)
    own_lower = chip(y, x, 1) + lower_near.astype(jnp.float32) + lower_far.astype(jnp.float32)
    return jnp.concatenate([own_upper, own_lower], axis=0)


def small_halved(value):
    n_wide = lax.axis_size("wide")
    for bit, place in list(zip((1, 2, 4), wide_places()))[::-1]:
        half = value.shape[1] // 2
        give = lax.dynamic_slice_in_dim(value, (1 - place) * half, half, 1).astype(jnp.bfloat16)
        keep = lax.dynamic_slice_in_dim(value, place * half, half, 1)
        value = keep + lax.ppermute(give, "wide", swap_pairs(n_wide, bit)).astype(jnp.float32)
    return value


def small_update(grad, first, second, weight):
    first = BETA * first + (1.0 - BETA) * grad.astype(jnp.float32)
    return first, first / (jnp.sqrt(second) + OPT_EPS) + DECAY * weight


def shards(
    token_ids,
    doc_ids,
    mlm_pos,
    mlm_labels,
    mlm_valid,
    table,
    table_m,
    table_v,
    small,
    small_m,
    small_v,
    layer,
    layer_m,
    layer_v,
    worker_err,
    server_err,
):
    n_wide, n_narrow = lax.axis_size("wide"), lax.axis_size("narrow")
    narrow_me = lax.axis_index("narrow")
    wide_me = lax.axis_index("wide")
    seqs = doc_ids.shape[0]
    paired = paired_mesh()
    vshard = table.shape[0]
    count = summed_over(jnp.sum(mlm_valid.astype(jnp.float32)), "wide")
    table_low, layer_low = table.astype(jnp.bfloat16), layer.astype(jnp.bfloat16)
    if paired:
        token_ids, mlm_labels, mlm_valid, doc_ids, mlm_pos = hosted_rows(
            token_ids, mlm_labels, mlm_valid, doc_ids, mlm_pos
        )
        table_cut = vshard * 5 // 8 // 16 * 16
        table_first = lax.all_gather(table_low[0:table_cut], "wide", axis=1, tiled=True)
        owners = Owners(token_ids.reshape(n_narrow, n_wide * L), vshard)
        picked = packed_rows(owners.slots, table)
        layer_rows, picked = gathered_near(layer_low, picked)
        layer_rows, table_first = together(layer_rows, table_first)
    else:
        layer_rows = lax.all_gather(layer_low, "narrow", axis=0, tiled=True)
    weights = lax.all_gather(layer_rows, "wide", axis=1, tiled=True)
    if paired:

        def looked_up(room):
            rows = sent_around(picked[:, 0:room])
            return taken_rows(owners.behind_slots(room), jnp.concatenate(rows, axis=0))

        layer_rows, picked = together(layer_rows, picked)
        looked = looked_up(owners.room)
        looked = lax.cond(owners.full, lambda: looked_up(owners.count), lambda: looked)
        looked = lax.all_to_all(looked.reshape(n_wide, L, -1), "wide", 0, 0)
        looked = looked.transpose(1, 0, 2).reshape(1, L, D)
        looked, count, doc_ids, mlm_pos = together(looked, count, doc_ids, mlm_pos)
    else:
        local_ids = token_ids - narrow_me * vshard
        inside = (local_ids >= 0) & (local_ids < vshard)
        slots = jnp.where(inside, local_ids, vshard).reshape(-1)
        table_cols = lax.all_gather(table_low, "wide", axis=1, tiled=True)
        picked = jnp.take(table_cols, jnp.clip(local_ids, 0, vshard - 1), axis=0)
        picked = jnp.where(inside[..., None], picked, 0.0)
        looked = lax.psum_scatter(picked, "narrow", scatter_dimension=0, tiled=True)
    looked = looked.astype(jnp.float32)
    even_doc = (doc_ids % 2 == 0)[..., None]
    embedded = looked + small[0:L][None] + jnp.where(even_doc, small[L], small[L + 1])
    embedded = embedded.reshape(seqs * L, D)
    x0 = norm_rows(embedded, small[L + 2], small[L + 3])
    act = x0.astype(jnp.bfloat16)
    if paired:
        table_cols = jnp.zeros((vshard, D), jnp.bfloat16)
        table_cols = lax.dynamic_update_slice(table_cols, table_first, (0, 0))
        table_last, weights, act, table_cols = together(
            table_low[table_cut:], weights, act, table_cols
        )
        table_last = lax.all_gather(table_last, "wide", axis=1, tiled=True)
        table_cols = lax.dynamic_update_slice(table_cols, table_last, (table_cut, 0))
    htwo, kept = layer_forward(embedded, x0, act, doc_ids, small, weights)
    hmask = jnp.take_along_axis(htwo.reshape(seqs, L, D), mlm_pos[..., None], axis=1)
    hmask = hmask.reshape(seqs * MPS, D).astype(jnp.bfloat16)
    if paired:
        group_h = gathered_near(hmask)
    else:
        group_h = lax.all_gather(hmask, "narrow", axis=0, tiled=True)
    vocab = narrow_me * vshard + jnp.arange(vshard)
    logits = jnp.where((vocab < VREAL)[None], matmul_nt(group_h, table_cols), -1000000000.0)
    labels = mlm_labels.reshape(-1)
    hit = vocab[None] == labels[:, None]
    top = jnp.max(logits, axis=1)
    total = jnp.sum(jnp.exp(logits - top[:, None]), axis=1)
    target = jnp.sum(jnp.where(hit, logits, 0.0), axis=1)
    if paired:
        stats = gathered_near(jnp.stack([top, total, target])[None])
        top, total, target = stats[0]
        for place in range(1, stats.shape[0]):
            top, total, target = merge_rows((top, total, target), tuple(stats[place]))
    else:
        top, total, target = joined((top, total, target), "narrow", merge_rows)
    lse = top + jnp.log(total)
    flags = mlm_valid.reshape(-1).astype(jnp.float32)
    own = seqs * MPS
    own_loss = lax.dynamic_slice_in_dim(flags * (lse - target), narrow_me * own, own)
    dlogit = (
        (jnp.exp(logits - lse[:, None]) - hit.astype(jnp.float32)) * (flags / count)[:, None]
    ).astype(jnp.bfloat16)
    dhmask = matmul(dlogit, table_cols)
    if paired:
        dhmask = scattered_near(dhmask)
        blocks = group_h.reshape(-1, n_wide, D // n_wide)
        table_head = jnp.einsum("sv,swc->wvc", dlogit, blocks, preferred_element_type=jnp.float32)
        table_head, dhmask = together(table_head.astype(jnp.bfloat16), dhmask)
        table_head = lax.psum_scatter(table_head, "wide", scatter_dimension=0)
    else:
        dhmask = lax.psum_scatter(dhmask, "narrow", scatter_dimension=0, tiled=True)
    dhtwo = (
        jnp.zeros((seqs, L, D), jnp.float32)
        .at[jnp.arange(seqs)[:, None], mlm_pos]
        .add(dhmask.reshape(seqs, MPS, D))
    )
    dembed, vectors, pieces = layer_backward(
        dhtwo.reshape(seqs * L, D), kept, doc_ids, small, weights
    )
    dembed_rows = dembed.reshape(seqs, L, D)
    small_grad = jnp.concatenate([jnp.sum(dembed_rows, axis=0), vectors], axis=0)
    mixed = pieces[0]
    if paired:
        cut = dembed.astype(jnp.bfloat16).reshape(L, n_wide, D // n_wide).transpose(1, 0, 2)
        cut = lax.all_to_all(cut, "wide", 0, 0).reshape(n_wide * L, D // n_wide)
        halved = small_halved(small_grad).astype(jnp.bfloat16)
        down, up = pieces[2], pieces[1]
        mixed.away, down.result = together(mixed.away, down.result)
        mixed.finish()
        spans = [span_of(layer_m, up.result, worker_err, 4 * D)]
        spans.append(span_of(layer_m, down.result, worker_err, 8 * D))
        cut, mixed.result, spans, table_head = together(
            jnp.concatenate([cut, halved]), mixed.result, spans, table_head
        )
        group_rows = lax.all_gather(cut, "narrow", axis=0)
    else:
        mixed.finish()
        group_rows = lax.all_gather(dembed_rows.astype(jnp.bfloat16), "narrow", axis=0, tiled=True)
        table_grad = matmul_tn(dlogit, group_h).at[slots].add(
            group_rows.reshape(-1, D).astype(jnp.float32), mode="drop"
        )
        cut = table_grad.astype(jnp.bfloat16).reshape(vshard, n_wide, D // n_wide)
        table_grad = lax.psum_scatter(cut.transpose(1, 0, 2), "wide", scatter_dimension=0)
        table_grad = table_grad.astype(jnp.float32)
    part_cols = layer.shape[1]
    if paired:
        spans.insert(0, span_of(layer_m, mixed.result, worker_err, 0))
        total = sum(amount for _, amount in spans)
        spans = [span for span, _ in spans]
        scale = total / (layer_m.shape[0] * layer_m.shape[1]) + MAG_EPS
        new_worker, give, keep = pressed(spans, scale, n_wide)
        server_in = scattered_sum(give, keep) / n_wide + server_err
    else:
        worker_grad = jnp.concatenate([piece.result for piece in pieces], axis=1)
        span = BETA * layer_m + (1.0 - BETA) * worker_grad.astype(jnp.float32) + worker_err[0]
        scale = jnp.mean(jnp.abs(span)) + MAG_EPS
        sent = scale * jnp.tanh(span / scale)
        new_worker = (span - sent)[None]
        summed = lax.psum(sent.astype(jnp.bfloat16), "wide").astype(jnp.float32)
        mixed = lax.dynamic_slice_in_dim(summed, wide_me * part_cols, part_cols, 1) / n_wide
        server_in = mixed + server_err
    sscale = jnp.mean(jnp.abs(server_in)) + MAG_EPS
    server_out = sscale * jnp.tanh(server_in / sscale)
    new_server = server_in - server_out
    server_low = server_out.astype(jnp.bfloat16)
    layer_upd = server_out / (jnp.sqrt(layer_v) + OPT_EPS) + DECAY * layer
    column = wide_me * part_cols + jnp.arange(part_cols)
    which = (
        (column >= 3 * D).astype(jnp.int32)
        + (column >= 4 * D).astype(jnp.int32)
        + (column >= 4 * D + FF).astype(jnp.int32)
    )
    onehot = (which[:, None] == jnp.arange(4)[None]).astype(jnp.float32)
    wsq = jnp.sum(jnp.sum(layer * layer, axis=0)[:, None] * onehot, axis=0)
    usq = jnp.sum(jnp.sum(layer_upd * layer_upd, axis=0)[:, None] * onehot, axis=0)
    small_square = jnp.sum(small * small)[None]
    if paired:
        new_server, wsq, usq, small_square, group_rows = together(
            new_server, wsq, usq, small_square, group_rows
        )
        table_grad = added_rows(owners.slots, group_rows, vshard)
        table_mom, table_upd, table_norms = table_update(
            table_grad, table_head, table, table_m, table_v
        )
        eighth = D // n_wide
        small_grad = jnp.sum(group_rows[:, n_wide * L :].astype(jnp.float32), axis=0)
        small_grad = small_grad.astype(jnp.bfloat16)

        def own(value):
            return lax.dynamic_slice_in_dim(value, wide_me * eighth, eighth, 1)

        _, own_upd = small_update(small_grad, own(small_m), own(small_v), own(small))
        small_norm = jnp.where(narrow_me == 0, jnp.sum(own_upd * own_upd), 0.0)
    else:
        small_grad = lax.psum(small_grad, ("wide", "narrow"))
        table_mom = BETA * table_m + (1.0 - BETA) * table_grad
        table_upd = table_mom / (jnp.sqrt(table_v) + OPT_EPS) + DECAY * table
        table_norms = (jnp.sum(table * table)[None], jnp.sum(table_upd * table_upd)[None])
    new_m = lax.all_gather(server_low, "wide", axis=1, tiled=True)
    if paired:
        small_grad, new_m, table_norms = together(small_grad, new_m, table_norms)
        small_grad = lax.all_gather(small_grad, "wide", axis=1, tiled=True)
    if not paired:
        _, small_upd = small_update(small_grad, small_m, small_v, small)
        small_norm = jnp.where((wide_me == 0) & (narrow_me == 0), jnp.sum(small_upd * small_upd), 0.0)
    parts = jnp.concatenate([wsq, usq, *table_norms, jnp.sum(own_loss)[None], small_norm[None]])
    sums = summed_over(summed_over(parts, "wide"), "narrow")
    if paired:
        sums, small_grad = together(sums, small_grad)
    small_mom, small_upd = small_update(small_grad, small_m, small_v, small)
    loss_sum = sums[10]
    wnorm = jnp.sqrt(jnp.concatenate([sums[0:4], sums[8:9], small_square]))
    unorm = jnp.sqrt(jnp.concatenate([sums[4:8], sums[9:10], sums[11:12]]))
    ratio = wnorm / unorm
    new_layer = layer - RATE * jnp.sum(onehot * ratio[None, 0:4], axis=1)[None] * layer_upd
    new_table = table - RATE * ratio[4] * table_upd
    new_small = small - RATE * ratio[5] * small_upd
    return (
        jnp.stack([loss_sum, count]),
        new_table,
        table_mom,
        new_small,
        small_mom,
        new_layer,
        new_m.astype(jnp.float32),
        new_worker,
        new_server,
        jnp.stack([wnorm, unorm]),
    )


def solution(mesh):
    placed = (
        P("wide", None),
        P(("wide", "narrow"), None),
        P(("wide", "narrow"), None),
        P("wide", None),
        P("wide", None),
        P("narrow", "wide"),
        P("narrow", "wide"),
        P("narrow", "wide"),
        P(),
        P(),
        P(),
        P("narrow", "wide"),
        P("narrow", None),
        P("narrow", "wide"),
        P("wide", "narrow", None),
        P("narrow", "wide"),
    )
    return jax.shard_map(
        shards,
        mesh=mesh,
        in_specs=placed,
        out_specs=(
            P(),
            P("narrow", "wide"),
            P("narrow", "wide"),
            P(),
            P(),
            P("narrow", "wide"),
            P("narrow", None),
            P("wide", "narrow", None),
            P("narrow", "wide"),
            P(),
        ),
        check_vma=False,
    )
```

```python
import functools

import jax
import jax.numpy as jnp
from jax import lax
from jax.experimental import pallas as pl
from jax.experimental.pallas import tpu as pltpu
from jax.sharding import PartitionSpec as P

D = 1024
HEADS = 16
HEAD = 64
FF = 4096
VREAL = 30522
L = 512
MPS = 80


LN_EPS = 1e-12
BETA = 0.9
DECAY = 0.01
RATE = 0.25
OPT_EPS = 1e-06
MAG_EPS = 1e-08

FREE = pl.CostEstimate(flops=0, bytes_accessed=0, transcendentals=0)


def joined(value, axis, join):
    pieces = jax.tree.map(lambda part: lax.all_gather(part, axis), value)
    head = jax.tree.map(lambda part: part[0], pieces)
    tail = jax.tree.map(lambda part: part[1:], pieces)
    subtotal, _ = lax.scan(lambda subtotal, slab: (join(subtotal, slab), None), head, tail)
    return subtotal


def norm_rows(x, gain, shift):
    mean = jnp.mean(x, axis=-1, keepdims=True)
    cent = x - mean
    var = jnp.mean(cent * cent, axis=-1, keepdims=True)
    return cent * lax.rsqrt(var + LN_EPS) * gain + shift


def matmul(left, right):
    return jnp.dot(left, right, preferred_element_type=jnp.float32)


def matmul_tn(left, right):
    return lax.dot_general(
        left, right, (((0,), (0,)), ((), ())), preferred_element_type=jnp.float32
    )


def matmul_nt(left, right):
    return lax.dot_general(
        left, right, (((1,), (1,)), ((), ())), preferred_element_type=jnp.float32
    )


def attend_kernel(q_ref, k_ref, v_ref, key_doc_ref, query_doc_ref, out_ref, lse_ref):
    same = key_doc_ref[...] == query_doc_ref[...]
    lane = lax.broadcasted_iota(jnp.int32, (1, 2 * HEAD), 1)
    outs = []
    for head in range(2):
        mine = lane // HEAD == head
        query = jnp.where(mine, q_ref[...] * 0.125, 0).astype(jnp.bfloat16)
        scores = jnp.where(same, matmul_nt(k_ref[...], query), -1000000000.0)
        top = jnp.max(scores, axis=0, keepdims=True)
        power = jnp.exp(scores - top)
        total = jnp.sum(power, axis=0, keepdims=True)
        lse_ref[0, head : head + 1, :] = top + jnp.log(total)
        prob = (power * (1.0 / total)).astype(jnp.bfloat16)
        outs.append(matmul_tn(prob, v_ref[...]))
    out_ref[...] = jnp.where(lane < HEAD, outs[0], outs[1]).astype(jnp.bfloat16)


def head_pairs(offset):
    return pl.BlockSpec((L, 2 * HEAD), lambda pair: (0, offset * HEADS // 2 + pair))


def attend(qkv, docs):
    return pl.pallas_call(
        attend_kernel,
        grid=(HEADS // 2,),
        in_specs=[
            head_pairs(0),
            head_pairs(1),
            head_pairs(2),
            pl.BlockSpec((L, 1), lambda pair: (0, 0)),
            pl.BlockSpec((1, L), lambda pair: (0, 0)),
        ],
        out_specs=[head_pairs(0), pl.BlockSpec((1, 2, L), lambda pair: (pair, 0, 0))],
        out_shape=[
            jax.ShapeDtypeStruct((L, D), jnp.bfloat16),
            jax.ShapeDtypeStruct((HEADS // 2, 2, L), jnp.float32),
        ],
        compiler_params=pltpu.CompilerParams(vmem_limit_bytes=40 * 2**20),
        cost_estimate=FREE,
        name="attend",
    )(qkv, qkv, qkv, docs.reshape(L, 1), docs.reshape(1, L))


def attend_back_kernel(q_ref, k_ref, v_ref, do_ref, lse_ref, key_doc_ref, query_doc_ref, out_ref):
    pair = pl.program_id(0)
    same = key_doc_ref[...] == query_doc_ref[...]
    lane = lax.broadcasted_iota(jnp.int32, (1, 2 * HEAD), 1)
    both = []
    for head in range(2):
        mine = lane // HEAD == head
        query = jnp.where(mine, q_ref[...] * 0.125, 0).astype(jnp.bfloat16)
        dout = jnp.where(mine, do_ref[...], 0).astype(jnp.bfloat16)
        scores = jnp.where(same, matmul_nt(k_ref[...], query), -1000000000.0)
        prob = jnp.exp(scores - lse_ref[0, head : head + 1, :])
        dvalue = matmul(prob.astype(jnp.bfloat16), dout)
        dprob = matmul_nt(v_ref[...], dout)
        delta = jnp.sum(prob * dprob, axis=0, keepdims=True)
        dscore = (prob * (dprob - delta)).astype(jnp.bfloat16)
        both.append((matmul_tn(dscore, k_ref[...]) * 0.125, matmul(dscore, query), dvalue))
    for part in range(3):
        value = jnp.where(lane < HEAD, both[0][part], both[1][part]).astype(jnp.bfloat16)
        start = pl.multiple_of(part * D + pair * 2 * HEAD, 2 * HEAD)
        out_ref[:, pl.ds(start, 2 * HEAD)] = value


def attend_back(qkv, dout, lse, docs):
    return pl.pallas_call(
        attend_back_kernel,
        grid=(HEADS // 2,),
        in_specs=[
            head_pairs(0),
            head_pairs(1),
            head_pairs(2),
            head_pairs(0),
            pl.BlockSpec((1, 2, L), lambda pair: (pair, 0, 0)),
            pl.BlockSpec((L, 1), lambda pair: (0, 0)),
            pl.BlockSpec((1, L), lambda pair: (0, 0)),
        ],
        out_specs=pl.BlockSpec((L, 3 * D), lambda pair: (0, 0)),
        out_shape=jax.ShapeDtypeStruct((L, 3 * D), jnp.bfloat16),
        compiler_params=pltpu.CompilerParams(vmem_limit_bytes=40 * 2**20),
        cost_estimate=FREE,
        name="attend_back",
    )(qkv, qkv, qkv, dout, lse, docs.reshape(L, 1), docs.reshape(1, L))


def merge_rows(first, second):
    peak = jnp.maximum(first[0], second[0])
    total = first[1] * jnp.exp(first[0] - peak) + second[1] * jnp.exp(second[0] - peak)
    return (peak, total, first[2] + second[2])


def embed_back_kernel(dqkv_ref, weight_ref, drone_ref, embedded_ref, gain_ref, even_ref, *refs):
    dembed_ref, rows_ref, sums_ref, total = refs
    step = pl.program_id(0)
    dqkv = dqkv_ref[...]
    part = matmul_nt(dqkv, weight_ref[...])
    sums_ref[...] = jnp.sum(dqkv.astype(jnp.float32), axis=0, keepdims=True)

    @pl.when(step == 0)
    def _():
        total[...] = drone_ref[...] + part

    @pl.when(step > 0)
    def _():
        total[...] += part

    @pl.when(step == pl.num_programs(0) - 1)
    def _():
        grad = total[...]
        embedded = embedded_ref[...]
        cent = embedded - jnp.mean(embedded, axis=1, keepdims=True)
        scale = lax.rsqrt(jnp.mean(cent * cent, axis=1, keepdims=True) + LN_EPS)
        normed = cent * scale
        inner = grad * gain_ref[...]
        inner_mean = jnp.mean(inner, axis=1, keepdims=True)
        along = jnp.mean(inner * normed, axis=1, keepdims=True)
        dembed = scale * (inner - inner_mean - normed * along)
        dembed_ref[...] = dembed
        even = even_ref[...]
        rows_ref[0:1, :] = jnp.sum(grad * normed, axis=0, keepdims=True)
        rows_ref[1:2, :] = jnp.sum(grad, axis=0, keepdims=True)
        rows_ref[2:3, :] = jnp.sum(dembed * even, axis=0, keepdims=True)
        rows_ref[3:4, :] = jnp.sum(dembed * (1.0 - even), axis=0, keepdims=True)
        rows_ref[4:8, :] = jnp.zeros((4, D), jnp.float32)


def embed_back(dqkv, weights, drone, embedded, gain, even):
    tokens = dqkv.shape[0]
    whole = pl.BlockSpec((tokens, D), lambda step: (0, 0))
    return pl.pallas_call(
        embed_back_kernel,
        grid=(3,),
        in_specs=[
            pl.BlockSpec((tokens, D), lambda step: (0, step)),
            pl.BlockSpec((D, D), lambda step: (0, step)),
            whole,
            whole,
            pl.BlockSpec((1, D), lambda step: (0, 0)),
            pl.BlockSpec((tokens, 1), lambda step: (0, 0)),
        ],
        out_specs=[
            whole,
            pl.BlockSpec((8, D), lambda step: (0, 0)),
            pl.BlockSpec((1, D), lambda step: (0, step)),
        ],
        out_shape=[
            jax.ShapeDtypeStruct((tokens, D), jnp.float32),
            jax.ShapeDtypeStruct((8, D), jnp.float32),
            jax.ShapeDtypeStruct((1, 3 * D), jnp.float32),
        ],
        scratch_shapes=[pltpu.VMEM((tokens, D), jnp.float32)],
        compiler_params=pltpu.CompilerParams(vmem_limit_bytes=40 * 2**20),
        cost_estimate=FREE,
        name="embed_back",
    )(dqkv, weights, drone, embedded, gain[None], even)


def ffn_kernel(fin_ref, weight_ref, bias_ref, gated_ref, slope_ref):
    upper = matmul(fin_ref[...], weight_ref[...]) + bias_ref[...]
    below = 0.5 + 0.5 * lax.erf(upper * 0.7071067811865476)
    gated_ref[...] = (upper * below).astype(jnp.bfloat16)
    density = 0.3989422804014327 * jnp.exp(-0.5 * upper * upper)
    slope_ref[...] = (below + upper * density).astype(jnp.bfloat16)


def ffn_up(fin, weights, bias):
    tokens = fin.shape[0]
    block = 512
    first = 4 * D // block
    out = pl.BlockSpec((tokens, block), lambda step: (0, step))
    return pl.pallas_call(
        ffn_kernel,
        grid=(FF // block,),
        in_specs=[
            pl.BlockSpec((tokens, D), lambda step: (0, 0)),
            pl.BlockSpec((D, block), lambda step: (0, first + step)),
            pl.BlockSpec((1, block), lambda step: (0, step)),
        ],
        out_specs=[out, out],
        out_shape=[jax.ShapeDtypeStruct((tokens, FF), jnp.bfloat16)] * 2,
        compiler_params=pltpu.CompilerParams(vmem_limit_bytes=32 * 2**20),
        cost_estimate=pl.CostEstimate(flops=2 * tokens * D * FF, bytes_accessed=0, transcendentals=0),
        name="ffn_up",
    )(fin, weights, bias)


def layer_forward(embedded, x0, act, docs, small, weights):
    base = L + 2
    bias = jnp.concatenate([small[base + 6], jnp.zeros((D,), jnp.float32), small[base + 7]])
    qkv = (matmul(act, weights[:, 0 : 3 * D]) + bias).astype(jnp.bfloat16)
    out, lse = attend(qkv, docs)
    rone = x0 + (matmul(out, weights[:, 3 * D : 4 * D]) + small[base + 8])
    hone = norm_rows(rone, small[base + 2], small[base + 3])
    fin = hone.astype(jnp.bfloat16)
    gated, slope = ffn_up(fin, weights, small[base + 10 :].reshape(1, FF))
    rtwo = hone + (matmul_nt(gated, weights[:, 4 * D + FF :]) + small[base + 9])
    htwo = norm_rows(rtwo, small[base + 4], small[base + 5])
    return (htwo, (embedded, act, qkv, lse, out, rone, fin, slope, gated, rtwo))


def layer_backward(dhtwo, kept, docs, small, weights):
    embedded, act, qkv, lse, out, rone, fin, slope, gated, rtwo = kept
    base = L + 2
    _, pull = jax.vjp(norm_rows, rtwo, small[base + 4], small[base + 5])
    drtwo, dgain_two, dshift_two = pull(dhtwo)
    dffn = drtwo.astype(jnp.bfloat16)
    down = WorkerPiece((dffn, gated))
    dgated = matmul(dffn, weights[:, 4 * D + FF :])
    dupper = (dgated * slope.astype(jnp.float32)).astype(jnp.bfloat16)
    dupper = down.received(dupper)
    dupper = down.across(dupper)
    up = WorkerPiece((fin, dupper))
    dhone = drtwo + matmul_nt(dupper, weights[:, 4 * D : 4 * D + FF])
    _, pull = jax.vjp(norm_rows, rone, small[base + 2], small[base + 3])
    drone, dgain_one, dshift_one = pull(dhone)
    dattn = drone.astype(jnp.bfloat16)
    dout = matmul_nt(dattn, weights[:, 3 * D : 4 * D]).astype(jnp.bfloat16)
    dout = up.received(dout)
    dout = up.across(dout)
    dqkv = attend_back(qkv, dout, lse, docs)
    (dqkv,) = down.crossed(dqkv)
    down.finish()
    mixed = WorkerPiece((act, dqkv), (out, dattn))
    even = (docs.reshape(L, 1) % 2 == 0).astype(jnp.float32)
    dembed, embed_rows, bias_qkv = embed_back(
        mixed.across(dqkv), weights, drone, embedded, small[base], even
    )
    (dembed,) = up.crossed(dembed)
    up.finish()
    vectors = jnp.stack(
        [
            embed_rows[0],
            embed_rows[1],
            dgain_one,
            dshift_one,
            dgain_two,
            dshift_two,
            bias_qkv[0, 0:D],
            bias_qkv[0, 2 * D : 3 * D],
            jnp.sum(dattn, axis=0, dtype=jnp.float32),
            jnp.sum(dffn, axis=0, dtype=jnp.float32),
        ]
    )
    bias_up = jnp.sum(dupper, axis=0, dtype=jnp.float32).reshape(FF // D, D)
    vectors = jnp.concatenate([embed_rows[2:4], vectors, bias_up], axis=0)
    return (dembed, vectors, (mixed, up, down))


def paired_mesh():
    return lax.axis_size("wide") == 8 and lax.axis_size("narrow") == 4


def together(*values):
    return lax.optimization_barrier(values)


def swap_pairs(size, bit):
    return [(place, place ^ bit) for place in range(size)]


def cycle(size, by):
    return [(place, (place + by) % size) for place in range(size)]


def summed_over(value, axis):
    size = lax.axis_size(axis)
    if size & (size - 1):
        return lax.psum(value, axis)
    bit = 1
    while bit < size:
        value = value + lax.ppermute(value, axis, swap_pairs(size, bit))
        bit *= 2
    return value


def gathered_near(value, beside=None):
    size = lax.axis_size("narrow")
    rows = value.shape[0]
    around = [value]
    for by in range(1, size):
        around.append(lax.ppermute(value, "narrow", cycle(size, size - by)))
    if beside is not None:
        *around, beside = together(*around, beside)
    place = lax.axis_index("narrow")
    whole = jnp.zeros((size * rows,) + value.shape[1:], value.dtype)
    for by, part in enumerate(around):
        start = lax.rem(place + by, size) * rows
        whole = lax.dynamic_update_slice_in_dim(whole, part, start, 0)
    return whole if beside is None else (whole, beside)


def scattered_near(value):
    size = lax.axis_size("narrow")
    rows = value.shape[0] // size
    place = lax.axis_index("narrow")
    total = lax.dynamic_slice_in_dim(value, place * rows, rows, 0)
    for by in range(1, size):
        target = lax.rem(place + by, size)
        give = lax.dynamic_slice_in_dim(value, target * rows, rows, 0).astype(jnp.bfloat16)
        take = lax.ppermute(give, "narrow", cycle(size, by))
        total = total + take.astype(jnp.float32)
    return total


def sent_around(blocks):
    size = lax.axis_size("narrow")
    place = lax.axis_index("narrow")

    def block(by):
        return lax.dynamic_index_in_dim(blocks, lax.rem(place + by, size), 0, keepdims=False)

    return [block(0)] + [
        lax.ppermute(block(by), "narrow", cycle(size, by)) for by in range(1, size)
    ]


def block_kernel(steps, place_ref, *refs):
    pairs = len(steps) - 1
    lefts, rights, terms, out_ref = refs[:pairs], refs[pairs : 2 * pairs], refs[2 * pairs : -1], refs[-1]
    step = pl.program_id(0)
    for index in range(pairs):

        @pl.when((step >= steps[index]) & (step < steps[index + 1]))
        def _():
            total = matmul_tn(lefts[index][...], rights[index][...])
            for term_ref in terms:
                total = total + term_ref[...].astype(jnp.float32)
            out_ref[...] = total.astype(jnp.bfloat16)


def gradient_block(pairs, place, terms):
    block = D
    size = D // lax.axis_size("narrow")
    steps = [0]
    for _, right in pairs:
        steps.append(steps[-1] + right.shape[1] // block)
    tokens = pairs[0][0].shape[0]

    def right_of(index):
        low, count = steps[index], steps[index + 1] - steps[index]
        return pl.BlockSpec(
            (tokens, block), lambda step, place: (0, jnp.clip(step - low, 0, count - 1))
        )

    piece = pl.BlockSpec((size, block), lambda step, place: (0, step))
    return pl.pallas_call(
        functools.partial(block_kernel, steps),
        grid_spec=pltpu.PrefetchScalarGridSpec(
            num_scalar_prefetch=1,
            grid=(steps[-1],),
            in_specs=[pl.BlockSpec((tokens, size), lambda step, place: (0, place[0]))] * len(pairs)
            + [right_of(index) for index in range(len(pairs))]
            + [piece] * len(terms),
            out_specs=piece,
        ),
        out_shape=jax.ShapeDtypeStruct((size, steps[-1] * block), jnp.bfloat16),
        compiler_params=pltpu.CompilerParams(vmem_limit_bytes=24 * 2**20),
        cost_estimate=FREE,
        name="gradient_block",
    )(place[None], *[left for left, _ in pairs], *[right for _, right in pairs], *terms)


class WorkerPiece:
    def __init__(self, *pairs):
        self.pairs = pairs
        self.paired = paired_mesh()
        if not self.paired:
            return
        self.core = lax.axis_index("wide") % 2
        self.pair, self.side = lax.axis_index("narrow") // 2, lax.axis_index("narrow") % 2
        cores = swap_pairs(lax.axis_size("wide"), 1)
        self.far = lax.ppermute(self.block(1 - self.core, 1 - self.side), "wide", cores)
        self.near = lax.ppermute(self.block(1 - self.core, self.side), "wide", cores)

    def block(self, core, side, *terms):
        return gradient_block(self.pairs, 2 * core + side, terms)

    def received(self, value):
        if self.paired:
            value, self.far, self.near = together(value, self.far, self.near)
        return value

    def across(self, value):
        if self.paired:
            sides = swap_pairs(lax.axis_size("narrow"), 1)
            away = self.block(self.core, 1 - self.side, self.far)
            away, value = together(away, value)
            self.away = lax.ppermute(away, "narrow", sides)
        return value

    def crossed(self, *values):
        if self.paired:
            *values, self.away = together(*values, self.away)
        return values

    def finish(self, *values):
        if not self.paired:
            blocks = [matmul_tn(left, right).astype(jnp.bfloat16) for left, right in self.pairs]
            grad = jnp.concatenate(blocks, axis=1)
            self.result = lax.psum_scatter(grad, "narrow", scatter_dimension=0, tiled=True)
            return values
        n_wide, n_narrow = lax.axis_size("wide"), lax.axis_size("narrow")
        total = self.block(self.core, self.side, self.near, self.away)
        moves = []
        for wide in range(n_wide):
            for narrow in range(n_narrow):
                if narrow // 2 != wide % 2:
                    target_wide = wide - wide % 2 + narrow // 2
                    target = target_wide * n_narrow + 2 * (wide % 2) + narrow % 2
                    moves.append((wide * n_narrow + narrow, target))
        total, *values = together(total, *values)
        moved = lax.ppermute(total, ("wide", "narrow"), moves)
        self.stays = (self.pair == self.core).astype(jnp.int32)
        self.result = (total, moved)
        return values


def hosted_rows(token_ids, mlm_labels, mlm_valid, doc_ids, mlm_pos):
    n_wide, n_narrow = lax.axis_size("wide"), lax.axis_size("narrow")
    packed = jnp.concatenate([token_ids, mlm_labels, mlm_valid], axis=1)[None]
    for bit, place in zip((1, 2, 4), wide_places()):
        other = lax.ppermute(packed, "wide", swap_pairs(n_wide, bit))
        first, second = jnp.where(place == 0, packed, other), jnp.where(place == 0, other, packed)
        packed = jnp.concatenate([first, second], axis=0)
    width = packed.shape[2]
    hosted = packed.reshape(n_wide // 2, 2, 2, 2, width).transpose(1, 2, 0, 3, 4)
    hosted = hosted.reshape(n_narrow, n_wide, width)
    column = lax.dynamic_index_in_dim(hosted, lax.axis_index("wide"), 1, keepdims=False)
    moves = []
    for wide in range(n_wide):
        for row in range(n_narrow):
            target_wide = wide - wide % 2 + row % 2
            target_narrow = 2 * (wide % 2) + row // 2
            moves.append((wide * n_narrow + row, target_wide * n_narrow + target_narrow))
    own = lax.ppermute(jnp.concatenate([doc_ids, mlm_pos], axis=1), ("wide", "narrow"), moves)
    return (
        hosted[:, :, 0:L],
        column[:, L : L + MPS],
        column[:, L + MPS :],
        own[:, 0:L],
        own[:, L:],
    )


STREAMS = 2


class Owners:
    def __init__(self, tokens, vshard):
        size = lax.axis_size("narrow")
        place = lax.axis_index("narrow")
        count = tokens.shape[1]
        self.room = count * 7 // 16
        owner = tokens // vshard
        held = (owner[None] == jnp.arange(size)[:, None, None]).astype(jnp.bfloat16)
        tiles = held.reshape(-1, count // 128, 128)
        order = jnp.arange(128)
        within = jnp.einsum(
            "btl,lm->btm",
            tiles,
            (order[:, None] < order[None]).astype(jnp.bfloat16),
            preferred_element_type=jnp.float32,
        )
        sums = jnp.sum(tiles.astype(jnp.float32), axis=2)
        tile = jnp.arange(count // 128)
        before = jnp.sum(jnp.where(tile[:, None] < tile[None], sums[:, :, None], 0.0), axis=1)
        rank = (within + before[..., None]).reshape(size, size, count) * held.astype(jnp.float32)
        rank = jnp.sum(rank, axis=0).astype(jnp.int32)
        self.full = jnp.max(jnp.sum(sums, axis=1)) > self.room
        self.count, self.vshard = count, vshard
        own = lax.dynamic_index_in_dim(owner, place, 0, keepdims=False)
        self.rank = lax.dynamic_index_in_dim(rank, place, 0, keepdims=False)
        self.behind = lax.rem(place - own + size, size)
        self.slots = jnp.where(owner == place, tokens - place * vshard, vshard)

    def behind_slots(self, room):
        return self.behind * room + jnp.minimum(self.rank, room - 1)


def pack_kernel(ids_ref, table_ref, out_ref, held, *rows):
    step, count, size = pl.program_id(0), out_ref.shape[1], table_ref.shape[0]

    @pl.when(step == 0)
    def _():
        held[0:size, :] = table_ref[...]
        held[size:, :] = jnp.zeros((8, table_ref.shape[1]), jnp.float32)
        for part in rows:
            part[...] = jnp.zeros_like(part)

    base = [(step * len(rows) + index) * count for index in range(len(rows))]

    def some(turn, used):
        used = list(used)
        for by in range(8):
            for index, part in enumerate(rows):
                place = ids_ref[base[index] + turn * 8 + by]
                part[pl.ds(used[index], 1), :] = held[pl.ds(place, 1), :]
                used[index] = used[index] + jnp.where(place < size, 1, 0)
        return tuple(used)

    lax.fori_loop(0, count // 8, some, (0,) * len(rows))
    for index, part in enumerate(rows):
        out_ref[index] = part[0:count, :].astype(out_ref.dtype)


def packed_rows(ids, table):
    size, cols = table.shape
    places, count = ids.shape
    return pl.pallas_call(
        pack_kernel,
        grid_spec=pltpu.PrefetchScalarGridSpec(
            num_scalar_prefetch=1,
            grid=(places // STREAMS,),
            in_specs=[pl.BlockSpec((size, cols), lambda step, ids: (0, 0))],
            out_specs=pl.BlockSpec((STREAMS, count, cols), lambda step, ids: (step, 0, 0)),
            scratch_shapes=[pltpu.VMEM((size + 8, cols), jnp.float32)]
            + [pltpu.VMEM((count + 8, cols), jnp.float32)] * STREAMS,
        ),
        out_shape=jax.ShapeDtypeStruct((places, count, cols), jnp.bfloat16),
        compiler_params=pltpu.CompilerParams(vmem_limit_bytes=40 * 2**20),
        cost_estimate=pl.CostEstimate(flops=0, bytes_accessed=0, transcendentals=0),
        name="pack_rows",
    )(ids.reshape(-1), table)


def take_kernel(ids_ref, table_ref, out_ref, held, rows):
    held[...] = table_ref[...].astype(jnp.float32)

    @pl.loop(0, out_ref.shape[0], step=16)
    def _(first):
        for by in range(16):
            rows[pl.ds(first + by, 1), :] = held[pl.ds(ids_ref[first + by], 1), :]

    out_ref[...] = rows[...].astype(out_ref.dtype)


def taken_rows(ids, table):
    count, cols = ids.shape[0], table.shape[1]
    return pl.pallas_call(
        take_kernel,
        grid_spec=pltpu.PrefetchScalarGridSpec(
            num_scalar_prefetch=1,
            grid=(1,),
            in_specs=[pl.BlockSpec(table.shape, lambda step, ids: (0, 0))],
            out_specs=pl.BlockSpec((count, cols), lambda step, ids: (0, 0)),
            scratch_shapes=[
                pltpu.VMEM(table.shape, jnp.float32),
                pltpu.VMEM((count, cols), jnp.float32),
            ],
        ),
        out_shape=jax.ShapeDtypeStruct((count, cols), table.dtype),
        compiler_params=pltpu.CompilerParams(vmem_limit_bytes=40 * 2**20),
        cost_estimate=FREE,
        name="take_rows",
    )(ids, table)


def add_kernel(ids_ref, values_ref, out_ref, rows, *sums):
    size = out_ref.shape[0]
    places, length = rows.shape[0:2]
    split = len(sums) // places
    each = length // split
    for part in sums:
        part[...] = jnp.zeros_like(part)
    rows[...] = values_ref[:, 0:length, :].astype(jnp.float32)

    @pl.loop(0, each, step=8)
    def _(first):
        for by in range(8):
            for index, part in enumerate(sums):
                at = index % split * each + first + by
                place = ids_ref[index // split * length + at]
                part[pl.ds(place, 1), :] += rows[index // split, pl.ds(at, 1), :]

    total = sums[0][0:size, :]
    for part in sums[1:]:
        total = total + part[0:size, :]
    out_ref[...] = total


def added_rows(ids, values, size):
    places, length = ids.shape
    cols = values.shape[2]
    return pl.pallas_call(
        add_kernel,
        grid_spec=pltpu.PrefetchScalarGridSpec(
            num_scalar_prefetch=1,
            grid=(1,),
            in_specs=[pl.BlockSpec(values.shape, lambda step, ids: (0, 0, 0))],
            out_specs=pl.BlockSpec((size, cols), lambda step, ids: (0, 0)),
            scratch_shapes=[pltpu.VMEM((places, length, cols), jnp.float32)]
            + [pltpu.VMEM((size + 8, cols), jnp.float32)] * (2 * places),
        ),
        out_shape=jax.ShapeDtypeStruct((size, cols), jnp.float32),
        compiler_params=pltpu.CompilerParams(vmem_limit_bytes=62 * 2**20),
        cost_estimate=FREE,
        name="add_rows",
    )(ids.reshape(-1), values)


def span_kernel(stays_ref, momentum_ref, total_ref, moved_ref, error_ref, span_ref, sum_ref):
    @pl.when(pl.program_id(0) == 0)
    def _():
        sum_ref[...] = jnp.zeros_like(sum_ref)

    def write(grad_ref):
        grad = grad_ref[...].astype(jnp.float32)
        span = BETA * momentum_ref[...] + (1.0 - BETA) * grad + error_ref[0]
        span_ref[...] = span
        sum_ref[...] += jnp.sum(jnp.abs(span), axis=0, keepdims=True)

    @pl.when(stays_ref[0] == 1)
    def _():
        write(total_ref)

    @pl.when(stays_ref[0] != 1)
    def _():
        write(moved_ref)


def span_of(momentum, piece, error, start):
    total, moved = piece.result
    rows, cols = total.shape
    block = 1024
    first = start // block
    grad = pl.BlockSpec((rows, block), lambda step, _: (0, step))
    span, sums = pl.pallas_call(
        span_kernel,
        grid_spec=pltpu.PrefetchScalarGridSpec(
            num_scalar_prefetch=1,
            grid=(cols // block,),
            in_specs=[
                pl.BlockSpec((rows, block), lambda step, _: (0, first + step)),
                grad,
                grad,
                pl.BlockSpec((1, rows, block), lambda step, _: (0, 0, first + step)),
            ],
            out_specs=[grad, pl.BlockSpec((1, block), lambda step, _: (0, 0))],
        ),
        out_shape=[
            jax.ShapeDtypeStruct((rows, cols), jnp.float32),
            jax.ShapeDtypeStruct((1, block), jnp.float32),
        ],
        compiler_params=pltpu.CompilerParams(vmem_limit_bytes=60 * 2**20),
        cost_estimate=pl.CostEstimate(flops=0, bytes_accessed=2 * 10**7, transcendentals=0),
        name="span",
    )(piece.stays[None], momentum, total, moved, error)
    return span, jnp.sum(sums)


def press_kernel(steps, core_ref, scale_ref, *refs):
    *span_refs, error_ref, give_ref, keep_ref = refs
    core = pl.program_id(2)
    step = pressed_step(pl.program_id(0), pl.program_id(1), core)
    scale = scale_ref[0]
    inverse = scale_ref[1]
    for index, span_ref in enumerate(span_refs):

        @pl.when((step >= steps[index]) & (step < steps[index + 1]))
        def _():
            span = span_ref[...]
            sent = scale * jnp.tanh(span * inverse)
            error_ref[0] = span - sent
            low = sent.astype(jnp.bfloat16)

            @pl.when(core == core_ref[0])
            def _():
                keep_ref[0] = low

            @pl.when(core != core_ref[0])
            def _():
                give_ref[0] = low


def pressed_step(chip, column, core):
    return (2 * chip + core) * 3 + column


def pressed(spans, scale, parts):
    rows = spans[0].shape[0]
    cols = sum(span.shape[1] for span in spans)
    block = cols // parts // 3
    steps = [0]
    for span in spans:
        steps.append(steps[-1] + span.shape[1] // block)

    def of(index):
        low, count = steps[index], steps[index + 1] - steps[index]

        def place(chip, column, core, _):
            return (0, jnp.clip(pressed_step(chip, column, core) - low, 0, count - 1))

        return pl.BlockSpec((rows, block), place)

    half = pl.BlockSpec((1, rows, block), lambda chip, column, core, _: (chip, 0, column))
    half_shape = jax.ShapeDtypeStruct((parts // 2, rows, cols // parts), jnp.bfloat16)
    return pl.pallas_call(
        functools.partial(press_kernel, steps),
        grid_spec=pltpu.PrefetchScalarGridSpec(
            num_scalar_prefetch=1,
            grid=(parts // 2, 3, 2),
            in_specs=[pl.BlockSpec(memory_space=pltpu.SMEM)] + [of(i) for i in range(len(spans))],
            out_specs=[
                pl.BlockSpec(
                    (1, rows, block),
                    lambda chip, column, core, _: (0, 0, pressed_step(chip, column, core)),
                ),
                half,
                half,
            ],
        ),
        out_shape=[jax.ShapeDtypeStruct((1, rows, cols), jnp.float32), half_shape, half_shape],
        compiler_params=pltpu.CompilerParams(vmem_limit_bytes=60 * 2**20),
        cost_estimate=FREE,
        name="press",
    )(wide_places()[0][None], jnp.stack([scale, 1.0 / scale]), *spans)


def update_kernel(grad_ref, head_ref, table_ref, first_ref, second_ref, *out_refs):
    first_out, update_ref, weight_sum, update_sum = out_refs
    grad = grad_ref[...] + head_ref[...].astype(jnp.float32)
    first = BETA * first_ref[...] + (1.0 - BETA) * grad
    table = table_ref[...]
    update = first / (jnp.sqrt(second_ref[...]) + OPT_EPS) + DECAY * table
    first_out[...] = first
    update_ref[...] = update

    @pl.when(pl.program_id(0) == 0)
    def _():
        weight_sum[...] = jnp.zeros_like(weight_sum)
        update_sum[...] = jnp.zeros_like(update_sum)

    weight_sum[...] += jnp.sum(table * table, axis=0, keepdims=True)
    update_sum[...] += jnp.sum(update * update, axis=0, keepdims=True)


def table_update(grad, head, table, first, second):
    size, cols = table.shape
    block = size // 9 if size % 9 == 0 and size // 9 % 16 == 0 else size
    whole = pl.BlockSpec((block, cols), lambda step: (step, 0))
    line = pl.BlockSpec((1, cols), lambda step: (0, 0))
    moment, update, *sums = pl.pallas_call(
        update_kernel,
        grid=(size // block,),
        in_specs=[whole] * 5,
        out_specs=[whole, whole, line, line],
        out_shape=[jax.ShapeDtypeStruct((size, cols), jnp.float32)] * 2
        + [jax.ShapeDtypeStruct((1, cols), jnp.float32)] * 2,
        compiler_params=pltpu.CompilerParams(vmem_limit_bytes=56 * 2**20),
        cost_estimate=FREE,
        name="update",
    )(grad, head, table, first, second)
    return moment, update, tuple(jnp.sum(part)[None] for part in sums)


def wide_places():
    wide_me = lax.axis_index("wide")
    return wide_me % 2, wide_me // 2 % 2, wide_me // 4


def scattered_sum(give, keep):
    n_wide = lax.axis_size("wide")
    _, x, y = wide_places()

    def send(value, bit):
        return lax.ppermute(value.astype(jnp.bfloat16), "wide", swap_pairs(n_wide, bit))

    take = send(give, 1)
    half = keep.shape[1] // 2

    def chip(y_of, x_of, part):
        start, size = (2 * y_of + x_of, part * half, 0), (1, half, keep.shape[2])
        own, other = lax.dynamic_slice(keep, start, size), lax.dynamic_slice(take, start, size)
        return own[0].astype(jnp.float32) + other[0].astype(jnp.float32)

    upper_far = send(chip(1 - y, 1 - x, 0), 2)
    lower_far = send(chip(1 - y, 1 - x, 1), 4)
    upper_near = send(chip(y, 1 - x, 0), 2)
    lower_near = send(chip(1 - y, x, 1), 4)
    upper_far = send(chip(1 - y, x, 0) + upper_far.astype(jnp.float32), 4)
    lower_far = send(chip(y, 1 - x, 1) + lower_far.astype(jnp.float32), 2)
    own_upper = chip(y, x, 0) + upper_near.astype(jnp.float32) + upper_far.astype(jnp.float32)
    own_lower = chip(y, x, 1) + lower_near.astype(jnp.float32) + lower_far.astype(jnp.float32)
    return jnp.concatenate([own_upper, own_lower], axis=0)


def small_halved(value):
    n_wide = lax.axis_size("wide")
    for bit, place in list(zip((1, 2, 4), wide_places()))[::-1]:
        half = value.shape[1] // 2
        give = lax.dynamic_slice_in_dim(value, (1 - place) * half, half, 1).astype(jnp.bfloat16)
        keep = lax.dynamic_slice_in_dim(value, place * half, half, 1)
        value = keep + lax.ppermute(give, "wide", swap_pairs(n_wide, bit)).astype(jnp.float32)
    return value


def small_update(grad, first, second, weight):
    first = BETA * first + (1.0 - BETA) * grad.astype(jnp.float32)
    return first, first / (jnp.sqrt(second) + OPT_EPS) + DECAY * weight


def shards(
    token_ids,
    doc_ids,
    mlm_pos,
    mlm_labels,
    mlm_valid,
    table,
    table_m,
    table_v,
    small,
    small_m,
    small_v,
    layer,
    layer_m,
    layer_v,
    worker_err,
    server_err,
):
    n_wide, n_narrow = lax.axis_size("wide"), lax.axis_size("narrow")
    narrow_me = lax.axis_index("narrow")
    wide_me = lax.axis_index("wide")
    seqs = doc_ids.shape[0]
    paired = paired_mesh()
    vshard = table.shape[0]
    count = summed_over(jnp.sum(mlm_valid.astype(jnp.float32)), "wide")
    table_low, layer_low = table.astype(jnp.bfloat16), layer.astype(jnp.bfloat16)
    if paired:
        token_ids, mlm_labels, mlm_valid, doc_ids, mlm_pos = hosted_rows(
            token_ids, mlm_labels, mlm_valid, doc_ids, mlm_pos
        )
        table_cut = vshard * 5 // 8 // 16 * 16
        table_first = lax.all_gather(table_low[0:table_cut], "wide", axis=1, tiled=True)
        owners = Owners(token_ids.reshape(n_narrow, n_wide * L), vshard)
        picked = packed_rows(owners.slots, table)
        layer_rows, picked = gathered_near(layer_low, picked)
        layer_rows, table_first = together(layer_rows, table_first)
    else:
        layer_rows = lax.all_gather(layer_low, "narrow", axis=0, tiled=True)
    weights = lax.all_gather(layer_rows, "wide", axis=1, tiled=True)
    if paired:

        def looked_up(room):
            rows = sent_around(picked[:, 0:room])
            return taken_rows(owners.behind_slots(room), jnp.concatenate(rows, axis=0))

        layer_rows, picked = together(layer_rows, picked)
        looked = looked_up(owners.room)
        looked = lax.cond(owners.full, lambda: looked_up(owners.count), lambda: looked)
        looked = lax.all_to_all(looked.reshape(n_wide, L, -1), "wide", 0, 0)
        looked = looked.transpose(1, 0, 2).reshape(1, L, D)
        looked, count, doc_ids, mlm_pos = together(looked, count, doc_ids, mlm_pos)
    else:
        local_ids = token_ids - narrow_me * vshard
        inside = (local_ids >= 0) & (local_ids < vshard)
        slots = jnp.where(inside, local_ids, vshard).reshape(-1)
        table_cols = lax.all_gather(table_low, "wide", axis=1, tiled=True)
        picked = jnp.take(table_cols, jnp.clip(local_ids, 0, vshard - 1), axis=0)
        picked = jnp.where(inside[..., None], picked, 0.0)
        looked = lax.psum_scatter(picked, "narrow", scatter_dimension=0, tiled=True)
    looked = looked.astype(jnp.float32)
    even_doc = (doc_ids % 2 == 0)[..., None]
    embedded = looked + small[0:L][None] + jnp.where(even_doc, small[L], small[L + 1])
    embedded = embedded.reshape(seqs * L, D)
    x0 = norm_rows(embedded, small[L + 2], small[L + 3])
    act = x0.astype(jnp.bfloat16)
    if paired:
        table_cols = jnp.zeros((vshard, D), jnp.bfloat16)
        table_cols = lax.dynamic_update_slice(table_cols, table_first, (0, 0))
        table_last, weights, act, table_cols = together(
            table_low[table_cut:], weights, act, table_cols
        )
        table_last = lax.all_gather(table_last, "wide", axis=1, tiled=True)
        table_cols = lax.dynamic_update_slice(table_cols, table_last, (table_cut, 0))
    htwo, kept = layer_forward(embedded, x0, act, doc_ids, small, weights)
    hmask = jnp.take_along_axis(htwo.reshape(seqs, L, D), mlm_pos[..., None], axis=1)
    hmask = hmask.reshape(seqs * MPS, D).astype(jnp.bfloat16)
    if paired:
        group_h = gathered_near(hmask)
    else:
        group_h = lax.all_gather(hmask, "narrow", axis=0, tiled=True)
    vocab = narrow_me * vshard + jnp.arange(vshard)
    logits = jnp.where((vocab < VREAL)[None], matmul_nt(group_h, table_cols), -1000000000.0)
    labels = mlm_labels.reshape(-1)
    hit = vocab[None] == labels[:, None]
    top = jnp.max(logits, axis=1)
    total = jnp.sum(jnp.exp(logits - top[:, None]), axis=1)
    target = jnp.sum(jnp.where(hit, logits, 0.0), axis=1)
    if paired:
        stats = gathered_near(jnp.stack([top, total, target])[None])
        top, total, target = stats[0]
        for place in range(1, stats.shape[0]):
            top, total, target = merge_rows((top, total, target), tuple(stats[place]))
    else:
        top, total, target = joined((top, total, target), "narrow", merge_rows)
    lse = top + jnp.log(total)
    flags = mlm_valid.reshape(-1).astype(jnp.float32)
    own = seqs * MPS
    own_loss = lax.dynamic_slice_in_dim(flags * (lse - target), narrow_me * own, own)
    dlogit = (
        (jnp.exp(logits - lse[:, None]) - hit.astype(jnp.float32)) * (flags / count)[:, None]
    ).astype(jnp.bfloat16)
    dhmask = matmul(dlogit, table_cols)
    if paired:
        dhmask = scattered_near(dhmask)
        blocks = group_h.reshape(-1, n_wide, D // n_wide)
        table_head = jnp.einsum("sv,swc->wvc", dlogit, blocks, preferred_element_type=jnp.float32)
        table_head, dhmask = together(table_head.astype(jnp.bfloat16), dhmask)
        table_head = lax.psum_scatter(table_head, "wide", scatter_dimension=0)
    else:
        dhmask = lax.psum_scatter(dhmask, "narrow", scatter_dimension=0, tiled=True)
    dhtwo = (
        jnp.zeros((seqs, L, D), jnp.float32)
        .at[jnp.arange(seqs)[:, None], mlm_pos]
        .add(dhmask.reshape(seqs, MPS, D))
    )
    dembed, vectors, pieces = layer_backward(
        dhtwo.reshape(seqs * L, D), kept, doc_ids, small, weights
    )
    dembed_rows = dembed.reshape(seqs, L, D)
    small_grad = jnp.concatenate([jnp.sum(dembed_rows, axis=0), vectors], axis=0)
    mixed = pieces[0]
    if paired:
        cut = dembed.astype(jnp.bfloat16).reshape(L, n_wide, D // n_wide).transpose(1, 0, 2)
        cut = lax.all_to_all(cut, "wide", 0, 0).reshape(n_wide * L, D // n_wide)
        halved = small_halved(small_grad).astype(jnp.bfloat16)
        down, up = pieces[2], pieces[1]
        mixed.away, down.result = together(mixed.away, down.result)
        mixed.finish()
        spans = [span_of(layer_m, up, worker_err, 4 * D)]
        spans.append(span_of(layer_m, down, worker_err, 8 * D))
        cut, mixed.result, spans, table_head = together(
            jnp.concatenate([cut, halved]), mixed.result, spans, table_head
        )
        group_rows = lax.all_gather(cut, "narrow", axis=0)
    else:
        mixed.finish()
        group_rows = lax.all_gather(dembed_rows.astype(jnp.bfloat16), "narrow", axis=0, tiled=True)
        table_grad = matmul_tn(dlogit, group_h).at[slots].add(
            group_rows.reshape(-1, D).astype(jnp.float32), mode="drop"
        )
        cut = table_grad.astype(jnp.bfloat16).reshape(vshard, n_wide, D // n_wide)
        table_grad = lax.psum_scatter(cut.transpose(1, 0, 2), "wide", scatter_dimension=0)
        table_grad = table_grad.astype(jnp.float32)
    part_cols = layer.shape[1]
    if paired:
        spans.insert(0, span_of(layer_m, pieces[0], worker_err, 0))
        total = sum(amount for _, amount in spans)
        spans = [span for span, _ in spans]
        scale = total / (layer_m.shape[0] * layer_m.shape[1]) + MAG_EPS
        new_worker, give, keep = pressed(spans, scale, n_wide)
        server_in = scattered_sum(give, keep) / n_wide + server_err
    else:
        worker_grad = jnp.concatenate([piece.result for piece in pieces], axis=1)
        span = BETA * layer_m + (1.0 - BETA) * worker_grad.astype(jnp.float32) + worker_err[0]
        scale = jnp.mean(jnp.abs(span)) + MAG_EPS
        sent = scale * jnp.tanh(span / scale)
        new_worker = (span - sent)[None]
        summed = lax.psum(sent.astype(jnp.bfloat16), "wide").astype(jnp.float32)
        mixed = lax.dynamic_slice_in_dim(summed, wide_me * part_cols, part_cols, 1) / n_wide
        server_in = mixed + server_err
    sscale = jnp.mean(jnp.abs(server_in)) + MAG_EPS
    server_out = sscale * jnp.tanh(server_in / sscale)
    new_server = server_in - server_out
    server_low = server_out.astype(jnp.bfloat16)
    layer_upd = server_out / (jnp.sqrt(layer_v) + OPT_EPS) + DECAY * layer
    column = wide_me * part_cols + jnp.arange(part_cols)
    which = (
        (column >= 3 * D).astype(jnp.int32)
        + (column >= 4 * D).astype(jnp.int32)
        + (column >= 4 * D + FF).astype(jnp.int32)
    )
    onehot = (which[:, None] == jnp.arange(4)[None]).astype(jnp.float32)
    wsq = jnp.sum(jnp.sum(layer * layer, axis=0)[:, None] * onehot, axis=0)
    usq = jnp.sum(jnp.sum(layer_upd * layer_upd, axis=0)[:, None] * onehot, axis=0)
    small_square = jnp.sum(small * small)[None]
    if paired:
        new_server, wsq, usq, small_square, group_rows = together(
            new_server, wsq, usq, small_square, group_rows
        )
        table_grad = added_rows(owners.slots, group_rows, vshard)
        table_mom, table_upd, table_norms = table_update(
            table_grad, table_head, table, table_m, table_v
        )
        eighth = D // n_wide
        small_grad = jnp.sum(group_rows[:, n_wide * L :].astype(jnp.float32), axis=0)
        small_grad = small_grad.astype(jnp.bfloat16)

        def own(value):
            return lax.dynamic_slice_in_dim(value, wide_me * eighth, eighth, 1)

        _, own_upd = small_update(small_grad, own(small_m), own(small_v), own(small))
        small_norm = jnp.where(narrow_me == 0, jnp.sum(own_upd * own_upd), 0.0)
    else:
        small_grad = lax.psum(small_grad, ("wide", "narrow"))
        table_mom = BETA * table_m + (1.0 - BETA) * table_grad
        table_upd = table_mom / (jnp.sqrt(table_v) + OPT_EPS) + DECAY * table
        table_norms = (jnp.sum(table * table)[None], jnp.sum(table_upd * table_upd)[None])
    new_m = lax.all_gather(server_low, "wide", axis=1, tiled=True)
    if paired:
        small_grad, new_m, table_norms = together(small_grad, new_m, table_norms)
        small_grad = lax.all_gather(small_grad, "wide", axis=1, tiled=True)
    if not paired:
        _, small_upd = small_update(small_grad, small_m, small_v, small)
        small_norm = jnp.where((wide_me == 0) & (narrow_me == 0), jnp.sum(small_upd * small_upd), 0.0)
    parts = jnp.concatenate([wsq, usq, *table_norms, jnp.sum(own_loss)[None], small_norm[None]])
    sums = summed_over(summed_over(parts, "wide"), "narrow")
    if paired:
        sums, small_grad = together(sums, small_grad)
    small_mom, small_upd = small_update(small_grad, small_m, small_v, small)
    loss_sum = sums[10]
    wnorm = jnp.sqrt(jnp.concatenate([sums[0:4], sums[8:9], small_square]))
    unorm = jnp.sqrt(jnp.concatenate([sums[4:8], sums[9:10], sums[11:12]]))
    ratio = wnorm / unorm
    new_layer = layer - RATE * jnp.sum(onehot * ratio[None, 0:4], axis=1)[None] * layer_upd
    new_table = table - RATE * ratio[4] * table_upd
    new_small = small - RATE * ratio[5] * small_upd
    return (
        jnp.stack([loss_sum, count]),
        new_table,
        table_mom,
        new_small,
        small_mom,
        new_layer,
        new_m.astype(jnp.float32),
        new_worker,
        new_server,
        jnp.stack([wnorm, unorm]),
    )


def solution(mesh):
    placed = (
        P("wide", None),
        P(("wide", "narrow"), None),
        P(("wide", "narrow"), None),
        P("wide", None),
        P("wide", None),
        P("narrow", "wide"),
        P("narrow", "wide"),
        P("narrow", "wide"),
        P(),
        P(),
        P(),
        P("narrow", "wide"),
        P("narrow", None),
        P("narrow", "wide"),
        P("wide", "narrow", None),
        P("narrow", "wide"),
    )
    return jax.shard_map(
        shards,
        mesh=mesh,
        in_specs=placed,
        out_specs=(
            P(),
            P("narrow", "wide"),
            P("narrow", "wide"),
            P(),
            P(),
            P("narrow", "wide"),
            P("narrow", None),
            P("wide", "narrow", None),
            P("narrow", "wide"),
            P(),
        ),
        check_vma=False,
    )
```

```python
import functools

import jax
import jax.numpy as jnp
from jax import lax
from jax.experimental import pallas as pl
from jax.experimental.pallas import tpu as pltpu
from jax.sharding import PartitionSpec as P

D = 1024
HEADS = 16
HEAD = 64
FF = 4096
VREAL = 30522
L = 512
MPS = 80


LN_EPS = 1e-12
BETA = 0.9
DECAY = 0.01
RATE = 0.25
OPT_EPS = 1e-06
MAG_EPS = 1e-08

FREE = pl.CostEstimate(flops=0, bytes_accessed=0, transcendentals=0)


def joined(value, axis, join):
    pieces = jax.tree.map(lambda part: lax.all_gather(part, axis), value)
    head = jax.tree.map(lambda part: part[0], pieces)
    tail = jax.tree.map(lambda part: part[1:], pieces)
    subtotal, _ = lax.scan(lambda subtotal, slab: (join(subtotal, slab), None), head, tail)
    return subtotal


def norm_rows(x, gain, shift):
    mean = jnp.mean(x, axis=-1, keepdims=True)
    cent = x - mean
    var = jnp.mean(cent * cent, axis=-1, keepdims=True)
    return cent * lax.rsqrt(var + LN_EPS) * gain + shift


def matmul(left, right):
    return jnp.dot(left, right, preferred_element_type=jnp.float32)


def matmul_tn(left, right):
    return lax.dot_general(
        left, right, (((0,), (0,)), ((), ())), preferred_element_type=jnp.float32
    )


def matmul_nt(left, right):
    return lax.dot_general(
        left, right, (((1,), (1,)), ((), ())), preferred_element_type=jnp.float32
    )


def attend_kernel(q_ref, k_ref, v_ref, key_doc_ref, query_doc_ref, out_ref, lse_ref):
    same = key_doc_ref[...] == query_doc_ref[...]
    lane = lax.broadcasted_iota(jnp.int32, (1, 2 * HEAD), 1)
    outs = []
    for head in range(2):
        mine = lane // HEAD == head
        query = jnp.where(mine, q_ref[...] * 0.125, 0).astype(jnp.bfloat16)
        scores = jnp.where(same, matmul_nt(k_ref[...], query), -1000000000.0)
        top = jnp.max(scores, axis=0, keepdims=True)
        power = jnp.exp(scores - top)
        total = jnp.sum(power, axis=0, keepdims=True)
        lse_ref[0, head : head + 1, :] = top + jnp.log(total)
        prob = (power * (1.0 / total)).astype(jnp.bfloat16)
        outs.append(matmul_tn(prob, v_ref[...]))
    out_ref[...] = jnp.where(lane < HEAD, outs[0], outs[1]).astype(jnp.bfloat16)


def head_pairs(offset):
    return pl.BlockSpec((L, 2 * HEAD), lambda pair: (0, offset * HEADS // 2 + pair))


def attend(qkv, docs):
    return pl.pallas_call(
        attend_kernel,
        grid=(HEADS // 2,),
        in_specs=[
            head_pairs(0),
            head_pairs(1),
            head_pairs(2),
            pl.BlockSpec((L, 1), lambda pair: (0, 0)),
            pl.BlockSpec((1, L), lambda pair: (0, 0)),
        ],
        out_specs=[head_pairs(0), pl.BlockSpec((1, 2, L), lambda pair: (pair, 0, 0))],
        out_shape=[
            jax.ShapeDtypeStruct((L, D), jnp.bfloat16),
            jax.ShapeDtypeStruct((HEADS // 2, 2, L), jnp.float32),
        ],
        compiler_params=pltpu.CompilerParams(vmem_limit_bytes=40 * 2**20),
        cost_estimate=FREE,
        name="attend",
    )(qkv, qkv, qkv, docs.reshape(L, 1), docs.reshape(1, L))


def attend_back_kernel(q_ref, k_ref, v_ref, do_ref, lse_ref, key_doc_ref, query_doc_ref, out_ref):
    pair = pl.program_id(0)
    same = key_doc_ref[...] == query_doc_ref[...]
    lane = lax.broadcasted_iota(jnp.int32, (1, 2 * HEAD), 1)
    both = []
    for head in range(2):
        mine = lane // HEAD == head
        query = jnp.where(mine, q_ref[...] * 0.125, 0).astype(jnp.bfloat16)
        dout = jnp.where(mine, do_ref[...], 0).astype(jnp.bfloat16)
        scores = jnp.where(same, matmul_nt(k_ref[...], query), -1000000000.0)
        prob = jnp.exp(scores - lse_ref[0, head : head + 1, :])
        dvalue = matmul(prob.astype(jnp.bfloat16), dout)
        dprob = matmul_nt(v_ref[...], dout)
        delta = jnp.sum(prob * dprob, axis=0, keepdims=True)
        dscore = (prob * (dprob - delta)).astype(jnp.bfloat16)
        both.append((matmul_tn(dscore, k_ref[...]) * 0.125, matmul(dscore, query), dvalue))
    for part in range(3):
        value = jnp.where(lane < HEAD, both[0][part], both[1][part]).astype(jnp.bfloat16)
        start = pl.multiple_of(part * D + pair * 2 * HEAD, 2 * HEAD)
        out_ref[:, pl.ds(start, 2 * HEAD)] = value


def attend_back(qkv, dout, lse, docs):
    return pl.pallas_call(
        attend_back_kernel,
        grid=(HEADS // 2,),
        in_specs=[
            head_pairs(0),
            head_pairs(1),
            head_pairs(2),
            head_pairs(0),
            pl.BlockSpec((1, 2, L), lambda pair: (pair, 0, 0)),
            pl.BlockSpec((L, 1), lambda pair: (0, 0)),
            pl.BlockSpec((1, L), lambda pair: (0, 0)),
        ],
        out_specs=pl.BlockSpec((L, 3 * D), lambda pair: (0, 0)),
        out_shape=jax.ShapeDtypeStruct((L, 3 * D), jnp.bfloat16),
        compiler_params=pltpu.CompilerParams(vmem_limit_bytes=40 * 2**20),
        cost_estimate=FREE,
        name="attend_back",
    )(qkv, qkv, qkv, dout, lse, docs.reshape(L, 1), docs.reshape(1, L))


def merge_rows(first, second):
    peak = jnp.maximum(first[0], second[0])
    total = first[1] * jnp.exp(first[0] - peak) + second[1] * jnp.exp(second[0] - peak)
    return (peak, total, first[2] + second[2])


def embed_back_kernel(dqkv_ref, weight_ref, drone_ref, embedded_ref, gain_ref, even_ref, *refs):
    dembed_ref, rows_ref, sums_ref, total = refs
    step = pl.program_id(0)
    dqkv = dqkv_ref[...]
    part = matmul_nt(dqkv, weight_ref[...])
    sums_ref[...] = jnp.sum(dqkv.astype(jnp.float32), axis=0, keepdims=True)

    @pl.when(step == 0)
    def _():
        total[...] = drone_ref[...] + part

    @pl.when(step > 0)
    def _():
        total[...] += part

    @pl.when(step == pl.num_programs(0) - 1)
    def _():
        grad = total[...]
        embedded = embedded_ref[...]
        cent = embedded - jnp.mean(embedded, axis=1, keepdims=True)
        scale = lax.rsqrt(jnp.mean(cent * cent, axis=1, keepdims=True) + LN_EPS)
        normed = cent * scale
        inner = grad * gain_ref[...]
        inner_mean = jnp.mean(inner, axis=1, keepdims=True)
        along = jnp.mean(inner * normed, axis=1, keepdims=True)
        dembed = scale * (inner - inner_mean - normed * along)
        dembed_ref[...] = dembed
        even = even_ref[...]
        rows_ref[0:1, :] = jnp.sum(grad * normed, axis=0, keepdims=True)
        rows_ref[1:2, :] = jnp.sum(grad, axis=0, keepdims=True)
        rows_ref[2:3, :] = jnp.sum(dembed * even, axis=0, keepdims=True)
        rows_ref[3:4, :] = jnp.sum(dembed * (1.0 - even), axis=0, keepdims=True)
        rows_ref[4:8, :] = jnp.zeros((4, D), jnp.float32)


def embed_back(dqkv, weights, drone, embedded, gain, even):
    tokens = dqkv.shape[0]
    whole = pl.BlockSpec((tokens, D), lambda step: (0, 0))
    return pl.pallas_call(
        embed_back_kernel,
        grid=(3,),
        in_specs=[
            pl.BlockSpec((tokens, D), lambda step: (0, step)),
            pl.BlockSpec((D, D), lambda step: (0, step)),
            whole,
            whole,
            pl.BlockSpec((1, D), lambda step: (0, 0)),
            pl.BlockSpec((tokens, 1), lambda step: (0, 0)),
        ],
        out_specs=[
            whole,
            pl.BlockSpec((8, D), lambda step: (0, 0)),
            pl.BlockSpec((1, D), lambda step: (0, step)),
        ],
        out_shape=[
            jax.ShapeDtypeStruct((tokens, D), jnp.float32),
            jax.ShapeDtypeStruct((8, D), jnp.float32),
            jax.ShapeDtypeStruct((1, 3 * D), jnp.float32),
        ],
        scratch_shapes=[pltpu.VMEM((tokens, D), jnp.float32)],
        compiler_params=pltpu.CompilerParams(vmem_limit_bytes=40 * 2**20),
        cost_estimate=FREE,
        name="embed_back",
    )(dqkv, weights, drone, embedded, gain[None], even)


def ffn_kernel(fin_ref, weight_ref, bias_ref, gated_ref, slope_ref):
    upper = matmul(fin_ref[...], weight_ref[...]) + bias_ref[...]
    below = 0.5 + 0.5 * lax.erf(upper * 0.7071067811865476)
    gated_ref[...] = (upper * below).astype(jnp.bfloat16)
    density = 0.3989422804014327 * jnp.exp(-0.5 * upper * upper)
    slope_ref[...] = (below + upper * density).astype(jnp.bfloat16)


def ffn_up(fin, weights, bias):
    tokens = fin.shape[0]
    block = 512
    first = 4 * D // block
    out = pl.BlockSpec((tokens, block), lambda step: (0, step))
    return pl.pallas_call(
        ffn_kernel,
        grid=(FF // block,),
        in_specs=[
            pl.BlockSpec((tokens, D), lambda step: (0, 0)),
            pl.BlockSpec((D, block), lambda step: (0, first + step)),
            pl.BlockSpec((1, block), lambda step: (0, step)),
        ],
        out_specs=[out, out],
        out_shape=[jax.ShapeDtypeStruct((tokens, FF), jnp.bfloat16)] * 2,
        compiler_params=pltpu.CompilerParams(vmem_limit_bytes=32 * 2**20),
        cost_estimate=pl.CostEstimate(flops=2 * tokens * D * FF, bytes_accessed=0, transcendentals=0),
        name="ffn_up",
    )(fin, weights, bias)


def layer_forward(embedded, x0, act, docs, small, weights):
    base = L + 2
    bias = jnp.concatenate([small[base + 6], jnp.zeros((D,), jnp.float32), small[base + 7]])
    qkv = (matmul(act, weights[:, 0 : 3 * D]) + bias).astype(jnp.bfloat16)
    out, lse = attend(qkv, docs)
    rone = x0 + (matmul(out, weights[:, 3 * D : 4 * D]) + small[base + 8])
    hone = norm_rows(rone, small[base + 2], small[base + 3])
    fin = hone.astype(jnp.bfloat16)
    gated, slope = ffn_up(fin, weights, small[base + 10 :].reshape(1, FF))
    rtwo = hone + (matmul_nt(gated, weights[:, 4 * D + FF :]) + small[base + 9])
    htwo = norm_rows(rtwo, small[base + 4], small[base + 5])
    return (htwo, (embedded, act, qkv, lse, out, rone, fin, slope, gated, rtwo))


def layer_backward(dhtwo, kept, docs, small, weights):
    embedded, act, qkv, lse, out, rone, fin, slope, gated, rtwo = kept
    base = L + 2
    _, pull = jax.vjp(norm_rows, rtwo, small[base + 4], small[base + 5])
    drtwo, dgain_two, dshift_two = pull(dhtwo)
    dffn = drtwo.astype(jnp.bfloat16)
    down = WorkerPiece((dffn, gated))
    dgated = matmul(dffn, weights[:, 4 * D + FF :])
    dupper = (dgated * slope.astype(jnp.float32)).astype(jnp.bfloat16)
    dupper = down.received(dupper)
    dupper = down.across(dupper)
    up = WorkerPiece((fin, dupper))
    dhone = drtwo + matmul_nt(dupper, weights[:, 4 * D : 4 * D + FF])
    _, pull = jax.vjp(norm_rows, rone, small[base + 2], small[base + 3])
    drone, dgain_one, dshift_one = pull(dhone)
    dattn = drone.astype(jnp.bfloat16)
    dout = matmul_nt(dattn, weights[:, 3 * D : 4 * D]).astype(jnp.bfloat16)
    dout = up.received(dout)
    dout = up.across(dout)
    dqkv = attend_back(qkv, dout, lse, docs)
    (dqkv,) = down.crossed(dqkv)
    down.finish()
    mixed = WorkerPiece((act, dqkv), (out, dattn))
    even = (docs.reshape(L, 1) % 2 == 0).astype(jnp.float32)
    dembed, embed_rows, bias_qkv = embed_back(
        mixed.across(dqkv), weights, drone, embedded, small[base], even
    )
    (dembed,) = up.crossed(dembed)
    up.finish()
    vectors = jnp.stack(
        [
            embed_rows[0],
            embed_rows[1],
            dgain_one,
            dshift_one,
            dgain_two,
            dshift_two,
            bias_qkv[0, 0:D],
            bias_qkv[0, 2 * D : 3 * D],
            jnp.sum(dattn, axis=0, dtype=jnp.float32),
            jnp.sum(dffn, axis=0, dtype=jnp.float32),
        ]
    )
    bias_up = jnp.sum(dupper, axis=0, dtype=jnp.float32).reshape(FF // D, D)
    vectors = jnp.concatenate([embed_rows[2:4], vectors, bias_up], axis=0)
    return (dembed, vectors, (mixed, up, down))


def paired_mesh():
    return lax.axis_size("wide") == 8 and lax.axis_size("narrow") == 4


def together(*values):
    return lax.optimization_barrier(values)


def swap_pairs(size, bit):
    return [(place, place ^ bit) for place in range(size)]


def cycle(size, by):
    return [(place, (place + by) % size) for place in range(size)]


def summed_over(value, axis):
    size = lax.axis_size(axis)
    if size & (size - 1):
        return lax.psum(value, axis)
    bit = 1
    while bit < size:
        value = value + lax.ppermute(value, axis, swap_pairs(size, bit))
        bit *= 2
    return value


def gathered_near(value, beside=None):
    size = lax.axis_size("narrow")
    rows = value.shape[0]
    around = [value]
    for by in range(1, size):
        around.append(lax.ppermute(value, "narrow", cycle(size, size - by)))
    if beside is not None:
        *around, beside = together(*around, beside)
    place = lax.axis_index("narrow")
    whole = jnp.zeros((size * rows,) + value.shape[1:], value.dtype)
    for by, part in enumerate(around):
        start = lax.rem(place + by, size) * rows
        whole = lax.dynamic_update_slice_in_dim(whole, part, start, 0)
    return whole if beside is None else (whole, beside)


def scattered_near(value):
    size = lax.axis_size("narrow")
    rows = value.shape[0] // size
    place = lax.axis_index("narrow")
    total = lax.dynamic_slice_in_dim(value, place * rows, rows, 0)
    for by in range(1, size):
        target = lax.rem(place + by, size)
        give = lax.dynamic_slice_in_dim(value, target * rows, rows, 0).astype(jnp.bfloat16)
        take = lax.ppermute(give, "narrow", cycle(size, by))
        total = total + take.astype(jnp.float32)
    return total


def sent_around(blocks):
    size = lax.axis_size("narrow")
    place = lax.axis_index("narrow")

    def block(by):
        return lax.dynamic_index_in_dim(blocks, lax.rem(place + by, size), 0, keepdims=False)

    return [block(0)] + [
        lax.ppermute(block(by), "narrow", cycle(size, by)) for by in range(1, size)
    ]


def block_kernel(steps, place_ref, *refs):
    pairs = len(steps) - 1
    lefts, rights, terms, out_ref = refs[:pairs], refs[pairs : 2 * pairs], refs[2 * pairs : -1], refs[-1]
    step = pl.program_id(0)
    for index in range(pairs):

        @pl.when((step >= steps[index]) & (step < steps[index + 1]))
        def _():
            total = matmul_tn(lefts[index][...], rights[index][...])
            for term_ref in terms:
                total = total + term_ref[...].astype(jnp.float32)
            out_ref[...] = total.astype(jnp.bfloat16)


def gradient_block(pairs, place, terms):
    block = D
    size = D // lax.axis_size("narrow")
    steps = [0]
    for _, right in pairs:
        steps.append(steps[-1] + right.shape[1] // block)
    tokens = pairs[0][0].shape[0]

    def right_of(index):
        low, count = steps[index], steps[index + 1] - steps[index]
        return pl.BlockSpec(
            (tokens, block), lambda step, place: (0, jnp.clip(step - low, 0, count - 1))
        )

    piece = pl.BlockSpec((size, block), lambda step, place: (0, step))
    return pl.pallas_call(
        functools.partial(block_kernel, steps),
        grid_spec=pltpu.PrefetchScalarGridSpec(
            num_scalar_prefetch=1,
            grid=(steps[-1],),
            in_specs=[pl.BlockSpec((tokens, size), lambda step, place: (0, place[0]))] * len(pairs)
            + [right_of(index) for index in range(len(pairs))]
            + [piece] * len(terms),
            out_specs=piece,
        ),
        out_shape=jax.ShapeDtypeStruct((size, steps[-1] * block), jnp.bfloat16),
        compiler_params=pltpu.CompilerParams(vmem_limit_bytes=24 * 2**20),
        cost_estimate=FREE,
        name="gradient_block",
    )(place[None], *[left for left, _ in pairs], *[right for _, right in pairs], *terms)


class WorkerPiece:
    def __init__(self, *pairs):
        self.pairs = pairs
        self.paired = paired_mesh()
        if not self.paired:
            return
        self.core = lax.axis_index("wide") % 2
        self.pair, self.side = lax.axis_index("narrow") // 2, lax.axis_index("narrow") % 2
        cores = swap_pairs(lax.axis_size("wide"), 1)
        self.far = lax.ppermute(self.block(1 - self.core, 1 - self.side), "wide", cores)
        self.near = lax.ppermute(self.block(1 - self.core, self.side), "wide", cores)

    def block(self, core, side, *terms):
        return gradient_block(self.pairs, 2 * core + side, terms)

    def received(self, value):
        if self.paired:
            value, self.far, self.near = together(value, self.far, self.near)
        return value

    def across(self, value):
        if self.paired:
            sides = swap_pairs(lax.axis_size("narrow"), 1)
            away = self.block(self.core, 1 - self.side, self.far)
            away, value = together(away, value)
            self.away = lax.ppermute(away, "narrow", sides)
        return value

    def crossed(self, *values):
        if self.paired:
            *values, self.away = together(*values, self.away)
        return values

    def finish(self, *values):
        if not self.paired:
            blocks = [matmul_tn(left, right).astype(jnp.bfloat16) for left, right in self.pairs]
            grad = jnp.concatenate(blocks, axis=1)
            self.result = lax.psum_scatter(grad, "narrow", scatter_dimension=0, tiled=True)
            return values
        n_wide, n_narrow = lax.axis_size("wide"), lax.axis_size("narrow")
        total = self.block(self.core, self.side, self.near, self.away)
        moves = []
        for wide in range(n_wide):
            for narrow in range(n_narrow):
                if narrow // 2 != wide % 2:
                    target_wide = wide - wide % 2 + narrow // 2
                    target = target_wide * n_narrow + 2 * (wide % 2) + narrow % 2
                    moves.append((wide * n_narrow + narrow, target))
        total, *values = together(total, *values)
        moved = lax.ppermute(total, ("wide", "narrow"), moves)
        self.stays = (self.pair == self.core).astype(jnp.int32)
        self.result = (total, moved)
        return values


def hosted_rows(token_ids, mlm_labels, mlm_valid, doc_ids, mlm_pos):
    n_wide, n_narrow = lax.axis_size("wide"), lax.axis_size("narrow")
    packed = jnp.concatenate([token_ids, mlm_labels, mlm_valid], axis=1)[None]
    for bit, place in zip((1, 2, 4), wide_places()):
        other = lax.ppermute(packed, "wide", swap_pairs(n_wide, bit))
        first, second = jnp.where(place == 0, packed, other), jnp.where(place == 0, other, packed)
        packed = jnp.concatenate([first, second], axis=0)
    width = packed.shape[2]
    hosted = packed.reshape(n_wide // 2, 2, 2, 2, width).transpose(1, 2, 0, 3, 4)
    hosted = hosted.reshape(n_narrow, n_wide, width)
    column = lax.dynamic_index_in_dim(hosted, lax.axis_index("wide"), 1, keepdims=False)
    moves = []
    for wide in range(n_wide):
        for row in range(n_narrow):
            target_wide = wide - wide % 2 + row % 2
            target_narrow = 2 * (wide % 2) + row // 2
            moves.append((wide * n_narrow + row, target_wide * n_narrow + target_narrow))
    own = lax.ppermute(jnp.concatenate([doc_ids, mlm_pos], axis=1), ("wide", "narrow"), moves)
    return (
        hosted[:, :, 0:L],
        column[:, L : L + MPS],
        column[:, L + MPS :],
        own[:, 0:L],
        own[:, L:],
    )


STREAMS = 2


class Owners:
    def __init__(self, tokens, vshard):
        size = lax.axis_size("narrow")
        place = lax.axis_index("narrow")
        count = tokens.shape[1]
        self.room = count * 7 // 16
        owner = tokens // vshard
        held = (owner[None] == jnp.arange(size)[:, None, None]).astype(jnp.bfloat16)
        tiles = held.reshape(-1, count // 128, 128)
        order = jnp.arange(128)
        within = jnp.einsum(
            "btl,lm->btm",
            tiles,
            (order[:, None] < order[None]).astype(jnp.bfloat16),
            preferred_element_type=jnp.float32,
        )
        sums = jnp.sum(tiles.astype(jnp.float32), axis=2)
        tile = jnp.arange(count // 128)
        before = jnp.sum(jnp.where(tile[:, None] < tile[None], sums[:, :, None], 0.0), axis=1)
        rank = (within + before[..., None]).reshape(size, size, count) * held.astype(jnp.float32)
        rank = jnp.sum(rank, axis=0).astype(jnp.int32)
        self.full = jnp.max(jnp.sum(sums, axis=1)) > self.room
        self.count, self.vshard = count, vshard
        own = lax.dynamic_index_in_dim(owner, place, 0, keepdims=False)
        self.rank = lax.dynamic_index_in_dim(rank, place, 0, keepdims=False)
        self.behind = lax.rem(place - own + size, size)
        self.slots = jnp.where(owner == place, tokens - place * vshard, vshard)

    def behind_slots(self, room):
        return self.behind * room + jnp.minimum(self.rank, room - 1)


def pack_kernel(ids_ref, table_ref, out_ref, held, *rows):
    step, count, size = pl.program_id(0), out_ref.shape[1], table_ref.shape[0]

    @pl.when(step == 0)
    def _():
        held[0:size, :] = table_ref[...]
        held[size:, :] = jnp.zeros((8, table_ref.shape[1]), jnp.float32)
        for part in rows:
            part[...] = jnp.zeros_like(part)

    base = [(step * len(rows) + index) * count for index in range(len(rows))]

    def some(turn, used):
        used = list(used)
        for by in range(8):
            for index, part in enumerate(rows):
                place = ids_ref[base[index] + turn * 8 + by]
                part[pl.ds(used[index], 1), :] = held[pl.ds(place, 1), :]
                used[index] = used[index] + jnp.where(place < size, 1, 0)
        return tuple(used)

    lax.fori_loop(0, count // 8, some, (0,) * len(rows))
    for index, part in enumerate(rows):
        out_ref[index] = part[0:count, :].astype(out_ref.dtype)


def packed_rows(ids, table):
    size, cols = table.shape
    places, count = ids.shape
    return pl.pallas_call(
        pack_kernel,
        grid_spec=pltpu.PrefetchScalarGridSpec(
            num_scalar_prefetch=1,
            grid=(places // STREAMS,),
            in_specs=[pl.BlockSpec((size, cols), lambda step, ids: (0, 0))],
            out_specs=pl.BlockSpec((STREAMS, count, cols), lambda step, ids: (step, 0, 0)),
            scratch_shapes=[pltpu.VMEM((size + 8, cols), jnp.float32)]
            + [pltpu.VMEM((count + 8, cols), jnp.float32)] * STREAMS,
        ),
        out_shape=jax.ShapeDtypeStruct((places, count, cols), jnp.bfloat16),
        compiler_params=pltpu.CompilerParams(vmem_limit_bytes=40 * 2**20),
        cost_estimate=pl.CostEstimate(flops=0, bytes_accessed=0, transcendentals=0),
        name="pack_rows",
    )(ids.reshape(-1), table)


def take_kernel(ids_ref, table_ref, out_ref, held, rows):
    held[...] = table_ref[...].astype(jnp.float32)

    @pl.loop(0, out_ref.shape[0], step=16)
    def _(first):
        for by in range(16):
            rows[pl.ds(first + by, 1), :] = held[pl.ds(ids_ref[first + by], 1), :]

    out_ref[...] = rows[...].astype(out_ref.dtype)


def taken_rows(ids, table):
    count, cols = ids.shape[0], table.shape[1]
    return pl.pallas_call(
        take_kernel,
        grid_spec=pltpu.PrefetchScalarGridSpec(
            num_scalar_prefetch=1,
            grid=(1,),
            in_specs=[pl.BlockSpec(table.shape, lambda step, ids: (0, 0))],
            out_specs=pl.BlockSpec((count, cols), lambda step, ids: (0, 0)),
            scratch_shapes=[
                pltpu.VMEM(table.shape, jnp.float32),
                pltpu.VMEM((count, cols), jnp.float32),
            ],
        ),
        out_shape=jax.ShapeDtypeStruct((count, cols), table.dtype),
        compiler_params=pltpu.CompilerParams(vmem_limit_bytes=40 * 2**20),
        cost_estimate=FREE,
        name="take_rows",
    )(ids, table)


def add_kernel(ids_ref, values_ref, out_ref, rows, *sums):
    size = out_ref.shape[0]
    places, length = rows.shape[0:2]
    split = len(sums) // places
    each = length // split
    for part in sums:
        part[...] = jnp.zeros_like(part)
    rows[...] = values_ref[:, 0:length, :].astype(jnp.float32)

    @pl.loop(0, each, step=8)
    def _(first):
        for by in range(8):
            for index, part in enumerate(sums):
                at = index % split * each + first + by
                place = ids_ref[index // split * length + at]
                part[pl.ds(place, 1), :] += rows[index // split, pl.ds(at, 1), :]

    total = sums[0][0:size, :]
    for part in sums[1:]:
        total = total + part[0:size, :]
    out_ref[...] = total


def added_rows(ids, values, size):
    places, length = ids.shape
    cols = values.shape[2]
    return pl.pallas_call(
        add_kernel,
        grid_spec=pltpu.PrefetchScalarGridSpec(
            num_scalar_prefetch=1,
            grid=(1,),
            in_specs=[pl.BlockSpec(values.shape, lambda step, ids: (0, 0, 0))],
            out_specs=pl.BlockSpec((size, cols), lambda step, ids: (0, 0)),
            scratch_shapes=[pltpu.VMEM((places, length, cols), jnp.float32)]
            + [pltpu.VMEM((size + 8, cols), jnp.float32)] * (2 * places),
        ),
        out_shape=jax.ShapeDtypeStruct((size, cols), jnp.float32),
        compiler_params=pltpu.CompilerParams(vmem_limit_bytes=62 * 2**20),
        cost_estimate=FREE,
        name="add_rows",
    )(ids.reshape(-1), values)


def span_kernel(stays_ref, momentum_ref, total_ref, moved_ref, error_ref, span_ref, sum_ref):
    @pl.when(pl.program_id(0) == 0)
    def _():
        sum_ref[...] = jnp.zeros_like(sum_ref)

    def write(grad_ref):
        grad = grad_ref[...].astype(jnp.float32)
        span = BETA * momentum_ref[...] + (1.0 - BETA) * grad + error_ref[0]
        span_ref[...] = span
        sum_ref[...] += jnp.sum(jnp.abs(span), axis=0, keepdims=True)

    @pl.when(stays_ref[0] == 1)
    def _():
        write(total_ref)

    @pl.when(stays_ref[0] != 1)
    def _():
        write(moved_ref)


def span_of(momentum, piece, error, start):
    total, moved = piece.result
    rows, cols = total.shape
    block = 1024
    first = start // block
    grad = pl.BlockSpec((rows, block), lambda step, _: (0, step))
    span, sums = pl.pallas_call(
        span_kernel,
        grid_spec=pltpu.PrefetchScalarGridSpec(
            num_scalar_prefetch=1,
            grid=(cols // block,),
            in_specs=[
                pl.BlockSpec((rows, block), lambda step, _: (0, first + step)),
                grad,
                grad,
                pl.BlockSpec((1, rows, block), lambda step, _: (0, 0, first + step)),
            ],
            out_specs=[grad, pl.BlockSpec((1, block), lambda step, _: (0, 0))],
        ),
        out_shape=[
            jax.ShapeDtypeStruct((rows, cols), jnp.float32),
            jax.ShapeDtypeStruct((1, block), jnp.float32),
        ],
        compiler_params=pltpu.CompilerParams(vmem_limit_bytes=60 * 2**20),
        cost_estimate=pl.CostEstimate(flops=0, bytes_accessed=2 * 10**7, transcendentals=0),
        name="span",
    )(piece.stays[None], momentum, total, moved, error)
    return span, jnp.sum(sums)


def press_kernel(steps, core_ref, scale_ref, *refs):
    *span_refs, error_ref, give_ref, keep_ref = refs
    core = pl.program_id(2)
    step = pressed_step(pl.program_id(0), pl.program_id(1), core)
    scale = scale_ref[0]
    inverse = scale_ref[1]
    for index, span_ref in enumerate(span_refs):

        @pl.when((step >= steps[index]) & (step < steps[index + 1]))
        def _():
            span = span_ref[...]
            sent = scale * jnp.tanh(span * inverse)
            error_ref[0] = span - sent
            low = sent.astype(jnp.bfloat16)

            @pl.when(core == core_ref[0])
            def _():
                keep_ref[0] = low

            @pl.when(core != core_ref[0])
            def _():
                give_ref[0] = low


def pressed_step(chip, column, core):
    return (2 * chip + core) * 3 + column


def pressed(spans, scale, parts):
    rows = spans[0].shape[0]
    cols = sum(span.shape[1] for span in spans)
    block = cols // parts // 3
    steps = [0]
    for span in spans:
        steps.append(steps[-1] + span.shape[1] // block)

    def of(index):
        low, count = steps[index], steps[index + 1] - steps[index]

        def place(chip, column, core, _):
            return (0, jnp.clip(pressed_step(chip, column, core) - low, 0, count - 1))

        return pl.BlockSpec((rows, block), place)

    half = pl.BlockSpec((1, rows, block), lambda chip, column, core, _: (chip, 0, column))
    half_shape = jax.ShapeDtypeStruct((parts // 2, rows, cols // parts), jnp.bfloat16)
    return pl.pallas_call(
        functools.partial(press_kernel, steps),
        grid_spec=pltpu.PrefetchScalarGridSpec(
            num_scalar_prefetch=1,
            grid=(parts // 2, 3, 2),
            in_specs=[pl.BlockSpec(memory_space=pltpu.SMEM)] + [of(i) for i in range(len(spans))],
            out_specs=[
                pl.BlockSpec(
                    (1, rows, block),
                    lambda chip, column, core, _: (0, 0, pressed_step(chip, column, core)),
                ),
                half,
                half,
            ],
        ),
        out_shape=[jax.ShapeDtypeStruct((1, rows, cols), jnp.float32), half_shape, half_shape],
        compiler_params=pltpu.CompilerParams(vmem_limit_bytes=60 * 2**20),
        cost_estimate=FREE,
        name="press",
    )(wide_places()[0][None], jnp.stack([scale, 1.0 / scale]), *spans)


def update_kernel(grad_ref, head_ref, table_ref, first_ref, second_ref, *out_refs):
    first_out, update_ref, weight_sum, update_sum = out_refs
    grad = grad_ref[...] + head_ref[...].astype(jnp.float32)
    first = BETA * first_ref[...] + (1.0 - BETA) * grad
    table = table_ref[...]
    update = first / (jnp.sqrt(second_ref[...]) + OPT_EPS) + DECAY * table
    first_out[...] = first
    update_ref[...] = update

    @pl.when(pl.program_id(0) == 0)
    def _():
        weight_sum[...] = jnp.zeros_like(weight_sum)
        update_sum[...] = jnp.zeros_like(update_sum)

    weight_sum[...] += jnp.sum(table * table, axis=0, keepdims=True)
    update_sum[...] += jnp.sum(update * update, axis=0, keepdims=True)


def table_update(grad, head, table, first, second):
    size, cols = table.shape
    block = size // 9 if size % 9 == 0 and size // 9 % 16 == 0 else size
    whole = pl.BlockSpec((block, cols), lambda step: (step, 0))
    line = pl.BlockSpec((1, cols), lambda step: (0, 0))
    moment, update, *sums = pl.pallas_call(
        update_kernel,
        grid=(size // block,),
        in_specs=[whole] * 5,
        out_specs=[whole, whole, line, line],
        out_shape=[jax.ShapeDtypeStruct((size, cols), jnp.float32)] * 2
        + [jax.ShapeDtypeStruct((1, cols), jnp.float32)] * 2,
        compiler_params=pltpu.CompilerParams(vmem_limit_bytes=56 * 2**20),
        cost_estimate=FREE,
        name="update",
    )(grad, head, table, first, second)
    return moment, update, tuple(jnp.sum(part)[None] for part in sums)


def wide_places():
    wide_me = lax.axis_index("wide")
    return wide_me % 2, wide_me // 2 % 2, wide_me // 4


def scattered_sum(give, keep):
    n_wide = lax.axis_size("wide")
    _, x, y = wide_places()

    def send(value, bit):
        return lax.ppermute(value.astype(jnp.bfloat16), "wide", swap_pairs(n_wide, bit))

    take = send(give, 1)
    half = keep.shape[1] // 2

    def chip(y_of, x_of, part):
        start, size = (2 * y_of + x_of, part * half, 0), (1, half, keep.shape[2])
        own, other = lax.dynamic_slice(keep, start, size), lax.dynamic_slice(take, start, size)
        return own[0].astype(jnp.float32) + other[0].astype(jnp.float32)

    upper_far = send(chip(1 - y, 1 - x, 0), 2)
    lower_far = send(chip(1 - y, 1 - x, 1), 4)
    upper_near = send(chip(y, 1 - x, 0), 2)
    lower_near = send(chip(1 - y, x, 1), 4)
    upper_far = send(chip(1 - y, x, 0) + upper_far.astype(jnp.float32), 4)
    lower_far = send(chip(y, 1 - x, 1) + lower_far.astype(jnp.float32), 2)
    own_upper = chip(y, x, 0) + upper_near.astype(jnp.float32) + upper_far.astype(jnp.float32)
    own_lower = chip(y, x, 1) + lower_near.astype(jnp.float32) + lower_far.astype(jnp.float32)
    return jnp.concatenate([own_upper, own_lower], axis=0)


def small_halved(value):
    n_wide = lax.axis_size("wide")
    for bit, place in list(zip((1, 2, 4), wide_places()))[::-1]:
        half = value.shape[1] // 2
        give = lax.dynamic_slice_in_dim(value, (1 - place) * half, half, 1).astype(jnp.bfloat16)
        keep = lax.dynamic_slice_in_dim(value, place * half, half, 1)
        value = keep + lax.ppermute(give, "wide", swap_pairs(n_wide, bit)).astype(jnp.float32)
    return value


def small_update(grad, first, second, weight):
    first = BETA * first + (1.0 - BETA) * grad.astype(jnp.float32)
    return first, first / (jnp.sqrt(second) + OPT_EPS) + DECAY * weight


def shards(
    token_ids,
    doc_ids,
    mlm_pos,
    mlm_labels,
    mlm_valid,
    table,
    table_m,
    table_v,
    small,
    small_m,
    small_v,
    layer,
    layer_m,
    layer_v,
    worker_err,
    server_err,
):
    n_wide, n_narrow = lax.axis_size("wide"), lax.axis_size("narrow")
    narrow_me = lax.axis_index("narrow")
    wide_me = lax.axis_index("wide")
    seqs = doc_ids.shape[0]
    paired = paired_mesh()
    vshard = table.shape[0]
    count = summed_over(jnp.sum(mlm_valid.astype(jnp.float32)), "wide")
    table_low, layer_low = table.astype(jnp.bfloat16), layer.astype(jnp.bfloat16)
    if paired:
        token_ids, mlm_labels, mlm_valid, doc_ids, mlm_pos = hosted_rows(
            token_ids, mlm_labels, mlm_valid, doc_ids, mlm_pos
        )
        table_cut = vshard * 5 // 8 // 16 * 16
        table_first = lax.all_gather(table_low[0:table_cut], "wide", axis=1, tiled=True)
        owners = Owners(token_ids.reshape(n_narrow, n_wide * L), vshard)
        picked = packed_rows(owners.slots, table)
        layer_rows, picked = gathered_near(layer_low, picked)
        layer_rows, table_first = together(layer_rows, table_first)
    else:
        layer_rows = lax.all_gather(layer_low, "narrow", axis=0, tiled=True)
    weights = lax.all_gather(layer_rows, "wide", axis=1, tiled=True)
    if paired:

        def looked_up(room):
            rows = sent_around(picked[:, 0:room])
            return taken_rows(owners.behind_slots(room), jnp.concatenate(rows, axis=0))

        layer_rows, picked = together(layer_rows, picked)
        looked = looked_up(owners.room)
        looked = lax.cond(owners.full, lambda: looked_up(owners.count), lambda: looked)
        looked = lax.all_to_all(looked.reshape(n_wide, L, -1), "wide", 0, 0)
        looked = looked.transpose(1, 0, 2).reshape(1, L, D)
        looked, count, doc_ids, mlm_pos = together(looked, count, doc_ids, mlm_pos)
    else:
        local_ids = token_ids - narrow_me * vshard
        inside = (local_ids >= 0) & (local_ids < vshard)
        slots = jnp.where(inside, local_ids, vshard).reshape(-1)
        table_cols = lax.all_gather(table_low, "wide", axis=1, tiled=True)
        picked = jnp.take(table_cols, jnp.clip(local_ids, 0, vshard - 1), axis=0)
        picked = jnp.where(inside[..., None], picked, 0.0)
        looked = lax.psum_scatter(picked, "narrow", scatter_dimension=0, tiled=True)
    looked = looked.astype(jnp.float32)
    even_doc = (doc_ids % 2 == 0)[..., None]
    embedded = looked + small[0:L][None] + jnp.where(even_doc, small[L], small[L + 1])
    embedded = embedded.reshape(seqs * L, D)
    x0 = norm_rows(embedded, small[L + 2], small[L + 3])
    act = x0.astype(jnp.bfloat16)
    if paired:
        table_cols = jnp.zeros((vshard, D), jnp.bfloat16)
        table_cols = lax.dynamic_update_slice(table_cols, table_first, (0, 0))
        table_last, weights, act, table_cols = together(
            table_low[table_cut:], weights, act, table_cols
        )
        table_last = lax.all_gather(table_last, "wide", axis=1, tiled=True)
        table_cols = lax.dynamic_update_slice(table_cols, table_last, (table_cut, 0))
    htwo, kept = layer_forward(embedded, x0, act, doc_ids, small, weights)
    hmask = jnp.take_along_axis(htwo.reshape(seqs, L, D), mlm_pos[..., None], axis=1)
    hmask = hmask.reshape(seqs * MPS, D).astype(jnp.bfloat16)
    if paired:
        group_h = gathered_near(hmask)
    else:
        group_h = lax.all_gather(hmask, "narrow", axis=0, tiled=True)
    vocab = narrow_me * vshard + jnp.arange(vshard)
    logits = jnp.where((vocab < VREAL)[None], matmul_nt(group_h, table_cols), -1000000000.0)
    labels = mlm_labels.reshape(-1)
    hit = vocab[None] == labels[:, None]
    top = jnp.max(logits, axis=1)
    total = jnp.sum(jnp.exp(logits - top[:, None]), axis=1)
    target = jnp.sum(jnp.where(hit, logits, 0.0), axis=1)
    if paired:
        stats = gathered_near(jnp.stack([top, total, target])[None])
        top, total, target = stats[0]
        for place in range(1, stats.shape[0]):
            top, total, target = merge_rows((top, total, target), tuple(stats[place]))
    else:
        top, total, target = joined((top, total, target), "narrow", merge_rows)
    lse = top + jnp.log(total)
    flags = mlm_valid.reshape(-1).astype(jnp.float32)
    own = seqs * MPS
    own_loss = lax.dynamic_slice_in_dim(flags * (lse - target), narrow_me * own, own)
    dlogit = (
        (jnp.exp(logits - lse[:, None]) - hit.astype(jnp.float32)) * (flags / count)[:, None]
    ).astype(jnp.bfloat16)
    dhmask = matmul(dlogit, table_cols)
    if paired:
        dhmask = scattered_near(dhmask)
        blocks = group_h.reshape(-1, n_wide, D // n_wide)
        table_head = jnp.einsum("sv,swc->wvc", dlogit, blocks, preferred_element_type=jnp.float32)
        table_head, dhmask = together(table_head.astype(jnp.bfloat16), dhmask)
        table_head = lax.psum_scatter(table_head, "wide", scatter_dimension=0)
    else:
        dhmask = lax.psum_scatter(dhmask, "narrow", scatter_dimension=0, tiled=True)
    dhtwo = (
        jnp.zeros((seqs, L, D), jnp.float32)
        .at[jnp.arange(seqs)[:, None], mlm_pos]
        .add(dhmask.reshape(seqs, MPS, D))
    )
    dembed, vectors, pieces = layer_backward(
        dhtwo.reshape(seqs * L, D), kept, doc_ids, small, weights
    )
    dembed_rows = dembed.reshape(seqs, L, D)
    small_grad = jnp.concatenate([jnp.sum(dembed_rows, axis=0), vectors], axis=0)
    mixed = pieces[0]
    if paired:
        cut = dembed.astype(jnp.bfloat16).reshape(L, n_wide, D // n_wide).transpose(1, 0, 2)
        cut = lax.all_to_all(cut, "wide", 0, 0).reshape(n_wide * L, D // n_wide)
        halved = small_halved(small_grad).astype(jnp.bfloat16)
        down, up = pieces[2], pieces[1]
        mixed.away, down.result = together(mixed.away, down.result)
        mixed.finish()
        spans = [span_of(layer_m, up, worker_err, 4 * D)]
        spans.append(span_of(layer_m, down, worker_err, 8 * D))
        cut, mixed.result, spans, table_head = together(
            jnp.concatenate([cut, halved]), mixed.result, spans, table_head
        )
        group_rows = lax.all_gather(cut, "narrow", axis=0)
    else:
        mixed.finish()
        group_rows = lax.all_gather(dembed_rows.astype(jnp.bfloat16), "narrow", axis=0, tiled=True)
        table_grad = matmul_tn(dlogit, group_h).at[slots].add(
            group_rows.reshape(-1, D).astype(jnp.float32), mode="drop"
        )
        cut = table_grad.astype(jnp.bfloat16).reshape(vshard, n_wide, D // n_wide)
        table_grad = lax.psum_scatter(cut.transpose(1, 0, 2), "wide", scatter_dimension=0)
        table_grad = table_grad.astype(jnp.float32)
    part_cols = layer.shape[1]
    if paired:
        spans.insert(0, span_of(layer_m, pieces[0], worker_err, 0))
        total = sum(amount for _, amount in spans)
        spans = [span for span, _ in spans]
        scale = total / (layer_m.shape[0] * layer_m.shape[1]) + MAG_EPS
        new_worker, give, keep = pressed(spans, scale, n_wide)
        server_in = scattered_sum(give, keep) / n_wide + server_err
    else:
        worker_grad = jnp.concatenate([piece.result for piece in pieces], axis=1)
        span = BETA * layer_m + (1.0 - BETA) * worker_grad.astype(jnp.float32) + worker_err[0]
        scale = jnp.mean(jnp.abs(span)) + MAG_EPS
        sent = scale * jnp.tanh(span / scale)
        new_worker = (span - sent)[None]
        summed = lax.psum(sent.astype(jnp.bfloat16), "wide").astype(jnp.float32)
        mixed = lax.dynamic_slice_in_dim(summed, wide_me * part_cols, part_cols, 1) / n_wide
        server_in = mixed + server_err
    sscale = jnp.mean(jnp.abs(server_in)) + MAG_EPS
    server_out = sscale * jnp.tanh(server_in / sscale)
    new_server = server_in - server_out
    server_low = server_out.astype(jnp.bfloat16)
    layer_upd = server_out / (jnp.sqrt(layer_v) + OPT_EPS) + DECAY * layer
    column = wide_me * part_cols + jnp.arange(part_cols)
    which = (
        (column >= 3 * D).astype(jnp.int32)
        + (column >= 4 * D).astype(jnp.int32)
        + (column >= 4 * D + FF).astype(jnp.int32)
    )
    onehot = (which[:, None] == jnp.arange(4)[None]).astype(jnp.float32)
    wsq = jnp.sum(jnp.sum(layer * layer, axis=0)[:, None] * onehot, axis=0)
    usq = jnp.sum(jnp.sum(layer_upd * layer_upd, axis=0)[:, None] * onehot, axis=0)
    small_square = jnp.sum(small * small)[None]
    if paired:
        new_server, wsq, usq, small_square, group_rows = together(
            new_server, wsq, usq, small_square, group_rows
        )
        table_grad = added_rows(owners.slots, group_rows, vshard)
        table_mom, table_upd, table_norms = table_update(
            table_grad, table_head, table, table_m, table_v
        )
        eighth = D // n_wide
        small_grad = jnp.sum(group_rows[:, n_wide * L :].astype(jnp.float32), axis=0)
        small_grad = small_grad.astype(jnp.bfloat16)

        def own(value):
            return lax.dynamic_slice_in_dim(value, wide_me * eighth, eighth, 1)

        _, own_upd = small_update(small_grad, own(small_m), own(small_v), own(small))
        small_norm = jnp.where(narrow_me == 0, jnp.sum(own_upd * own_upd), 0.0)
    else:
        small_grad = lax.psum(small_grad, ("wide", "narrow"))
        table_mom = BETA * table_m + (1.0 - BETA) * table_grad
        table_upd = table_mom / (jnp.sqrt(table_v) + OPT_EPS) + DECAY * table
        table_norms = (jnp.sum(table * table)[None], jnp.sum(table_upd * table_upd)[None])
    new_m = lax.all_gather(server_low, "wide", axis=1, tiled=True)
    if paired:
        small_grad, new_m, table_norms = together(small_grad, new_m, table_norms)
        small_grad = lax.all_gather(small_grad, "wide", axis=1, tiled=True)
    if not paired:
        _, small_upd = small_update(small_grad, small_m, small_v, small)
        small_norm = jnp.where((wide_me == 0) & (narrow_me == 0), jnp.sum(small_upd * small_upd), 0.0)
    alone = (wide_me == 0) & (narrow_me == 0)
    none = jnp.zeros((1,), jnp.float32)
    loss_part, small_part = jnp.sum(own_loss)[None], jnp.where(alone, small_square, 0.0)
    parts = jnp.stack(
        [
            jnp.concatenate([wsq, table_norms[0], small_part, loss_part, none]),
            jnp.concatenate([usq, table_norms[1], small_norm[None], none, none]),
        ]
    )
    sums = summed_over(summed_over(parts, "wide"), "narrow")
    if paired:
        sums, small_grad = together(sums, small_grad)
    small_mom, small_upd = small_update(small_grad, small_m, small_v, small)
    loss_sum = sums[0, 6]
    norms = jnp.sqrt(sums[:, 0:6])
    ratio = norms[0] / norms[1]
    new_layer = layer - RATE * jnp.sum(onehot * ratio[None, 0:4], axis=1)[None] * layer_upd
    new_table = table - RATE * ratio[4] * table_upd
    new_small = small - RATE * ratio[5] * small_upd
    return (
        jnp.stack([loss_sum, count]),
        new_table,
        table_mom,
        new_small,
        small_mom,
        new_layer,
        new_m.astype(jnp.float32),
        new_worker,
        new_server,
        norms,
    )


def solution(mesh):
    placed = (
        P("wide", None),
        P(("wide", "narrow"), None),
        P(("wide", "narrow"), None),
        P("wide", None),
        P("wide", None),
        P("narrow", "wide"),
        P("narrow", "wide"),
        P("narrow", "wide"),
        P(),
        P(),
        P(),
        P("narrow", "wide"),
        P("narrow", None),
        P("narrow", "wide"),
        P("wide", "narrow", None),
        P("narrow", "wide"),
    )
    return jax.shard_map(
        shards,
        mesh=mesh,
        in_specs=placed,
        out_specs=(
            P(),
            P("narrow", "wide"),
            P("narrow", "wide"),
            P(),
            P(),
            P("narrow", "wide"),
            P("narrow", None),
            P("wide", "narrow", None),
            P("narrow", "wide"),
            P(),
        ),
        check_vma=False,
    )
```

```python
import functools

import jax
import jax.numpy as jnp
from jax import lax
from jax.experimental import pallas as pl
from jax.experimental.pallas import tpu as pltpu
from jax.sharding import PartitionSpec as P

D = 1024
HEADS = 16
HEAD = 64
FF = 4096
VREAL = 30522
L = 512
MPS = 80


LN_EPS = 1e-12
BETA = 0.9
DECAY = 0.01
RATE = 0.25
OPT_EPS = 1e-06
MAG_EPS = 1e-08

FREE = pl.CostEstimate(flops=0, bytes_accessed=0, transcendentals=0)


def joined(value, axis, join):
    pieces = jax.tree.map(lambda part: lax.all_gather(part, axis), value)
    head = jax.tree.map(lambda part: part[0], pieces)
    tail = jax.tree.map(lambda part: part[1:], pieces)
    subtotal, _ = lax.scan(lambda subtotal, slab: (join(subtotal, slab), None), head, tail)
    return subtotal


def norm_rows(x, gain, shift):
    mean = jnp.mean(x, axis=-1, keepdims=True)
    cent = x - mean
    var = jnp.mean(cent * cent, axis=-1, keepdims=True)
    return cent * lax.rsqrt(var + LN_EPS) * gain + shift


def matmul(left, right):
    return jnp.dot(left, right, preferred_element_type=jnp.float32)


def matmul_tn(left, right):
    return lax.dot_general(
        left, right, (((0,), (0,)), ((), ())), preferred_element_type=jnp.float32
    )


def matmul_nt(left, right):
    return lax.dot_general(
        left, right, (((1,), (1,)), ((), ())), preferred_element_type=jnp.float32
    )


def attend_kernel(q_ref, k_ref, v_ref, key_doc_ref, query_doc_ref, out_ref, lse_ref):
    same = key_doc_ref[...] == query_doc_ref[...]
    lane = lax.broadcasted_iota(jnp.int32, (1, 2 * HEAD), 1)
    outs = []
    for head in range(2):
        mine = lane // HEAD == head
        query = jnp.where(mine, q_ref[...] * 0.125, 0).astype(jnp.bfloat16)
        scores = jnp.where(same, matmul_nt(k_ref[...], query), -1000000000.0)
        top = jnp.max(scores, axis=0, keepdims=True)
        power = jnp.exp(scores - top)
        total = jnp.sum(power, axis=0, keepdims=True)
        lse_ref[0, head : head + 1, :] = top + jnp.log(total)
        prob = (power * (1.0 / total)).astype(jnp.bfloat16)
        outs.append(matmul_tn(prob, v_ref[...]))
    out_ref[...] = jnp.where(lane < HEAD, outs[0], outs[1]).astype(jnp.bfloat16)


def head_pairs(offset):
    return pl.BlockSpec((L, 2 * HEAD), lambda pair: (0, offset * HEADS // 2 + pair))


def attend(qkv, docs):
    return pl.pallas_call(
        attend_kernel,
        grid=(HEADS // 2,),
        in_specs=[
            head_pairs(0),
            head_pairs(1),
            head_pairs(2),
            pl.BlockSpec((L, 1), lambda pair: (0, 0)),
            pl.BlockSpec((1, L), lambda pair: (0, 0)),
        ],
        out_specs=[head_pairs(0), pl.BlockSpec((1, 2, L), lambda pair: (pair, 0, 0))],
        out_shape=[
            jax.ShapeDtypeStruct((L, D), jnp.bfloat16),
            jax.ShapeDtypeStruct((HEADS // 2, 2, L), jnp.float32),
        ],
        compiler_params=pltpu.CompilerParams(vmem_limit_bytes=40 * 2**20),
        cost_estimate=FREE,
        name="attend",
    )(qkv, qkv, qkv, docs.reshape(L, 1), docs.reshape(1, L))


def attend_back_kernel(q_ref, k_ref, v_ref, do_ref, lse_ref, key_doc_ref, query_doc_ref, out_ref):
    pair = pl.program_id(0)
    same = key_doc_ref[...] == query_doc_ref[...]
    lane = lax.broadcasted_iota(jnp.int32, (1, 2 * HEAD), 1)
    both = []
    for head in range(2):
        mine = lane // HEAD == head
        query = jnp.where(mine, q_ref[...] * 0.125, 0).astype(jnp.bfloat16)
        dout = jnp.where(mine, do_ref[...], 0).astype(jnp.bfloat16)
        scores = jnp.where(same, matmul_nt(k_ref[...], query), -1000000000.0)
        prob = jnp.exp(scores - lse_ref[0, head : head + 1, :])
        dvalue = matmul(prob.astype(jnp.bfloat16), dout)
        dprob = matmul_nt(v_ref[...], dout)
        delta = jnp.sum(prob * dprob, axis=0, keepdims=True)
        dscore = (prob * (dprob - delta)).astype(jnp.bfloat16)
        both.append((matmul_tn(dscore, k_ref[...]) * 0.125, matmul(dscore, query), dvalue))
    for part in range(3):
        value = jnp.where(lane < HEAD, both[0][part], both[1][part]).astype(jnp.bfloat16)
        start = pl.multiple_of(part * D + pair * 2 * HEAD, 2 * HEAD)
        out_ref[:, pl.ds(start, 2 * HEAD)] = value


def attend_back(qkv, dout, lse, docs):
    return pl.pallas_call(
        attend_back_kernel,
        grid=(HEADS // 2,),
        in_specs=[
            head_pairs(0),
            head_pairs(1),
            head_pairs(2),
            head_pairs(0),
            pl.BlockSpec((1, 2, L), lambda pair: (pair, 0, 0)),
            pl.BlockSpec((L, 1), lambda pair: (0, 0)),
            pl.BlockSpec((1, L), lambda pair: (0, 0)),
        ],
        out_specs=pl.BlockSpec((L, 3 * D), lambda pair: (0, 0)),
        out_shape=jax.ShapeDtypeStruct((L, 3 * D), jnp.bfloat16),
        compiler_params=pltpu.CompilerParams(vmem_limit_bytes=40 * 2**20),
        cost_estimate=FREE,
        name="attend_back",
    )(qkv, qkv, qkv, dout, lse, docs.reshape(L, 1), docs.reshape(1, L))


def merge_rows(first, second):
    peak = jnp.maximum(first[0], second[0])
    total = first[1] * jnp.exp(first[0] - peak) + second[1] * jnp.exp(second[0] - peak)
    return (peak, total, first[2] + second[2])


def embed_back_kernel(dqkv_ref, weight_ref, drone_ref, embedded_ref, gain_ref, even_ref, *refs):
    dembed_ref, rows_ref, sums_ref, total = refs
    step = pl.program_id(0)
    dqkv = dqkv_ref[...]
    part = matmul_nt(dqkv, weight_ref[...])
    sums_ref[...] = jnp.sum(dqkv.astype(jnp.float32), axis=0, keepdims=True)

    @pl.when(step == 0)
    def _():
        total[...] = drone_ref[...] + part

    @pl.when(step > 0)
    def _():
        total[...] += part

    @pl.when(step == pl.num_programs(0) - 1)
    def _():
        grad = total[...]
        embedded = embedded_ref[...]
        cent = embedded - jnp.mean(embedded, axis=1, keepdims=True)
        scale = lax.rsqrt(jnp.mean(cent * cent, axis=1, keepdims=True) + LN_EPS)
        normed = cent * scale
        inner = grad * gain_ref[...]
        inner_mean = jnp.mean(inner, axis=1, keepdims=True)
        along = jnp.mean(inner * normed, axis=1, keepdims=True)
        dembed = scale * (inner - inner_mean - normed * along)
        dembed_ref[...] = dembed
        even = even_ref[...]
        rows_ref[0:1, :] = jnp.sum(grad * normed, axis=0, keepdims=True)
        rows_ref[1:2, :] = jnp.sum(grad, axis=0, keepdims=True)
        rows_ref[2:3, :] = jnp.sum(dembed * even, axis=0, keepdims=True)
        rows_ref[3:4, :] = jnp.sum(dembed * (1.0 - even), axis=0, keepdims=True)
        rows_ref[4:8, :] = jnp.zeros((4, D), jnp.float32)


def embed_back(dqkv, weights, drone, embedded, gain, even):
    tokens = dqkv.shape[0]
    whole = pl.BlockSpec((tokens, D), lambda step: (0, 0))
    return pl.pallas_call(
        embed_back_kernel,
        grid=(3,),
        in_specs=[
            pl.BlockSpec((tokens, D), lambda step: (0, step)),
            pl.BlockSpec((D, D), lambda step: (0, step)),
            whole,
            whole,
            pl.BlockSpec((1, D), lambda step: (0, 0)),
            pl.BlockSpec((tokens, 1), lambda step: (0, 0)),
        ],
        out_specs=[
            whole,
            pl.BlockSpec((8, D), lambda step: (0, 0)),
            pl.BlockSpec((1, D), lambda step: (0, step)),
        ],
        out_shape=[
            jax.ShapeDtypeStruct((tokens, D), jnp.float32),
            jax.ShapeDtypeStruct((8, D), jnp.float32),
            jax.ShapeDtypeStruct((1, 3 * D), jnp.float32),
        ],
        scratch_shapes=[pltpu.VMEM((tokens, D), jnp.float32)],
        compiler_params=pltpu.CompilerParams(vmem_limit_bytes=40 * 2**20),
        cost_estimate=FREE,
        name="embed_back",
    )(dqkv, weights, drone, embedded, gain[None], even)


def ffn_kernel(fin_ref, weight_ref, bias_ref, gated_ref, slope_ref):
    upper = matmul(fin_ref[...], weight_ref[...]) + bias_ref[...]
    below = 0.5 + 0.5 * lax.erf(upper * 0.7071067811865476)
    gated_ref[...] = (upper * below).astype(jnp.bfloat16)
    density = 0.3989422804014327 * jnp.exp(-0.5 * upper * upper)
    slope_ref[...] = (below + upper * density).astype(jnp.bfloat16)


def ffn_up(fin, weights, bias):
    tokens = fin.shape[0]
    block = 1024
    first = 4 * D // block
    out = pl.BlockSpec((tokens, block), lambda step: (0, step))
    return pl.pallas_call(
        ffn_kernel,
        grid=(FF // block,),
        in_specs=[
            pl.BlockSpec((tokens, D), lambda step: (0, 0)),
            pl.BlockSpec((D, block), lambda step: (0, first + step)),
            pl.BlockSpec((1, block), lambda step: (0, step)),
        ],
        out_specs=[out, out],
        out_shape=[jax.ShapeDtypeStruct((tokens, FF), jnp.bfloat16)] * 2,
        compiler_params=pltpu.CompilerParams(vmem_limit_bytes=48 * 2**20),
        cost_estimate=pl.CostEstimate(flops=2 * tokens * D * FF, bytes_accessed=0, transcendentals=0),
        name="ffn_up",
    )(fin, weights, bias)


def layer_forward(embedded, x0, act, docs, small, weights):
    base = L + 2
    bias = jnp.concatenate([small[base + 6], jnp.zeros((D,), jnp.float32), small[base + 7]])
    qkv = (matmul(act, weights[:, 0 : 3 * D]) + bias).astype(jnp.bfloat16)
    out, lse = attend(qkv, docs)
    rone = x0 + (matmul(out, weights[:, 3 * D : 4 * D]) + small[base + 8])
    hone = norm_rows(rone, small[base + 2], small[base + 3])
    fin = hone.astype(jnp.bfloat16)
    gated, slope = ffn_up(fin, weights, small[base + 10 :].reshape(1, FF))
    rtwo = hone + (matmul_nt(gated, weights[:, 4 * D + FF :]) + small[base + 9])
    htwo = norm_rows(rtwo, small[base + 4], small[base + 5])
    return (htwo, (embedded, act, qkv, lse, out, rone, fin, slope, gated, rtwo))


def layer_backward(dhtwo, kept, docs, small, weights):
    embedded, act, qkv, lse, out, rone, fin, slope, gated, rtwo = kept
    base = L + 2
    _, pull = jax.vjp(norm_rows, rtwo, small[base + 4], small[base + 5])
    drtwo, dgain_two, dshift_two = pull(dhtwo)
    dffn = drtwo.astype(jnp.bfloat16)
    down = WorkerPiece((dffn, gated))
    dgated = matmul(dffn, weights[:, 4 * D + FF :])
    dupper = (dgated * slope.astype(jnp.float32)).astype(jnp.bfloat16)
    dupper = down.received(dupper)
    dupper = down.across(dupper)
    up = WorkerPiece((fin, dupper))
    dhone = drtwo + matmul_nt(dupper, weights[:, 4 * D : 4 * D + FF])
    _, pull = jax.vjp(norm_rows, rone, small[base + 2], small[base + 3])
    drone, dgain_one, dshift_one = pull(dhone)
    dattn = drone.astype(jnp.bfloat16)
    dout = matmul_nt(dattn, weights[:, 3 * D : 4 * D]).astype(jnp.bfloat16)
    dout = up.received(dout)
    dout = up.across(dout)
    dqkv = attend_back(qkv, dout, lse, docs)
    (dqkv,) = down.crossed(dqkv)
    down.finish()
    mixed = WorkerPiece((act, dqkv), (out, dattn))
    even = (docs.reshape(L, 1) % 2 == 0).astype(jnp.float32)
    dembed, embed_rows, bias_qkv = embed_back(
        mixed.across(dqkv), weights, drone, embedded, small[base], even
    )
    (dembed,) = up.crossed(dembed)
    up.finish()
    vectors = jnp.stack(
        [
            embed_rows[0],
            embed_rows[1],
            dgain_one,
            dshift_one,
            dgain_two,
            dshift_two,
            bias_qkv[0, 0:D],
            bias_qkv[0, 2 * D : 3 * D],
            jnp.sum(dattn, axis=0, dtype=jnp.float32),
            jnp.sum(dffn, axis=0, dtype=jnp.float32),
        ]
    )
    bias_up = jnp.sum(dupper, axis=0, dtype=jnp.float32).reshape(FF // D, D)
    vectors = jnp.concatenate([embed_rows[2:4], vectors, bias_up], axis=0)
    return (dembed, vectors, (mixed, up, down))


def paired_mesh():
    return lax.axis_size("wide") == 8 and lax.axis_size("narrow") == 4


def together(*values):
    return lax.optimization_barrier(values)


def swap_pairs(size, bit):
    return [(place, place ^ bit) for place in range(size)]


def cycle(size, by):
    return [(place, (place + by) % size) for place in range(size)]


def summed_over(value, axis):
    size = lax.axis_size(axis)
    if size & (size - 1):
        return lax.psum(value, axis)
    bit = 1
    while bit < size:
        value = value + lax.ppermute(value, axis, swap_pairs(size, bit))
        bit *= 2
    return value


def gathered_near(value, beside=None):
    size = lax.axis_size("narrow")
    rows = value.shape[0]
    around = [value]
    for by in range(1, size):
        around.append(lax.ppermute(value, "narrow", cycle(size, size - by)))
    if beside is not None:
        *around, beside = together(*around, beside)
    place = lax.axis_index("narrow")
    whole = jnp.zeros((size * rows,) + value.shape[1:], value.dtype)
    for by, part in enumerate(around):
        start = lax.rem(place + by, size) * rows
        whole = lax.dynamic_update_slice_in_dim(whole, part, start, 0)
    return whole if beside is None else (whole, beside)


def scattered_near(value):
    size = lax.axis_size("narrow")
    rows = value.shape[0] // size
    place = lax.axis_index("narrow")
    total = lax.dynamic_slice_in_dim(value, place * rows, rows, 0)
    for by in range(1, size):
        target = lax.rem(place + by, size)
        give = lax.dynamic_slice_in_dim(value, target * rows, rows, 0).astype(jnp.bfloat16)
        take = lax.ppermute(give, "narrow", cycle(size, by))
        total = total + take.astype(jnp.float32)
    return total


def sent_around(blocks):
    size = lax.axis_size("narrow")
    place = lax.axis_index("narrow")

    def block(by):
        return lax.dynamic_index_in_dim(blocks, lax.rem(place + by, size), 0, keepdims=False)

    return [block(0)] + [
        lax.ppermute(block(by), "narrow", cycle(size, by)) for by in range(1, size)
    ]


def block_kernel(steps, place_ref, *refs):
    pairs = len(steps) - 1
    lefts, rights, terms, out_ref = refs[:pairs], refs[pairs : 2 * pairs], refs[2 * pairs : -1], refs[-1]
    step = pl.program_id(0)
    for index in range(pairs):

        @pl.when((step >= steps[index]) & (step < steps[index + 1]))
        def _():
            total = matmul_tn(lefts[index][...], rights[index][...])
            for term_ref in terms:
                total = total + term_ref[...].astype(jnp.float32)
            out_ref[...] = total.astype(jnp.bfloat16)


def gradient_block(pairs, place, terms):
    block = D
    size = D // lax.axis_size("narrow")
    steps = [0]
    for _, right in pairs:
        steps.append(steps[-1] + right.shape[1] // block)
    tokens = pairs[0][0].shape[0]

    def right_of(index):
        low, count = steps[index], steps[index + 1] - steps[index]
        return pl.BlockSpec(
            (tokens, block), lambda step, place: (0, jnp.clip(step - low, 0, count - 1))
        )

    piece = pl.BlockSpec((size, block), lambda step, place: (0, step))
    return pl.pallas_call(
        functools.partial(block_kernel, steps),
        grid_spec=pltpu.PrefetchScalarGridSpec(
            num_scalar_prefetch=1,
            grid=(steps[-1],),
            in_specs=[pl.BlockSpec((tokens, size), lambda step, place: (0, place[0]))] * len(pairs)
            + [right_of(index) for index in range(len(pairs))]
            + [piece] * len(terms),
            out_specs=piece,
        ),
        out_shape=jax.ShapeDtypeStruct((size, steps[-1] * block), jnp.bfloat16),
        compiler_params=pltpu.CompilerParams(vmem_limit_bytes=24 * 2**20),
        cost_estimate=FREE,
        name="gradient_block",
    )(place[None], *[left for left, _ in pairs], *[right for _, right in pairs], *terms)


class WorkerPiece:
    def __init__(self, *pairs):
        self.pairs = pairs
        self.paired = paired_mesh()
        if not self.paired:
            return
        self.core = lax.axis_index("wide") % 2
        self.pair, self.side = lax.axis_index("narrow") // 2, lax.axis_index("narrow") % 2
        cores = swap_pairs(lax.axis_size("wide"), 1)
        self.far = lax.ppermute(self.block(1 - self.core, 1 - self.side), "wide", cores)
        self.near = lax.ppermute(self.block(1 - self.core, self.side), "wide", cores)

    def block(self, core, side, *terms):
        return gradient_block(self.pairs, 2 * core + side, terms)

    def received(self, value):
        if self.paired:
            value, self.far, self.near = together(value, self.far, self.near)
        return value

    def across(self, value):
        if self.paired:
            sides = swap_pairs(lax.axis_size("narrow"), 1)
            away = self.block(self.core, 1 - self.side, self.far)
            away, value = together(away, value)
            self.away = lax.ppermute(away, "narrow", sides)
        return value

    def crossed(self, *values):
        if self.paired:
            *values, self.away = together(*values, self.away)
        return values

    def finish(self, *values):
        if not self.paired:
            blocks = [matmul_tn(left, right).astype(jnp.bfloat16) for left, right in self.pairs]
            grad = jnp.concatenate(blocks, axis=1)
            self.result = lax.psum_scatter(grad, "narrow", scatter_dimension=0, tiled=True)
            return values
        n_wide, n_narrow = lax.axis_size("wide"), lax.axis_size("narrow")
        total = self.block(self.core, self.side, self.near, self.away)
        moves = []
        for wide in range(n_wide):
            for narrow in range(n_narrow):
                if narrow // 2 != wide % 2:
                    target_wide = wide - wide % 2 + narrow // 2
                    target = target_wide * n_narrow + 2 * (wide % 2) + narrow % 2
                    moves.append((wide * n_narrow + narrow, target))
        total, *values = together(total, *values)
        moved = lax.ppermute(total, ("wide", "narrow"), moves)
        self.stays = (self.pair == self.core).astype(jnp.int32)
        self.result = (total, moved)
        return values


def hosted_rows(token_ids, mlm_labels, mlm_valid, doc_ids, mlm_pos):
    n_wide, n_narrow = lax.axis_size("wide"), lax.axis_size("narrow")
    packed = jnp.concatenate([token_ids, mlm_labels, mlm_valid], axis=1)[None]
    for bit, place in zip((1, 2, 4), wide_places()):
        other = lax.ppermute(packed, "wide", swap_pairs(n_wide, bit))
        first, second = jnp.where(place == 0, packed, other), jnp.where(place == 0, other, packed)
        packed = jnp.concatenate([first, second], axis=0)
    width = packed.shape[2]
    hosted = packed.reshape(n_wide // 2, 2, 2, 2, width).transpose(1, 2, 0, 3, 4)
    hosted = hosted.reshape(n_narrow, n_wide, width)
    column = lax.dynamic_index_in_dim(hosted, lax.axis_index("wide"), 1, keepdims=False)
    moves = []
    for wide in range(n_wide):
        for row in range(n_narrow):
            target_wide = wide - wide % 2 + row % 2
            target_narrow = 2 * (wide % 2) + row // 2
            moves.append((wide * n_narrow + row, target_wide * n_narrow + target_narrow))
    own = lax.ppermute(jnp.concatenate([doc_ids, mlm_pos], axis=1), ("wide", "narrow"), moves)
    return (
        hosted[:, :, 0:L],
        column[:, L : L + MPS],
        column[:, L + MPS :],
        own[:, 0:L],
        own[:, L:],
    )


STREAMS = 2


class Owners:
    def __init__(self, tokens, vshard):
        size = lax.axis_size("narrow")
        place = lax.axis_index("narrow")
        count = tokens.shape[1]
        self.room = count * 7 // 16
        owner = tokens // vshard
        held = (owner[None] == jnp.arange(size)[:, None, None]).astype(jnp.bfloat16)
        tiles = held.reshape(-1, count // 128, 128)
        order = jnp.arange(128)
        within = jnp.einsum(
            "btl,lm->btm",
            tiles,
            (order[:, None] < order[None]).astype(jnp.bfloat16),
            preferred_element_type=jnp.float32,
        )
        sums = jnp.sum(tiles.astype(jnp.float32), axis=2)
        tile = jnp.arange(count // 128)
        before = jnp.sum(jnp.where(tile[:, None] < tile[None], sums[:, :, None], 0.0), axis=1)
        rank = (within + before[..., None]).reshape(size, size, count) * held.astype(jnp.float32)
        rank = jnp.sum(rank, axis=0).astype(jnp.int32)
        self.full = jnp.max(jnp.sum(sums, axis=1)) > self.room
        self.count, self.vshard = count, vshard
        own = lax.dynamic_index_in_dim(owner, place, 0, keepdims=False)
        self.rank = lax.dynamic_index_in_dim(rank, place, 0, keepdims=False)
        self.behind = lax.rem(place - own + size, size)
        self.slots = jnp.where(owner == place, tokens - place * vshard, vshard)

    def behind_slots(self, room):
        return self.behind * room + jnp.minimum(self.rank, room - 1)


def pack_kernel(ids_ref, table_ref, out_ref, held, *rows):
    step, count, size = pl.program_id(0), out_ref.shape[1], table_ref.shape[0]

    @pl.when(step == 0)
    def _():
        held[0:size, :] = table_ref[...]
        held[size:, :] = jnp.zeros((8, table_ref.shape[1]), jnp.float32)
        for part in rows:
            part[...] = jnp.zeros_like(part)

    base = [(step * len(rows) + index) * count for index in range(len(rows))]

    def some(turn, used):
        used = list(used)
        for by in range(8):
            for index, part in enumerate(rows):
                place = ids_ref[base[index] + turn * 8 + by]
                part[pl.ds(used[index], 1), :] = held[pl.ds(place, 1), :]
                used[index] = used[index] + jnp.where(place < size, 1, 0)
        return tuple(used)

    lax.fori_loop(0, count // 8, some, (0,) * len(rows))
    for index, part in enumerate(rows):
        out_ref[index] = part[0:count, :].astype(out_ref.dtype)


def packed_rows(ids, table):
    size, cols = table.shape
    places, count = ids.shape
    return pl.pallas_call(
        pack_kernel,
        grid_spec=pltpu.PrefetchScalarGridSpec(
            num_scalar_prefetch=1,
            grid=(places // STREAMS,),
            in_specs=[pl.BlockSpec((size, cols), lambda step, ids: (0, 0))],
            out_specs=pl.BlockSpec((STREAMS, count, cols), lambda step, ids: (step, 0, 0)),
            scratch_shapes=[pltpu.VMEM((size + 8, cols), jnp.float32)]
            + [pltpu.VMEM((count + 8, cols), jnp.float32)] * STREAMS,
        ),
        out_shape=jax.ShapeDtypeStruct((places, count, cols), jnp.bfloat16),
        compiler_params=pltpu.CompilerParams(vmem_limit_bytes=40 * 2**20),
        cost_estimate=pl.CostEstimate(flops=0, bytes_accessed=0, transcendentals=0),
        name="pack_rows",
    )(ids.reshape(-1), table)


def take_kernel(ids_ref, table_ref, out_ref, held, rows):
    held[...] = table_ref[...].astype(jnp.float32)

    @pl.loop(0, out_ref.shape[0], step=16)
    def _(first):
        for by in range(16):
            rows[pl.ds(first + by, 1), :] = held[pl.ds(ids_ref[first + by], 1), :]

    out_ref[...] = rows[...].astype(out_ref.dtype)


def taken_rows(ids, table):
    count, cols = ids.shape[0], table.shape[1]
    return pl.pallas_call(
        take_kernel,
        grid_spec=pltpu.PrefetchScalarGridSpec(
            num_scalar_prefetch=1,
            grid=(1,),
            in_specs=[pl.BlockSpec(table.shape, lambda step, ids: (0, 0))],
            out_specs=pl.BlockSpec((count, cols), lambda step, ids: (0, 0)),
            scratch_shapes=[
                pltpu.VMEM(table.shape, jnp.float32),
                pltpu.VMEM((count, cols), jnp.float32),
            ],
        ),
        out_shape=jax.ShapeDtypeStruct((count, cols), table.dtype),
        compiler_params=pltpu.CompilerParams(vmem_limit_bytes=40 * 2**20),
        cost_estimate=FREE,
        name="take_rows",
    )(ids, table)


def add_kernel(ids_ref, values_ref, out_ref, rows, *sums):
    size = out_ref.shape[0]
    places, length = rows.shape[0:2]
    split = len(sums) // places
    each = length // split
    for part in sums:
        part[...] = jnp.zeros_like(part)
    rows[...] = values_ref[:, 0:length, :].astype(jnp.float32)

    @pl.loop(0, each, step=8)
    def _(first):
        for by in range(8):
            for index, part in enumerate(sums):
                at = index % split * each + first + by
                place = ids_ref[index // split * length + at]
                part[pl.ds(place, 1), :] += rows[index // split, pl.ds(at, 1), :]

    total = sums[0][0:size, :]
    for part in sums[1:]:
        total = total + part[0:size, :]
    out_ref[...] = total


def added_rows(ids, values, size):
    places, length = ids.shape
    cols = values.shape[2]
    return pl.pallas_call(
        add_kernel,
        grid_spec=pltpu.PrefetchScalarGridSpec(
            num_scalar_prefetch=1,
            grid=(1,),
            in_specs=[pl.BlockSpec(values.shape, lambda step, ids: (0, 0, 0))],
            out_specs=pl.BlockSpec((size, cols), lambda step, ids: (0, 0)),
            scratch_shapes=[pltpu.VMEM((places, length, cols), jnp.float32)]
            + [pltpu.VMEM((size + 8, cols), jnp.float32)] * (2 * places),
        ),
        out_shape=jax.ShapeDtypeStruct((size, cols), jnp.float32),
        compiler_params=pltpu.CompilerParams(vmem_limit_bytes=62 * 2**20),
        cost_estimate=FREE,
        name="add_rows",
    )(ids.reshape(-1), values)


def span_kernel(stays_ref, momentum_ref, total_ref, moved_ref, error_ref, span_ref, sum_ref):
    @pl.when(pl.program_id(0) == 0)
    def _():
        sum_ref[...] = jnp.zeros_like(sum_ref)

    def write(grad_ref):
        grad = grad_ref[...].astype(jnp.float32)
        span = BETA * momentum_ref[...] + (1.0 - BETA) * grad + error_ref[0]
        span_ref[...] = span
        sum_ref[...] += jnp.sum(jnp.abs(span), axis=0, keepdims=True)

    @pl.when(stays_ref[0] == 1)
    def _():
        write(total_ref)

    @pl.when(stays_ref[0] != 1)
    def _():
        write(moved_ref)


def span_of(momentum, piece, error, start):
    total, moved = piece.result
    rows, cols = total.shape
    block = 1024
    first = start // block
    grad = pl.BlockSpec((rows, block), lambda step, _: (0, step))
    span, sums = pl.pallas_call(
        span_kernel,
        grid_spec=pltpu.PrefetchScalarGridSpec(
            num_scalar_prefetch=1,
            grid=(cols // block,),
            in_specs=[
                pl.BlockSpec((rows, block), lambda step, _: (0, first + step)),
                grad,
                grad,
                pl.BlockSpec((1, rows, block), lambda step, _: (0, 0, first + step)),
            ],
            out_specs=[grad, pl.BlockSpec((1, block), lambda step, _: (0, 0))],
        ),
        out_shape=[
            jax.ShapeDtypeStruct((rows, cols), jnp.float32),
            jax.ShapeDtypeStruct((1, block), jnp.float32),
        ],
        compiler_params=pltpu.CompilerParams(vmem_limit_bytes=60 * 2**20),
        cost_estimate=pl.CostEstimate(flops=0, bytes_accessed=2 * 10**7, transcendentals=0),
        name="span",
    )(piece.stays[None], momentum, total, moved, error)
    return span, jnp.sum(sums)


def press_kernel(steps, core_ref, scale_ref, *refs):
    *span_refs, error_ref, give_ref, keep_ref = refs
    core = pl.program_id(2)
    step = pressed_step(pl.program_id(0), pl.program_id(1), core)
    scale = scale_ref[0]
    inverse = scale_ref[1]
    for index, span_ref in enumerate(span_refs):

        @pl.when((step >= steps[index]) & (step < steps[index + 1]))
        def _():
            span = span_ref[...]
            sent = scale * jnp.tanh(span * inverse)
            error_ref[0] = span - sent
            low = sent.astype(jnp.bfloat16)

            @pl.when(core == core_ref[0])
            def _():
                keep_ref[0] = low

            @pl.when(core != core_ref[0])
            def _():
                give_ref[0] = low


def pressed_step(chip, column, core):
    return (2 * chip + core) * 3 + column


def pressed(spans, scale, parts):
    rows = spans[0].shape[0]
    cols = sum(span.shape[1] for span in spans)
    block = cols // parts // 3
    steps = [0]
    for span in spans:
        steps.append(steps[-1] + span.shape[1] // block)

    def of(index):
        low, count = steps[index], steps[index + 1] - steps[index]

        def place(chip, column, core, _):
            return (0, jnp.clip(pressed_step(chip, column, core) - low, 0, count - 1))

        return pl.BlockSpec((rows, block), place)

    half = pl.BlockSpec((1, rows, block), lambda chip, column, core, _: (chip, 0, column))
    half_shape = jax.ShapeDtypeStruct((parts // 2, rows, cols // parts), jnp.bfloat16)
    return pl.pallas_call(
        functools.partial(press_kernel, steps),
        grid_spec=pltpu.PrefetchScalarGridSpec(
            num_scalar_prefetch=1,
            grid=(parts // 2, 3, 2),
            in_specs=[pl.BlockSpec(memory_space=pltpu.SMEM)] + [of(i) for i in range(len(spans))],
            out_specs=[
                pl.BlockSpec(
                    (1, rows, block),
                    lambda chip, column, core, _: (0, 0, pressed_step(chip, column, core)),
                ),
                half,
                half,
            ],
        ),
        out_shape=[jax.ShapeDtypeStruct((1, rows, cols), jnp.float32), half_shape, half_shape],
        compiler_params=pltpu.CompilerParams(vmem_limit_bytes=60 * 2**20),
        cost_estimate=FREE,
        name="press",
    )(wide_places()[0][None], jnp.stack([scale, 1.0 / scale]), *spans)


def update_kernel(grad_ref, head_ref, table_ref, first_ref, second_ref, *out_refs):
    first_out, update_ref, weight_sum, update_sum = out_refs
    grad = grad_ref[...] + head_ref[...].astype(jnp.float32)
    first = BETA * first_ref[...] + (1.0 - BETA) * grad
    table = table_ref[...]
    update = first / (jnp.sqrt(second_ref[...]) + OPT_EPS) + DECAY * table
    first_out[...] = first
    update_ref[...] = update

    @pl.when(pl.program_id(0) == 0)
    def _():
        weight_sum[...] = jnp.zeros_like(weight_sum)
        update_sum[...] = jnp.zeros_like(update_sum)

    weight_sum[...] += jnp.sum(table * table, axis=0, keepdims=True)
    update_sum[...] += jnp.sum(update * update, axis=0, keepdims=True)


def table_update(grad, head, table, first, second):
    size, cols = table.shape
    block = size // 3 if size % 3 == 0 and size // 3 % 16 == 0 else size
    whole = pl.BlockSpec((block, cols), lambda step: (step, 0))
    line = pl.BlockSpec((1, cols), lambda step: (0, 0))
    moment, update, *sums = pl.pallas_call(
        update_kernel,
        grid=(size // block,),
        in_specs=[whole] * 5,
        out_specs=[whole, whole, line, line],
        out_shape=[jax.ShapeDtypeStruct((size, cols), jnp.float32)] * 2
        + [jax.ShapeDtypeStruct((1, cols), jnp.float32)] * 2,
        compiler_params=pltpu.CompilerParams(vmem_limit_bytes=56 * 2**20),
        cost_estimate=FREE,
        name="update",
    )(grad, head, table, first, second)
    return moment, update, tuple(jnp.sum(part)[None] for part in sums)


def wide_places():
    wide_me = lax.axis_index("wide")
    return wide_me % 2, wide_me // 2 % 2, wide_me // 4


def scattered_sum(give, keep):
    n_wide = lax.axis_size("wide")
    _, x, y = wide_places()

    def send(value, bit):
        return lax.ppermute(value.astype(jnp.bfloat16), "wide", swap_pairs(n_wide, bit))

    take = send(give, 1)
    half = keep.shape[1] // 2

    def chip(y_of, x_of, part):
        start, size = (2 * y_of + x_of, part * half, 0), (1, half, keep.shape[2])
        own, other = lax.dynamic_slice(keep, start, size), lax.dynamic_slice(take, start, size)
        return own[0].astype(jnp.float32) + other[0].astype(jnp.float32)

    upper_far = send(chip(1 - y, 1 - x, 0), 2)
    lower_far = send(chip(1 - y, 1 - x, 1), 4)
    upper_near = send(chip(y, 1 - x, 0), 2)
    lower_near = send(chip(1 - y, x, 1), 4)
    upper_far = send(chip(1 - y, x, 0) + upper_far.astype(jnp.float32), 4)
    lower_far = send(chip(y, 1 - x, 1) + lower_far.astype(jnp.float32), 2)
    own_upper = chip(y, x, 0) + upper_near.astype(jnp.float32) + upper_far.astype(jnp.float32)
    own_lower = chip(y, x, 1) + lower_near.astype(jnp.float32) + lower_far.astype(jnp.float32)
    return jnp.concatenate([own_upper, own_lower], axis=0)


def small_halved(value):
    n_wide = lax.axis_size("wide")
    for bit, place in list(zip((1, 2, 4), wide_places()))[::-1]:
        half = value.shape[1] // 2
        give = lax.dynamic_slice_in_dim(value, (1 - place) * half, half, 1).astype(jnp.bfloat16)
        keep = lax.dynamic_slice_in_dim(value, place * half, half, 1)
        value = keep + lax.ppermute(give, "wide", swap_pairs(n_wide, bit)).astype(jnp.float32)
    return value


def small_update(grad, first, second, weight):
    first = BETA * first + (1.0 - BETA) * grad.astype(jnp.float32)
    return first, first / (jnp.sqrt(second) + OPT_EPS) + DECAY * weight


def shards(
    token_ids,
    doc_ids,
    mlm_pos,
    mlm_labels,
    mlm_valid,
    table,
    table_m,
    table_v,
    small,
    small_m,
    small_v,
    layer,
    layer_m,
    layer_v,
    worker_err,
    server_err,
):
    n_wide, n_narrow = lax.axis_size("wide"), lax.axis_size("narrow")
    narrow_me = lax.axis_index("narrow")
    wide_me = lax.axis_index("wide")
    seqs = doc_ids.shape[0]
    paired = paired_mesh()
    vshard = table.shape[0]
    count = summed_over(jnp.sum(mlm_valid.astype(jnp.float32)), "wide")
    table_low, layer_low = table.astype(jnp.bfloat16), layer.astype(jnp.bfloat16)
    if paired:
        token_ids, mlm_labels, mlm_valid, doc_ids, mlm_pos = hosted_rows(
            token_ids, mlm_labels, mlm_valid, doc_ids, mlm_pos
        )
        table_cut = vshard * 5 // 8 // 16 * 16
        table_first = lax.all_gather(table_low[0:table_cut], "wide", axis=1, tiled=True)
        owners = Owners(token_ids.reshape(n_narrow, n_wide * L), vshard)
        picked = packed_rows(owners.slots, table)
        layer_rows, picked = gathered_near(layer_low, picked)
        layer_rows, table_first = together(layer_rows, table_first)
    else:
        layer_rows = lax.all_gather(layer_low, "narrow", axis=0, tiled=True)
    weights = lax.all_gather(layer_rows, "wide", axis=1, tiled=True)
    if paired:

        def looked_up(room):
            rows = sent_around(picked[:, 0:room])
            return taken_rows(owners.behind_slots(room), jnp.concatenate(rows, axis=0))

        layer_rows, picked = together(layer_rows, picked)
        looked = looked_up(owners.room)
        looked = lax.cond(owners.full, lambda: looked_up(owners.count), lambda: looked)
        looked = lax.all_to_all(looked.reshape(n_wide, L, -1), "wide", 0, 0)
        looked = looked.transpose(1, 0, 2).reshape(1, L, D)
        looked, count, doc_ids, mlm_pos = together(looked, count, doc_ids, mlm_pos)
    else:
        local_ids = token_ids - narrow_me * vshard
        inside = (local_ids >= 0) & (local_ids < vshard)
        slots = jnp.where(inside, local_ids, vshard).reshape(-1)
        table_cols = lax.all_gather(table_low, "wide", axis=1, tiled=True)
        picked = jnp.take(table_cols, jnp.clip(local_ids, 0, vshard - 1), axis=0)
        picked = jnp.where(inside[..., None], picked, 0.0)
        looked = lax.psum_scatter(picked, "narrow", scatter_dimension=0, tiled=True)
    looked = looked.astype(jnp.float32)
    even_doc = (doc_ids % 2 == 0)[..., None]
    embedded = looked + small[0:L][None] + jnp.where(even_doc, small[L], small[L + 1])
    embedded = embedded.reshape(seqs * L, D)
    x0 = norm_rows(embedded, small[L + 2], small[L + 3])
    act = x0.astype(jnp.bfloat16)
    if paired:
        table_cols = jnp.zeros((vshard, D), jnp.bfloat16)
        table_cols = lax.dynamic_update_slice(table_cols, table_first, (0, 0))
        table_last, weights, act, table_cols = together(
            table_low[table_cut:], weights, act, table_cols
        )
        table_last = lax.all_gather(table_last, "wide", axis=1, tiled=True)
        table_cols = lax.dynamic_update_slice(table_cols, table_last, (table_cut, 0))
    htwo, kept = layer_forward(embedded, x0, act, doc_ids, small, weights)
    hmask = jnp.take_along_axis(htwo.reshape(seqs, L, D), mlm_pos[..., None], axis=1)
    hmask = hmask.reshape(seqs * MPS, D).astype(jnp.bfloat16)
    if paired:
        group_h = gathered_near(hmask)
    else:
        group_h = lax.all_gather(hmask, "narrow", axis=0, tiled=True)
    vocab = narrow_me * vshard + jnp.arange(vshard)
    logits = jnp.where((vocab < VREAL)[None], matmul_nt(group_h, table_cols), -1000000000.0)
    labels = mlm_labels.reshape(-1)
    hit = vocab[None] == labels[:, None]
    top = jnp.max(logits, axis=1)
    total = jnp.sum(jnp.exp(logits - top[:, None]), axis=1)
    target = jnp.sum(jnp.where(hit, logits, 0.0), axis=1)
    if paired:
        stats = gathered_near(jnp.stack([top, total, target])[None])
        top, total, target = stats[0]
        for place in range(1, stats.shape[0]):
            top, total, target = merge_rows((top, total, target), tuple(stats[place]))
    else:
        top, total, target = joined((top, total, target), "narrow", merge_rows)
    lse = top + jnp.log(total)
    flags = mlm_valid.reshape(-1).astype(jnp.float32)
    own = seqs * MPS
    own_loss = lax.dynamic_slice_in_dim(flags * (lse - target), narrow_me * own, own)
    dlogit = (
        (jnp.exp(logits - lse[:, None]) - hit.astype(jnp.float32)) * (flags / count)[:, None]
    ).astype(jnp.bfloat16)
    dhmask = matmul(dlogit, table_cols)
    if paired:
        dhmask = scattered_near(dhmask)
        blocks = group_h.reshape(-1, n_wide, D // n_wide)
        table_head = jnp.einsum("sv,swc->wvc", dlogit, blocks, preferred_element_type=jnp.float32)
        table_head, dhmask = together(table_head.astype(jnp.bfloat16), dhmask)
        table_head = lax.psum_scatter(table_head, "wide", scatter_dimension=0)
    else:
        dhmask = lax.psum_scatter(dhmask, "narrow", scatter_dimension=0, tiled=True)
    dhtwo = (
        jnp.zeros((seqs, L, D), jnp.float32)
        .at[jnp.arange(seqs)[:, None], mlm_pos]
        .add(dhmask.reshape(seqs, MPS, D))
    )
    dembed, vectors, pieces = layer_backward(
        dhtwo.reshape(seqs * L, D), kept, doc_ids, small, weights
    )
    dembed_rows = dembed.reshape(seqs, L, D)
    small_grad = jnp.concatenate([jnp.sum(dembed_rows, axis=0), vectors], axis=0)
    mixed = pieces[0]
    if paired:
        cut = dembed.astype(jnp.bfloat16).reshape(L, n_wide, D // n_wide).transpose(1, 0, 2)
        cut = lax.all_to_all(cut, "wide", 0, 0).reshape(n_wide * L, D // n_wide)
        halved = small_halved(small_grad).astype(jnp.bfloat16)
        down, up = pieces[2], pieces[1]
        mixed.away, down.result = together(mixed.away, down.result)
        mixed.finish()
        spans = [span_of(layer_m, up, worker_err, 4 * D)]
        spans.append(span_of(layer_m, down, worker_err, 8 * D))
        cut, mixed.result, spans, table_head = together(
            jnp.concatenate([cut, halved]), mixed.result, spans, table_head
        )
        group_rows = lax.all_gather(cut, "narrow", axis=0)
    else:
        mixed.finish()
        group_rows = lax.all_gather(dembed_rows.astype(jnp.bfloat16), "narrow", axis=0, tiled=True)
        table_grad = matmul_tn(dlogit, group_h).at[slots].add(
            group_rows.reshape(-1, D).astype(jnp.float32), mode="drop"
        )
        cut = table_grad.astype(jnp.bfloat16).reshape(vshard, n_wide, D // n_wide)
        table_grad = lax.psum_scatter(cut.transpose(1, 0, 2), "wide", scatter_dimension=0)
        table_grad = table_grad.astype(jnp.float32)
    part_cols = layer.shape[1]
    if paired:
        spans.insert(0, span_of(layer_m, pieces[0], worker_err, 0))
        total = sum(amount for _, amount in spans)
        spans = [span for span, _ in spans]
        scale = total / (layer_m.shape[0] * layer_m.shape[1]) + MAG_EPS
        new_worker, give, keep = pressed(spans, scale, n_wide)
        server_in = scattered_sum(give, keep) / n_wide + server_err
    else:
        worker_grad = jnp.concatenate([piece.result for piece in pieces], axis=1)
        span = BETA * layer_m + (1.0 - BETA) * worker_grad.astype(jnp.float32) + worker_err[0]
        scale = jnp.mean(jnp.abs(span)) + MAG_EPS
        sent = scale * jnp.tanh(span / scale)
        new_worker = (span - sent)[None]
        summed = lax.psum(sent.astype(jnp.bfloat16), "wide").astype(jnp.float32)
        mixed = lax.dynamic_slice_in_dim(summed, wide_me * part_cols, part_cols, 1) / n_wide
        server_in = mixed + server_err
    sscale = jnp.mean(jnp.abs(server_in)) + MAG_EPS
    server_out = sscale * jnp.tanh(server_in / sscale)
    new_server = server_in - server_out
    server_low = server_out.astype(jnp.bfloat16)
    layer_upd = server_out / (jnp.sqrt(layer_v) + OPT_EPS) + DECAY * layer
    column = wide_me * part_cols + jnp.arange(part_cols)
    which = (
        (column >= 3 * D).astype(jnp.int32)
        + (column >= 4 * D).astype(jnp.int32)
        + (column >= 4 * D + FF).astype(jnp.int32)
    )
    onehot = (which[:, None] == jnp.arange(4)[None]).astype(jnp.float32)
    wsq = jnp.sum(jnp.sum(layer * layer, axis=0)[:, None] * onehot, axis=0)
    usq = jnp.sum(jnp.sum(layer_upd * layer_upd, axis=0)[:, None] * onehot, axis=0)
    small_square = jnp.sum(small * small)[None]
    if paired:
        new_server, wsq, usq, small_square, group_rows = together(
            new_server, wsq, usq, small_square, group_rows
        )
        table_grad = added_rows(owners.slots, group_rows, vshard)
        table_mom, table_upd, table_norms = table_update(
            table_grad, table_head, table, table_m, table_v
        )
        eighth = D // n_wide
        small_grad = jnp.sum(group_rows[:, n_wide * L :].astype(jnp.float32), axis=0)
        small_grad = small_grad.astype(jnp.bfloat16)

        def own(value):
            return lax.dynamic_slice_in_dim(value, wide_me * eighth, eighth, 1)

        _, own_upd = small_update(small_grad, own(small_m), own(small_v), own(small))
        small_norm = jnp.where(narrow_me == 0, jnp.sum(own_upd * own_upd), 0.0)
    else:
        small_grad = lax.psum(small_grad, ("wide", "narrow"))
        table_mom = BETA * table_m + (1.0 - BETA) * table_grad
        table_upd = table_mom / (jnp.sqrt(table_v) + OPT_EPS) + DECAY * table
        table_norms = (jnp.sum(table * table)[None], jnp.sum(table_upd * table_upd)[None])
    new_m = lax.all_gather(server_low, "wide", axis=1, tiled=True)
    if paired:
        small_grad, new_m, table_norms = together(small_grad, new_m, table_norms)
        small_grad = lax.all_gather(small_grad, "wide", axis=1, tiled=True)
    if not paired:
        _, small_upd = small_update(small_grad, small_m, small_v, small)
        small_norm = jnp.where((wide_me == 0) & (narrow_me == 0), jnp.sum(small_upd * small_upd), 0.0)
    alone = (wide_me == 0) & (narrow_me == 0)
    none = jnp.zeros((1,), jnp.float32)
    loss_part, small_part = jnp.sum(own_loss)[None], jnp.where(alone, small_square, 0.0)
    parts = jnp.stack(
        [
            jnp.concatenate([wsq, table_norms[0], small_part, loss_part, none]),
            jnp.concatenate([usq, table_norms[1], small_norm[None], none, none]),
        ]
    )
    sums = summed_over(summed_over(parts, "wide"), "narrow")
    if paired:
        sums, small_grad = together(sums, small_grad)
    small_mom, small_upd = small_update(small_grad, small_m, small_v, small)
    loss_sum = sums[0, 6]
    norms = jnp.sqrt(sums[:, 0:6])
    ratio = norms[0] / norms[1]
    new_layer = layer - RATE * jnp.sum(onehot * ratio[None, 0:4], axis=1)[None] * layer_upd
    new_table = table - RATE * ratio[4] * table_upd
    new_small = small - RATE * ratio[5] * small_upd
    return (
        jnp.stack([loss_sum, count]),
        new_table,
        table_mom,
        new_small,
        small_mom,
        new_layer,
        new_m.astype(jnp.float32),
        new_worker,
        new_server,
        norms,
    )


def solution(mesh):
    placed = (
        P("wide", None),
        P(("wide", "narrow"), None),
        P(("wide", "narrow"), None),
        P("wide", None),
        P("wide", None),
        P("narrow", "wide"),
        P("narrow", "wide"),
        P("narrow", "wide"),
        P(),
        P(),
        P(),
        P("narrow", "wide"),
        P("narrow", None),
        P("narrow", "wide"),
        P("wide", "narrow", None),
        P("narrow", "wide"),
    )
    return jax.shard_map(
        shards,
        mesh=mesh,
        in_specs=placed,
        out_specs=(
            P(),
            P("narrow", "wide"),
            P("narrow", "wide"),
            P(),
            P(),
            P("narrow", "wide"),
            P("narrow", None),
            P("wide", "narrow", None),
            P("narrow", "wide"),
            P(),
        ),
        check_vma=False,
    )
```
